32 devices in a mesh: dp: 8 (over z, y), seq: 4 (over x, core).
Axes of the slice: x: 2, y: 2, z: 4, core: 2. Of those that a mesh axis runs over, the one named last changes fastest.
Arguments:
- tokens: bfloat16 [8, 1024, 1024], P('dp', 'seq'), may hold values from -6 to 6
- lead_hours: int32 [8], P('dp'), may hold values from 6 to 168
- valid_counts: int32 [8], P('dp'), may hold values from 769 to 1024
- patch_mask: int32 [8, 1024], P('dp', 'seq'), may hold values 0 or 1
- first_gain: bfloat16 [1024], P(('dp', 'seq')), may hold values from 0.099609375 to 1.8984375
- first_shift: bfloat16 [1024], P(('dp', 'seq')), may hold values from -4 to 4
- qkv_weight: bfloat16 [1024, 3072], P(('dp', 'seq')), may hold values from -0.1875 to 0.1875
- query_bias: bfloat16 [1024], P(('dp', 'seq')), may hold values from -6 to 6
- value_bias: bfloat16 [1024], P(('dp', 'seq')), may hold values from -0.3125 to 0.3125
- out_weight: bfloat16 [1024, 1024], P(('dp', 'seq')), may hold values from -4 to 4
- out_bias: bfloat16 [1024], P(('dp', 'seq')), may hold values from -4 to 4
- second_gain: bfloat16 [1024], P(('dp', 'seq')), may hold values from 0.099609375 to 1.8984375
- second_shift: bfloat16 [1024], P(('dp', 'seq')), may hold values from -4 to 4
- up_weight: bfloat16 [1024, 4096], P(('dp', 'seq')), may hold values from -0.1875 to 0.1875
- up_bias: bfloat16 [4096], P(('dp', 'seq')), may hold values from -6 to 6
- down_weight: bfloat16 [4096, 1024], P(('dp', 'seq')), may hold values from -0.09375 to 0.09375
- down_bias: bfloat16 [1024], P(('dp', 'seq')), may hold values from -4 to 4
- lead_weight: bfloat16 [1024], P(('dp', 'seq')), may hold values from -6 to 6
- lead_bias: bfloat16 [1024], P(('dp', 'seq')), may hold values from -4 to 4
- cotangent: bfloat16 [8, 1024, 1024], P('dp', 'seq'), may hold values from -6 to 6
Outputs:
- block_out: bfloat16 [8, 1024, 1024], P('dp', 'seq')
- tokens_grad: bfloat16 [8, 1024, 1024], P('dp', 'seq')
- first_gain_grad: float32 [1024], P(('dp', 'seq'))
- first_shift_grad: float32 [1024], P(('dp', 'seq'))
- qkv_weight_grad: float32 [1024, 3072], P(('dp', 'seq'))
- query_bias_grad: float32 [1024], P(('dp', 'seq'))
- value_bias_grad: float32 [1024], P(('dp', 'seq'))
- out_weight_grad: float32 [1024, 1024], P(('dp', 'seq'))
- out_bias_grad: float32 [1024], P(('dp', 'seq'))
- second_gain_grad: float32 [1024], P(('dp', 'seq'))
- second_shift_grad: float32 [1024], P(('dp', 'seq'))
- up_weight_grad: float32 [1024, 4096], P(('dp', 'seq'))
- up_bias_grad: float32 [4096], P(('dp', 'seq'))
- down_weight_grad: float32 [4096, 1024], P(('dp', 'seq'))
- down_bias_grad: float32 [1024], P(('dp', 'seq'))
- lead_weight_grad: float32 [1024], P(('dp', 'seq'))
- lead_bias_grad: float32 [1024], P(('dp', 'seq'))
The draws below stay inside these ranges and needn't reach their ends.
All inputs are finite; a program needn't handle non-finite values. No bound on the sum of `patch_mask` on one device may be relied on, other than what follows from the above.
Results may differ from the reference program's by a relative error of at most 0.014.
Values may be sent and summed in bfloat16 or wider, within the bound.
No kernel may reach another device: no remote copies, remote signals or barrier semaphores. Data moves between devices by JAX's collectives and lax.ppermute only.
A program may use at most 256 MiB of HBM per device.

```python
import math
import jax
import jax.numpy as jnp
from jax import lax

D = 1024
HEADS = 16
HEAD_DIM = 64
FF = 4096
SAMPLES = 8
SEQ_LEN = 1024
TOK_DEV = 256


def with_ends(values, own_key, least, largest):
    longest = values.shape.index(max(values.shape))
    spots = []
    for shift in (0, 1):
        where = [jax.random.randint(jax.random.fold_in(own_key, axis), (), 0, length) for axis, length in enumerate(values.shape)]
        where[longest] = (where[longest] + shift) % values.shape[longest]
        spots.append(tuple(where))
    return values.at[spots[0]].set(least).at[spots[1]].set(largest)


def raised(array, rng, source, target, parts, factor):
    owner, partner = [(jnp.arange(array.shape[position]) // (array.shape[position] // parts)).reshape([-1 if axis == position else 1 for axis in range(array.ndim)]) for position in (source, target)]
    chosen = jax.random.permutation(rng, parts)[partner]
    strong = (owner == chosen) | (owner == (partner + parts // 2) % parts)
    return jnp.where(strong, factor * array, array)


def block_levels(own_key, shape, pieces, least, high):
    def one(dim, parts):
        draws = jax.random.uniform(jax.random.fold_in(jax.random.fold_in(own_key, 6), dim), (parts,), jnp.float32, least / len(pieces), high / len(pieces))
        return jnp.repeat(jnp.exp(draws), shape[dim] // parts).reshape((-1,) + (1,) * (len(shape) - dim - 1))

    factor_of = one(*pieces[0])
    for cut in pieces[1:]:
        factor_of = factor_of * one(*cut)
    return factor_of


def gaussian(own_key, extent, deviation, most, shards=(), dtype=jnp.bfloat16):
    values = jax.random.normal(own_key, extent, jnp.float32) * deviation
    if len(shards) > 0:
        values = block_levels(own_key, extent, shards, -0.22, 0.18) * values
    return jnp.clip(values, min=-most, max=most).astype(dtype)


def bell_draw_with(rng, shape, deviation, limit, pieces, heavy, dtype=jnp.bfloat16):
    entries = deviation * jax.random.normal(rng, shape, jnp.float32)
    if pieces:
        entries = entries * block_levels(rng, shape, pieces, -0.22, 0.18)
    return jnp.clip(raised(entries, jax.random.fold_in(rng, 3), *heavy), -limit, limit).astype(dtype)


def setup_inputs(seed: int = 0) -> dict:
    streams_of = jax.random.split(jax.random.key(seed), 21)
    tokens = bell_draw_with(streams_of[0], (SAMPLES, SEQ_LEN, D), 1.0, 6.0, ((0, 8), (1, 4)), (0, 2, 8, 2.0))
    lead_hours = with_ends(jax.random.randint(streams_of[1], (SAMPLES,), 6, 169), jax.random.fold_in(streams_of[1], 1), 6, 168).astype(jnp.int32)
    valid_counts = with_ends(jax.random.randint(streams_of[2], (SAMPLES,), SEQ_LEN - TOK_DEV + 1, SEQ_LEN + 1), jax.random.fold_in(streams_of[2], 1), SEQ_LEN - TOK_DEV + 1, SEQ_LEN).astype(jnp.int32)
    patch_mask = with_ends((jax.random.randint(streams_of[3], (SAMPLES, SEQ_LEN), 0, 8) < 7).astype(jnp.int32), jax.random.fold_in(streams_of[3], 1), 0, 1)
    first_gain = jnp.clip(1.0 + 0.18 * jax.random.normal(streams_of[4], (D,), jnp.float32), 0.099609375, 1.8984375).astype(jnp.bfloat16)
    first_shift = gaussian(streams_of[5], (D,), 0.3, 4.0, ((0, 32),))
    qkv_weight = gaussian(streams_of[6], (D, 3 * D), D ** -0.5, 0.1875, ((0, 32),))
    query_bias = gaussian(streams_of[7], (D,), 0.5, 6.0, ((0, 32),))
    value_bias = gaussian(streams_of[8], (D,), 0.02, 0.3125, ((0, 32),))
    out_weight = gaussian(streams_of[9], (D, D), (max(1, 2 * D // SEQ_LEN)) ** -0.5, 4.0, ((0, 32),))
    out_bias = gaussian(streams_of[10], (D,), 0.3, 4.0, ((0, 32),))
    second_gain = jnp.clip(1.0 + 0.18 * jax.random.normal(streams_of[11], (D,), jnp.float32), 0.099609375, 1.8984375).astype(jnp.bfloat16)
    second_shift = gaussian(streams_of[12], (D,), 0.3, 4.0, ((0, 32),))
    up_weight = gaussian(streams_of[13], (D, FF), D ** -0.5, 0.1875, ((0, 32),))
    up_bias = gaussian(streams_of[14], (FF,), 0.5, 6.0, ((0, 32),))
    down_weight = gaussian(streams_of[15], (FF, D), FF ** -0.5, 0.09375, ((0, 32),))
    down_bias = gaussian(streams_of[16], (D,), 0.3, 4.0, ((0, 32),))
    lead_weight = gaussian(streams_of[17], (D,), 0.5, 6.0, ((0, 32),))
    lead_bias = gaussian(streams_of[18], (D,), 0.3, 4.0, ((0, 32),))
    cotangent = gaussian(streams_of[19], (SAMPLES, SEQ_LEN, D), 1.0, 6.0, ((0, 8), (1, 4)))
    return dict(tokens=tokens, lead_hours=lead_hours, valid_counts=valid_counts, patch_mask=patch_mask, first_gain=first_gain, first_shift=first_shift, qkv_weight=qkv_weight, query_bias=query_bias, value_bias=value_bias, out_weight=out_weight, out_bias=out_bias, second_gain=second_gain, second_shift=second_shift, up_weight=up_weight, up_bias=up_bias, down_weight=down_weight, down_bias=down_bias, lead_weight=lead_weight, lead_bias=lead_bias, cotangent=cotangent)


@jax.custom_vjp
def low(v):
    return lax.optimization_barrier(v.astype(jnp.bfloat16)).astype(jnp.float32)

@jax.custom_vjp
def low_back(v):
    return v

def low_keep(v):
    return (low(v), None)

def low_pass(kept, grad):
    return (grad,)

def back_keep(v):
    return (v, None)

def back_low(kept, grad):
    return (low(grad),)
low.defvjp(low_keep, low_pass)
low_back.defvjp(back_keep, back_low)
EPSILON = 1e-06
MASKED = -1e+30
HIGHEST = lax.Precision.HIGHEST

def rounded(values):
    return low(low_back(values))

def layer_norm(values, norm_gain, offset):
    row_mean = lax.optimization_barrier(jnp.mean(values, axis=-1, keepdims=True))
    centered = values - row_mean
    spread = lax.optimization_barrier(jnp.mean(centered * centered, axis=-1, keepdims=True))
    return centered * lax.rsqrt(spread + EPSILON) * norm_gain + offset

def head_block(head_queries, head_keys, head_values, key_valid):
    score_scale = 1.0 / math.sqrt(HEAD_DIM)
    scores = low_back(jnp.einsum('qgd,kgd->gqk', head_queries, head_keys, precision=HIGHEST) * score_scale)
    scores = jnp.where(key_valid[None, None, :], scores, MASKED)
    top_score = lax.optimization_barrier(jnp.max(scores, axis=-1, keepdims=True))
    expo_scores = jnp.exp(scores - top_score)
    attn_probs = low(expo_scores / lax.optimization_barrier(jnp.sum(expo_scores, axis=-1, keepdims=True)))
    return jnp.einsum('gqk,kgd->qgd', attn_probs, head_values, precision=HIGHEST)

def attention(queries, key_rows, value_rows, key_valid):
    length = queries.shape[0]
    groups = HEADS // 4

    def regroup(values):
        return jnp.moveaxis(values.reshape(length, groups, 4, HEAD_DIM), 1, 0)

    def one_group(inputs):
        return head_block(inputs[0], inputs[1], inputs[2], key_valid)
    outputs = lax.map(jax.checkpoint(one_group), (regroup(queries), regroup(key_rows), regroup(value_rows)))
    return jnp.moveaxis(outputs, 0, 1).reshape(length, groups * 4 * HEAD_DIM)

def sample_block(params, tokens_in, lead_scaled, key_valid):
    first_gain, first_shift, qkv_weight, query_bias, value_bias, out_weight, out_bias, second_gain, second_shift, up_weight, up_bias, down_weight, down_bias, lead_weight, lead_bias = params
    model_width = tokens_in.shape[-1]
    start_sum = tokens_in + lead_scaled * lead_weight + lead_bias
    normed = low(layer_norm(start_sum, first_gain, first_shift))
    projected = jnp.dot(normed, qkv_weight, precision=HIGHEST)
    queries = rounded(projected[:, :model_width] + query_bias)
    key_rows = rounded(projected[:, model_width:2 * model_width])
    value_rows = rounded(projected[:, 2 * model_width:] + value_bias)
    attended = rounded(attention(queries, key_rows, value_rows, key_valid))
    branch_one = low_back(jnp.dot(attended, out_weight, precision=HIGHEST) + out_bias)
    middle = start_sum + branch_one
    normed_two = low(layer_norm(middle, second_gain, second_shift))
    hidden_pre = low_back(jnp.dot(normed_two, up_weight, precision=HIGHEST) + up_bias)
    hidden = low(jax.nn.gelu(hidden_pre, approximate=False))
    branch_two = low_back(jnp.dot(hidden, down_weight, precision=HIGHEST) + down_bias)
    return middle + branch_two

def add_pair(earlier, latest):
    return earlier + latest

def reference(tokens, lead_hours, valid_counts, patch_mask, first_gain, first_shift, qkv_weight, query_bias, value_bias, out_weight, out_bias, second_gain, second_shift, up_weight, up_bias, down_weight, down_bias, lead_weight, lead_bias, cotangent):
    params = tuple((weight.astype(jnp.float32) for weight in (first_gain, first_shift, qkv_weight, query_bias, value_bias, out_weight, out_bias, second_gain, second_shift, up_weight, up_bias, down_weight, down_bias, lead_weight, lead_bias)))
    positions = jnp.arange(SEQ_LEN).astype(jnp.int32)

    def per_sample(totals, inputs):
        sample_tokens, hours, count, mask_row, cot_row = inputs
        lead_scaled = hours.astype(jnp.float32) / 100.0
        key_valid = positions < count
        loss_weight = (mask_row * key_valid.astype(jnp.int32)).astype(jnp.float32)

        def forward(params_in, tokens_in):
            return sample_block(params_in, tokens_in, lead_scaled, key_valid)
        result, pullback = jax.vjp(forward, params, sample_tokens.astype(jnp.float32))
        param_grads, token_grad = pullback(cot_row.astype(jnp.float32) * loss_weight[:, None])
        totals = jax.tree.map(add_pair, totals, param_grads)
        return (totals, (result.astype(jnp.bfloat16), token_grad.astype(jnp.bfloat16)))
    zeros = tuple((jnp.zeros_like(weight) for weight in params))
    totals, (outputs, grads) = lax.scan(per_sample, zeros, (tokens, lead_hours, valid_counts, patch_mask, cotangent))
    return (outputs, grads, totals[0], totals[1], totals[2], totals[3], totals[4], totals[5], totals[6], totals[7], totals[8], totals[9], totals[10], totals[11], totals[12], totals[13], totals[14])
```

```python
import math

import jax
import jax.numpy as jnp
from jax import lax
from jax.sharding import PartitionSpec as P

HEADS = 16
HEAD_DIM = 64
EPSILON = 1e-06
MASKED = -1e30
F32 = jnp.float32
BF16 = jnp.bfloat16


def dot(left, right, contract):
    return lax.dot_general(left, right, (contract, ((), ())), preferred_element_type=F32)


def normalise(values):
    centered = values - jnp.mean(values, axis=-1, keepdims=True)
    rate = lax.rsqrt(jnp.mean(centered * centered, axis=-1, keepdims=True) + EPSILON)
    return centered * rate, rate


def norm_back(upstream, xhat, rate, gain):
    scaled = upstream * gain
    inner = jnp.mean(scaled * xhat, axis=-1, keepdims=True)
    return rate * (scaled - jnp.mean(scaled, axis=-1, keepdims=True) - xhat * inner)


def swap(values, bit, size):
    return lax.ppermute(values, "seq", [(i, i ^ bit) for i in range(size)])


def far_bits(size):
    bits, bit = [], 2
    while bit < size:
        bits.append(bit)
        bit *= 2
    return bits


def gather_seq(own, size):
    me = lax.axis_index("seq")
    held = [(0, own)]
    for bit in far_bits(size):
        held = held + [(mask ^ bit, swap(piece, bit, size)) for mask, piece in held]
    if size > 1:
        held = held + [(mask ^ 1, swap(piece, 1, size)) for mask, piece in held]
    out = jnp.zeros((size,) + own.shape, own.dtype)
    for mask, piece in held:
        out = lax.dynamic_update_index_in_dim(out, piece, me ^ mask, 0)
    return out


def scatter_seq(terms, size):
    me = lax.axis_index("seq")
    bits = ([1] if size > 1 else []) + far_bits(size)
    masks = list(range(size))
    held = {mask: lax.dynamic_index_in_dim(terms, me ^ mask, 0, keepdims=False) for mask in masks}
    for bit in bits:
        kept = {}
        for mask in sorted(held):
            if mask & bit:
                continue
            kept[mask] = held[mask] + swap(held[mask ^ bit].astype(BF16), bit, size).astype(F32)
        held = kept
    return held[0]


def exchange_seq(blocks, size):
    me = lax.axis_index("seq")
    out = lax.dynamic_update_index_in_dim(
        jnp.zeros_like(blocks), lax.dynamic_index_in_dim(blocks, me, 0, keepdims=False), me, 0
    )
    for mask in range(1, size):
        sent = lax.dynamic_index_in_dim(blocks, me ^ mask, 0, keepdims=False)
        out = lax.dynamic_update_index_in_dim(out, swap(sent, mask, size), me ^ mask, 0)
    return out


def gather_dp(own):
    return lax.all_gather(own, "dp", axis=0, tiled=False)


def scatter_dp(terms):
    return lax.psum_scatter(terms.astype(BF16), "dp", scatter_dimension=0, tiled=False).astype(F32)


def gelu(values):
    return jax.nn.gelu(values, approximate=False)


def head_probs(queries, keys, key_valid):
    scores = dot(queries, keys, ((1,), (1,))) * (1.0 / math.sqrt(HEAD_DIM))
    scores = jnp.where(key_valid[None, :], scores, MASKED)
    weights = jnp.exp(scores - jnp.max(scores, axis=-1, keepdims=True))
    return weights / jnp.sum(weights, axis=-1, keepdims=True)


def make_body(n_dp, n_seq):
    def body(
        tokens,
        lead_hours,
        valid_counts,
        patch_mask,
        first_gain,
        first_shift,
        qkv_weight,
        query_bias,
        value_bias,
        out_weight,
        out_bias,
        second_gain,
        second_shift,
        up_weight,
        up_bias,
        down_weight,
        down_bias,
        lead_weight,
        lead_bias,
        cotangent,
    ):
        me = lax.axis_index("seq")
        rows, width = tokens.shape[1], tokens.shape[2]
        length = rows * n_seq
        part = qkv_weight.shape[0]
        ff_part = down_weight.shape[0]
        ff = up_weight.shape[1]
        cols = width // n_seq
        ff_cols = ff // n_seq
        heads = HEADS // n_seq
        lead = lead_hours[0].astype(F32) / 100.0
        key_valid = jnp.arange(length, dtype=jnp.int32) < valid_counts[0]
        positions = me * rows + jnp.arange(rows, dtype=jnp.int32)
        loss_weight = (patch_mask[0] * (positions < valid_counts[0]).astype(jnp.int32)).astype(BF16)

        small = jnp.concatenate(
            [
                first_gain,
                first_shift,
                query_bias,
                value_bias,
                out_bias,
                second_gain,
                second_shift,
                down_bias,
                lead_weight,
                lead_bias,
                up_bias,
            ]
        )
        tokens_all = gather_seq(tokens[0], n_seq).reshape(length, width)
        small_all = lax.all_gather(small, ("dp", "seq"), axis=0).astype(F32)
        vector = [small_all[:, i * part : (i + 1) * part].reshape(width) for i in range(10)]
        gain_one, shift_one, q_bias, v_bias, o_bias, gain_two, shift_two, d_bias, l_weight, l_bias = vector
        u_bias = lax.dynamic_index_in_dim(
            small_all[:, 10 * part :].reshape(n_dp, n_seq, ff_part), me, 1, keepdims=False
        ).reshape(ff_cols)
        q_bias = lax.dynamic_slice_in_dim(q_bias, me * cols, cols)
        v_bias = lax.dynamic_slice_in_dim(v_bias, me * cols, cols)

        qkv_blocks = jnp.moveaxis(qkv_weight.reshape(part, 3, n_seq, cols), 2, 0).reshape(n_seq, part, 3 * cols)
        up_blocks = jnp.moveaxis(up_weight.reshape(part, n_dp, n_seq, ff_part), 2, 0).reshape(n_seq, part, ff_cols)
        mixed = exchange_seq(jnp.concatenate([qkv_blocks, up_blocks], axis=2), n_seq)
        mixed = mixed.reshape(n_seq * part, 3 * cols + ff_cols)
        qkv = gather_dp(mixed[:, : 3 * cols]).reshape(width, 3 * cols)
        out_rows = gather_dp(out_weight)
        out_full = jnp.moveaxis(gather_seq(out_rows, n_seq), 0, 1).reshape(width, width)
        up = gather_dp(mixed[:, 3 * cols :]).reshape(width, ff_cols)
        down = gather_dp(down_weight).reshape(ff_cols, width)
        grad_out_own = cotangent[0] * loss_weight[:, None]
        grad_out = gather_seq(grad_out_own, n_seq).reshape(length, width)

        start_sum = tokens_all.astype(F32) + lead * l_weight + l_bias
        xhat_one, rate_one = normalise(start_sum)
        normed = (xhat_one * gain_one + shift_one).astype(BF16)
        projected = dot(normed, qkv, ((1,), (0,)))
        queries = (projected[:, :cols] + q_bias).astype(BF16)
        keys = projected[:, cols : 2 * cols].astype(BF16)
        values = (projected[:, 2 * cols :] + v_bias).astype(BF16)
        split = [slice(i * HEAD_DIM, (i + 1) * HEAD_DIM) for i in range(heads)]
        pieces = []
        for piece in split:
            probs = head_probs(queries[:, piece], keys[:, piece], key_valid)
            pieces.append(dot(probs.astype(BF16), values[:, piece], ((1,), (0,))).astype(BF16))
        attended_own = jnp.concatenate(pieces, axis=1)
        attended = jnp.moveaxis(gather_seq(attended_own, n_seq), 0, 1).reshape(length, width)
        middle = start_sum + (dot(attended, out_full, ((1,), (0,))) + o_bias)
        xhat_two, rate_two = normalise(middle)
        normed_two = (xhat_two * gain_two + shift_two).astype(BF16)
        hidden_pre = dot(normed_two, up, ((1,), (0,))) + u_bias
        hidden, gelu_back = jax.vjp(gelu, hidden_pre)
        hidden = hidden.astype(BF16)

        def own_rows(whole):
            return lax.dynamic_slice_in_dim(whole, me * rows, rows, 0)

        branch = scatter_seq(dot(hidden, down, ((1,), (0,))).reshape(n_seq, rows, width), n_seq)
        middle_own = own_rows(middle)
        block_out = (middle_own + (branch + d_bias)).astype(BF16)

        grad_hidden = dot(grad_out, down, ((1,), (1,)))
        grad_pre = gelu_back(grad_hidden)[0].astype(BF16)
        u_bias_grad = jnp.sum(grad_pre.astype(F32), axis=0)
        down_grad = scatter_dp(dot(hidden, grad_out, ((0,), (0,))).reshape(n_dp, ff_part, width))
        up_grad = scatter_dp(dot(normed_two, grad_pre, ((0,), (0,))).reshape(n_dp, n_seq * part, ff_cols))
        grad_two = scatter_seq(dot(grad_pre, up, ((1,), (1,))).reshape(n_seq, rows, width), n_seq)
        xhat_two_own, rate_two_own = own_rows(xhat_two), own_rows(rate_two)
        gain_two_grad = jnp.sum(grad_two * xhat_two_own, axis=0)
        shift_two_grad = jnp.sum(grad_two, axis=0)
        grad_middle = grad_out_own.astype(F32) + norm_back(grad_two, xhat_two_own, rate_two_own, gain_two)
        grad_one_own = grad_middle.astype(BF16)
        o_bias_grad = jnp.sum(grad_one_own.astype(F32), axis=0)
        d_bias_grad = jnp.sum(grad_out_own.astype(F32), axis=0)
        grad_one = gather_seq(grad_one_own, n_seq).reshape(length, width)
        out_mine = lax.dynamic_slice_in_dim(out_full, me * cols, cols, 0)
        grad_attended = dot(grad_one, out_mine, ((1,), (1,))).astype(BF16)
        out_grad = scatter_dp(dot(attended_own, grad_one, ((0,), (0,))).reshape(n_dp, cols // n_dp, width))
        q_pieces, k_pieces, v_pieces = [], [], []
        scale = 1.0 / math.sqrt(HEAD_DIM)
        for piece in split:
            probs = head_probs(queries[:, piece], keys[:, piece], key_valid)
            upstream = grad_attended[:, piece]
            v_pieces.append(dot(probs.astype(BF16), upstream, ((0,), (0,))).astype(BF16))
            grad_probs = dot(upstream, values[:, piece], ((1,), (1,)))
            inner = jnp.sum(probs * grad_probs, axis=-1, keepdims=True)
            grad_scores = (probs * (grad_probs - inner)).astype(BF16)
            q_pieces.append((dot(grad_scores, keys[:, piece], ((1,), (0,))) * scale).astype(BF16))
            k_pieces.append((dot(grad_scores, queries[:, piece], ((0,), (0,))) * scale).astype(BF16))
        grad_qkv = jnp.concatenate(q_pieces + k_pieces + v_pieces, axis=1)
        grad_first = scatter_seq(dot(grad_qkv, qkv, ((1,), (1,))).reshape(n_seq, rows, width), n_seq)
        qkv_grad = scatter_dp(dot(normed, grad_qkv, ((0,), (0,))).reshape(n_dp, n_seq * part, 3 * cols))
        column_sums = jnp.sum(grad_qkv.astype(F32), axis=0)
        xhat_one_own, rate_one_own = own_rows(xhat_one), own_rows(rate_one)
        gain_one_grad = jnp.sum(grad_first * xhat_one_own, axis=0)
        shift_one_grad = jnp.sum(grad_first, axis=0)
        grad_start = grad_middle + norm_back(grad_first, xhat_one_own, rate_one_own, gain_one)
        tokens_grad = grad_start.astype(BF16)
        l_bias_grad = jnp.sum(grad_start, axis=0)
        l_weight_grad = lead * l_bias_grad

        blocks = jnp.concatenate(
            [qkv_grad.reshape(n_seq, part, 3 * cols), up_grad.reshape(n_seq, part, ff_cols)], axis=2
        )
        blocks = exchange_seq(blocks.astype(BF16), n_seq).astype(F32)
        qkv_weight_grad = jnp.moveaxis(blocks[:, :, : 3 * cols].reshape(n_seq, part, 3, cols), 0, 2).reshape(part, 3 * width)
        up_weight_grad = jnp.moveaxis(
            blocks[:, :, 3 * cols :].reshape(n_seq, part, n_dp, ff_part), 0, 2
        ).reshape(part, ff)
        moves = []
        for dp_at in range(n_dp):
            for seq_at in range(n_seq):
                moves.append((dp_at * n_seq + seq_at, seq_at * n_dp + dp_at))
        out_weight_grad = lax.ppermute(out_grad.astype(BF16), ("dp", "seq"), moves).astype(F32)

        def placed_columns(vec):
            return lax.dynamic_update_slice_in_dim(jnp.zeros((width,), F32), vec, me * cols, 0)

        u_placed = lax.dynamic_update_index_in_dim(
            jnp.zeros((n_dp, n_seq, ff_part), F32), u_bias_grad.reshape(n_dp, ff_part), me, 1
        )
        sums = [
            gain_one_grad,
            shift_one_grad,
            placed_columns(column_sums[:cols]),
            placed_columns(column_sums[2 * cols :]),
            o_bias_grad,
            gain_two_grad,
            shift_two_grad,
            d_bias_grad,
            l_weight_grad,
            l_bias_grad,
        ]
        sums = [value.reshape(n_dp * n_seq, part) for value in sums] + [u_placed.reshape(n_dp * n_seq, ff_part)]
        owned = lax.psum_scatter(jnp.concatenate(sums, axis=1), ("dp", "seq"), scatter_dimension=0, tiled=False)
        owned = [owned[i * part : (i + 1) * part] for i in range(10)] + [owned[10 * part :]]
        return (
            block_out[None],
            tokens_grad[None],
            owned[0],
            owned[1],
            qkv_weight_grad,
            owned[2],
            owned[3],
            out_weight_grad,
            owned[4],
            owned[5],
            owned[6],
            up_weight_grad,
            owned[10],
            down_grad,
            owned[7],
            owned[8],
            owned[9],
        )

    return body


def solution(mesh):
    both = P(("dp", "seq"))
    matrix = P(("dp", "seq"), None)
    tokens = P("dp", "seq", None)
    vectors = dict(
        in_specs=(
            tokens,
            P("dp"),
            P("dp"),
            P("dp", "seq"),
            both,
            both,
            matrix,
            both,
            both,
            matrix,
            both,
            both,
            both,
            matrix,
            both,
            matrix,
            both,
            both,
            both,
            tokens,
        ),
        out_specs=(
            tokens,
            tokens,
            both,
            both,
            matrix,
            both,
            both,
            matrix,
            both,
            both,
            both,
            matrix,
            both,
            matrix,
            both,
            both,
            both,
        ),
    )
    return jax.shard_map(
        make_body(mesh.shape["dp"], mesh.shape["seq"]), mesh=mesh, check_vma=False, **vectors
    )
```

```python
import functools
import math

import jax
import jax.numpy as jnp
import numpy as np
from jax import lax
from jax.experimental import pallas as pl
from jax.experimental.pallas import tpu as pltpu
from jax.sharding import PartitionSpec as P

HEADS = 16
HEAD_DIM = 64
PAIR = 2 * HEAD_DIM
SCALE = 1.0 / math.sqrt(HEAD_DIM)
EPSILON = 1e-06
MASKED = -1e30
F32 = jnp.float32
BF16 = jnp.bfloat16
NN, NT, TN = ((1,), (0,)), ((1,), (1,)), ((0,), (0,))
HALVES = 2
MIB = 1024 * 1024
NEAR = pl.BlockSpec(memory_space=pltpu.VMEM)
AWAY = pl.BlockSpec(memory_space=pl.ANY)
NUMBERS = pl.BlockSpec(memory_space=pltpu.SMEM)


def dot(left, right, contract):
    return lax.dot_general(left, right, (contract, ((), ())), preferred_element_type=F32)


def shape(dims, dtype=BF16):
    return jax.ShapeDtypeStruct(dims, dtype)


def call(kernel, *, in_specs, out_shape, near_in=(), near_out=(), **options):
    def large(value):
        return math.prod(value.shape) * value.dtype.itemsize >= 65536

    def run(*args):
        kept = []
        for i, a in enumerate(args):
            if large(a):
                a = pltpu.with_memory_space_constraint(a, pltpu.VMEM if i in near_in else pltpu.HBM)
            kept.append(a)
        single = not isinstance(out_shape, (list, tuple))
        outs = [out_shape] if single else list(out_shape)
        outs = [
            ((pltpu.VMEM if i in near_out else pltpu.HBM)(o.shape, o.dtype) if large(o) else o)
            for i, o in enumerate(outs)
        ]
        return pl.pallas_call(kernel, in_specs=in_specs, out_shape=outs[0] if single else outs, **options)(*kept)

    return run


def vmem(mib):
    return pltpu.CompilerParams(vmem_limit_bytes=mib * MIB)


def cost(flops, moved, exps=0):
    return pl.CostEstimate(flops=int(flops), bytes_accessed=int(moved), transcendentals=int(exps))


def standardise(values):
    centered = values - jnp.mean(values, axis=-1, keepdims=True)
    rate = lax.rsqrt(jnp.mean(centered * centered, axis=-1, keepdims=True) + EPSILON)
    return centered * rate, rate


def norm_back(upstream, xhat, rate, gain):
    scaled = upstream * gain
    inner = jnp.mean(scaled * xhat, axis=-1, keepdims=True)
    return rate * (scaled - jnp.mean(scaled, axis=-1, keepdims=True) - xhat * inner)


def pack_kernel(n_dp, n_seq, me_ref, qkv_ref, up_ref, *refs):
    vectors, out_refs = refs[:-n_seq], refs[-n_seq:]
    me = me_ref[0]
    part = qkv_ref.shape[0]
    cols = qkv_ref.shape[1] // (3 * n_seq)
    piece = up_ref.shape[1] // (n_dp * n_seq)
    rows = [ref[...].astype(F32)[:, i : i + part] for ref in vectors for i in range(0, ref.shape[1], part)]
    kinds = len(rows)
    rows = jnp.concatenate(rows + [jnp.zeros((128 - kinds, part), F32)], axis=0)
    rows = jnp.concatenate([rows, jnp.zeros((128, 128 - part), F32)], axis=1)
    small = rows.T[:part, :].astype(BF16)
    for mask, ref in enumerate(out_refs):
        place = me ^ mask
        for i in range(3):
            start = pl.multiple_of((i * n_seq + place) * cols, 128)
            ref[:, i * cols : (i + 1) * cols] = qkv_ref[:, pl.ds(start, cols)]
        at = 3 * cols
        ref[:, at : at + 128] = small
        for i in range(n_dp):
            start = pl.multiple_of((i * n_seq + place) * piece, 128)
            ref[:, at + 128 + i * piece : at + 128 + (i + 1) * piece] = up_ref[:, pl.ds(start, piece)]


def pack(n_dp, n_seq, me, qkv, up, vectors):
    part = qkv.shape[0]
    wide = qkv.shape[1] // n_seq + 128 + up.shape[1] // n_seq
    if up.shape[1] // (n_dp * n_seq) % 128 or part % 16:
        small = jnp.concatenate(vectors).reshape(-1, part).T
        small = jnp.pad(small, ((0, 0), (0, 128 - small.shape[1])))
        qkv_split = qkv.reshape(part, 3, n_seq, -1)
        up_split = up.reshape(part, n_dp, n_seq, -1)

        def block(place):
            q = lax.dynamic_index_in_dim(qkv_split, place, 2, keepdims=False).reshape(part, -1)
            u = lax.dynamic_index_in_dim(up_split, place, 2, keepdims=False).reshape(part, -1)
            return jnp.concatenate([q, small, u], axis=1)

        return [block(me[0] ^ m) for m in range(n_seq)]
    args = [qkv, up] + [v.reshape(1, -1) for v in vectors]
    args = [pltpu.with_memory_space_constraint(a, pltpu.HBM) for a in args]
    return pl.pallas_call(
        functools.partial(pack_kernel, n_dp, n_seq),
        grid=(1,),
        in_specs=[pl.BlockSpec(memory_space=pltpu.SMEM)] + [pl.BlockSpec(a.shape, lambda i: (0, 0)) for a in args],
        out_specs=[pl.BlockSpec((part, wide), lambda i: (0, 0))] * n_seq,
        out_shape=[shape((part, wide))] * n_seq,
        compiler_params=vmem(8),
        name="pack",
    )(me, *args)


def join_kernel(n_seq, split, me_ref, *refs):
    out_ref, left_ref, right_ref = refs[-3:]
    part, wide = out_ref.shape
    cols = wide // n_seq
    edge = split - 128
    for t, ref in enumerate(refs[:-3]):
        rows = pl.ds(pl.multiple_of((me_ref[0] ^ t) * part, part), part)
        left_ref[rows, :edge] = ref[:, :edge]
        left_ref[rows, edge + cols :] = ref[:, edge:split]
        right_ref[rows, :] = ref[:, split:]
        left_ref[t * part : (t + 1) * part, edge : edge + cols] = out_ref[:, t * cols : (t + 1) * cols]


def join(n_seq, split, me, pieces, out_weight):
    part, wide = pieces[0].shape
    cols = out_weight.shape[1] // n_seq
    rows = part * n_seq
    if part % 16:
        whole = flipped(dict(enumerate(pieces)), n_seq).reshape(rows, wide)
        beside = jnp.moveaxis(out_weight.reshape(part, n_seq, cols), 1, 0).reshape(rows, cols)
        left = [whole[:, : split - 128], beside, whole[:, split - 128 : split]]
        return jnp.concatenate(left, axis=1), whole[:, split:]
    args = list(pieces) + [pltpu.with_memory_space_constraint(out_weight, pltpu.HBM)]
    return pl.pallas_call(
        functools.partial(join_kernel, n_seq, split),
        grid=(1,),
        in_specs=[pl.BlockSpec(memory_space=pltpu.SMEM)] + [pl.BlockSpec(a.shape, lambda i: (0, 0)) for a in args],
        out_specs=[
            pl.BlockSpec((rows, split + cols), lambda i: (0, 0)),
            pl.BlockSpec((rows, wide - split), lambda i: (0, 0)),
        ],
        out_shape=[shape((rows, split + cols)), shape((rows, wide - split))],
        compiler_params=vmem(8),
        name="join",
    )(me, *args)


def ordered(order, pieces):
    if pieces[0].shape[0] % 128 == 0:
        return list(pieces)
    whole = jnp.stack(pieces)
    out = whole
    for k in range(len(pieces)):
        out = lax.dynamic_update_index_in_dim(out, whole[k], order[k], 0)
    return [out.reshape(-1, out.shape[-1])]


def lay(order_ref, pieces, target, cols=slice(None)):
    if len(pieces) == 1:
        target[...] = pieces[0][:, cols]
        return
    rows = pieces[0].shape[0]
    for k, piece in enumerate(pieces):
        target[pl.ds(pl.multiple_of(order_ref[k] * rows, rows), rows), :] = piece[:, cols]


def middle_columns_kernel(*refs):
    out_ref = refs[-1]
    rows = refs[0].shape[0]
    for k, ref in enumerate(refs[:-1]):
        out_ref[k * rows : (k + 1) * rows, :] = ref[...]


def middle_columns(pieces, start, cols):
    rows = pieces[0].shape[0]
    if rows % 128 or start % cols:
        return jnp.concatenate([piece[:, start : start + cols] for piece in pieces], axis=0)
    total = rows * len(pieces)
    return call(
        middle_columns_kernel,
        grid=(1,),
        in_specs=[pl.BlockSpec((rows, cols), lambda i: (0, start // cols))] * len(pieces),
        out_specs=pl.BlockSpec((total, cols), lambda i: (0, 0)),
        out_shape=shape((total, cols)),
        compiler_params=vmem(4),
        name="middle_columns",
    )(*pieces)


def project_kernel(n_seq, n_pieces, me_ref, order_ref, lead_ref, *refs):
    tokens = refs[:n_seq]
    pieces = refs[n_seq : n_seq + n_pieces]
    normed_ref, q_ref, k_ref, v_ref, qkv_ref, table_ref, vec_ref, small_ref = refs[n_seq + n_pieces :]
    cols = q_ref.shape[1]

    @pl.when(pl.program_id(0) == 0)
    def _():
        lay(order_ref, pieces, qkv_ref, slice(0, 3 * cols))
        lay(order_ref, pieces, small_ref, slice(4 * cols, 4 * cols + 128))
        table_ref[...] = small_ref[...].astype(F32).T[: table_ref.shape[0], :]
        for i, kind in enumerate((0, 0, 1, 4, 5, 6, 7, 7)):
            vec_ref[i : i + 1, :] = table_ref[kind : kind + 1, :]
        vec_ref[0:1, :] = lead_ref[0] * table_ref[8:9, :] + table_ref[9:10, :]

    start = jnp.concatenate([ref[...] for ref in tokens], axis=0).astype(F32) + vec_ref[0:1, :]
    xhat, _ = standardise(start)
    normed = (xhat * vec_ref[1:2, :] + vec_ref[2:3, :]).astype(BF16)
    normed_ref[...] = normed
    mine = pl.ds(pl.multiple_of(me_ref[0] * cols, 128), cols)
    found = dot(normed, qkv_ref[...], NN)
    q_ref[...] = (found[:, :cols] + table_ref[2:3, mine]).astype(BF16)
    k_ref[...] = found[:, cols : 2 * cols].astype(BF16)
    v_ref[...] = (found[:, 2 * cols :] + table_ref[3:4, mine]).astype(BF16)


def project(me, order, lead, tokens, pieces, kinds):
    rows, width = tokens[0].shape
    n_seq = len(tokens)
    cols = width // n_seq
    length = rows * n_seq
    half = rows // HALVES
    count = length // HALVES
    numbers = pl.BlockSpec(memory_space=pltpu.SMEM)

    def whole(dims):
        return pl.BlockSpec(dims, lambda i: (0, 0))

    def step(wide):
        return pl.BlockSpec((count, wide), lambda i: (i, 0))

    return call(
        functools.partial(project_kernel, n_seq, len(pieces)),
        near_out=(1, 2, 3),
        grid=(HALVES,),
        in_specs=[numbers] * 3
        + [pl.BlockSpec((half, width), lambda i: (i, 0))] * n_seq
        + [whole(piece.shape) for piece in pieces],
        out_specs=[step(width), step(cols), step(cols), step(cols)]
        + [whole((width, 3 * cols)), whole((kinds, width)), whole((8, width))],
        out_shape=[shape((length, width))]
        + [shape((length, cols))] * 3
        + [shape((width, 3 * cols)), shape((kinds, width), F32), shape((8, width), F32)],
        scratch_shapes=[pltpu.VMEM((width, 128), BF16)],
        compiler_params=vmem(28),
        cost_estimate=cost(6 * length * width * cols, 10 * length * width),
        name="project",
    )(me, order, lead, *tokens, *pieces)


def key_bias(n_seq, length, me, count):
    half = length // (n_seq * HALVES)
    parts = []
    for h in range(HALVES):
        for m in block_masks(n_seq):
            at = lax.broadcasted_iota(jnp.int32, (half, 1), 0) + ((me ^ m) * HALVES + h) * half
            parts.append(jnp.where(at < count, 0.0, MASKED).astype(F32))
    return jnp.concatenate(parts, axis=0)


def attend_kernel(n_seq, me_ref, count_ref, q_ref, k_ref, v_ref, out_ref, lse_ref):
    bias = key_bias(n_seq, k_ref.shape[0], me_ref[0], count_ref[0])
    for half in range(2):
        cols = slice(half * HEAD_DIM, (half + 1) * HEAD_DIM)
        scores = dot(k_ref[:, cols], q_ref[:, cols] * SCALE, NT) + bias
        top = jnp.max(scores, axis=0, keepdims=True)
        weights = jnp.exp(scores - top)
        total = jnp.sum(weights, axis=0, keepdims=True)
        mixed = dot(v_ref[:, cols], weights.astype(BF16), TN) / total
        out_ref[:, cols] = mixed.T.astype(BF16)
        lse_ref[half] = top + jnp.log(total)


def attend(n_seq, me, valid, q, k, v):
    length, cols = q.shape
    pair = pl.BlockSpec((length, PAIR), lambda g: (0, g))
    return call(
        functools.partial(attend_kernel, n_seq),
        near_in=(2, 3, 4),
        grid=(cols // PAIR,),
        in_specs=[pl.BlockSpec(memory_space=pltpu.SMEM)] * 2 + [pair, pair, pair],
        out_specs=[pair, pl.BlockSpec((2, 1, length), lambda g: (g, 0, 0))],
        out_shape=[shape((length, cols)), shape((cols // HEAD_DIM, 1, length), F32)],
        compiler_params=vmem(32),
        cost_estimate=cost(4 * length * length * cols, 8 * length * cols, length * length * cols // HEAD_DIM),
        name="attend",
    )(me, valid, q, k, v)


def attend_back_kernel(first, n_seq, *refs):
    me_ref, count_ref, q_ref, k_ref, v_ref, lse_ref, out_w_ref = refs[:7]
    grads = refs[7 : 7 + n_seq]
    rest = refs[7 + n_seq :]
    if first:
        dq_ref, dk_ref, dv_ref = rest
    else:
        dq_in, dk_in, dv_in, whole_ref, q_out, k_out, v_out, sems = rest
    length = k_ref.shape[0]
    count = q_ref.shape[0]
    pair = pl.program_id(0)
    spot = pair % 2
    bias = key_bias(n_seq, length, me_ref[0], count_ref[0])
    upstream = jnp.concatenate([dot(ref[...], out_w_ref[...], NT).astype(BF16) for ref in grads], axis=0)
    for half in range(2):
        cols = slice(half * HEAD_DIM, (half + 1) * HEAD_DIM)
        k = k_ref[:, cols]
        q = q_ref[:, cols] * SCALE
        g = upstream[:, cols]
        probs = jnp.exp(dot(k, q, NT) + bias - lse_ref[half])
        dv = dot(probs.astype(BF16), g, NN)
        term = probs * dot(v_ref[:, cols], g, NT)
        grad = (term - probs * jnp.sum(term, axis=0, keepdims=True)).astype(BF16)
        dk = dot(grad, q, NN)
        dq = (dot(k, grad, TN) * SCALE).T.astype(BF16)
        if first:
            dq_ref[:, cols] = dq
            dk_ref[:, cols] = dk
            dv_ref[:, cols] = dv
        else:
            q_out[spot, :count, cols] = dq_in[:, cols]
            q_out[spot, count:, cols] = dq
            k_out[spot, :, cols] = (dk + dk_in[:, cols]).astype(BF16)
            v_out[spot, :, cols] = (dv + dv_in[:, cols]).astype(BF16)
    if first:
        return
    pairs = pl.num_programs(0)

    def copies(at):
        found = []
        for i, source in enumerate((q_out, k_out, v_out)):
            start = pl.multiple_of((i * pairs + at) * PAIR, PAIR)
            target = whole_ref.at[:, pl.ds(start, PAIR)]
            found.append(pltpu.make_async_copy(source.at[at % 2], target, sems.at[at % 2, i]))
        return found

    for copy in copies(pair):
        copy.start()

    @pl.when(pair > 0)
    def _():
        for copy in copies(pair - 1):
            copy.wait()

    @pl.when(pair == pairs - 1)
    def _():
        for copy in copies(pair):
            copy.wait()


def attend_back(at, me, valid, q, k, v, lse, out_mine, grads, earlier):
    length, cols = k.shape
    width = out_mine.shape[1]
    count = length // HALVES
    pair = pl.BlockSpec((length, PAIR), lambda g: (0, g))
    mine = pl.BlockSpec((count, PAIR), lambda g: (at, g))
    here = pl.BlockSpec((count, PAIR), lambda g: (0, g))
    first = earlier is None
    in_specs = [NUMBERS] * 2 + [
        mine,
        pair,
        pair,
        pl.BlockSpec((2, 1, count), lambda g: (g, 0, at)),
        pl.BlockSpec((PAIR, width), lambda g: (g, 0)),
    ]
    in_specs += [pl.BlockSpec(piece.shape, lambda g: (0, 0)) for piece in grads]
    args = [me, valid, q, k, v, lse, out_mine] + list(grads)
    if first:
        out_specs = [here, pair, pair]
        out_shape = [shape((count, cols))] + [shape((length, cols), F32)] * 2
        scratch = []
    else:
        in_specs += [here, pair, pair]
        args += list(earlier)
        out_specs = AWAY
        out_shape = shape((length, 3 * cols))
        scratch = [pltpu.VMEM((2, length, PAIR), BF16)] * 3 + [pltpu.SemaphoreType.DMA((2, 3))]
    return call(
        functools.partial(attend_back_kernel, first, len(grads)),
        grid=(cols // PAIR,),
        in_specs=in_specs,
        out_specs=out_specs,
        out_shape=out_shape,
        scratch_shapes=scratch,
        compiler_params=vmem(36),
        cost_estimate=cost(10 * count * length * cols, 8 * length * cols, count * length * cols // HEAD_DIM),
        name="attend_back",
    )(*args)


def middle_kernel(n_seq, n_out, me_ref, order_ref, *refs):
    tokens = refs[:n_seq]
    att = refs[n_seq : 2 * n_seq]
    outs = refs[2 * n_seq : 2 * n_seq + n_out]
    vec_ref, normed_ref, middle_ref, mine_ref, out_ref = refs[2 * n_seq + n_out :]
    masks = block_masks(n_seq)
    me = me_ref[0]
    cols = att[0].shape[1]
    half = middle_ref.shape[0]
    width = normed_ref.shape[1]
    step = pl.program_id(0)

    @pl.when(step == 0)
    def _():
        if n_out == 1:
            out_ref[...] = outs[0][...]
        else:
            n_dp = order_ref.shape[0]
            part = width // (n_dp * n_seq)
            for mask, ref in enumerate(outs):
                for k in range(n_dp):
                    start = pl.multiple_of((order_ref[k] * n_seq + (me ^ mask)) * part, part)
                    for t in range(n_seq):
                        at = (k * n_seq + t) * part
                        out_ref[pl.ds(start, part), t * cols : (t + 1) * cols] = ref[at : at + part, :]
        mine_ref[...] = out_ref[pl.ds(pl.multiple_of(me * cols, cols), cols), :]

    near = [tokens[i][...] for i in range(n_seq // 2)]
    other = [tokens[i][...] for i in range(n_seq // 2, n_seq)]
    start = [jnp.where(step % 2 == 0, a, b) for a, b in zip(near, other)]
    middle = jnp.concatenate(start, axis=0).astype(F32) + vec_ref[0:1, :] + vec_ref[3:4, :]
    for mask, ref in zip(masks, att):
        at = pl.multiple_of((me ^ mask) * cols, cols)
        spots = [t ^ (mask >> 1) for t in range(n_seq // 2)]
        found = jnp.concatenate([ref[t * half : (t + 1) * half, :] for t in spots], axis=0)
        middle = middle + dot(found, out_ref[pl.ds(at, cols), :], NN)
    xhat, _ = standardise(middle)
    normed_ref[...] = (xhat * vec_ref[4:5, :] + vec_ref[5:6, :]).astype(BF16)

    @pl.when(step % 2 == 0)
    def _():
        middle_ref[...] = middle[:half, :]


def middle_norm(me, order, tokens, att, outs, vecs):
    rows, width = tokens[0].shape
    n_seq = len(att)
    length = rows * n_seq
    cols = width // n_seq
    block = length // (2 * HALVES)
    half = rows // HALVES
    numbers = pl.BlockSpec(memory_space=pltpu.SMEM)
    return call(
        functools.partial(middle_kernel, n_seq, len(outs)),
        near_out=(0,),
        grid=(2 * HALVES,),
        in_specs=[numbers] * 2
        + [pl.BlockSpec((half, width), lambda i: (i // 2, 0))] * n_seq
        + [pl.BlockSpec((block, cols), lambda i, side=mask & 1: (i ^ side, 0)) for mask in block_masks(n_seq)]
        + [pl.BlockSpec(out.shape, lambda i: (0, 0)) for out in outs]
        + [pl.BlockSpec(vecs.shape, lambda i: (0, 0))],
        out_specs=[
            pl.BlockSpec((block, width), lambda i: (i, 0)),
            pl.BlockSpec((half, width), lambda i: (i // 2, 0)),
            pl.BlockSpec((cols, width), lambda i: (0, 0)),
        ],
        out_shape=[shape((length, width)), shape((rows, width), F32), shape((cols, width))],
        scratch_shapes=[pltpu.VMEM((width, width), BF16)],
        compiler_params=vmem(24),
        cost_estimate=cost(2 * length * width * width, 10 * length * width),
        name="middle_norm",
    )(me, order, *tokens, *att, *outs, vecs)


def fetch(pairs, sems):
    copies = [pltpu.make_async_copy(a, b, sems.at[i]) for i, (a, b) in enumerate(pairs)]
    for copy in copies:
        copy.start()

    def wait():
        for copy in copies:
            copy.wait()

    return wait


def placed(order_ref, pieces, target):
    if len(pieces) == 1:
        return [(pieces[0], target)]
    rows = pieces[0].shape[0]
    return [
        (piece, target.at[pl.ds(pl.multiple_of(order_ref[k] * rows, rows), rows), :]) for k, piece in enumerate(pieces)
    ]


def up_kernel(n_pieces, block, order_ref, normed_ref, bias_ref, *refs):
    up_ref, hidden_ref, slope_ref, sems = refs[n_pieces:]
    fetch(placed(order_ref, refs[:n_pieces], up_ref), sems)()

    def step(i, carry):
        cols = pl.ds(pl.multiple_of(i * block, block), block)
        pre = dot(normed_ref[...], up_ref[:, cols], NN) + bias_ref[:, cols]
        phi = 0.5 + 0.5 * lax.erf(pre * math.sqrt(0.5))
        hidden_ref[:, cols] = (pre * phi).astype(BF16)
        slope_ref[:, cols] = phi + pre * (jnp.exp(-0.5 * pre * pre) * (1.0 / math.sqrt(2.0 * math.pi)))
        return carry

    lax.fori_loop(0, up_ref.shape[1] // block, step, 0)


def up_part(order, normed, bias, pieces, block=256):
    length, width = normed.shape
    ff = pieces[0].shape[1]
    return call(
        functools.partial(up_kernel, len(pieces), block),
        near_in=(1,),
        near_out=(0, 1, 2),
        in_specs=[NUMBERS, NEAR, NEAR] + [AWAY] * len(pieces),
        out_specs=[NEAR] * 3,
        out_shape=[shape((width, ff)), shape((length, ff)), shape((length, ff), F32)],
        scratch_shapes=[pltpu.SemaphoreType.DMA((len(pieces),))],
        compiler_params=vmem(12),
        cost_estimate=cost(2 * length * width * ff, 8 * width * ff, 2 * length * ff),
        name="up_part",
    )(order, normed, bias, *pieces)


def down_terms_kernel(n_grads, block, hidden_ref, *refs):
    out_ref, grad_ref, sems = refs[n_grads:]
    rows = refs[0].shape[0]
    half = rows // HALVES
    pairs = [
        (ref.at[pl.ds(h * half, half), :], grad_ref.at[pl.ds((h * n_grads + i) * half, half), :])
        for h in range(HALVES)
        for i, ref in enumerate(refs[:n_grads])
    ]
    fetch(pairs, sems)()

    def step(i, carry):
        cols = pl.ds(pl.multiple_of(i * block, block), block)
        out_ref[cols, :] = dot(hidden_ref[:, cols], grad_ref[...], TN).astype(BF16)
        return carry

    lax.fori_loop(0, hidden_ref.shape[1] // block, step, 0)


def down_part(hidden, grads, block=256):
    length, ff = hidden.shape
    width = grads[0].shape[1]
    return call(
        functools.partial(down_terms_kernel, len(grads), block),
        near_in=(0,),
        in_specs=[NEAR] + [AWAY] * len(grads),
        out_specs=NEAR,
        near_out=(0,),
        out_shape=shape((ff, width)),
        scratch_shapes=[pltpu.VMEM((length, width), BF16), pltpu.SemaphoreType.DMA((HALVES * len(grads),))],
        compiler_params=vmem(12),
        cost_estimate=cost(2 * length * width * ff, 4 * width * ff),
        name="down_part",
    )(hidden, *grads)


def mlp_back_kernel(first, at, block, n_pieces, n_grads, order_ref, hidden_ref, slope_ref, up_ref, *refs):
    pieces, refs = refs[:n_pieces], refs[n_pieces:]
    grads, refs = refs[:n_grads], refs[n_grads:]
    if not first:
        refs = refs[1:]
    pre_ref, keep_ref, send_ref, branch_keep, branch_send, sum_ref, back_acc, branch_acc, down_ref, grad_ref, sems = refs
    count = grad_ref.shape[0]
    half = count // n_grads
    pairs = placed(order_ref, pieces, down_ref)
    pairs += [
        (ref.at[pl.ds(at * half, half), :], grad_ref.at[pl.ds(i * half, half), :]) for i, ref in enumerate(grads)
    ]
    fetch(pairs, sems)()
    rows = pl.ds(at * count, count)

    def terms(i):
        cols = pl.ds(pl.multiple_of(i * block, block), block)
        grad = (slope_ref[rows, cols] * dot(grad_ref[...], down_ref[cols, :], NT)).astype(BF16)
        pre_ref[rows, cols] = grad
        sum_ref[:, cols] = jnp.sum(grad.astype(F32), axis=0, keepdims=True)
        return dot(grad, up_ref[:, cols], NT), dot(hidden_ref[rows, cols], down_ref[cols, :], NN)

    back_acc[...], branch_acc[...] = terms(0)

    def step(i, carry):
        back, branch = terms(i)
        back_acc[...] += back
        branch_acc[...] += branch
        return carry

    lax.fori_loop(1, up_ref.shape[1] // block, step, 0)
    side = keep_ref.shape[0]
    keep_ref[...] = back_acc[:side, :].astype(BF16)
    send_ref[...] = back_acc[side:, :].astype(BF16)
    branch_keep[...] = branch_acc[:side, :].astype(BF16)
    branch_send[...] = branch_acc[side:, :].astype(BF16)


def mlp_back(at, order, hidden, slope, up, downs, grads, earlier, block=512):
    width = up.shape[0]
    length, ff = hidden.shape
    count = length // HALVES
    first = earlier is None
    given = 4 + len(downs) + len(grads)
    return call(
        functools.partial(mlp_back_kernel, first, at, min(block, ff // 2), len(downs), len(grads)),
        near_in=(1, 2, 3, given),
        near_out=(0, 1, 2, 3, 4),
        in_specs=[NUMBERS, NEAR, NEAR, NEAR] + [AWAY] * (given - 4) + ([] if first else [NEAR]),
        out_specs=[NEAR] * 6,
        out_shape=[shape((length, ff))] + [shape((count // 2, width))] * 4 + [shape((1, ff), F32)],
        scratch_shapes=[pltpu.VMEM((count, width), F32)] * 2
        + [pltpu.VMEM((ff, width), BF16), pltpu.VMEM((count, width), BF16)]
        + [pltpu.SemaphoreType.DMA((given - 4,))],
        input_output_aliases={} if first else {given: 0},
        compiler_params=vmem(20),
        cost_estimate=cost(6 * count * width * ff, 8 * width * ff),
        name="mlp_back",
    )(order, hidden, slope, up, *downs, *grads, *([] if first else [earlier]))


def second_back_kernel(middle_ref, keep_ref, near_ref, far_ref, out_ref, vec_ref, grad_ref, one_ref, sum_ref):
    upstream = keep_ref[...].astype(F32) + near_ref[...].astype(F32) + far_ref[...].astype(F32)
    xhat, rate = standardise(middle_ref[...])
    grad_out = out_ref[...].astype(F32)
    grad = grad_out + norm_back(upstream, xhat, rate, vec_ref[4:5, :])
    one = grad.astype(BF16)
    grad_ref[...] = grad
    one_ref[...] = one
    sums = [upstream * xhat, upstream, one.astype(F32), grad_out]
    sum_ref[...] = jnp.concatenate([jnp.sum(s, axis=0, keepdims=True) for s in sums], axis=0)


def second_back(at, middle_own, keep, near, far, grad_out_own, vecs):
    half, width = far.shape
    first = pl.BlockSpec((half, width), lambda i: (0, 0))
    mine = pl.BlockSpec((half, width), lambda i: (at, 0))
    return call(
        second_back_kernel,
        near_in=(1, 2, 3),
        near_out=(0, 1),
        grid=(1,),
        in_specs=[mine, first, first, first, mine, pl.BlockSpec(vecs.shape, lambda i: (0, 0))],
        out_specs=[first, first, pl.BlockSpec((4, width), lambda i: (0, 0))],
        out_shape=[shape((half, width), F32), shape((half, width)), shape((4, width), F32)],
        compiler_params=vmem(10),
        cost_estimate=cost(30 * half * width, 16 * half * width),
        name="second_back",
    )(middle_own, keep, near, far, grad_out_own, vecs)


def first_grad_kernel(grad_ref, qkv_ref, keep_ref, send_ref, sum_ref):
    step = pl.program_id(0)
    grad = grad_ref[...]
    total = dot(grad, qkv_ref[...], NT).astype(BF16)
    column = jnp.sum(grad.astype(F32), axis=0, keepdims=True)

    @pl.when(step == 0)
    def _():
        sum_ref[...] = column

    @pl.when(step > 0)
    def _():
        sum_ref[...] += column

    @pl.when(step % 2 == 0)
    def _():
        keep_ref[...] = total

    @pl.when(step % 2 == 1)
    def _():
        send_ref[...] = total


def first_grad(grad_qkv, qkv):
    length, wide = grad_qkv.shape
    width = qkv.shape[0]
    block = length // (2 * HALVES)
    kept = pl.BlockSpec((block, width), lambda i: (i // 2, 0))
    return call(
        first_grad_kernel,
        near_out=(0, 1),
        grid=(2 * HALVES,),
        in_specs=[pl.BlockSpec((block, wide), lambda i: (i, 0)), pl.BlockSpec(qkv.shape, lambda i: (0, 0))],
        out_specs=[kept, kept, pl.BlockSpec((1, wide), lambda i: (0, 0))],
        out_shape=[shape((length // 2, width))] * 2 + [shape((1, wide), F32)],
        compiler_params=vmem(16),
        cost_estimate=cost(2 * length * wide * width, 4 * length * width),
        name="first_grad",
    )(grad_qkv, qkv)


def out_terms_kernel(*refs):
    att_ref, out_ref = refs[0], refs[-1]
    total = None
    at = 0
    for ref in refs[1:-1]:
        rows = ref.shape[0]
        term = dot(att_ref[at : at + rows, :], ref[...], TN)
        total = term if total is None else total + term
        at += rows
    out_ref[...] = total.astype(BF16)


def out_terms(attended, grads):
    length, cols = attended.shape
    width = grads[0].shape[1]
    args = [attended] + list(grads)
    return call(
        out_terms_kernel,
        grid=(1,),
        in_specs=[pl.BlockSpec(a.shape, lambda i: (0, 0)) for a in args],
        out_specs=pl.BlockSpec((cols, width), lambda i: (0, 0)),
        out_shape=shape((cols, width)),
        compiler_params=vmem(16),
        cost_estimate=cost(2 * length * cols * width, 2 * length * width),
        name="out_terms",
    )(*args)


def first_back_kernel(tokens_ref, keep_ref, near_ref, far_ref, grad_ref, vec_ref, out_ref, sum_ref):
    upstream = keep_ref[...].astype(F32) + near_ref[...].astype(F32) + far_ref[...].astype(F32)
    xhat, rate = standardise(tokens_ref[...].astype(F32) + vec_ref[0:1, :])
    grad = grad_ref[...] + norm_back(upstream, xhat, rate, vec_ref[1:2, :])
    out_ref[...] = grad.astype(BF16)
    sums = [upstream * xhat, upstream, grad]
    found = jnp.concatenate([jnp.sum(s, axis=0, keepdims=True) for s in sums], axis=0)

    @pl.when(pl.program_id(0) == 0)
    def _():
        sum_ref[...] = found

    @pl.when(pl.program_id(0) > 0)
    def _():
        sum_ref[...] += found


def first_back(tokens_own, keep, near, far, grad_middle, vecs):
    rows, width = tokens_own.shape
    half = rows // HALVES
    mine = pl.BlockSpec((half, width), lambda i: (i, 0))
    spread = pl.BlockSpec((half, width), lambda i: (i * (keep.shape[0] // rows), 0))
    return call(
        first_back_kernel,
        grid=(HALVES,),
        in_specs=[mine, spread, spread, mine, mine, pl.BlockSpec(vecs.shape, lambda i: (0, 0))],
        out_specs=[mine, pl.BlockSpec((3, width), lambda i: (0, 0))],
        out_shape=[shape((rows, width)), shape((3, width), F32)],
        compiler_params=vmem(10),
        cost_estimate=cost(30 * rows * width, 16 * rows * width),
        name="first_back",
    )(tokens_own, keep, near, far, grad_middle, vecs)


def block_masks(size):
    return [m for m in range(size) if not m & 1] + [m for m in range(size) if m & 1]


def far_bits(size):
    bits, bit = [], 2
    while bit < size:
        bits.append(bit)
        bit *= 2
    return bits


def tied(*values):
    return lax.optimization_barrier(values)


class Line:
    def __init__(self, token):
        self.token = token

    def slot(self, sends=(), work=lambda: (), inputs=(), begin=(), end=()):
        values, begun, inputs, token = tied(
            [s[0] for s in sends], [s[0] for s in begin], list(inputs), self.token
        )
        found = [lax.ppermute(value, s[1], s[2]) for value, s in zip(values, sends)]
        started = [lax.ppermute(value, s[1], s[2]) for value, s in zip(begun, begin)]
        found, done, ended, self.token = tied(found, work(*inputs), list(end), token)
        return found, done, started, ended


def swap(value, bit, size):
    return (value, "seq", [(i, i ^ bit) for i in range(size)])


def cycle(n_dp):
    wide = int(round(math.sqrt(n_dp / 2)))
    if wide < 2 or wide * (n_dp // wide) != n_dp or (n_dp // wide) % 2:
        return list(range(n_dp))
    high = n_dp // wide
    order = [z * wide for z in range(high)]
    for turn, z in enumerate(range(high - 1, -1, -1)):
        line = list(range(1, wide))
        order += [z * wide + y for y in (line[::-1] if turn % 2 else line)]
    return order


class Ring:
    def __init__(self, n_dp):
        self.n = n_dp
        order = cycle(n_dp)
        where = np.argsort(np.array(order))
        table = np.array([[order[(where[d] + k) % n_dp] for k in range(n_dp)] for d in range(n_dp)], np.int32)
        row = lax.dynamic_index_in_dim(jnp.asarray(table), lax.axis_index("dp"), 0, keepdims=False)
        self.order = row
        self.ahead = [(order[i], order[(i + 1) % n_dp]) for i in range(n_dp)]
        self.back = [(order[i], order[(i - 1) % n_dp]) for i in range(n_dp)]
        self.far = n_dp // 2
        self.near = (n_dp - 1) // 2


class Gather:
    def __init__(self, ring, owns):
        self.ring = ring
        self.step = 0
        self.ahead = list(owns)
        self.back = list(owns)
        self.pieces = [[o] + [None] * (ring.n - 1) for o in owns]

    def sends(self):
        self.step += 1
        found = []
        if self.step <= self.ring.far:
            found += [(v, "dp", self.ring.ahead) for v in self.ahead]
        if self.step <= self.ring.near:
            found += [(v, "dp", self.ring.back) for v in self.back]
        return found

    def take(self, found):
        count = len(self.pieces)
        if self.step <= self.ring.far:
            self.ahead, found = list(found[:count]), found[count:]
            for held, value in zip(self.pieces, self.ahead):
                held[-self.step % self.ring.n] = value
        if self.step <= self.ring.near:
            self.back = list(found[:count])
            for held, value in zip(self.pieces, self.back):
                held[self.step] = value

    @property
    def left(self):
        return self.ring.far - self.step


def ring_kernel(adds, *refs):
    count = len(adds)
    values = list(refs[1 + count : -count])
    for i, (add, out) in enumerate(zip(adds, refs[-count:])):
        total = refs[1 + i][0].astype(F32)
        for _ in range(add):
            total = total + values.pop(0)[...].astype(F32)
        out[...] = total.astype(out.dtype)


def ring_blocks(order, items, dtype=BF16):
    n_dp = order.shape[0]
    args, in_specs, outs, out_specs = [], [], [], []
    for terms, k, _ in items:
        dims = terms.shape[1:]
        in_specs.append(pl.BlockSpec((1,) + dims, lambda i, at, k=k % n_dp: (at[k], 0, 0)))
        out_specs.append(pl.BlockSpec(dims, lambda i, at: (0, 0)))
        outs.append(shape(dims, dtype))
        args.append(terms)
    for _, _, values in items:
        for value in values:
            in_specs.append(pl.BlockSpec(value.shape, lambda i, at: (0, 0)))
            args.append(value)
    return pl.pallas_call(
        functools.partial(ring_kernel, [len(i[2]) for i in items]),
        grid_spec=pltpu.PrefetchScalarGridSpec(
            num_scalar_prefetch=1, grid=(1,), in_specs=in_specs, out_specs=out_specs
        ),
        out_shape=outs,
        compiler_params=vmem(16),
        name="ring_blocks",
    )(order, *args)


def table_kernel(me_ref, lead_ref, a_ref, b_ref, last_ref, ua_ref, ub_ref, column_ref, out_ref):
    me = me_ref[0]
    width = out_ref.shape[1]
    cols = column_ref.shape[1] // 3
    extra = ua_ref.shape[1] * (width // cols) // width
    part = 128 // extra
    sums = a_ref[...] + b_ref[...]
    last = last_ref[...]
    out_ref[...] = jnp.zeros_like(out_ref)
    out_ref[0:2, :] = last[0:2]
    mine = pl.ds(pl.multiple_of(me * cols, 128), cols)
    out_ref[2:3, mine] = column_ref[:, :cols]
    out_ref[3:4, mine] = column_ref[:, 2 * cols :]
    out_ref[4:5, :] = sums[2:3]
    out_ref[5:7, :] = sums[0:2]
    out_ref[7:8, :] = sums[3:4]
    out_ref[8:9, :] = lead_ref[0] * last[2:3]
    out_ref[9:10, :] = last[2:3]
    up = jnp.broadcast_to(ua_ref[...] + ub_ref[...], (8, width))
    here = lax.broadcasted_iota(jnp.int32, (1, width), 1) % 128 // part == me
    for k in range(extra):
        moved = pltpu.roll(up, ((me - k) * part + width) % width, 1)
        out_ref[10 + k : 11 + k, :] = jnp.where(here, moved[0:1, :], 0.0)


def small_table(me, lead, sums_a, sums_b, last, up_a, up_b, columns):
    width = last.shape[1]
    args = [sums_a, sums_b, last, up_a, up_b, columns]
    numbers = pl.BlockSpec(memory_space=pltpu.SMEM)
    return pl.pallas_call(
        table_kernel,
        grid=(1,),
        in_specs=[numbers] * 2 + [pl.BlockSpec(a.shape, lambda i: (0, 0)) for a in args],
        out_specs=pl.BlockSpec((16, width), lambda i: (0, 0)),
        out_shape=shape((16, width), F32),
        compiler_params=vmem(4),
        name="small_table",
    )(me, lead, *args)


def halve_kernel(side_ref, *refs):
    mine_ref, other_ref = refs[-2:]
    wide = mine_ref.shape[1]
    side = side_ref[0]
    for at, target in ((side, mine_ref), (1 - side, other_ref)):
        total = 0.0
        for ref in refs[:-2]:
            total = total + ref[:, pl.ds(pl.multiple_of(at * wide, 128), wide)]
        target[...] = total


def halve(side, values):
    rows, wide = values[0].shape
    half = pl.BlockSpec((rows, wide // 2), lambda i: (0, 0))
    return pl.pallas_call(
        halve_kernel,
        grid=(1,),
        in_specs=[pl.BlockSpec(memory_space=pltpu.SMEM)] + [pl.BlockSpec(v.shape, lambda i: (0, 0)) for v in values],
        out_specs=[half] * 2,
        out_shape=[shape((rows, wide // 2), F32)] * 2,
        compiler_params=vmem(4),
        name="halve",
    )(side, *values)


def owner_kernel(count, order_ref, me_ref, term_ref, *refs):
    part = refs[-1].shape[0]
    outs = refs[-count:]
    for mask, out in enumerate(outs):
        rows = pl.ds(pl.multiple_of((me_ref[0] ^ mask) * part, part), part)
        total = term_ref[0, rows, :].astype(F32)
        for ref in refs[:-count]:
            total = total + ref[rows, :].astype(F32)
        out[...] = total.astype(BF16)


def owner_blocks(order, me, terms, values, n_seq):
    _, rows, wide = terms.shape
    part = rows // n_seq
    if part % 16:
        (total,) = ring_blocks(order, [(terms, 0, values)])
        blocks = total.reshape(n_seq, part, wide)
        return [lax.dynamic_index_in_dim(blocks, me[0] ^ m, 0, keepdims=False) for m in range(n_seq)]
    return pl.pallas_call(
        functools.partial(owner_kernel, n_seq),
        grid_spec=pltpu.PrefetchScalarGridSpec(
            num_scalar_prefetch=2,
            grid=(1,),
            in_specs=[pl.BlockSpec((1, rows, wide), lambda i, at, me: (at[0], 0, 0))]
            + [pl.BlockSpec((rows, wide), lambda i, at, me: (0, 0))] * len(values),
            out_specs=[pl.BlockSpec((part, wide), lambda i, at, me: (0, 0))] * n_seq,
        ),
        out_shape=[shape((part, wide))] * n_seq,
        compiler_params=vmem(8),
        name="owner_blocks",
    )(order, me, terms, *values)


def unpack_kernel(groups, me_ref, *refs):
    out_ref = refs[-1]
    n_seq = len(refs) - 1
    wide = refs[0].shape[1] // groups
    for mask, ref in enumerate(refs[:-1]):
        for i in range(groups):
            start = pl.multiple_of((i * n_seq + (me_ref[0] ^ mask)) * wide, 128)
            out_ref[:, pl.ds(start, wide)] = ref[:, i * wide : (i + 1) * wide].astype(F32)


def unpack(groups, me, pieces):
    part, wide = pieces[0].shape
    n_seq = len(pieces)
    if (wide // groups) % 128:
        whole = flipped(dict(enumerate(pieces)), n_seq).reshape(n_seq, part, groups, -1)
        return jnp.moveaxis(whole, 0, 2).reshape(part, -1).astype(F32)
    return pl.pallas_call(
        functools.partial(unpack_kernel, groups),
        grid=(1,),
        in_specs=[pl.BlockSpec(memory_space=pltpu.SMEM)] + [pl.BlockSpec((part, wide), lambda i: (0, 0))] * n_seq,
        out_specs=pl.BlockSpec((part, wide * n_seq), lambda i: (0, 0)),
        out_shape=shape((part, wide * n_seq), F32),
        compiler_params=vmem(8),
        name="unpack",
    )(me, *pieces)


class Scatter:
    def __init__(self, ring, terms):
        self.ring = ring
        self.terms = terms
        self.step = 0
        count = len(terms)
        found = ring_blocks(
            ring.order, [(t, ring.far, ()) for t in terms] + [(t, -ring.near, ()) for t in terms]
        )
        self.ahead, self.back = found[:count], found[count:]

    def sends(self):
        self.step += 1
        found = [(v, "dp", self.ring.ahead) for v in self.ahead]
        if self.step > self.ring.far - self.ring.near:
            found += [(v, "dp", self.ring.back) for v in self.back]
        return found

    def take(self, found):
        count = len(self.terms)
        left = self.ring.far - self.step
        ahead, back = found[:count], found[count:]
        if left:
            items = [(t, left, (v,)) for t, v in zip(self.terms, ahead)]
            items += [(t, -left, (v,)) for t, v in zip(self.terms, back)]
            found = ring_blocks(self.ring.order, items)
            ahead, back = found[:count], found[count:]
        self.ahead = ahead
        if back:
            self.back = back

    @property
    def left(self):
        return self.ring.far - self.step

    def total(self, dtype=F32):
        items = [(t, 0, (a, b)) for t, a, b in zip(self.terms, self.ahead, self.back)]
        return ring_blocks(self.ring.order, items, dtype)


def flipped(pieces, bits):
    me = lax.axis_index("seq")
    size = len(pieces)
    held = [pieces[m] for m in range(size)]
    bit = 1
    while bit < size:
        turned = (me & bit) != 0
        held = [jnp.where(turned, held[m ^ bit], held[m]) for m in range(size)]
        bit *= 2
    return jnp.stack(held)


def make_body(n_dp, n_seq):
    masks = block_masks(n_seq)
    far = far_bits(n_seq)
    far_masks = [m for m in range(n_seq) if not m & 1]

    def body(
        tokens,
        lead_hours,
        valid_counts,
        patch_mask,
        first_gain,
        first_shift,
        qkv_weight,
        query_bias,
        value_bias,
        out_weight,
        out_bias,
        second_gain,
        second_shift,
        up_weight,
        up_bias,
        down_weight,
        down_bias,
        lead_weight,
        lead_bias,
        cotangent,
    ):
        me = lax.axis_index("seq")
        rows, width = tokens.shape[1], tokens.shape[2]
        length = rows * n_seq
        half = rows // HALVES
        part = qkv_weight.shape[0]
        ff_part = down_weight.shape[0]
        ff = up_weight.shape[1]
        extra = ff_part // part
        cols = width // n_seq
        ff_cols = ff // n_seq
        lead = lead_hours[0].astype(F32) / 100.0
        count = valid_counts[0]
        positions = me * rows + jnp.arange(rows, dtype=jnp.int32)
        loss_weight = (patch_mask[0] * (positions < count).astype(jnp.int32)).astype(BF16)
        ring = Ring(n_dp)
        me_ref = me.reshape(1).astype(jnp.int32)
        lead_ref = lead.reshape(1)
        order = ring.order

        def far_gather(own, at_bit):
            return [swap(own[m], far[at_bit], n_seq) for m in sorted(own)]

        line = Line(me_ref)

        def run(parts, sends=(), work=lambda: (), inputs=(), begin=(), end=()):
            mine = [part.sends() if part.left > 0 else [] for part in parts]
            flat = [m for group in mine for m in group]
            found, done, started, ended = line.slot(flat + list(sends), work, inputs, begin, end)
            found = list(found)
            for part, group in zip(parts, mine):
                if group:
                    part.take(found[: len(group)])
                    found = found[len(group) :]
            return found, done, started, ended

        def near_all(held):
            return [swap(held[m], 1, n_seq) for m in sorted(held)]

        def with_near(held, found):
            held.update({m ^ 1: v for m, v in zip(sorted(held), found)})

        def with_far(held, found, at_bit):
            held.update({m ^ far[at_bit]: v for m, v in zip(sorted(held), found)})

        def rest_far(held):
            for i in range(1, len(far)):
                found, _, _, _ = line.slot(far_gather(held, i))
                with_far(held, found, i)

        vectors = [
            first_gain,
            first_shift,
            query_bias,
            value_bias,
            out_bias,
            second_gain,
            second_shift,
            down_bias,
            lead_weight,
            lead_bias,
            up_bias,
        ]
        kinds = 10 + extra
        gather_down = Gather(ring, [down_weight])
        _, packed, _, _ = run(
            [gather_down], work=lambda *a: tuple(pack(n_dp, n_seq, *a)), inputs=(me_ref, qkv_weight, up_weight, vectors)
        )
        found, (grad_out_own,), _, _ = run(
            [gather_down],
            [swap(packed[m], m, n_seq) for m in range(1, n_seq)],
            lambda c, w: (c * w[:, None],),
            (cotangent[0], loss_weight),
        )
        one_own, up_own = join(n_seq, 3 * cols + 128, me_ref, [packed[0]] + list(found), out_weight)

        gather_one = Gather(ring, [one_own])
        tokens_held = {0: tokens[0]}
        _, _, tokens_far, _ = run([gather_one], begin=far_gather(tokens_held, 0))
        _, _, _, tokens_far = run([gather_one], end=tokens_far)
        with_far(tokens_held, tokens_far, 0)
        rest_far(tokens_held)
        grad_held = {0: grad_out_own}
        found, _, grad_far, _ = run([gather_one], near_all(tokens_held), begin=far_gather(grad_held, 0))
        with_near(tokens_held, found)
        while gather_one.left > 1:
            run([gather_one])
        gather_up = Gather(ring, [up_own])
        _, _, _, grad_far = run([gather_one, gather_up], end=grad_far)
        with_far(grad_held, grad_far, 0)
        rest_far(grad_held)
        tokens_by = [tokens_held[m] for m in masks]
        out_held = {0: middle_columns(gather_one.pieces[0], 3 * cols, cols)}
        valid = count.reshape(1)

        def attention(*a):
            normed, q, k, v, qkv, table, vecs = project(
                me_ref, order, lead_ref, a[:n_seq], ordered(order, a[n_seq:]), kinds
            )
            return normed, q, k, v, qkv, table, vecs, *attend(n_seq, me_ref, valid, q, k, v)

        found, (normed, q, k, v, qkv, table, vecs, attended, lse), _, _ = run(
            [gather_down, gather_up],
            far_gather(out_held, 0) + near_all(grad_held),
            work=attention,
            inputs=tokens_by + gather_one.pieces[0],
        )
        n = len(out_held)
        with_near(grad_held, found[n:])
        with_far(out_held, found[:n], 0)
        rest_far(out_held)

        def up_bias_of(table):
            u_bias = table[10 : 10 + extra].reshape(extra, n_dp, n_seq, part)
            u_bias = lax.dynamic_index_in_dim(u_bias, me, 2, keepdims=False)
            u_bias = jnp.swapaxes(u_bias, 0, 1).reshape(1, ff_cols)
            return (u_bias,)

        att_held = {0: attended}
        found, (u_bias,), _, _ = run(
            [gather_down, gather_up],
            near_all(out_held) + far_gather(att_held, 0),
            work=up_bias_of,
            inputs=[table],
        )
        n = len(out_held)
        with_near(out_held, found[:n])
        with_far(att_held, found[n:], 0)
        rest_far(att_held)
        found, _, _, _ = run([gather_down, gather_up], near_all(att_held))
        with_near(att_held, found)

        def out_whole(pieces):
            if part % 16 == 0:
                return pieces
            blocks = [ordered(order, [p[i * n_seq * part : (i + 1) * n_seq * part] for i in range(n_dp)])[0] for p in pieces]
            blocks = flipped(dict(enumerate(blocks)), n_seq).reshape(n_seq, n_dp, n_seq, part, cols)
            return [jnp.transpose(blocks, (1, 0, 3, 2, 4)).reshape(width, width)]

        _, (normed_two, middle_own, out_mine), _, _ = run(
            [gather_down, gather_up],
            work=lambda tok, att, outs, vecs: tuple(middle_norm(me_ref, order, tok, att, out_whole(outs), vecs)),
            inputs=(tokens_by, [att_held[m] for m in masks], [out_held[m] for m in range(n_seq)], vecs),
        )
        while gather_up.left or gather_down.left:
            run([gather_down, gather_up])
        up, hidden, slope = up_part(order, normed_two, u_bias, ordered(order, gather_up.pieces[0]))
        grads = [grad_held[m] for m in masks]
        down_terms = down_part(hidden, grads).reshape(n_dp, ff_part, width)
        downs = ordered(order, gather_down.pieces[0])

        def half_sum(keep, other):
            found = {}
            for at, m in enumerate(far_masks):
                if m:
                    rows_at = slice(at * half, (at + 1) * half)
                    found[m] = (keep[rows_at].astype(F32) + other[rows_at].astype(F32)).astype(BF16)
            return found

        def far_first(held):
            bit = far[-1]
            return [swap(held[m], bit, n_seq) for m in sorted(held) if m & bit]

        def far_rest(held, found):
            for at, bit in enumerate(reversed(far)):
                upper = sorted(m for m in held if m & bit)
                if at:
                    found, _, _, _ = line.slot([swap(held[m], bit, n_seq) for m in upper])
                kept = {m: held[m] for m in held if not m & bit}
                for m, value in zip(upper, found):
                    low = m ^ bit
                    if low in kept:
                        value = (kept[low].astype(F32) + value.astype(F32)).astype(BF16)
                    kept[low] = value
                held = kept
            return held[0]

        scatter_down = Scatter(ring, [down_terms])
        _, (pre, keep_a, send_a, branch_keep_a, branch_send_a, sum_a), _, _ = run(
            [scatter_down],
            work=lambda *a: tuple(mlp_back(0, order, *a, None)),
            inputs=(hidden, slope, up, downs, grads),
        )
        (near_a,), (pre, keep_b, send_b, branch_keep_b, branch_send_b, sum_b), _, _ = run(
            [scatter_down],
            [swap(send_a, 1, n_seq)],
            work=lambda *a: tuple(mlp_back(1, order, *a)),
            inputs=(hidden, slope, up, downs, grads, pre),
        )
        held_a = half_sum(keep_a, near_a)
        sends = far_first(held_a)
        found, (up_terms,), _, _ = run(
            [scatter_down],
            sends + [swap(send_b, 1, n_seq)],
            work=lambda n, p: (dot(n, p, TN).astype(BF16).reshape(n_dp, n_seq * part, ff_cols),),
            inputs=(normed_two, pre),
        )
        far_a, near_b = far_rest(held_a, found[: len(sends)]), found[-1]
        held_b = half_sum(keep_b, near_b)

        def back_half(at):
            return lambda *a: tuple(second_back(at, *a))

        sends = far_first(held_b)
        found, (grad_mid_a, one_a, sums_a), _, _ = run(
            [scatter_down],
            sends + [swap(branch_send_a, 1, n_seq), swap(branch_send_b, 1, n_seq)],
            work=back_half(0),
            inputs=(middle_own, keep_a, near_a, far_a, grad_out_own, vecs),
        )
        far_b, branch_other = far_rest(held_b, found[: len(sends)]), found[-2:]
        while scatter_down.left:
            run([scatter_down])

        scatter_up = Scatter(ring, [up_terms])
        one_held_a = {0: one_a}
        found, (grad_mid_b, one_b, sums_b), _, _ = run(
            [scatter_up],
            far_gather(one_held_a, 0),
            work=back_half(1),
            inputs=(middle_own, keep_b, near_b, far_b, grad_out_own, vecs),
        )
        with_far(one_held_a, found, 0)
        rest_far(one_held_a)
        found, _, _, _ = line.slot(near_all(one_held_a))
        with_near(one_held_a, found)
        one_held_b = {0: one_b}
        found, (dq_a, dk_a, dv_a), _, _ = run(
            [scatter_up],
            far_gather(one_held_b, 0),
            work=lambda *a: tuple(attend_back(0, me_ref, valid, *a, None)),
            inputs=(q, k, v, lse, out_mine, [one_held_a[m] for m in masks]),
        )
        with_far(one_held_b, found, 0)
        rest_far(one_held_b)
        found, _, _, _ = line.slot(near_all(one_held_b))
        with_near(one_held_b, found)
        branch_held = {
            m: jnp.concatenate([value, half_sum(branch_keep_b, branch_other[1])[m]], axis=0)
            for m, value in half_sum(branch_keep_a, branch_other[0]).items()
        }
        ones = [one_held_a[m] for m in masks] + [one_held_b[m] for m in masks]
        sends = far_first(branch_held)

        def second_attend(q, k, v, lse, out_mine, grads, earlier):
            return (attend_back(1, me_ref, valid, q, k, v, lse, out_mine, grads, earlier),)

        found, (grad_qkv,), _, _ = run(
            [scatter_up],
            sends,
            work=second_attend,
            inputs=(q, k, v, lse, out_mine, [one_held_b[m] for m in masks], (dq_a, dk_a, dv_a)),
        )
        branch_far = far_rest(branch_held, found)

        def last_terms(normed, grad_qkv, attended, ones):
            terms = dot(normed, grad_qkv, TN).astype(BF16).reshape(n_dp, n_seq * part, 3 * cols)
            return terms, out_terms(attended, ones).reshape(n_dp, part, width)

        gn_keep, gn_send, column_sums = first_grad(grad_qkv, qkv)
        (gn_near,), (qkv_terms, out_sums), _, _ = run(
            [scatter_up], [swap(gn_send, 1, n_seq)], last_terms, (normed, grad_qkv, attended, ones)
        )
        while scatter_up.left:
            run([scatter_up])
        size = half * len(far_masks)
        gn_held = {
            m: jnp.concatenate([value, half_sum(gn_keep[size:], gn_near[size:])[m]], axis=0)
            for m, value in half_sum(gn_keep[:size], gn_near[:size]).items()
        }

        def final_rows(keep_a, keep_b, near_a, near_b, far_part, mid, bias):
            total = jnp.concatenate([keep_a[:half], keep_b[:half]], axis=0).astype(F32)
            total = total + jnp.concatenate([near_a[:half], near_b[:half]], axis=0).astype(F32)
            return ((mid + (total + far_part.astype(F32) + bias[6:7])).astype(BF16),)

        scatter_one = Scatter(ring, [qkv_terms, out_sums])
        _, up_blocks, gn_far, _ = run(
            [scatter_one],
            work=lambda t, v: tuple(owner_blocks(order, me_ref, t, v, n_seq)),
            inputs=(up_terms, (scatter_up.ahead[0], scatter_up.back[0])),
            begin=far_first(gn_held),
        )
        _, (block_out, down_grad), _, gn_far = run(
            [scatter_one],
            work=lambda a, b: (*final_rows(*a), *ring_blocks(order, [(b[0], 0, b[1])], F32)),
            inputs=(
                (branch_keep_a, branch_keep_b, branch_other[0], branch_other[1], branch_far, middle_own, vecs),
                (down_terms, (scatter_down.ahead[0], scatter_down.back[0])),
            ),
            end=gn_far,
        )
        gn_far = far_rest(gn_held, gn_far)
        grad_middle = jnp.concatenate([grad_mid_a, grad_mid_b], axis=0)
        plain = (width // n_dp) % 128 == 0 and extra == n_seq and n_seq * part == 128

        def last_norm(*a):
            tokens_grad, last_sums = first_back(*a)
            if not plain:
                return tokens_grad, last_sums
            return tokens_grad, small_table(
                me_ref, lead_ref, sums_a, sums_b, last_sums, sum_a, sum_b, column_sums
            )

        found, (tokens_grad, table), _, _ = run(
            [scatter_one],
            [swap(up_blocks[m], m, n_seq) for m in range(1, n_seq)],
            work=last_norm,
            inputs=(tokens[0], gn_keep, gn_near, gn_far, grad_middle, vecs),
        )
        up_pieces = [up_blocks[0]] + list(found)

        bits = []
        while 2 ** len(bits) < n_dp:
            bits.append(2 ** len(bits))
        bits.reverse()
        if plain:
            held = [table]
            at_dp = lax.axis_index("dp")
        else:
            sums = sums_a + sums_b
            q_sum = lax.dynamic_update_slice(jnp.zeros((1, width), F32), column_sums[:, :cols], (0, me * cols))
            v_sum = lax.dynamic_update_slice(jnp.zeros((1, width), F32), column_sums[:, 2 * cols :], (0, me * cols))
            u_sum = jnp.swapaxes((sum_a + sum_b).reshape(n_dp, extra, part), 0, 1)
            u_sum = lax.dynamic_update_index_in_dim(jnp.zeros((extra, n_dp, n_seq, part), F32), u_sum, me, 2)
            rows_out = [table[0:2], q_sum, v_sum, sums[2:3], sums[0:2], sums[3:4], lead * table[2:3], table[2:3]]
            table = jnp.concatenate(rows_out + [u_sum.reshape(extra, width)], axis=0)
            table = lax.psum_scatter(table, ("dp", "seq"), scatter_dimension=1, tiled=True)
            bits = []

        def halved(bit):
            return halve(((at_dp // bit) % 2).reshape(1).astype(jnp.int32), held)

        while scatter_one.left:
            if bits:
                bit = bits.pop(0)
                mine, other = halved(bit)
                found, _, _, _ = run([scatter_one], [(other, "dp", [(i, i ^ bit) for i in range(n_dp)])])
                held = [mine, found[0]]
            else:
                run([scatter_one])
        qkv_blocks = owner_blocks(order, me_ref, qkv_terms, (scatter_one.ahead[0], scatter_one.back[0]), n_seq)
        (out_sum,) = ring_blocks(order, [(out_sums, 0, (scatter_one.ahead[1], scatter_one.back[1]))])
        moves = []
        for dp_at in range(n_dp):
            for seq_at in range(n_seq):
                moves.append((dp_at * n_seq + seq_at, seq_at * n_dp + dp_at))
        final = [(out_sum, ("dp", "seq"), moves)] + [swap(qkv_blocks[m], m, n_seq) for m in range(1, n_seq)]
        last = None
        while bits:
            bit = bits.pop(0)
            mine, other = halved(bit)
            found, done, begun, _ = line.slot(
                [(other, "dp", [(i, i ^ bit) for i in range(n_dp)])],
                lambda *a: (unpack(n_dp, me_ref, a),) if last is None else (),
                up_pieces,
                begin=final if last is None else (),
            )
            if last is None:
                last = begun
                (up_weight_grad,) = done
            held = [mine, found[0]]
        if last is None:
            last, (up_weight_grad,), _, _ = line.slot(final, lambda *a: (unpack(n_dp, me_ref, a),), up_pieces)
        if plain:
            table = held[0] + held[1]
            for bit in far + ([1] if n_seq > 1 else []):
                found, _, _, _ = line.slot([swap(table, bit, n_seq)])
                table = table + found[0]
            table = lax.dynamic_slice_in_dim(table, me * part, part, 1)
        owned = table[:kinds]
        out_weight_grad = last[0].astype(F32)
        qkv_weight_grad = unpack(3, me_ref, [qkv_blocks[0]] + list(last[1:]))
        return (
            block_out[None],
            tokens_grad[None],
            owned[0],
            owned[1],
            qkv_weight_grad,
            owned[2],
            owned[3],
            out_weight_grad,
            owned[4],
            owned[5],
            owned[6],
            up_weight_grad,
            owned[10 : 10 + extra].reshape(ff_part),
            down_grad[0] if down_grad.ndim == 3 else down_grad,
            owned[7],
            owned[8],
            owned[9],
        )

    return body


def solution(mesh):
    both = P(("dp", "seq"))
    matrix = P(("dp", "seq"), None)
    tokens = P("dp", "seq", None)
    in_specs = (tokens, P("dp"), P("dp"), P("dp", "seq"), both, both, matrix, both, both, matrix, both, both, both)
    in_specs += (matrix, both, matrix, both, both, both, tokens)
    out_specs = (tokens, tokens, both, both, matrix, both, both, matrix, both, both, both, matrix, both, matrix)
    out_specs += (both, both, both)
    return jax.shard_map(
        make_body(mesh.shape["dp"], mesh.shape["seq"]),
        mesh=mesh,
        in_specs=in_specs,
        out_specs=out_specs,
        check_vma=False,
    )
```

```python
import functools
import math

import jax
import jax.numpy as jnp
import numpy as np
from jax import lax
from jax.experimental import pallas as pl
from jax.experimental.pallas import tpu as pltpu
from jax.sharding import PartitionSpec as P

HEADS = 16
HEAD_DIM = 64
PAIR = 2 * HEAD_DIM
SCALE = 1.0 / math.sqrt(HEAD_DIM)
EPSILON = 1e-06
MASKED = -1e30
F32 = jnp.float32
BF16 = jnp.bfloat16
NN, NT, TN = ((1,), (0,)), ((1,), (1,)), ((0,), (0,))
HALVES = 2
MIB = 1024 * 1024
NEAR = pl.BlockSpec(memory_space=pltpu.VMEM)
AWAY = pl.BlockSpec(memory_space=pl.ANY)
NUMBERS = pl.BlockSpec(memory_space=pltpu.SMEM)


def dot(left, right, contract):
    return lax.dot_general(left, right, (contract, ((), ())), preferred_element_type=F32)


def shape(dims, dtype=BF16):
    return jax.ShapeDtypeStruct(dims, dtype)


def call(kernel, *, in_specs, out_shape, near_in=(), near_out=(), **options):
    def large(value):
        return math.prod(value.shape) * value.dtype.itemsize >= 65536

    def run(*args):
        kept = []
        for i, a in enumerate(args):
            if large(a):
                a = pltpu.with_memory_space_constraint(a, pltpu.VMEM if i in near_in else pltpu.HBM)
            kept.append(a)
        single = not isinstance(out_shape, (list, tuple))
        outs = [out_shape] if single else list(out_shape)
        outs = [
            ((pltpu.VMEM if i in near_out else pltpu.HBM)(o.shape, o.dtype) if large(o) else o)
            for i, o in enumerate(outs)
        ]
        return pl.pallas_call(kernel, in_specs=in_specs, out_shape=outs[0] if single else outs, **options)(*kept)

    return run


def away(value):
    return pltpu.with_memory_space_constraint(value, pltpu.HBM)


def near(value):
    return pltpu.with_memory_space_constraint(value, pltpu.VMEM)


def vmem(mib):
    return pltpu.CompilerParams(vmem_limit_bytes=mib * MIB)


def cost(flops, moved, exps=0):
    return pl.CostEstimate(flops=int(flops), bytes_accessed=int(moved), transcendentals=int(exps))


def standardise(values):
    centered = values - jnp.mean(values, axis=-1, keepdims=True)
    rate = lax.rsqrt(jnp.mean(centered * centered, axis=-1, keepdims=True) + EPSILON)
    return centered * rate, rate


def norm_back(upstream, xhat, rate, gain):
    scaled = upstream * gain
    inner = jnp.mean(scaled * xhat, axis=-1, keepdims=True)
    return rate * (scaled - jnp.mean(scaled, axis=-1, keepdims=True) - xhat * inner)


def pack_kernel(n_dp, n_seq, me_ref, qkv_ref, up_ref, *refs):
    vectors, out_refs = refs[: -2 * n_seq], refs[-2 * n_seq :]
    out_refs, up_refs = out_refs[:n_seq], out_refs[n_seq:]
    me = me_ref[0]
    part = qkv_ref.shape[0]
    cols = qkv_ref.shape[1] // (3 * n_seq)
    piece = up_ref.shape[1] // (n_dp * n_seq)
    rows = [ref[...].astype(F32)[:, i : i + part] for ref in vectors for i in range(0, ref.shape[1], part)]
    kinds = len(rows)
    rows = jnp.concatenate(rows + [jnp.zeros((128 - kinds, part), F32)], axis=0)
    rows = jnp.concatenate([rows, jnp.zeros((128, 128 - part), F32)], axis=1)
    small = rows.T[:part, :].astype(BF16)
    for mask, ref in enumerate(out_refs):
        place = me ^ mask
        for i in range(3):
            start = pl.multiple_of((i * n_seq + place) * cols, 128)
            ref[:, i * cols : (i + 1) * cols] = qkv_ref[:, pl.ds(start, cols)]
        at = 3 * cols
        ref[:, at : at + 128] = small
        for i in range(n_dp):
            start = pl.multiple_of((i * n_seq + place) * piece, 128)
            up_refs[mask][:, i * piece : (i + 1) * piece] = up_ref[:, pl.ds(start, piece)]


def pack(n_dp, n_seq, me, qkv, up, vectors):
    part = qkv.shape[0]
    wide = qkv.shape[1] // n_seq + 128
    ff = up.shape[1] // n_seq
    if up.shape[1] // (n_dp * n_seq) % 128 or part % 16:
        small = jnp.concatenate(vectors).reshape(-1, part).T
        small = jnp.pad(small, ((0, 0), (0, 128 - small.shape[1])))
        qkv_split = qkv.reshape(part, 3, n_seq, -1)
        up_split = up.reshape(part, n_dp, n_seq, -1)

        def block(place):
            q = lax.dynamic_index_in_dim(qkv_split, place, 2, keepdims=False).reshape(part, -1)
            u = lax.dynamic_index_in_dim(up_split, place, 2, keepdims=False).reshape(part, -1)
            return jnp.concatenate([q, small], axis=1), u

        blocks = [block(me[0] ^ m) for m in range(n_seq)]
        return [b[0] for b in blocks] + [b[1] for b in blocks]
    args = [qkv, up] + [v.reshape(1, -1) for v in vectors]
    args = [pltpu.with_memory_space_constraint(a, pltpu.HBM) for a in args]
    return pl.pallas_call(
        functools.partial(pack_kernel, n_dp, n_seq),
        grid=(1,),
        in_specs=[pl.BlockSpec(memory_space=pltpu.SMEM)] + [pl.BlockSpec(a.shape, lambda i: (0, 0)) for a in args],
        out_specs=[pl.BlockSpec((part, wide), lambda i: (0, 0))] * n_seq
        + [pl.BlockSpec((part, ff), lambda i: (0, 0))] * n_seq,
        out_shape=[shape((part, wide))] * n_seq + [shape((part, ff))] * n_seq,
        compiler_params=vmem(8),
        name="pack",
    )(me, *args)


def join_one_kernel(n_seq, me_ref, *refs):
    out_ref, left_ref = refs[-2:]
    part, wide = out_ref.shape
    cols = wide // n_seq
    edge = refs[0].shape[1] - 128
    for t, ref in enumerate(refs[:-2]):
        rows = pl.ds(pl.multiple_of((me_ref[0] ^ t) * part, part), part)
        left_ref[rows, :edge] = ref[:, :edge]
        left_ref[rows, edge + cols :] = ref[:, edge:]
        left_ref[t * part : (t + 1) * part, edge : edge + cols] = out_ref[:, t * cols : (t + 1) * cols]


def join_two_kernel(n_seq, me_ref, *refs):
    down_ref, right_ref = refs[-2:]
    half = down_ref.shape[1]
    part = refs[0].shape[0]
    right_ref[:, -half:] = down_ref[...]
    for t, ref in enumerate(refs[:-2]):
        right_ref[pl.ds(pl.multiple_of((me_ref[0] ^ t) * part, part), part), :-half] = ref[...]


def join(kernel, n_seq, me, pieces, weight, wide):
    rows = pieces[0].shape[0] * n_seq
    args = list(pieces) + [away(weight)]
    return pl.pallas_call(
        functools.partial(kernel, n_seq),
        grid=(1,),
        in_specs=[NUMBERS] + [pl.BlockSpec(a.shape, lambda i: (0, 0)) for a in args],
        out_specs=pl.BlockSpec((rows, wide), lambda i: (0, 0)),
        out_shape=shape((rows, wide)),
        compiler_params=vmem(8),
        name="join",
    )(me, *args)


def join_one(n_seq, me, pieces, out_weight):
    part, edge = pieces[0].shape
    edge -= 128
    cols = out_weight.shape[1] // n_seq
    if part % 16:
        whole = flipped(dict(enumerate(pieces)), n_seq).reshape(part * n_seq, edge + 128)
        beside = jnp.moveaxis(out_weight.reshape(part, n_seq, cols), 1, 0).reshape(part * n_seq, cols)
        return jnp.concatenate([whole[:, :edge], beside, whole[:, edge:]], axis=1)
    return join(join_one_kernel, n_seq, me, pieces, out_weight, edge + cols + 128)


def join_two(n_seq, me, pieces, down_weight):
    part, wide = pieces[0].shape
    rows = part * n_seq
    if part % 16:
        whole = flipped(dict(enumerate(pieces)), n_seq).reshape(rows, wide)
        return jnp.concatenate([whole, down_weight.reshape(rows, -1)], axis=1)
    return join(join_two_kernel, n_seq, me, pieces, down_weight, wide + down_weight.shape[1])


def ordered(order, pieces):
    if pieces[0].shape[0] % 128 == 0:
        return list(pieces)
    whole = jnp.stack(pieces)
    out = whole
    for k in range(len(pieces)):
        out = lax.dynamic_update_index_in_dim(out, whole[k], order[k], 0)
    return [out.reshape(-1, out.shape[-1])]


def lay(order_ref, pieces, target, cols=slice(None)):
    if len(pieces) == 1:
        target[...] = pieces[0][:, cols]
        return
    rows = pieces[0].shape[0]
    for k, piece in enumerate(pieces):
        target[pl.ds(pl.multiple_of(order_ref[k] * rows, rows), rows), :] = piece[:, cols]


def middle_columns_kernel(*refs):
    out_ref = refs[-1]
    rows = refs[0].shape[0]
    for k, ref in enumerate(refs[:-1]):
        out_ref[k * rows : (k + 1) * rows, :] = ref[...]


def middle_columns(pieces, start, cols):
    rows = pieces[0].shape[0]
    if rows % 128 or start % cols:
        return jnp.concatenate([piece[:, start : start + cols] for piece in pieces], axis=0)
    total = rows * len(pieces)
    return call(
        middle_columns_kernel,
        grid=(1,),
        in_specs=[pl.BlockSpec((rows, cols), lambda i: (0, start // cols))] * len(pieces),
        out_specs=pl.BlockSpec((total, cols), lambda i: (0, 0)),
        out_shape=shape((total, cols)),
        compiler_params=vmem(4),
        name="middle_columns",
    )(*pieces)


def project_kernel(n_seq, n_pieces, me_ref, order_ref, lead_ref, *refs):
    tokens = refs[:n_seq]
    pieces = refs[n_seq : n_seq + n_pieces]
    normed_ref, q_ref, k_ref, v_ref, qkv_ref, table_ref, vec_ref, small_ref = refs[n_seq + n_pieces :]
    cols = q_ref.shape[1]

    @pl.when(pl.program_id(0) == 0)
    def _():
        lay(order_ref, pieces, qkv_ref, slice(0, 3 * cols))
        lay(order_ref, pieces, small_ref, slice(4 * cols, 4 * cols + 128))
        table_ref[...] = small_ref[...].astype(F32).T[: table_ref.shape[0], :]
        for i, kind in enumerate((0, 0, 1, 4, 5, 6, 7, 7)):
            vec_ref[i : i + 1, :] = table_ref[kind : kind + 1, :]
        vec_ref[0:1, :] = lead_ref[0] * table_ref[8:9, :] + table_ref[9:10, :]

    start = jnp.concatenate([ref[...] for ref in tokens], axis=0).astype(F32) + vec_ref[0:1, :]
    xhat, _ = standardise(start)
    normed = (xhat * vec_ref[1:2, :] + vec_ref[2:3, :]).astype(BF16)
    normed_ref[...] = normed
    mine = pl.ds(pl.multiple_of(me_ref[0] * cols, 128), cols)
    found = dot(normed, qkv_ref[...], NN)
    q_ref[...] = (found[:, :cols] + table_ref[2:3, mine]).astype(BF16)
    k_ref[...] = found[:, cols : 2 * cols].astype(BF16)
    v_ref[...] = (found[:, 2 * cols :] + table_ref[3:4, mine]).astype(BF16)


def project(me, order, lead, tokens, pieces, kinds):
    rows, width = tokens[0].shape
    n_seq = len(tokens)
    cols = width // n_seq
    length = rows * n_seq
    half = rows // HALVES
    count = length // HALVES
    numbers = pl.BlockSpec(memory_space=pltpu.SMEM)

    def whole(dims):
        return pl.BlockSpec(dims, lambda i: (0, 0))

    def step(wide):
        return pl.BlockSpec((count, wide), lambda i: (i, 0))

    return call(
        functools.partial(project_kernel, n_seq, len(pieces)),
        near_out=(1, 2, 3),
        grid=(HALVES,),
        in_specs=[numbers] * 3
        + [pl.BlockSpec((half, width), lambda i: (i, 0))] * n_seq
        + [whole(piece.shape) for piece in pieces],
        out_specs=[step(width), step(cols), step(cols), step(cols)]
        + [whole((width, 3 * cols)), whole((kinds, width)), whole((8, width))],
        out_shape=[shape((length, width))]
        + [shape((length, cols))] * 3
        + [shape((width, 3 * cols)), shape((kinds, width), F32), shape((8, width), F32)],
        scratch_shapes=[pltpu.VMEM((width, 128), BF16)],
        compiler_params=vmem(28),
        cost_estimate=cost(6 * length * width * cols, 10 * length * width),
        name="project",
    )(me, order, lead, *tokens, *pieces)


def key_bias(n_seq, length, me, count):
    half = length // (n_seq * HALVES)
    parts = []
    for h in range(HALVES):
        for m in block_masks(n_seq):
            at = lax.broadcasted_iota(jnp.int32, (half, 1), 0) + ((me ^ m) * HALVES + h) * half
            parts.append(jnp.where(at < count, 0.0, MASKED).astype(F32))
    return jnp.concatenate(parts, axis=0)


def attend_kernel(n_seq, me_ref, count_ref, q_ref, k_ref, v_ref, out_ref, lse_ref):
    bias = key_bias(n_seq, k_ref.shape[0], me_ref[0], count_ref[0])
    for half in range(2):
        cols = slice(half * HEAD_DIM, (half + 1) * HEAD_DIM)
        scores = dot(k_ref[:, cols], q_ref[:, cols] * SCALE, NT) + bias
        top = jnp.max(scores, axis=0, keepdims=True)
        weights = jnp.exp(scores - top)
        total = jnp.sum(weights, axis=0, keepdims=True)
        mixed = dot(v_ref[:, cols], weights.astype(BF16), TN) / total
        out_ref[:, cols] = mixed.T.astype(BF16)
        lse_ref[half] = top + jnp.log(total)


def attend(n_seq, pair_at, me, valid, q, k, v):
    length = q.shape[0]
    pair = pl.BlockSpec((length, PAIR), lambda g: (0, pair_at))
    return call(
        functools.partial(attend_kernel, n_seq),
        near_in=(2, 3, 4),
        grid=(1,),
        in_specs=[NUMBERS] * 2 + [pair, pair, pair],
        out_specs=[
            pl.BlockSpec((length, PAIR), lambda g: (0, 0)),
            pl.BlockSpec((2, 1, length), lambda g: (0, 0, 0)),
        ],
        out_shape=[shape((length, PAIR)), shape((2, 1, length), F32)],
        compiler_params=vmem(32),
        cost_estimate=cost(4 * length * length * PAIR, 8 * length * PAIR, 2 * length * length),
        name="attend",
    )(me, valid, q, k, v)


def attend_back_kernel(first, n_seq, *refs):
    me_ref, count_ref, q_ref, k_ref, v_ref, lse_ref, out_w_ref = refs[:7]
    grads = refs[7 : 7 + n_seq]
    rest = refs[7 + n_seq :]
    if first:
        dq_ref, dk_ref, dv_ref = rest
    else:
        dq_in, dk_in, dv_in, whole_ref, q_out, k_out, v_out, sems = rest
    length = k_ref.shape[0]
    count = q_ref.shape[0]
    pair = pl.program_id(0)
    spot = pair % 2
    bias = key_bias(n_seq, length, me_ref[0], count_ref[0])
    upstream = jnp.concatenate([dot(ref[...], out_w_ref[...], NT).astype(BF16) for ref in grads], axis=0)
    for half in range(2):
        cols = slice(half * HEAD_DIM, (half + 1) * HEAD_DIM)
        k = k_ref[:, cols]
        q = q_ref[:, cols] * SCALE
        g = upstream[:, cols]
        probs = jnp.exp(dot(k, q, NT) + bias - lse_ref[half])
        dv = dot(probs.astype(BF16), g, NN)
        term = probs * dot(v_ref[:, cols], g, NT)
        grad = (term - probs * jnp.sum(term, axis=0, keepdims=True)).astype(BF16)
        dk = dot(grad, q, NN)
        dq = (dot(k, grad, TN) * SCALE).T.astype(BF16)
        if first:
            dq_ref[:, cols] = dq
            dk_ref[:, cols] = dk
            dv_ref[:, cols] = dv
        else:
            q_out[spot, :count, cols] = dq_in[:, cols]
            q_out[spot, count:, cols] = dq
            k_out[spot, :, cols] = (dk + dk_in[:, cols]).astype(BF16)
            v_out[spot, :, cols] = (dv + dv_in[:, cols]).astype(BF16)
    if first:
        return
    pairs = pl.num_programs(0)

    def copies(at):
        found = []
        for i, source in enumerate((q_out, k_out, v_out)):
            start = pl.multiple_of((i * pairs + at) * PAIR, PAIR)
            target = whole_ref.at[:, pl.ds(start, PAIR)]
            found.append(pltpu.make_async_copy(source.at[at % 2], target, sems.at[at % 2, i]))
        return found

    for copy in copies(pair):
        copy.start()

    @pl.when(pair > 0)
    def _():
        for copy in copies(pair - 1):
            copy.wait()

    @pl.when(pair == pairs - 1)
    def _():
        for copy in copies(pair):
            copy.wait()


def attend_back(at, me, valid, q, k, v, lse, out_mine, grads, earlier):
    length, cols = k.shape
    width = out_mine.shape[1]
    count = length // HALVES
    pair = pl.BlockSpec((length, PAIR), lambda g: (0, g))
    mine = pl.BlockSpec((count, PAIR), lambda g: (at, g))
    here = pl.BlockSpec((count, PAIR), lambda g: (0, g))
    first = earlier is None
    near_out = () if first else (0,)
    in_specs = [NUMBERS] * 2 + [
        mine,
        pair,
        pair,
        pl.BlockSpec((2, 1, count), lambda g: (g, 0, at)),
        pl.BlockSpec((PAIR, width), lambda g: (g, 0)),
    ]
    in_specs += [pl.BlockSpec(piece.shape, lambda g: (0, 0)) for piece in grads]
    args = [me, valid, q, k, v, lse, out_mine] + list(grads)
    if first:
        out_specs = [here, pair, pair]
        out_shape = [shape((count, cols))] + [shape((length, cols), F32)] * 2
        scratch = []
    else:
        in_specs += [here, pair, pair]
        args += list(earlier)
        out_specs = AWAY
        out_shape = shape((length, 3 * cols))
        scratch = [pltpu.VMEM((2, length, PAIR), BF16)] * 3 + [pltpu.SemaphoreType.DMA((2, 3))]
    return call(
        functools.partial(attend_back_kernel, first, len(grads)),
        near_out=near_out,
        grid=(cols // PAIR,),
        in_specs=in_specs,
        out_specs=out_specs,
        out_shape=out_shape,
        scratch_shapes=scratch,
        compiler_params=vmem(36),
        cost_estimate=cost(10 * count * length * cols, 8 * length * cols, count * length * cols // HEAD_DIM),
        name="attend_back",
    )(*args)


def middle_kernel(n_seq, n_out, me_ref, order_ref, *refs):
    tokens, refs = refs[:n_seq], refs[n_seq:]
    outs, refs = refs[:n_out], refs[n_out:]
    att, refs = refs[:-5], refs[-5:]
    vec_ref, normed_ref, middle_ref, mine_ref, out_ref = refs
    masks = block_masks(n_seq)
    me = me_ref[0]
    pairs = len(att) // n_seq
    cols = pairs * PAIR
    half = middle_ref.shape[0]
    width = normed_ref.shape[1]
    step = pl.program_id(0)

    @pl.when(step == 0)
    def _():
        if n_out == 1:
            out_ref[...] = outs[0][...]
        else:
            n_dp = order_ref.shape[0]
            part = width // (n_dp * n_seq)
            for mask, ref in enumerate(outs):
                for k in range(n_dp):
                    start = pl.multiple_of((order_ref[k] * n_seq + (me ^ mask)) * part, part)
                    for t in range(n_seq):
                        at = (k * n_seq + t) * part
                        out_ref[pl.ds(start, part), t * cols : (t + 1) * cols] = ref[at : at + part, :]
        mine_ref[...] = out_ref[pl.ds(pl.multiple_of(me * cols, cols), cols), :]

    near = [tokens[i][...] for i in range(n_seq // 2)]
    other = [tokens[i][...] for i in range(n_seq // 2, n_seq)]
    start = [jnp.where(step % 2 == 0, a, b) for a, b in zip(near, other)]
    middle = jnp.concatenate(start, axis=0).astype(F32) + vec_ref[0:1, :] + vec_ref[3:4, :]
    for i, mask in enumerate(masks):
        at = pl.multiple_of((me ^ mask) * cols, cols)
        spots = [t ^ (mask >> 1) for t in range(n_seq // 2)]
        group = att[i * pairs : (i + 1) * pairs]
        found = [jnp.concatenate([ref[t * half : (t + 1) * half, :] for t in spots], axis=0) for ref in group]
        found = jnp.concatenate(found, axis=1)
        middle = middle + dot(found, out_ref[pl.ds(at, cols), :], NN)
    xhat, _ = standardise(middle)
    normed_ref[...] = (xhat * vec_ref[4:5, :] + vec_ref[5:6, :]).astype(BF16)

    @pl.when(step % 2 == 0)
    def _():
        middle_ref[...] = middle[:half, :]


def middle_norm(me, order, tokens, att, outs, vecs):
    rows, width = tokens[0].shape
    n_seq = len(tokens)
    length = rows * n_seq
    cols = width // n_seq
    block = length // (2 * HALVES)
    half = rows // HALVES
    numbers = pl.BlockSpec(memory_space=pltpu.SMEM)
    return call(
        functools.partial(middle_kernel, n_seq, len(outs)),
        near_out=(0,),
        grid=(2 * HALVES,),
        in_specs=[numbers] * 2
        + [pl.BlockSpec((half, width), lambda i: (i // 2, 0))] * n_seq
        + [pl.BlockSpec(out.shape, lambda i: (0, 0)) for out in outs]
        + [
            pl.BlockSpec((block, PAIR), lambda i, side=mask & 1: (i ^ side, 0))
            for mask in block_masks(n_seq)
            for _ in range(len(att) // n_seq)
        ]
        + [pl.BlockSpec(vecs.shape, lambda i: (0, 0))],
        out_specs=[
            pl.BlockSpec((block, width), lambda i: (i, 0)),
            pl.BlockSpec((half, width), lambda i: (i // 2, 0)),
            pl.BlockSpec((cols, width), lambda i: (0, 0)),
        ],
        out_shape=[shape((length, width)), shape((rows, width), F32), shape((cols, width))],
        scratch_shapes=[pltpu.VMEM((width, width), BF16)],
        compiler_params=vmem(24),
        cost_estimate=cost(2 * length * width * width, 10 * length * width),
        name="middle_norm",
    )(me, order, *tokens, *outs, *att, vecs)


def fetch(pairs, sems):
    copies = [pltpu.make_async_copy(a, b, sems.at[i]) for i, (a, b) in enumerate(pairs)]
    for copy in copies:
        copy.start()

    def wait():
        for copy in copies:
            copy.wait()

    return wait


def placed(order_ref, pieces, target, start):
    cols = pl.ds(start, target.shape[1])
    if len(pieces) == 1:
        return [(pieces[0], target)]
    rows = pieces[0].shape[0]
    return [
        (piece.at[:, cols], target.at[pl.ds(pl.multiple_of(order_ref[k] * rows, rows), rows), :])
        for k, piece in enumerate(pieces)
    ]


def up_kernel(n_pieces, block, order_ref, normed_ref, bias_ref, *refs):
    up_ref, hidden_ref, slope_ref, sems = refs[n_pieces:]
    fetch(placed(order_ref, refs[:n_pieces], up_ref, 0), sems)()

    def step(i, carry):
        cols = pl.ds(pl.multiple_of(i * block, block), block)
        pre = dot(normed_ref[...], up_ref[:, cols], NN) + bias_ref[:, cols]
        phi = 0.5 + 0.5 * lax.erf(pre * math.sqrt(0.5))
        hidden_ref[:, cols] = (pre * phi).astype(BF16)
        slope_ref[:, cols] = phi + pre * (jnp.exp(-0.5 * pre * pre) * (1.0 / math.sqrt(2.0 * math.pi)))
        return carry

    lax.fori_loop(0, up_ref.shape[1] // block, step, 0)


def up_part(order, normed, bias, pieces, block=256):
    length, width = normed.shape
    ff = bias.shape[1]
    return call(
        functools.partial(up_kernel, len(pieces), block),
        near_in=(1,),
        near_out=(0, 1, 2),
        in_specs=[NUMBERS, NEAR, NEAR] + [AWAY] * len(pieces),
        out_specs=[NEAR] * 3,
        out_shape=[shape((width, ff)), shape((length, ff)), shape((length, ff), F32)],
        scratch_shapes=[pltpu.SemaphoreType.DMA((len(pieces),))],
        compiler_params=vmem(12),
        cost_estimate=cost(2 * length * width * ff, 8 * width * ff, 2 * length * ff),
        name="up_part",
    )(order, normed, bias, *pieces)


def down_terms_kernel(n_grads, block, hidden_ref, *refs):
    out_ref, grad_ref, sems = refs[n_grads:]
    rows = refs[0].shape[0]
    half = rows // HALVES
    pairs = [
        (ref.at[pl.ds(h * half, half), :], grad_ref.at[pl.ds((h * n_grads + i) * half, half), :])
        for h in range(HALVES)
        for i, ref in enumerate(refs[:n_grads])
    ]
    fetch(pairs, sems)()

    def step(i, carry):
        cols = pl.ds(pl.multiple_of(i * block, block), block)
        out_ref[cols, :] = dot(hidden_ref[:, cols], grad_ref[...], TN).astype(BF16)
        return carry

    lax.fori_loop(0, hidden_ref.shape[1] // block, step, 0)


def down_part(hidden, grads, block=256):
    length, ff = hidden.shape
    width = grads[0].shape[1]
    return call(
        functools.partial(down_terms_kernel, len(grads), block),
        near_in=(0,),
        in_specs=[NEAR] + [AWAY] * len(grads),
        out_specs=NEAR,
        near_out=(0,),
        out_shape=shape((ff, width)),
        scratch_shapes=[pltpu.VMEM((length, width), BF16), pltpu.SemaphoreType.DMA((HALVES * len(grads),))],
        compiler_params=vmem(12),
        cost_estimate=cost(2 * length * width * ff, 4 * width * ff),
        name="down_part",
    )(hidden, *grads)


def mlp_back_kernel(first, at, block, n_pieces, n_grads, order_ref, hidden_ref, slope_ref, up_ref, *refs):
    pieces, refs = refs[:n_pieces], refs[n_pieces:]
    grads, refs = refs[:n_grads], refs[n_grads:]
    if not first:
        refs = refs[1:]
    pre_ref, keep_ref, send_ref, branch_keep, branch_send, sum_ref, back_acc, branch_acc, down_ref, grad_ref, sems = refs
    count = grad_ref.shape[0]
    half = count // n_grads
    pairs = placed(order_ref, pieces, down_ref, up_ref.shape[1])
    pairs += [
        (ref.at[pl.ds(at * half, half), :], grad_ref.at[pl.ds(i * half, half), :]) for i, ref in enumerate(grads)
    ]
    fetch(pairs, sems)()
    rows = pl.ds(at * count, count)

    def terms(i):
        cols = pl.ds(pl.multiple_of(i * block, block), block)
        grad = (slope_ref[rows, cols] * dot(grad_ref[...], down_ref[cols, :], NT)).astype(BF16)
        pre_ref[rows, cols] = grad
        sum_ref[:, cols] = jnp.sum(grad.astype(F32), axis=0, keepdims=True)
        return dot(grad, up_ref[:, cols], NT), dot(hidden_ref[rows, cols], down_ref[cols, :], NN)

    back_acc[...] = jnp.zeros_like(back_acc)
    branch_acc[...] = jnp.zeros_like(branch_acc)

    def step(i, carry):
        back, branch = terms(i)
        back_acc[...] += back
        branch_acc[...] += branch
        return carry

    lax.fori_loop(0, up_ref.shape[1] // block, step, 0)
    side = keep_ref.shape[0]
    keep_ref[...] = back_acc[:side, :].astype(BF16)
    send_ref[...] = back_acc[side:, :].astype(BF16)
    branch_keep[...] = branch_acc[:side, :].astype(BF16)
    branch_send[...] = branch_acc[side:, :].astype(BF16)


def mlp_back(at, order, hidden, slope, up, downs, grads, earlier, block=512):
    width = up.shape[0]
    length, ff = hidden.shape
    count = length // HALVES
    first = earlier is None
    given = 4 + len(downs) + len(grads)
    return call(
        functools.partial(mlp_back_kernel, first, at, min(block, ff // 2), len(downs), len(grads)),
        near_in=(1, 2, 3, given),
        near_out=(0, 1, 2, 3, 4),
        in_specs=[NUMBERS, NEAR, NEAR, NEAR] + [AWAY] * (given - 4) + ([] if first else [NEAR]),
        out_specs=[NEAR] * 6,
        out_shape=[shape((length, ff))] + [shape((count // 2, width))] * 4 + [shape((1, ff), F32)],
        scratch_shapes=[pltpu.VMEM((count, width), F32)] * 2
        + [pltpu.VMEM((ff, width), BF16), pltpu.VMEM((count, width), BF16)]
        + [pltpu.SemaphoreType.DMA((given - 4,))],
        input_output_aliases={} if first else {given: 0},
        compiler_params=vmem(20),
        cost_estimate=cost(6 * count * width * ff, 8 * width * ff),
        name="mlp_back",
    )(order, hidden, slope, up, *downs, *grads, *([] if first else [earlier]))


def second_back_kernel(middle_ref, keep_ref, near_ref, far_ref, out_ref, vec_ref, grad_ref, one_ref, sum_ref):
    upstream = keep_ref[...].astype(F32) + near_ref[...].astype(F32) + far_ref[...].astype(F32)
    xhat, rate = standardise(middle_ref[...])
    grad_out = out_ref[...].astype(F32)
    grad = grad_out + norm_back(upstream, xhat, rate, vec_ref[4:5, :])
    one = grad.astype(BF16)
    grad_ref[...] = grad
    one_ref[...] = one
    sums = [upstream * xhat, upstream, one.astype(F32), grad_out, grad]
    sum_ref[...] = jnp.concatenate([jnp.sum(s, axis=0, keepdims=True) for s in sums], axis=0)


def second_back(at, middle_own, keep, near, far, grad_out_own, vecs):
    half, width = far.shape
    first = pl.BlockSpec((half, width), lambda i: (0, 0))
    mine = pl.BlockSpec((half, width), lambda i: (at, 0))
    return call(
        second_back_kernel,
        near_in=(1, 2, 3),
        near_out=(0, 1),
        grid=(1,),
        in_specs=[mine, first, first, first, mine, pl.BlockSpec(vecs.shape, lambda i: (0, 0))],
        out_specs=[first, first, pl.BlockSpec((5, width), lambda i: (0, 0))],
        out_shape=[shape((half, width), F32), shape((half, width)), shape((5, width), F32)],
        compiler_params=vmem(10),
        cost_estimate=cost(30 * half * width, 16 * half * width),
        name="second_back",
    )(middle_own, keep, near, far, grad_out_own, vecs)


def first_grad_kernel(n_seq, grad_ref, qkv_ref, vec_ref, *refs):
    tokens, (keep_ref, send_ref, sum_ref, last_ref) = refs[:n_seq], refs[n_seq:]
    step = pl.program_id(0)
    grad = grad_ref[...]
    total = dot(grad, qkv_ref[...], NT)
    column = jnp.sum(grad.astype(F32), axis=0, keepdims=True)
    sides = zip(tokens[: n_seq // 2], tokens[n_seq // 2 :])
    start = jnp.concatenate([jnp.where(step % 2 == 0, a[...], b[...]) for a, b in sides], axis=0).astype(F32)
    xhat, rate = standardise(start + vec_ref[0:1, :])
    back = norm_back(total, xhat, rate, vec_ref[1:2, :])
    last = jnp.concatenate([jnp.sum(t, axis=0, keepdims=True) for t in (total * xhat, total, back)], axis=0)
    total = total.astype(BF16)

    @pl.when(step == 0)
    def _():
        sum_ref[...] = column
        last_ref[...] = last

    @pl.when(step > 0)
    def _():
        sum_ref[...] += column
        last_ref[...] += last

    @pl.when(step % 2 == 0)
    def _():
        keep_ref[...] = total

    @pl.when(step % 2 == 1)
    def _():
        send_ref[...] = total


def first_grad(grad_qkv, qkv, vecs, tokens):
    length, wide = grad_qkv.shape
    n_seq = len(tokens)
    half = tokens[0].shape[0] // HALVES
    width = qkv.shape[0]
    block = length // (2 * HALVES)
    kept = pl.BlockSpec((block, width), lambda i: (i // 2, 0))
    return call(
        functools.partial(first_grad_kernel, n_seq),
        near_in=(0,),
        near_out=(0, 1),
        grid=(2 * HALVES,),
        in_specs=[
            pl.BlockSpec((block, wide), lambda i: (i, 0)),
            pl.BlockSpec(qkv.shape, lambda i: (0, 0)),
            pl.BlockSpec(vecs.shape, lambda i: (0, 0)),
        ]
        + [pl.BlockSpec((half, width), lambda i: (i // 2, 0))] * n_seq,
        out_specs=[kept, kept, pl.BlockSpec((1, wide), lambda i: (0, 0)), pl.BlockSpec((3, width), lambda i: (0, 0))],
        out_shape=[shape((length // 2, width))] * 2 + [shape((1, wide), F32), shape((3, width), F32)],
        compiler_params=vmem(20),
        cost_estimate=cost(length * wide * width, 4 * length * width),
        name="first_grad",
    )(grad_qkv, qkv, vecs, *tokens)


def out_terms_kernel(pairs, *refs):
    att, out_ref = refs[:pairs], refs[-1]
    total = None
    at = 0
    for ref in refs[pairs:-1]:
        rows = ref.shape[0]
        term = dot(jnp.concatenate([a[at : at + rows, :] for a in att], axis=1), ref[...], TN)
        total = term if total is None else total + term
        at += rows
    n_dp, rows, wide = out_ref.shape
    if wide == total.shape[1]:
        out_ref[...] = total.astype(BF16).reshape(out_ref.shape)
        return
    part = total.shape[0] // n_dp
    for i in range(n_dp):
        for t in range(rows // part):
            piece = total[i * part : (i + 1) * part, t * wide : (t + 1) * wide]
            out_ref[i, t * part : (t + 1) * part, :] = piece.astype(BF16)


def out_terms(att, grads, n_dp, rows):
    length = att[0].shape[0]
    cols = len(att) * PAIR
    width = grads[0].shape[1]
    dims = (n_dp, rows, cols * width // (n_dp * rows))
    args = list(att) + list(grads)
    return call(
        functools.partial(out_terms_kernel, len(att)),
        near_out=(0,),
        grid=(1,),
        in_specs=[pl.BlockSpec(a.shape, lambda i: (0, 0)) for a in args],
        out_specs=pl.BlockSpec(dims, lambda i: (0, 0, 0)),
        out_shape=shape(dims),
        compiler_params=vmem(16),
        cost_estimate=cost(2 * length * cols * width, 2 * length * width),
        name="out_terms",
    )(*args)


def first_back_kernel(tokens_ref, keep_ref, near_ref, far_ref, a_ref, b_ref, vec_ref, out_ref):
    upstream = keep_ref[...].astype(F32) + near_ref[...].astype(F32) + far_ref[...].astype(F32)
    xhat, rate = standardise(tokens_ref[...].astype(F32) + vec_ref[0:1, :])
    grad = jnp.where(pl.program_id(0) == 0, a_ref[...], b_ref[...])
    grad = grad + norm_back(upstream, xhat, rate, vec_ref[1:2, :])
    out_ref[...] = grad.astype(BF16)


def first_back(tokens_own, keep, near_part, far_part, grad_a, grad_b, vecs):
    rows, width = tokens_own.shape
    half = rows // HALVES
    mine = pl.BlockSpec((half, width), lambda i: (i, 0))
    spread = pl.BlockSpec((half, width), lambda i: (i * (keep.shape[0] // rows), 0))
    whole = pl.BlockSpec((half, width), lambda i: (0, 0))
    return call(
        first_back_kernel,
        near_in=(3,),
        grid=(HALVES,),
        in_specs=[mine, spread, spread, mine, whole, whole, pl.BlockSpec(vecs.shape, lambda i: (0, 0))],
        out_specs=mine,
        out_shape=shape((rows, width)),
        compiler_params=vmem(10),
        cost_estimate=cost(30 * rows * width, 16 * rows * width),
        name="first_back",
    )(tokens_own, keep, near_part, far_part, grad_a, grad_b, vecs)


def block_masks(size):
    return [m for m in range(size) if not m & 1] + [m for m in range(size) if m & 1]


def far_bits(size):
    bits, bit = [], 2
    while bit < size:
        bits.append(bit)
        bit *= 2
    return bits


def tied(*values):
    return lax.optimization_barrier(values)


class Line:
    def __init__(self, token):
        self.token = token

    def slot(self, sends=(), work=lambda: (), inputs=(), begin=(), end=()):
        values, begun, inputs, token = tied(
            [s[0] for s in sends], [s[0] for s in begin], list(inputs), self.token
        )
        found = [lax.ppermute(value, s[1], s[2]) for value, s in zip(values, sends)]
        started = [lax.ppermute(value, s[1], s[2]) for value, s in zip(begun, begin)]
        found, done, ended, self.token = tied(found, work(*inputs), list(end), token)
        return found, done, started, ended


def swap(value, bit, size):
    return (value, "seq", [(i, i ^ bit) for i in range(size)])


def cycle(n_dp):
    wide = int(round(math.sqrt(n_dp / 2)))
    if wide < 2 or wide * (n_dp // wide) != n_dp or (n_dp // wide) % 2:
        return list(range(n_dp))
    high = n_dp // wide
    order = [z * wide for z in range(high)]
    for turn, z in enumerate(range(high - 1, -1, -1)):
        line = list(range(1, wide))
        order += [z * wide + y for y in (line[::-1] if turn % 2 else line)]
    return order


class Ring:
    def __init__(self, n_dp):
        self.n = n_dp
        order = cycle(n_dp)
        where = np.argsort(np.array(order))
        table = np.array([[order[(where[d] + k) % n_dp] for k in range(n_dp)] for d in range(n_dp)], np.int32)
        row = lax.dynamic_index_in_dim(jnp.asarray(table), lax.axis_index("dp"), 0, keepdims=False)
        self.order = row
        self.ahead = [(order[i], order[(i + 1) % n_dp]) for i in range(n_dp)]
        self.back = [(order[i], order[(i - 1) % n_dp]) for i in range(n_dp)]
        self.far = n_dp // 2
        self.near = (n_dp - 1) // 2


class Gather:
    def __init__(self, ring, owns):
        self.ring = ring
        self.step = 0
        self.pending = None
        self.ahead = list(owns)
        self.back = list(owns)
        self.pieces = [[o] + [None] * (ring.n - 1) for o in owns]

    def sends(self):
        self.step += 1
        found = []
        if self.step <= self.ring.far:
            found += [(v, "dp", self.ring.ahead) for v in self.ahead]
        if self.step <= self.ring.near:
            found += [(v, "dp", self.ring.back) for v in self.back]
        return found

    def take(self, found):
        count = len(self.pieces)
        if self.step <= self.ring.far:
            self.ahead, found = list(found[:count]), found[count:]
            for held, value in zip(self.pieces, self.ahead):
                held[-self.step % self.ring.n] = value
        if self.step <= self.ring.near:
            self.back = list(found[:count])
            for held, value in zip(self.pieces, self.back):
                held[self.step] = value

    @property
    def left(self):
        return self.ring.far - self.step


def ring_kernel(adds, *refs):
    count = len(adds)
    values = list(refs[1 + count : -count])
    for i, (add, out) in enumerate(zip(adds, refs[-count:])):
        total = refs[1 + i][0].astype(F32)
        for _ in range(add):
            total = total + values.pop(0)[...].astype(F32)
        out[...] = total.astype(out.dtype)


def ring_blocks(order, items, dtype=BF16):
    n_dp = order.shape[0]
    args, in_specs, outs, out_specs = [], [], [], []
    for terms, k, _ in items:
        dims = terms.shape[1:]
        in_specs.append(pl.BlockSpec((1,) + dims, lambda i, at, k=k % n_dp: (at[k], 0, 0)))
        out_specs.append(pl.BlockSpec(dims, lambda i, at: (0, 0)))
        outs.append(shape(dims, dtype))
        args.append(terms)
    for _, _, values in items:
        for value in values:
            in_specs.append(pl.BlockSpec(value.shape, lambda i, at: (0, 0)))
            args.append(value)
    return pl.pallas_call(
        functools.partial(ring_kernel, [len(i[2]) for i in items]),
        grid_spec=pltpu.PrefetchScalarGridSpec(
            num_scalar_prefetch=1, grid=(1,), in_specs=in_specs, out_specs=out_specs
        ),
        out_shape=outs,
        compiler_params=vmem(16),
        name="ring_blocks",
    )(order, *args)


def table_kernel(me_ref, lead_ref, a_ref, b_ref, last_ref, ua_ref, ub_ref, column_ref, out_ref):
    me = me_ref[0]
    width = out_ref.shape[1]
    cols = column_ref.shape[1] // 3
    extra = ua_ref.shape[1] * (width // cols) // width
    part = 128 // extra
    sums = a_ref[...] + b_ref[...]
    last = last_ref[...]
    column = column_ref[...]
    out_ref[...] = jnp.zeros_like(out_ref)
    out_ref[0:2, :] = last[0:2]
    mine = pl.ds(pl.multiple_of(me * cols, 128), cols)
    out_ref[2:3, mine] = column[:, :cols]
    out_ref[3:4, mine] = column[:, 2 * cols :]
    out_ref[4:5, :] = sums[2:3]
    out_ref[5:7, :] = sums[0:2]
    out_ref[7:8, :] = sums[3:4]
    start = last[2:3] + sums[4:5]
    out_ref[8:9, :] = lead_ref[0] * start
    out_ref[9:10, :] = start
    up = jnp.broadcast_to(ua_ref[...] + ub_ref[...], (8, width))
    here = lax.broadcasted_iota(jnp.int32, (1, width), 1) % 128 // part == me
    for k in range(extra):
        moved = pltpu.roll(up, ((me - k) * part + width) % width, 1)
        out_ref[10 + k : 11 + k, :] = jnp.where(here, moved[0:1, :], 0.0)


def small_table(me, lead, *args):
    width = args[0].shape[1]
    numbers = pl.BlockSpec(memory_space=pltpu.SMEM)
    return pl.pallas_call(
        table_kernel,
        grid=(1,),
        in_specs=[numbers] * 2 + [pl.BlockSpec(a.shape, lambda i: (0, 0)) for a in args],
        out_specs=pl.BlockSpec((16, width), lambda i: (0, 0)),
        out_shape=shape((16, width), F32),
        compiler_params=vmem(4),
        name="small_table",
    )(me, lead, *args)


def halve_kernel(side_ref, *refs):
    mine_ref, other_ref = refs[-2:]
    wide = mine_ref.shape[1]
    side = side_ref[0]
    for at, target in ((side, mine_ref), (1 - side, other_ref)):
        total = 0.0
        for ref in refs[:-2]:
            total = total + ref[:, pl.ds(pl.multiple_of(at * wide, 128), wide)]
        target[...] = total


def halve(side, values):
    rows, wide = values[0].shape
    half = pl.BlockSpec((rows, wide // 2), lambda i: (0, 0))
    return pl.pallas_call(
        halve_kernel,
        grid=(1,),
        in_specs=[pl.BlockSpec(memory_space=pltpu.SMEM)] + [pl.BlockSpec(v.shape, lambda i: (0, 0)) for v in values],
        out_specs=[half] * 2,
        out_shape=[shape((rows, wide // 2), F32)] * 2,
        compiler_params=vmem(4),
        name="halve",
    )(side, *values)


def owner_kernel(count, order_ref, me_ref, term_ref, *refs):
    part = refs[-1].shape[0]
    outs = refs[-count:]
    for mask, out in enumerate(outs):
        rows = pl.ds(pl.multiple_of((me_ref[0] ^ mask) * part, part), part)
        total = term_ref[0, rows, :].astype(F32)
        for ref in refs[:-count]:
            total = total + ref[rows, :].astype(F32)
        out[...] = total.astype(BF16)


def owner_blocks(order, me, terms, values, n_seq):
    _, rows, wide = terms.shape
    part = rows // n_seq
    if part % 16:
        (total,) = ring_blocks(order, [(terms, 0, values)])
        blocks = total.reshape(n_seq, part, wide)
        return [lax.dynamic_index_in_dim(blocks, me[0] ^ m, 0, keepdims=False) for m in range(n_seq)]
    return pl.pallas_call(
        functools.partial(owner_kernel, n_seq),
        grid_spec=pltpu.PrefetchScalarGridSpec(
            num_scalar_prefetch=2,
            grid=(1,),
            in_specs=[pl.BlockSpec((1, rows, wide), lambda i, at, me: (at[0], 0, 0))]
            + [pl.BlockSpec((rows, wide), lambda i, at, me: (0, 0))] * len(values),
            out_specs=[pl.BlockSpec((part, wide), lambda i, at, me: (0, 0))] * n_seq,
        ),
        out_shape=[shape((part, wide))] * n_seq,
        compiler_params=vmem(8),
        name="owner_blocks",
    )(order, me, terms, *values)


def unpack_kernel(groups, me_ref, *refs):
    outs = refs[-len(groups) :]
    pieces = refs[: -len(groups)]
    n_seq = len(pieces)
    for mask, ref in enumerate(pieces):
        at = 0
        for count, out in zip(groups, outs):
            wide = out.shape[1] // (count * n_seq)
            for i in range(count):
                start = pl.multiple_of((i * n_seq + (me_ref[0] ^ mask)) * wide, 128)
                out[:, pl.ds(start, wide)] = ref[:, at : at + wide].astype(F32)
                at += wide


def unpack(groups, widths, me, pieces):
    part = pieces[0].shape[0]
    n_seq = len(pieces)
    if any((wide // n_seq // count) % 128 for count, wide in zip(groups, widths)):
        whole = flipped(dict(enumerate(pieces)), n_seq)
        outs, at = [], 0
        for count, wide in zip(groups, widths):
            mine = whole[:, :, at : at + wide // n_seq].reshape(n_seq, part, count, -1)
            outs.append(jnp.moveaxis(mine, 0, 2).reshape(part, wide).astype(F32))
            at += wide // n_seq
        return outs
    return pl.pallas_call(
        functools.partial(unpack_kernel, groups),
        grid=(1,),
        in_specs=[NUMBERS] + [pl.BlockSpec(pieces[0].shape, lambda i: (0, 0))] * n_seq,
        out_specs=[pl.BlockSpec((part, wide), lambda i: (0, 0)) for wide in widths],
        out_shape=[shape((part, wide), F32) for wide in widths],
        compiler_params=vmem(8),
        name="unpack",
    )(me, *pieces)


class Scatter:
    def __init__(self, ring, terms):
        self.ring = ring
        self.terms = terms
        self.step = 0
        self.pending = None
        count = len(terms)
        found = ring_blocks(
            ring.order, [(t, ring.far, ()) for t in terms] + [(t, -ring.near, ()) for t in terms]
        )
        self.ahead, self.back = found[:count], found[count:]

    def sends(self):
        self.step += 1
        found = [(v, "dp", self.ring.ahead) for v in self.ahead]
        if self.step > self.ring.far - self.ring.near:
            found += [(v, "dp", self.ring.back) for v in self.back]
        return found

    def take(self, found):
        count = len(self.terms)
        left = self.ring.far - self.step
        ahead, back = found[:count], found[count:]
        if left:
            items = [(t, left, (v,)) for t, v in zip(self.terms, ahead)]
            items += [(t, -left, (v,)) for t, v in zip(self.terms, back)]
            found = ring_blocks(self.ring.order, items)
            ahead, back = found[:count], found[count:]
        self.ahead = ahead
        if back:
            self.back = back

    @property
    def left(self):
        return self.ring.far - self.step

    def total(self, dtype=F32):
        items = [(t, 0, (a, b)) for t, a, b in zip(self.terms, self.ahead, self.back)]
        return ring_blocks(self.ring.order, items, dtype)


def joint_kernel(items, order_ref, q_ref, o_ref, *refs):
    values, outs = list(refs[: -len(items)]), refs[-len(items) :]
    _, rows, edge = q_ref.shape
    _, part, width = o_ref.shape
    for (k, add), target in zip(items, outs):
        cols = target.shape[1] - edge
        mine = [values.pop(0) for _ in range(add)]
        at = order_ref[k]

        def total(first, where):
            found = first.astype(F32)
            for ref in mine:
                found = found + ref[where].astype(F32)
            return found.astype(BF16)

        every = (slice(0, rows), slice(0, edge))
        target[every] = total(q_ref[at], every)
        for t in range(rows // part):
            where = (slice(t * part, (t + 1) * part), slice(edge, edge + cols))
            target[where] = total(o_ref[at, :, t * cols : (t + 1) * cols], where)


class JointScatter:
    def __init__(self, ring, qkv, out):
        self.ring = ring
        self.qkv = qkv
        self.out = out
        self.step = 0
        self.pending = None
        self.ahead, self.back = self.blocks([(ring.far, ()), (-ring.near, ())])

    def blocks(self, items):
        n_dp, rows, edge = self.qkv.shape
        _, part, width = self.out.shape
        wide = edge + width * part // rows
        values = [v for _, mine in items for v in mine]
        every = range(1, 3 + len(values))
        return call(
            functools.partial(joint_kernel, [(k % n_dp, len(mine)) for k, mine in items]),
            near_in=every,
            near_out=range(len(items)),
            in_specs=[NUMBERS] + [NEAR] * (2 + len(values)),
            out_specs=[NEAR] * len(items),
            out_shape=[shape((rows, wide))] * len(items),
            compiler_params=vmem(4),
            name="joint_blocks",
        )(self.ring.order, self.qkv, self.out, *values)

    def sends(self):
        self.step += 1
        found = [(self.ahead, "dp", self.ring.ahead)]
        if self.step > self.ring.far - self.ring.near:
            found.append((self.back, "dp", self.ring.back))
        return found

    def take(self, found):
        left = self.ring.far - self.step
        if left:
            signs = (1, -1)
            found = self.blocks([(sign * left, (v,)) for sign, v in zip(signs, found)])
        self.ahead = found[0]
        if len(found) > 1:
            self.back = found[1]

    @property
    def left(self):
        return self.ring.far - self.step

    def total(self, me, n_seq, dtype=BF16, beside=()):
        n_dp, rows, edge = self.qkv.shape
        _, part, width = self.out.shape
        wide = edge + width * part // rows
        values = [self.ahead, self.back]
        cuts = 1 if rows // n_seq % 16 else n_seq
        more = list(beside) if cuts > 1 else []
        full = edge + (more[0].shape[1] if more else 0)
        found = pl.pallas_call(
            functools.partial(joint_owner_kernel, cuts, edge),
            grid_spec=pltpu.PrefetchScalarGridSpec(
                num_scalar_prefetch=2,
                grid=(1,),
                in_specs=[
                    pl.BlockSpec((1, rows, edge), lambda i, at, me: (at[0], 0, 0)),
                    pl.BlockSpec((1, part, width), lambda i, at, me: (at[0], 0, 0)),
                ]
                + [pl.BlockSpec((rows, wide), lambda i, at, me: (0, 0))] * len(values)
                + [pl.BlockSpec(m.shape, lambda i, at, me: (0, 0)) for m in more],
                out_specs=[pl.BlockSpec((rows // cuts, full), lambda i, at, me: (0, 0))] * cuts
                + [pl.BlockSpec((part, width), lambda i, at, me: (0, 0))],
            ),
            out_shape=[shape((rows // cuts, full))] * cuts + [shape((part, width), dtype)],
            compiler_params=vmem(8),
            name="joint_owner",
        )(self.ring.order, me, away(self.qkv), away(self.out), *[away(v) for v in values], *more)
        if cuts == n_seq:
            return list(found[:n_seq]), found[n_seq]
        blocks = found[0].reshape(n_seq, rows // n_seq, edge)
        blocks = [lax.dynamic_index_in_dim(blocks, me[0] ^ m, 0, keepdims=False) for m in range(n_seq)]
        return beside_all(blocks, beside), found[1]


def beside_all(blocks, beside):
    return [jnp.concatenate(pair, axis=1) for pair in zip(blocks, beside)] if beside else blocks


def joint_owner_kernel(cuts, edge, order_ref, me_ref, q_ref, o_ref, *refs):
    values, outs = refs[: -cuts - 1], refs[-cuts - 1 :]
    values, more = values[:2], values[2:]
    part = outs[0].shape[0]
    for mask, target in enumerate(outs[:-1]):
        rows = pl.ds(pl.multiple_of((me_ref[0] ^ mask) * part, part), part) if cuts > 1 else slice(None)
        total = q_ref[0, rows, :].astype(F32)
        for ref in values:
            total = total + ref[rows, :edge].astype(F32)
        target[:, :edge] = total.astype(BF16)
        if more:
            target[:, edge:] = more[mask][...]
    part, width = outs[-1].shape
    cols = values[0].shape[1] - edge
    for t in range(width // cols):
        total = o_ref[0, :, t * cols : (t + 1) * cols].astype(F32)
        for ref in values:
            total = total + ref[t * part : (t + 1) * part, edge:].astype(F32)
        outs[-1][:, t * cols : (t + 1) * cols] = total.astype(outs[-1].dtype)


class ApartScatter(Scatter):
    def __init__(self, ring, qkv, out):
        super().__init__(ring, [qkv, out])

    def total(self, me, n_seq, dtype=BF16, beside=()):
        qkv, out = self.terms
        blocks = owner_blocks(self.ring.order, me, qkv, (self.ahead[0], self.back[0]), n_seq)
        (out_sum,) = ring_blocks(self.ring.order, [(out, 0, (self.ahead[1], self.back[1]))])
        return beside_all(blocks, beside), out_sum


def flipped(pieces, bits):
    me = lax.axis_index("seq")
    size = len(pieces)
    held = [pieces[m] for m in range(size)]
    bit = 1
    while bit < size:
        turned = (me & bit) != 0
        held = [jnp.where(turned, held[m ^ bit], held[m]) for m in range(size)]
        bit *= 2
    return jnp.stack(held)


def make_body(n_dp, n_seq):
    masks = block_masks(n_seq)
    far = far_bits(n_seq)
    far_masks = [m for m in range(n_seq) if not m & 1]

    def body(
        tokens,
        lead_hours,
        valid_counts,
        patch_mask,
        first_gain,
        first_shift,
        qkv_weight,
        query_bias,
        value_bias,
        out_weight,
        out_bias,
        second_gain,
        second_shift,
        up_weight,
        up_bias,
        down_weight,
        down_bias,
        lead_weight,
        lead_bias,
        cotangent,
    ):
        me = lax.axis_index("seq")
        rows, width = tokens.shape[1], tokens.shape[2]
        length = rows * n_seq
        half = rows // HALVES
        part = qkv_weight.shape[0]
        ff_part = down_weight.shape[0]
        ff = up_weight.shape[1]
        extra = ff_part // part
        cols = width // n_seq
        ff_cols = ff // n_seq
        lead = lead_hours[0].astype(F32) / 100.0
        count = valid_counts[0]
        positions = me * rows + jnp.arange(rows, dtype=jnp.int32)
        loss_weight = (patch_mask[0] * (positions < count).astype(jnp.int32)).astype(BF16)
        ring = Ring(n_dp)
        me_ref = me.reshape(1).astype(jnp.int32)
        lead_ref = lead.reshape(1)
        order = ring.order

        def far_gather(own, at_bit):
            return [swap(own[m], far[at_bit], n_seq) for m in sorted(own)]

        line = Line(me_ref)

        def run(sends=(), work=lambda: (), inputs=(), start=(), finish=(), begin=(), end=()):
            sends, begin, end = list(sends), list(begin), list(end)
            plan = []
            for ring_part in finish:
                if ring_part.pending is not None:
                    plan.append((ring_part, "end", len(end), len(ring_part.pending)))
                    end += ring_part.pending
                    ring_part.pending = None
            n_sends, n_begin = len(sends), len(begin)
            ahead = []
            for ring_part in start:
                mine = ring_part.sends()
                if ring_part in finish:
                    plan.append((ring_part, "now", len(ahead), len(mine)))
                    ahead += mine
                else:
                    plan.append((ring_part, "later", len(begin), len(mine)))
                    begin += mine
            found, done, begun, ended = line.slot(ahead + sends, work, inputs, begin, end)
            early, found = found[: len(ahead)], found[len(ahead) :]
            n_end = len(end) - sum(p[3] for p in plan if p[1] == "end")
            for ring_part, kind, at, size in plan:
                if kind == "end":
                    ring_part.take(list(ended[at : at + size]))
                elif kind == "now":
                    ring_part.take(list(early[at : at + size]))
                else:
                    ring_part.pending = list(begun[at : at + size])
            return list(found[:n_sends]), done, list(begun[:n_begin]), list(ended[:n_end])

        def near_all(held):
            return [swap(held[m], 1, n_seq) for m in sorted(held)]

        def with_near(held, found):
            held.update({m ^ 1: v for m, v in zip(sorted(held), found)})

        def with_far(held, found, at_bit):
            held.update({m ^ far[at_bit]: v for m, v in zip(sorted(held), found)})

        def rest_far(held):
            for i in range(1, len(far)):
                found, _, _, _ = line.slot(far_gather(held, i))
                with_far(held, found, i)

        vectors = [
            first_gain,
            first_shift,
            query_bias,
            value_bias,
            out_bias,
            second_gain,
            second_shift,
            down_bias,
            lead_weight,
            lead_bias,
            up_bias,
        ]
        kinds = 10 + extra
        packed = pack(n_dp, n_seq, me_ref, qkv_weight, up_weight, vectors)
        found, (grad_out_own,), _, _ = run(
            [swap(packed[m], m, n_seq) for m in range(1, n_seq)],
            lambda c, w: (c * w[:, None],),
            (cotangent[0], loss_weight),
        )
        one_own = join_one(n_seq, me_ref, [packed[0]] + list(found), out_weight)

        g_one = Gather(ring, [one_own])

        def steps(*rings):
            mine = [g for g in rings if g.left]
            return dict(start=mine, finish=mine)

        tokens_held = {0: tokens[0]}
        grad_held = {0: grad_out_own}
        found, _, _, _ = run([swap(packed[n_seq + m], m, n_seq) for m in range(1, n_seq)], **steps(g_one))
        up_found = [packed[n_seq]] + list(found)
        _, (two_own,), tokens_far, _ = run(
            work=lambda *a: (join_two(n_seq, me_ref, a[:-1], a[-1]),),
            inputs=(*up_found, down_weight),
            begin=far_gather(tokens_held, 0),
            **steps(g_one),
        )
        g_two = Gather(ring, [two_own])
        late = [g_two] if g_two.left else []
        _, _, _, tokens_far = run(
            end=tokens_far, start=([g_one] if g_one.left else []) + late, finish=[g_one]
        )
        with_far(tokens_held, tokens_far, 0)
        rest_far(tokens_held)
        while g_one.left > 1:
            run(**steps(g_one))
        last = [g_one] if g_one.left else []
        found, _, _, _ = run(near_all(tokens_held), start=last, finish=last + late)
        with_near(tokens_held, found)

        tokens_by = [tokens_held[m] for m in masks]
        valid = count.reshape(1)
        pairs = cols // PAIR

        def begun(part_of):
            return dict(start=[part_of] if part_of.left else [])

        _, (out_pack,), _, _ = run(
            work=lambda *a: (middle_columns(a, 3 * cols, cols),), inputs=g_one.pieces[0], **begun(g_two)
        )
        out_held = {0: out_pack}
        _, (normed, q, k, v, qkv, table, vecs), out_far, _ = run(
            work=lambda *a: project(me_ref, order, lead_ref, a[:n_seq], ordered(order, a[n_seq:]), kinds),
            inputs=tokens_by + g_one.pieces[0],
            begin=far_gather(out_held, 0),
        )

        def up_bias_of(table):
            u_bias = table[10 : 10 + extra].reshape(extra, n_dp, n_seq, part)
            u_bias = lax.dynamic_index_in_dim(u_bias, me, 2, keepdims=False)
            return jnp.swapaxes(u_bias, 0, 1).reshape(1, ff_cols)

        def attend_pair(p):
            return lambda *a: attend(n_seq, p, me_ref, valid, *a)

        _, (attended, lse), _, out_far = run(work=attend_pair(0), inputs=(q, k, v), end=out_far, finish=[g_two])
        with_far(out_held, out_far, 0)
        rest_far(out_held)
        att_held = [{0: attended}]
        lses = [lse]
        nearby = near_all(out_held)
        for p in range(1, pairs):
            sends = nearby + far_gather(att_held[-1], 0)
            found, (attended, lse), _, _ = run(
                sends, work=attend_pair(p), inputs=(q, k, v), **(begun(g_two) if p == 1 else {})
            )
            if nearby:
                with_near(out_held, found[: len(nearby)])
                found = found[len(nearby) :]
                nearby = []
            with_far(att_held[-1], found, 0)
            rest_far(att_held[-1])
            att_held.append({0: attended})
            lses.append(lse)
        earlier = [(i, m) for i in range(pairs - 1) for m in near_all(att_held[i])]
        sends = [m[1] for m in earlier] + nearby
        found, (u_bias,), _, _ = run(
            sends + far_gather(att_held[-1], 0),
            work=lambda t: (up_bias_of(t),),
            inputs=(table,),
            **(dict(finish=[g_two]) if g_two.pending is not None else steps(g_two)),
        )
        for i in range(pairs - 1):
            n = len(att_held[i])
            with_near(att_held[i], found[:n])
            found = found[n:]
        if nearby:
            with_near(out_held, found[: len(nearby)])
            found = found[len(nearby) :]
        with_far(att_held[-1], found, 0)
        rest_far(att_held[-1])
        found, _, _, _ = run(near_all(att_held[-1]), **begun(g_two))
        with_near(att_held[-1], found)
        lse = jnp.concatenate(lses, axis=0)

        def out_whole(pieces):
            if part % 16 == 0:
                return pieces
            blocks = [ordered(order, [p[i * n_seq * part : (i + 1) * n_seq * part] for i in range(n_dp)])[0] for p in pieces]
            blocks = flipped(dict(enumerate(blocks)), n_seq).reshape(n_seq, n_dp, n_seq, part, cols)
            return [jnp.transpose(blocks, (1, 0, 3, 2, 4)).reshape(width, width)]

        found, (normed_two, middle_own, out_mine), _, _ = run(
            far_gather(grad_held, 0),
            work=lambda tok, att, outs, vecs: middle_norm(me_ref, order, tok, att, out_whole(outs), vecs),
            inputs=(
                tokens_by,
                [held[m] for m in masks for held in att_held],
                [out_held[m] for m in range(n_seq)],
                vecs,
            ),
            finish=[g_two],
        )
        with_far(grad_held, found, 0)
        rest_far(grad_held)
        while g_two.left:
            run(**steps(g_two))
        if g_two.pieces[0][0].shape[0] % 128:
            whole = ordered(order, g_two.pieces[0])[0]
            two_pieces = [whole[:, :ff_cols]], [whole[:, ff_cols:].reshape(ff_cols, width)]
        else:
            two_pieces = g_two.pieces[0], g_two.pieces[0]
        found, (up, hidden, slope), _, _ = run(
            near_all(grad_held), work=lambda *a: up_part(order, *a), inputs=(normed_two, u_bias, two_pieces[0])
        )
        with_near(grad_held, found)
        grads = [grad_held[m] for m in masks]
        downs = two_pieces[1]

        def half_sum(keep, other):
            found = {}
            for at, m in enumerate(far_masks):
                if m:
                    rows_at = slice(at * half, (at + 1) * half)
                    found[m] = (keep[rows_at].astype(F32) + other[rows_at].astype(F32)).astype(BF16)
            return found

        def far_first(held):
            bit = far[-1]
            return [swap(held[m], bit, n_seq) for m in sorted(held) if m & bit]

        def far_rest(held, found):
            for at, bit in enumerate(reversed(far)):
                upper = sorted(m for m in held if m & bit)
                if at:
                    found, _, _, _ = line.slot([swap(held[m], bit, n_seq) for m in upper])
                kept = {m: held[m] for m in held if not m & bit}
                for m, value in zip(upper, found):
                    low = m ^ bit
                    if low in kept:
                        value = (kept[low].astype(F32) + value.astype(F32)).astype(BF16)
                    kept[low] = value
                held = kept
            return held[0]

        _, (pre, keep_a, send_a, branch_keep_a, branch_send_a, sum_a), _, _ = run(
            work=lambda *a: mlp_back(0, order, *a, None), inputs=(hidden, slope, up, downs, grads)
        )
        (near_a,), (pre, keep_b, send_b, branch_keep_b, branch_send_b, sum_b), _, _ = run(
            [swap(send_a, 1, n_seq)],
            work=lambda *a: mlp_back(1, order, *a),
            inputs=(hidden, slope, up, downs, grads, pre),
        )
        def moved(value, axis, bit):
            count = n_dp if axis == "dp" else n_seq
            return lax.ppermute(value, axis, [(i, i ^ bit) for i in range(count)])

        held_a = half_sum(keep_a, near_a)
        sends = far_first(held_a)

        def weight_terms(hidden, grads, normed_two, pre):
            up_terms = dot(normed_two, pre, TN).astype(BF16).reshape(n_dp, n_seq * part, ff_cols)
            return down_part(hidden, grads).reshape(n_dp, ff_part, width), up_terms

        found, (down_terms, up_terms), _, _ = run(
            sends + [swap(send_b, 1, n_seq)], work=weight_terms, inputs=(hidden, grads, normed_two, pre)
        )
        far_a, near_b = far_rest(held_a, found[: len(sends)]), found[-1]
        held_b = half_sum(keep_b, near_b)

        def back_half(at):
            return lambda *a: tuple(second_back(at, *a))

        scatter_two = JointScatter(ring, up_terms, down_terms)
        def both_halves(held, mids, outs, vecs, keep_a, near_a, far_a, keep_b, near_b):
            far_b = {}
            if far:
                bit = far[-1]
                far_b = [lax.ppermute(held[m], "seq", [(i, i ^ bit) for i in range(n_seq)]) for m in sorted(held) if m & bit]
            first = second_back(0, mids, keep_a, near_a, far_a, outs, vecs)
            sent = [lax.ppermute(first[1], "seq", [(i, i ^ far[0]) for i in range(n_seq)])] if far else []
            far_b = far_rest(held, far_b)
            return first, second_back(1, mids, keep_b, near_b, far_b, outs, vecs), sent

        if len(far) == 1:
            branch_other, (first, second, one_far_a), _, _ = run(
                [swap(branch_send_a, 1, n_seq), swap(branch_send_b, 1, n_seq)],
                work=both_halves,
                inputs=(held_b, middle_own, grad_out_own, vecs, keep_a, near_a, far_a, keep_b, near_b),
                **steps(scatter_two),
            )
            grad_mid_a, one_a, sums_a = first
            grad_mid_b, one_b, sums_b = second
        else:
            _, (grad_mid_a, one_a, sums_a), far_b, _ = run(
                work=back_half(0),
                inputs=(middle_own, keep_a, near_a, far_a, grad_out_own, vecs),
                begin=far_first(held_b),
                **begun(scatter_two),
            )
            _, _, one_far_a, far_b = run(begin=far_gather({0: one_a}, 0), end=far_b)
            far_b = far_rest(held_b, far_b)
            branch_other, (grad_mid_b, one_b, sums_b), _, one_far_a = run(
                [swap(branch_send_a, 1, n_seq), swap(branch_send_b, 1, n_seq)],
                work=back_half(1),
                inputs=(middle_own, keep_b, near_b, far_b, grad_out_own, vecs),
                end=one_far_a,
                finish=[scatter_two],
            )
        one_held_a = {0: one_a}
        with_far(one_held_a, one_far_a, 0)
        rest_far(one_held_a)
        one_held_b = {0: one_b}
        found, _, one_far_b, _ = run(
            near_all(one_held_a), begin=far_gather(one_held_b, 0), **begun(scatter_two)
        )
        with_near(one_held_a, found)
        _, (dq_a, dk_a, dv_a), _, one_far_b = run(
            work=lambda *a: attend_back(0, me_ref, valid, *a, None),
            inputs=(q, k, v, lse, out_mine, [one_held_a[m] for m in masks]),
            end=one_far_b,
            finish=[scatter_two],
        )
        with_far(one_held_b, one_far_b, 0)
        rest_far(one_held_b)
        found, _, _, _ = run(near_all(one_held_b), **begun(scatter_two))
        with_near(one_held_b, found)
        ones = [one_held_a[m] for m in masks] + [one_held_b[m] for m in masks]

        branch_held = {
            m: jnp.concatenate([value, half_sum(branch_keep_b, branch_other[1])[m]], axis=0)
            for m, value in half_sum(branch_keep_a, branch_other[0]).items()
        }

        def second_attend(q, k, v, lse, out_mine, grads, earlier, att, ones):
            sums = out_terms(att, ones, n_dp, part if part % 16 else n_seq * part)
            return attend_back(1, me_ref, valid, q, k, v, lse, out_mine, grads, earlier), sums

        branch_far, (grad_qkv, out_sums), _, _ = run(
            far_first(branch_held),
            work=second_attend,
            inputs=(
                q,
                k,
                v,
                lse,
                out_mine,
                [one_held_b[m] for m in masks],
                (dq_a, dk_a, dv_a),
                [held[0] for held in att_held],
                ones,
            ),
            finish=[scatter_two],
        )
        branch_far = far_rest(branch_held, branch_far)

        qkv_terms = dot(normed, grad_qkv, TN).astype(BF16).reshape(n_dp, n_seq * part, 3 * cols)
        scatter_one = (ApartScatter if part % 16 else JointScatter)(ring, qkv_terms, out_sums)
        late = [scatter_two] if scatter_two.left else []

        def far_moved(held):
            if not far:
                return []
            return [moved(held[m], "seq", far[-1]) for m in sorted(held) if m & far[-1]]

        def now(*beside):
            mine = [scatter_one] if scatter_one.left else []
            return dict(start=mine, finish=mine + list(beside))

        _, (gn_keep, gn_send, column_sums, last_sums), _, _ = run(
            work=first_grad, inputs=(grad_qkv, qkv, vecs, tokens_by), **now()
        )
        plain = (width // n_dp) % 128 == 0 and extra == n_seq and n_seq * part == 128

        def final_rows(keep_a, keep_b, near_a, near_b, far_part, mid, bias):
            total = jnp.concatenate([keep_a[:half], keep_b[:half]], axis=0).astype(F32)
            total = total + jnp.concatenate([near_a[:half], near_b[:half]], axis=0).astype(F32)
            return ((mid + (total + far_part.astype(F32) + bias[6:7])).astype(BF16),)

        bits = []
        while 2 ** len(bits) < n_dp:
            bits.append(2 ** len(bits))
        bits = bits[::-1] if plain else []
        at_dp = lax.axis_index("dp")

        def loose_table():
            sums = sums_a + sums_b
            table = last_sums
            start_sums = table[2:3] + sums[4:5]
            q_sum = lax.dynamic_update_slice(jnp.zeros((1, width), F32), column_sums[:, :cols], (0, me * cols))
            v_sum = lax.dynamic_update_slice(jnp.zeros((1, width), F32), column_sums[:, 2 * cols :], (0, me * cols))
            u_sum = jnp.swapaxes((sum_a + sum_b).reshape(n_dp, extra, part), 0, 1)
            u_sum = lax.dynamic_update_index_in_dim(jnp.zeros((extra, n_dp, n_seq, part), F32), u_sum, me, 2)
            rows_out = [table[0:2], q_sum, v_sum, sums[2:3], sums[0:2], sums[3:4], lead * start_sums, start_sums]
            table = jnp.concatenate(rows_out + [u_sum.reshape(extra, width)], axis=0)
            return lax.psum_scatter(table, ("dp", "seq"), scatter_dimension=1, tiled=True)

        seq_bits = far + ([1] if n_seq > 1 else []) if plain else []

        def make_table():
            if not plain:
                return loose_table()
            return small_table(
                me_ref, lead_ref, sums_a, sums_b, last_sums, sum_a, sum_b, column_sums
            )

        def hop(held):
            if bits:
                bit = bits.pop(0)
                mine, other = halve(((at_dp // bit) % 2).reshape(1).astype(jnp.int32), held)
                return mine, [(other, "dp", [(i, i ^ bit) for i in range(n_dp)])]
            total = sum(held[1:], held[0])
            if seq_bits:
                return total, [swap(total, seq_bits.pop(0), n_seq)]
            return total, []

        (gn_near,), (table,), _, _ = run([swap(gn_send, 1, n_seq)], work=lambda: (make_table(),), start=late)
        size = half * len(far_masks)
        gn_held = {
            m: jnp.concatenate([value, half_sum(gn_keep[size:], gn_near[size:])[m]], axis=0)
            for m, value in half_sum(gn_keep[:size], gn_near[:size]).items()
        }
        mine, small = hop([table])
        sends = far_first(gn_held)
        found, _, _, _ = run(sends + small, **now(*late))
        gn_far = far_rest(gn_held, found[: len(sends)])
        held = [mine] + found[len(sends) :]
        while scatter_two.left:
            run(**steps(scatter_two))

        def totals():
            blocks, total = scatter_two.total(me_ref, n_seq, F32)
            return *blocks, total

        mine, small = hop(held)
        found, (tokens_grad, (*up_blocks, down_grad)), _, _ = run(
            small,
            work=lambda *a: (first_back(*a), totals()),
            inputs=(tokens[0], gn_keep, gn_near, gn_far, grad_mid_a, grad_mid_b, vecs),
            **now(),
        )
        held = [mine] + found

        mine, small = hop(held)
        found, (block_out,), _, _ = run(
            small,
            work=final_rows,
            inputs=(branch_keep_a, branch_keep_b, branch_other[0], branch_other[1], branch_far, middle_own, vecs),
            **now(),
        )
        held = [mine] + found
        while scatter_one.left:
            run(**steps(scatter_one))
        qkv_blocks, out_sum = scatter_one.total(me_ref, n_seq, beside=up_blocks)
        moves = []
        for dp_at in range(n_dp):
            for seq_at in range(n_seq):
                moves.append((dp_at * n_seq + seq_at, seq_at * n_dp + dp_at))
        final = [(out_sum, ("dp", "seq"), moves)] + [swap(qkv_blocks[m], m, n_seq) for m in range(1, n_seq)]

        mine, small = hop(held)
        found, _, _, _ = run(final + small)
        last, held = found[: len(final)], [mine] + found[len(final) :]
        while bits or seq_bits:
            mine, small = hop(held)
            found, _, _, _ = run(small)
            held = [mine] + found
        small_sums = sum(held[1:], held[0])
        if plain:
            small_sums = lax.dynamic_slice_in_dim(small_sums, me * part, part, 1)
        owned = small_sums[:kinds]
        qkv_weight_grad, up_weight_grad = unpack(
            (3, n_dp), (3 * width, ff), me_ref, [qkv_blocks[0]] + list(last[1:])
        )
        out_weight_grad = last[0].reshape(-1, part, width * part // last[0].shape[0])
        out_weight_grad = jnp.moveaxis(out_weight_grad, 0, 1).reshape(part, width).astype(F32)
        return (
            block_out[None],
            tokens_grad[None],
            owned[0],
            owned[1],
            qkv_weight_grad,
            owned[2],
            owned[3],
            out_weight_grad,
            owned[4],
            owned[5],
            owned[6],
            up_weight_grad,
            owned[10 : 10 + extra].reshape(ff_part),
            down_grad[0] if down_grad.ndim == 3 else down_grad,
            owned[7],
            owned[8],
            owned[9],
        )

    return body


def solution(mesh):
    both = P(("dp", "seq"))
    matrix = P(("dp", "seq"), None)
    tokens = P("dp", "seq", None)
    in_specs = (tokens, P("dp"), P("dp"), P("dp", "seq"), both, both, matrix, both, both, matrix, both, both, both)
    in_specs += (matrix, both, matrix, both, both, both, tokens)
    out_specs = (tokens, tokens, both, both, matrix, both, both, matrix, both, both, both, matrix, both, matrix)
    out_specs += (both, both, both)
    return jax.shard_map(
        make_body(mesh.shape["dp"], mesh.shape["seq"]),
        mesh=mesh,
        in_specs=in_specs,
        out_specs=out_specs,
        check_vma=False,
    )
```

```python
import functools
import math

import jax
import jax.numpy as jnp
import numpy as np
from jax import lax
from jax.experimental import pallas as pl
from jax.experimental.pallas import tpu as pltpu
from jax.sharding import PartitionSpec as P

HEADS = 16
HEAD_DIM = 64
PAIR = 2 * HEAD_DIM
SCALE = 1.0 / math.sqrt(HEAD_DIM)
EPSILON = 1e-06
MASKED = -1e30
F32 = jnp.float32
BF16 = jnp.bfloat16
NN, NT, TN = ((1,), (0,)), ((1,), (1,)), ((0,), (0,))
HALVES = 2
MIB = 1024 * 1024
NEAR = pl.BlockSpec(memory_space=pltpu.VMEM)
AWAY = pl.BlockSpec(memory_space=pl.ANY)
NUMBERS = pl.BlockSpec(memory_space=pltpu.SMEM)


def dot(left, right, contract):
    return lax.dot_general(left, right, (contract, ((), ())), preferred_element_type=F32)


def shape(dims, dtype=BF16):
    return jax.ShapeDtypeStruct(dims, dtype)


def call(kernel, *, in_specs, out_shape, near_in=(), near_out=(), **options):
    def large(value):
        return math.prod(value.shape) * value.dtype.itemsize >= 65536

    def run(*args):
        kept = []
        for i, a in enumerate(args):
            if large(a):
                a = pltpu.with_memory_space_constraint(a, pltpu.VMEM if i in near_in else pltpu.HBM)
            kept.append(a)
        single = not isinstance(out_shape, (list, tuple))
        outs = [out_shape] if single else list(out_shape)
        outs = [
            ((pltpu.VMEM if i in near_out else pltpu.HBM)(o.shape, o.dtype) if large(o) else o)
            for i, o in enumerate(outs)
        ]
        return pl.pallas_call(kernel, in_specs=in_specs, out_shape=outs[0] if single else outs, **options)(*kept)

    return run


def away(value):
    return pltpu.with_memory_space_constraint(value, pltpu.HBM)


def near(value):
    return pltpu.with_memory_space_constraint(value, pltpu.VMEM)


def vmem(mib):
    return pltpu.CompilerParams(vmem_limit_bytes=mib * MIB)


def cost(flops, moved, exps=0):
    return pl.CostEstimate(flops=int(flops), bytes_accessed=int(moved), transcendentals=int(exps))


def standardise(values):
    centered = values - jnp.mean(values, axis=-1, keepdims=True)
    rate = lax.rsqrt(jnp.mean(centered * centered, axis=-1, keepdims=True) + EPSILON)
    return centered * rate, rate


def norm_back(upstream, xhat, rate, gain):
    scaled = upstream * gain
    inner = jnp.mean(scaled * xhat, axis=-1, keepdims=True)
    return rate * (scaled - jnp.mean(scaled, axis=-1, keepdims=True) - xhat * inner)


def pack_kernel(n_dp, n_seq, me_ref, qkv_ref, up_ref, *refs):
    vectors, out_refs = refs[: -2 * n_seq], refs[-2 * n_seq :]
    out_refs, up_refs = out_refs[:n_seq], out_refs[n_seq:]
    me = me_ref[0]
    part = qkv_ref.shape[0]
    cols = qkv_ref.shape[1] // (3 * n_seq)
    piece = up_ref.shape[1] // (n_dp * n_seq)
    rows = [ref[...].astype(F32)[:, i : i + part] for ref in vectors for i in range(0, ref.shape[1], part)]
    kinds = len(rows)
    rows = jnp.concatenate(rows + [jnp.zeros((128 - kinds, part), F32)], axis=0)
    rows = jnp.concatenate([rows, jnp.zeros((128, 128 - part), F32)], axis=1)
    small = rows.T[:part, :].astype(BF16)
    for mask, ref in enumerate(out_refs):
        place = me ^ mask
        for i in range(3):
            start = pl.multiple_of((i * n_seq + place) * cols, 128)
            ref[:, i * cols : (i + 1) * cols] = qkv_ref[:, pl.ds(start, cols)]
        at = 3 * cols
        ref[:, at : at + 128] = small
        for i in range(n_dp):
            start = pl.multiple_of((i * n_seq + place) * piece, 128)
            up_refs[mask][:, i * piece : (i + 1) * piece] = up_ref[:, pl.ds(start, piece)]


def pack(n_dp, n_seq, me, qkv, up, vectors):
    part = qkv.shape[0]
    wide = qkv.shape[1] // n_seq + 128
    ff = up.shape[1] // n_seq
    if up.shape[1] // (n_dp * n_seq) % 128 or part % 16:
        small = jnp.concatenate(vectors).reshape(-1, part).T
        small = jnp.pad(small, ((0, 0), (0, 128 - small.shape[1])))
        qkv_split = qkv.reshape(part, 3, n_seq, -1)
        up_split = up.reshape(part, n_dp, n_seq, -1)

        def block(place):
            q = lax.dynamic_index_in_dim(qkv_split, place, 2, keepdims=False).reshape(part, -1)
            u = lax.dynamic_index_in_dim(up_split, place, 2, keepdims=False).reshape(part, -1)
            return jnp.concatenate([q, small], axis=1), u

        blocks = [block(me[0] ^ m) for m in range(n_seq)]
        return [b[0] for b in blocks] + [b[1] for b in blocks]
    args = [qkv, up] + [v.reshape(1, -1) for v in vectors]
    args = [pltpu.with_memory_space_constraint(a, pltpu.HBM) for a in args]
    return pl.pallas_call(
        functools.partial(pack_kernel, n_dp, n_seq),
        grid=(1,),
        in_specs=[pl.BlockSpec(memory_space=pltpu.SMEM)] + [pl.BlockSpec(a.shape, lambda i: (0, 0)) for a in args],
        out_specs=[pl.BlockSpec((part, wide), lambda i: (0, 0))] * n_seq
        + [pl.BlockSpec((part, ff), lambda i: (0, 0))] * n_seq,
        out_shape=[shape((part, wide))] * n_seq + [shape((part, ff))] * n_seq,
        compiler_params=vmem(8),
        name="pack",
    )(me, *args)


def join_one_kernel(n_seq, me_ref, *refs):
    out_ref, left_ref = refs[-2:]
    part, wide = out_ref.shape
    cols = wide // n_seq
    edge = refs[0].shape[1] - 128
    for t, ref in enumerate(refs[:-2]):
        rows = pl.ds(pl.multiple_of((me_ref[0] ^ t) * part, part), part)
        left_ref[rows, :edge] = ref[:, :edge]
        left_ref[rows, edge + cols :] = ref[:, edge:]
        left_ref[t * part : (t + 1) * part, edge : edge + cols] = out_ref[:, t * cols : (t + 1) * cols]


def join_two_kernel(n_seq, me_ref, *refs):
    down_ref, right_ref = refs[-2:]
    half = down_ref.shape[1]
    part = refs[0].shape[0]
    right_ref[:, -half:] = down_ref[...]
    for t, ref in enumerate(refs[:-2]):
        right_ref[pl.ds(pl.multiple_of((me_ref[0] ^ t) * part, part), part), :-half] = ref[...]


def join(kernel, n_seq, me, pieces, weight, wide):
    rows = pieces[0].shape[0] * n_seq
    args = list(pieces) + [away(weight)]
    return pl.pallas_call(
        functools.partial(kernel, n_seq),
        grid=(1,),
        in_specs=[NUMBERS] + [pl.BlockSpec(a.shape, lambda i: (0, 0)) for a in args],
        out_specs=pl.BlockSpec((rows, wide), lambda i: (0, 0)),
        out_shape=shape((rows, wide)),
        compiler_params=vmem(8),
        name="join",
    )(me, *args)


def join_one(n_seq, me, pieces, out_weight):
    part, edge = pieces[0].shape
    edge -= 128
    cols = out_weight.shape[1] // n_seq
    if part % 16:
        whole = flipped(dict(enumerate(pieces)), n_seq).reshape(part * n_seq, edge + 128)
        beside = jnp.moveaxis(out_weight.reshape(part, n_seq, cols), 1, 0).reshape(part * n_seq, cols)
        return jnp.concatenate([whole[:, :edge], beside, whole[:, edge:]], axis=1)
    return join(join_one_kernel, n_seq, me, pieces, out_weight, edge + cols + 128)


def join_two(n_seq, me, pieces, down_weight):
    part, wide = pieces[0].shape
    rows = part * n_seq
    if part % 16:
        whole = flipped(dict(enumerate(pieces)), n_seq).reshape(rows, wide)
        return jnp.concatenate([whole, down_weight.reshape(rows, -1)], axis=1)
    return join(join_two_kernel, n_seq, me, pieces, down_weight, wide + down_weight.shape[1])


class Blocks:
    def __init__(self, arrays, spots, rows):
        self.arrays = arrays
        self.spots = spots
        self.rows = rows

    def place(self, order_ref, i, source=None):
        k, start = self.spots[i]
        count = self.arrays[i].shape[0]
        if order_ref is None:
            return slice(k * self.rows + start, k * self.rows + start + count)
        return pl.ds(pl.multiple_of(order_ref[k] * self.rows + start, math.gcd(self.rows, start or self.rows)), count)


def ordered(order, pieces):
    rows = pieces[0].shape[0]
    if rows % 128 == 0:
        arrays, spots = [], []
        for k, piece in enumerate(pieces):
            halves = piece if isinstance(piece, tuple) else (piece,)
            for i, half in enumerate(halves):
                arrays.append(half)
                spots.append((k, i * rows // 2))
        return Blocks(arrays, spots, rows)
    whole = jnp.stack([jnp.concatenate(p, axis=0) if isinstance(p, tuple) else p for p in pieces])
    out = whole
    for k in range(len(pieces)):
        out = lax.dynamic_update_index_in_dim(out, whole[k], order[k], 0)
    return Blocks([out.reshape(-1, out.shape[-1])], [None], len(pieces) * rows)


def lay(order_ref, blocks, refs, target, cols=slice(None)):
    for i, ref in enumerate(refs):
        if blocks.spots[i] is None:
            target[...] = ref[:, cols]
        else:
            target[blocks.place(order_ref, i), :] = ref[:, cols]


def middle_columns_kernel(blocks, *refs):
    for i, ref in enumerate(refs[:-1]):
        refs[-1][blocks.place(None, i), :] = ref[...]


def middle_columns(blocks, start, cols, n_dp):
    if blocks.spots[0] is None or start % cols:
        return blocks.arrays[0][:, start : start + cols]
    total = blocks.rows * n_dp
    return call(
        functools.partial(middle_columns_kernel, blocks),
        grid=(1,),
        in_specs=[pl.BlockSpec((a.shape[0], cols), lambda i: (0, start // cols)) for a in blocks.arrays],
        out_specs=pl.BlockSpec((total, cols), lambda i: (0, 0)),
        out_shape=shape((total, cols)),
        compiler_params=vmem(4),
        name="middle_columns",
    )(*blocks.arrays)


def project_kernel(n_seq, blocks, me_ref, order_ref, lead_ref, *refs):
    n_pieces = len(blocks.arrays)
    tokens = refs[:n_seq]
    pieces = refs[n_seq : n_seq + n_pieces]
    normed_ref, q_ref, k_ref, v_ref, qkv_ref, table_ref, vec_ref, small_ref = refs[n_seq + n_pieces :]
    cols = q_ref.shape[1]

    @pl.when(pl.program_id(0) == 0)
    def _():
        lay(order_ref, blocks, pieces, qkv_ref, slice(0, 3 * cols))
        lay(order_ref, blocks, pieces, small_ref, slice(4 * cols, 4 * cols + 128))
        table_ref[...] = small_ref[...].astype(F32).T[: table_ref.shape[0], :]
        for i, kind in enumerate((0, 0, 1, 4, 5, 6, 7, 7)):
            vec_ref[i : i + 1, :] = table_ref[kind : kind + 1, :]
        vec_ref[0:1, :] = lead_ref[0] * table_ref[8:9, :] + table_ref[9:10, :]

    start = jnp.concatenate([ref[...] for ref in tokens], axis=0).astype(F32) + vec_ref[0:1, :]
    xhat, _ = standardise(start)
    normed = (xhat * vec_ref[1:2, :] + vec_ref[2:3, :]).astype(BF16)
    normed_ref[...] = normed
    mine = pl.ds(pl.multiple_of(me_ref[0] * cols, 128), cols)
    found = dot(normed, qkv_ref[...], NN)
    q_ref[...] = (found[:, :cols] + table_ref[2:3, mine]).astype(BF16)
    k_ref[...] = found[:, cols : 2 * cols].astype(BF16)
    v_ref[...] = (found[:, 2 * cols :] + table_ref[3:4, mine]).astype(BF16)


def project(me, order, lead, tokens, blocks, kinds):
    rows, width = tokens[0].shape
    n_seq = len(tokens)
    cols = width // n_seq
    length = rows * n_seq
    half = rows // HALVES
    count = length // HALVES
    numbers = pl.BlockSpec(memory_space=pltpu.SMEM)

    def whole(dims):
        return pl.BlockSpec(dims, lambda i: (0, 0))

    def step(wide):
        return pl.BlockSpec((count, wide), lambda i: (i, 0))

    return call(
        functools.partial(project_kernel, n_seq, blocks),
        near_out=(1, 2, 3),
        grid=(HALVES,),
        in_specs=[numbers] * 3
        + [pl.BlockSpec((half, width), lambda i: (i, 0))] * n_seq
        + [whole(a.shape) for a in blocks.arrays],
        out_specs=[step(width), step(cols), step(cols), step(cols)]
        + [whole((width, 3 * cols)), whole((kinds, width)), whole((8, width))],
        out_shape=[shape((length, width))]
        + [shape((length, cols))] * 3
        + [shape((width, 3 * cols)), shape((kinds, width), F32), shape((8, width), F32)],
        scratch_shapes=[pltpu.VMEM((width, 128), BF16)],
        compiler_params=vmem(28),
        cost_estimate=cost(6 * length * width * cols, 10 * length * width),
        name="project",
    )(me, order, lead, *tokens, *blocks.arrays)


def key_bias(n_seq, length, me, count):
    half = length // (n_seq * HALVES)
    parts = []
    for h in range(HALVES):
        for m in block_masks(n_seq):
            at = lax.broadcasted_iota(jnp.int32, (half, 1), 0) + ((me ^ m) * HALVES + h) * half
            parts.append(jnp.where(at < count, 0.0, MASKED).astype(F32))
    return jnp.concatenate(parts, axis=0)


def attend_kernel(n_seq, me_ref, count_ref, q_ref, k_ref, v_ref, *refs):
    out_ref, lse_ref = refs[-2:]
    bias = key_bias(n_seq, k_ref.shape[0], me_ref[0], count_ref[0])
    count = q_ref.shape[0] // 2

    def step(i, carry):
        rows = pl.ds(pl.multiple_of(i * count, count), count)
        for half in range(2):
            cols = slice(half * HEAD_DIM, (half + 1) * HEAD_DIM)
            scores = dot(k_ref[:, cols], q_ref[rows, cols] * SCALE, NT) + bias
            top = jnp.max(scores, axis=0, keepdims=True)
            weights = jnp.exp(scores - top)
            total = jnp.sum(weights, axis=0, keepdims=True)
            mixed = dot(v_ref[:, cols], weights.astype(BF16), TN) / total
            out_ref[rows, cols] = mixed.T.astype(BF16)
            lse_ref[half, :, rows] = top + jnp.log(total)
        return carry

    lax.fori_loop(0, 2, step, 0)


def attend(n_seq, pair_at, me, valid, q, k, v, earlier):
    length, cols = q.shape
    pair = pl.BlockSpec((length, PAIR), lambda g: (0, pair_at))
    given = [] if earlier is None else [earlier]
    return call(
        functools.partial(attend_kernel, n_seq),
        near_in=(2, 3, 4),
        grid=(1,),
        in_specs=[NUMBERS] * 2 + [pair, pair, pair] + [AWAY] * len(given),
        out_specs=[pair, pl.BlockSpec((2, 1, length), lambda g: (0, 0, 0))],
        out_shape=[shape((length, cols)), shape((2, 1, length), F32)],
        input_output_aliases={5: 0} if given else {},
        compiler_params=vmem(32),
        cost_estimate=cost(4 * length * length * PAIR, 8 * length * PAIR, 2 * length * length),
        name="attend",
    )(me, valid, q, k, v, *given)


def attend_back_kernel(first, n_seq, *refs):
    me_ref, count_ref, q_ref, k_ref, v_ref, lse_ref, out_w_ref = refs[:7]
    grads = refs[7 : 7 + n_seq]
    rest = refs[7 + n_seq :]
    if first:
        dq_ref, dk_ref, dv_ref = rest
    else:
        dq_in, dk_in, dv_in, whole_ref, q_out, k_out, v_out, sems = rest
    length = k_ref.shape[0]
    count = q_ref.shape[0]
    pair = pl.program_id(0)
    spot = pair % 2
    bias = key_bias(n_seq, length, me_ref[0], count_ref[0])
    upstream = jnp.concatenate([dot(ref[...], out_w_ref[...], NT).astype(BF16) for ref in grads], axis=0)
    for half in range(2):
        cols = slice(half * HEAD_DIM, (half + 1) * HEAD_DIM)
        k = k_ref[:, cols]
        q = q_ref[:, cols] * SCALE
        g = upstream[:, cols]
        probs = jnp.exp(dot(k, q, NT) + bias - lse_ref[half])
        dv = dot(probs.astype(BF16), g, NN)
        term = probs * dot(v_ref[:, cols], g, NT)
        grad = (term - probs * jnp.sum(term, axis=0, keepdims=True)).astype(BF16)
        dk = dot(grad, q, NN)
        dq = (dot(k, grad, TN) * SCALE).T.astype(BF16)
        if first:
            dq_ref[:, cols] = dq
            dk_ref[:, cols] = dk
            dv_ref[:, cols] = dv
        else:
            q_out[spot, :count, cols] = dq_in[:, cols]
            q_out[spot, count:, cols] = dq
            k_out[spot, :, cols] = (dk + dk_in[:, cols]).astype(BF16)
            v_out[spot, :, cols] = (dv + dv_in[:, cols]).astype(BF16)
    if first:
        return
    pairs = pl.num_programs(0)

    def copies(at):
        found = []
        for i, source in enumerate((q_out, k_out, v_out)):
            start = pl.multiple_of((i * pairs + at) * PAIR, PAIR)
            target = whole_ref.at[:, pl.ds(start, PAIR)]
            found.append(pltpu.make_async_copy(source.at[at % 2], target, sems.at[at % 2, i]))
        return found

    for copy in copies(pair):
        copy.start()

    @pl.when(pair > 0)
    def _():
        for copy in copies(pair - 1):
            copy.wait()

    @pl.when(pair == pairs - 1)
    def _():
        for copy in copies(pair):
            copy.wait()


def attend_back(at, me, valid, q, k, v, lse, out_mine, grads, earlier):
    length, cols = k.shape
    width = out_mine.shape[1]
    count = length // HALVES
    pair = pl.BlockSpec((length, PAIR), lambda g: (0, g))
    mine = pl.BlockSpec((count, PAIR), lambda g: (at, g))
    here = pl.BlockSpec((count, PAIR), lambda g: (0, g))
    first = earlier is None
    near_out = () if first else (0,)
    in_specs = [NUMBERS] * 2 + [
        mine,
        pair,
        pair,
        pl.BlockSpec((2, 1, count), lambda g: (g, 0, at)),
        pl.BlockSpec((PAIR, width), lambda g: (g, 0)),
    ]
    in_specs += [pl.BlockSpec(piece.shape, lambda g: (0, 0)) for piece in grads]
    args = [me, valid, q, k, v, lse, out_mine] + list(grads)
    if first:
        out_specs = [here, pair, pair]
        out_shape = [shape((count, cols))] + [shape((length, cols), F32)] * 2
        scratch = []
    else:
        in_specs += [here, pair, pair]
        args += list(earlier)
        out_specs = AWAY
        out_shape = shape((length, 3 * cols))
        scratch = [pltpu.VMEM((2, length, PAIR), BF16)] * 3 + [pltpu.SemaphoreType.DMA((2, 3))]
    return call(
        functools.partial(attend_back_kernel, first, len(grads)),
        near_out=near_out,
        grid=(cols // PAIR,),
        in_specs=in_specs,
        out_specs=out_specs,
        out_shape=out_shape,
        scratch_shapes=scratch,
        compiler_params=vmem(36),
        cost_estimate=cost(10 * count * length * cols, 8 * length * cols, count * length * cols // HEAD_DIM),
        name="attend_back",
    )(*args)


def middle_kernel(n_seq, n_out, me_ref, order_ref, *refs):
    tokens, refs = refs[:n_seq], refs[n_seq:]
    outs, refs = refs[:n_out], refs[n_out:]
    att, refs = refs[:-5], refs[-5:]
    vec_ref, normed_ref, middle_ref, mine_ref, out_ref = refs
    masks = block_masks(n_seq)
    me = me_ref[0]
    pairs = len(att) // n_seq
    cols = pairs * att[0].shape[1]
    half = middle_ref.shape[0]
    width = normed_ref.shape[1]
    step = pl.program_id(0)

    @pl.when(step == 0)
    def _():
        if n_out == 1:
            out_ref[...] = outs[0][...]
        else:
            n_dp = order_ref.shape[0]
            part = width // (n_dp * n_seq)
            for mask, ref in enumerate(outs):
                for k in range(n_dp):
                    start = pl.multiple_of((order_ref[k] * n_seq + (me ^ mask)) * part, part)
                    for t in range(n_seq):
                        at = (k * n_seq + t) * part
                        out_ref[pl.ds(start, part), t * cols : (t + 1) * cols] = ref[at : at + part, :]
        mine_ref[...] = out_ref[pl.ds(pl.multiple_of(me * cols, cols), cols), :]

    near = [tokens[i][...] for i in range(n_seq // 2)]
    other = [tokens[i][...] for i in range(n_seq // 2, n_seq)]
    start = [jnp.where(step % 2 == 0, a, b) for a, b in zip(near, other)]
    middle = jnp.concatenate(start, axis=0).astype(F32) + vec_ref[0:1, :] + vec_ref[3:4, :]
    for i, mask in enumerate(masks):
        at = pl.multiple_of((me ^ mask) * cols, cols)
        spots = [t ^ (mask >> 1) for t in range(n_seq // 2)]
        group = att[i * pairs : (i + 1) * pairs]
        found = [jnp.concatenate([ref[t * half : (t + 1) * half, :] for t in spots], axis=0) for ref in group]
        found = jnp.concatenate(found, axis=1)
        middle = middle + dot(found, out_ref[pl.ds(at, cols), :], NN)
    xhat, _ = standardise(middle)
    normed_ref[...] = (xhat * vec_ref[4:5, :] + vec_ref[5:6, :]).astype(BF16)

    @pl.when(step % 2 == 0)
    def _():
        middle_ref[...] = middle[:half, :]


def middle_norm(me, order, tokens, att, outs, vecs):
    rows, width = tokens[0].shape
    n_seq = len(tokens)
    length = rows * n_seq
    cols = width // n_seq
    block = length // (2 * HALVES)
    half = rows // HALVES
    numbers = pl.BlockSpec(memory_space=pltpu.SMEM)
    return call(
        functools.partial(middle_kernel, n_seq, len(outs)),
        near_out=(0,),
        grid=(2 * HALVES,),
        in_specs=[numbers] * 2
        + [pl.BlockSpec((half, width), lambda i: (i // 2, 0))] * n_seq
        + [pl.BlockSpec(out.shape, lambda i: (0, 0)) for out in outs]
        + [
            pl.BlockSpec((block, att[0].shape[1]), lambda i, side=mask & 1: (i ^ side, 0))
            for mask in block_masks(n_seq)
            for _ in range(len(att) // n_seq)
        ]
        + [pl.BlockSpec(vecs.shape, lambda i: (0, 0))],
        out_specs=[
            pl.BlockSpec((block, width), lambda i: (i, 0)),
            pl.BlockSpec((half, width), lambda i: (i // 2, 0)),
            pl.BlockSpec((cols, width), lambda i: (0, 0)),
        ],
        out_shape=[shape((length, width)), shape((rows, width), F32), shape((cols, width))],
        scratch_shapes=[pltpu.VMEM((width, width), BF16)],
        compiler_params=vmem(24),
        cost_estimate=cost(2 * length * width * width, 10 * length * width),
        name="middle_norm",
    )(me, order, *tokens, *outs, *att, vecs)


def fetch(pairs, sems):
    copies = [pltpu.make_async_copy(a, b, sems.at[i]) for i, (a, b) in enumerate(pairs)]
    for copy in copies:
        copy.start()

    def wait():
        for copy in copies:
            copy.wait()

    return wait


def placed(order_ref, blocks, refs, target, start):
    if blocks.spots[0] is None:
        return [(refs[0], target)]
    cols = pl.ds(start, target.shape[1])
    return [(ref.at[:, cols], target.at[blocks.place(order_ref, i), :]) for i, ref in enumerate(refs)]


def up_kernel(ups, downs, block, order_ref, normed_ref, bias_ref, *refs):
    up_pieces, refs = refs[: len(ups.arrays)], refs[len(ups.arrays) :]
    if downs is None:
        downs, down_pieces = ups, up_pieces
    else:
        down_pieces, refs = refs[: len(downs.arrays)], refs[len(downs.arrays) :]
    up_ref, down_ref, hidden_ref, slope_ref, up_sems, down_sems = refs
    here = fetch(placed(order_ref, ups, up_pieces, up_ref, 0), up_sems)
    later = fetch(placed(order_ref, downs, down_pieces, down_ref, up_ref.shape[1]), down_sems)
    here()

    def step(i, carry):
        cols = pl.ds(pl.multiple_of(i * block, block), block)
        pre = dot(normed_ref[...], up_ref[:, cols], NN) + bias_ref[:, cols]
        phi = 0.5 + 0.5 * lax.erf(pre * math.sqrt(0.5))
        hidden_ref[:, cols] = (pre * phi).astype(BF16)
        slope_ref[:, cols] = phi + pre * (jnp.exp(-0.5 * pre * pre) * (1.0 / math.sqrt(2.0 * math.pi)))
        return carry

    lax.fori_loop(0, up_ref.shape[1] // block, step, 0)
    later()


def up_part(order, normed, bias, ups, downs, block=256):
    length, width = normed.shape
    ff = bias.shape[1]
    pieces = list(ups.arrays) + (list(downs.arrays) if downs is not None else [])
    return call(
        functools.partial(up_kernel, ups, downs, block),
        near_in=(1,),
        near_out=(0, 1, 2, 3),
        in_specs=[NUMBERS, NEAR, NEAR] + [AWAY] * len(pieces),
        out_specs=[NEAR] * 4,
        out_shape=[shape((width, ff)), shape((ff, width)), shape((length, ff)), shape((length, ff), F32)],
        scratch_shapes=[pltpu.SemaphoreType.DMA((len(ups.arrays),)), pltpu.SemaphoreType.DMA((len((downs or ups).arrays),))],
        compiler_params=vmem(12),
        cost_estimate=cost(2 * length * width * ff, 8 * width * ff, 2 * length * ff),
        name="up_part",
    )(order, normed, bias, *pieces)


def lay_rows_kernel(*refs):
    out_ref, sems = refs[-2:]
    half = refs[0].shape[0]
    fetch([(ref, out_ref.at[pl.ds(i * half, half), :]) for i, ref in enumerate(refs[:-2])], sems)()


def lay_rows(pieces):
    half, width = pieces[0].shape
    return call(
        lay_rows_kernel,
        near_out=(0,),
        in_specs=[AWAY] * len(pieces),
        out_specs=NEAR,
        out_shape=shape((half * len(pieces), width)),
        scratch_shapes=[pltpu.SemaphoreType.DMA((len(pieces),))],
        compiler_params=vmem(4),
        name="lay_rows",
    )(*pieces)


def mlp_back_kernel(first, at, block, n_grads, hidden_ref, slope_ref, up_ref, down_ref, *refs):
    grads, refs = refs[:n_grads], refs[n_grads:]
    if not first:
        refs = refs[1:]
    pre_ref, keep_ref, send_ref, branch_keep, branch_send, sum_ref, grad_ref, sems = refs
    count = grad_ref.shape[0]
    half = count // n_grads
    ready = fetch([(ref, grad_ref.at[pl.ds(i * half, half), :]) for i, ref in enumerate(grads)], sems)
    rows = pl.ds(at * count, count)
    side = keep_ref.shape[0]
    sides = ((0, keep_ref, branch_keep), (side, send_ref, branch_send))
    for start, _, branch_out in sides:
        branch_out[...] = dot(hidden_ref[pl.ds(at * count + start, side), :], down_ref[...], NN).astype(BF16)
    ready()

    def step(i, carry):
        cols = pl.ds(pl.multiple_of(i * block, block), block)
        grad = (slope_ref[rows, cols] * dot(grad_ref[...], down_ref[cols, :], NT)).astype(BF16)
        pre_ref[rows, cols] = grad
        sum_ref[:, cols] = jnp.sum(grad.astype(F32), axis=0, keepdims=True)
        return carry

    lax.fori_loop(0, up_ref.shape[1] // block, step, 0)
    for start, back_out, _ in sides:
        back_out[...] = dot(pre_ref[pl.ds(at * count + start, side), :], up_ref[...], NT).astype(BF16)


def mlp_back(at, hidden, slope, up, down, grads, earlier, block=512):
    width = up.shape[0]
    length, ff = hidden.shape
    count = length // HALVES
    first = earlier is None
    given = 4 + len(grads)
    return call(
        functools.partial(mlp_back_kernel, first, at, min(block, ff // 2), len(grads)),
        near_in=(0, 1, 2, 3, given),
        near_out=(0, 1, 2, 3, 4),
        in_specs=[NEAR] * 4 + [AWAY] * len(grads) + ([] if first else [NEAR]),
        out_specs=[NEAR] * 6,
        out_shape=[shape((length, ff))] + [shape((count // 2, width))] * 4 + [shape((1, ff), F32)],
        scratch_shapes=[pltpu.VMEM((count, width), BF16), pltpu.SemaphoreType.DMA((len(grads),))],
        input_output_aliases={} if first else {given: 0},
        compiler_params=vmem(16),
        cost_estimate=cost(6 * count * width * ff, 8 * width * ff),
        name="mlp_back",
    )(hidden, slope, up, down, *grads, *([] if first else [earlier]))


def second_back_kernel(middle_ref, keep_ref, near_ref, far_ref, out_ref, vec_ref, grad_ref, one_ref, sum_ref):
    upstream = keep_ref[...].astype(F32) + near_ref[...].astype(F32) + far_ref[...].astype(F32)
    xhat, rate = standardise(middle_ref[...])
    grad_out = out_ref[...].astype(F32)
    grad = grad_out + norm_back(upstream, xhat, rate, vec_ref[4:5, :])
    one = grad.astype(BF16)
    grad_ref[...] = grad
    one_ref[...] = one
    sums = [upstream * xhat, upstream, one.astype(F32), grad_out, grad]
    sum_ref[...] = jnp.concatenate([jnp.sum(s, axis=0, keepdims=True) for s in sums], axis=0)


def second_back(at, middle_own, keep, near, far, grad_out_own, vecs):
    half, width = far.shape
    first = pl.BlockSpec((half, width), lambda i: (0, 0))
    mine = pl.BlockSpec((half, width), lambda i: (at, 0))
    return call(
        second_back_kernel,
        near_in=(1, 2, 3),
        near_out=(0, 1),
        grid=(1,),
        in_specs=[mine, first, first, first, first, pl.BlockSpec(vecs.shape, lambda i: (0, 0))],
        out_specs=[first, first, pl.BlockSpec((5, width), lambda i: (0, 0))],
        out_shape=[shape((half, width), F32), shape((half, width)), shape((5, width), F32)],
        compiler_params=vmem(10),
        cost_estimate=cost(30 * half * width, 16 * half * width),
        name="second_back",
    )(middle_own, keep, near, far, grad_out_own, vecs)


def first_grad_kernel(n_seq, grad_ref, qkv_ref, vec_ref, *refs):
    tokens, (keep_ref, send_ref, sum_ref, last_ref) = refs[:n_seq], refs[n_seq:]
    step = pl.program_id(0)
    grad = grad_ref[...]
    total = dot(grad, qkv_ref[...], NT)
    column = jnp.sum(grad.astype(F32), axis=0, keepdims=True)
    sides = zip(tokens[: n_seq // 2], tokens[n_seq // 2 :])
    start = jnp.concatenate([jnp.where(step % 2 == 0, a[...], b[...]) for a, b in sides], axis=0).astype(F32)
    xhat, rate = standardise(start + vec_ref[0:1, :])
    back = norm_back(total, xhat, rate, vec_ref[1:2, :])
    last = jnp.concatenate([jnp.sum(t, axis=0, keepdims=True) for t in (total * xhat, total, back)], axis=0)
    total = total.astype(BF16)

    @pl.when(step == 0)
    def _():
        sum_ref[...] = column
        last_ref[...] = last

    @pl.when(step > 0)
    def _():
        sum_ref[...] += column
        last_ref[...] += last

    @pl.when(step % 2 == 0)
    def _():
        keep_ref[...] = total

    @pl.when(step % 2 == 1)
    def _():
        send_ref[...] = total


def first_grad(grad_qkv, qkv, vecs, tokens):
    length, wide = grad_qkv.shape
    n_seq = len(tokens)
    half = tokens[0].shape[0] // HALVES
    width = qkv.shape[0]
    block = length // (2 * HALVES)
    kept = pl.BlockSpec((block, width), lambda i: (i // 2, 0))
    return call(
        functools.partial(first_grad_kernel, n_seq),
        near_in=(0,),
        near_out=(0, 1),
        grid=(2 * HALVES,),
        in_specs=[
            pl.BlockSpec((block, wide), lambda i: (i, 0)),
            pl.BlockSpec(qkv.shape, lambda i: (0, 0)),
            pl.BlockSpec(vecs.shape, lambda i: (0, 0)),
        ]
        + [pl.BlockSpec((half, width), lambda i: (i // 2, 0))] * n_seq,
        out_specs=[kept, kept, pl.BlockSpec((1, wide), lambda i: (0, 0)), pl.BlockSpec((3, width), lambda i: (0, 0))],
        out_shape=[shape((length // 2, width))] * 2 + [shape((1, wide), F32), shape((3, width), F32)],
        compiler_params=vmem(20),
        cost_estimate=cost(length * wide * width, 4 * length * width),
        name="first_grad",
    )(grad_qkv, qkv, vecs, *tokens)


def out_terms_kernel(pairs, *refs):
    att, out_ref = refs[:pairs], refs[-1]
    total = None
    at = 0
    for ref in refs[pairs:-1]:
        rows = ref.shape[0]
        term = dot(jnp.concatenate([a[at : at + rows, :] for a in att], axis=1), ref[...], TN)
        total = term if total is None else total + term
        at += rows
    n_dp, rows, wide = out_ref.shape
    if wide == total.shape[1]:
        out_ref[...] = total.astype(BF16).reshape(out_ref.shape)
        return
    part = total.shape[0] // n_dp
    for i in range(n_dp):
        for t in range(rows // part):
            piece = total[i * part : (i + 1) * part, t * wide : (t + 1) * wide]
            out_ref[i, t * part : (t + 1) * part, :] = piece.astype(BF16)


def out_terms(att, grads, n_dp, rows):
    length = att[0].shape[0]
    cols = len(att) * att[0].shape[1]
    width = grads[0].shape[1]
    dims = (n_dp, rows, cols * width // (n_dp * rows))
    args = list(att) + list(grads)
    return call(
        functools.partial(out_terms_kernel, len(att)),
        near_out=(0,),
        grid=(1,),
        in_specs=[pl.BlockSpec(a.shape, lambda i: (0, 0)) for a in args],
        out_specs=pl.BlockSpec(dims, lambda i: (0, 0, 0)),
        out_shape=shape(dims),
        compiler_params=vmem(16),
        cost_estimate=cost(2 * length * cols * width, 2 * length * width),
        name="out_terms",
    )(*args)


def first_back_kernel(tokens_ref, keep_ref, near_ref, far_a, far_b, a_ref, b_ref, vec_ref, out_ref):
    far_part = jnp.where(pl.program_id(0) == 0, far_a[...], far_b[...])
    upstream = keep_ref[...].astype(F32) + near_ref[...].astype(F32) + far_part.astype(F32)
    xhat, rate = standardise(tokens_ref[...].astype(F32) + vec_ref[0:1, :])
    grad = jnp.where(pl.program_id(0) == 0, a_ref[...], b_ref[...])
    grad = grad + norm_back(upstream, xhat, rate, vec_ref[1:2, :])
    out_ref[...] = grad.astype(BF16)


def first_back(tokens_own, keep, near_part, far_a, far_b, grad_a, grad_b, vecs):
    rows, width = tokens_own.shape
    half = rows // HALVES
    mine = pl.BlockSpec((half, width), lambda i: (i, 0))
    spread = pl.BlockSpec((half, width), lambda i: (i * (keep.shape[0] // rows), 0))
    whole = pl.BlockSpec((half, width), lambda i: (0, 0))
    return call(
        first_back_kernel,
        near_in=(3, 4),
        grid=(HALVES,),
        in_specs=[mine, spread, spread, whole, whole, whole, whole, pl.BlockSpec(vecs.shape, lambda i: (0, 0))],
        out_specs=mine,
        out_shape=shape((rows, width)),
        compiler_params=vmem(10),
        cost_estimate=cost(30 * rows * width, 16 * rows * width),
        name="first_back",
    )(tokens_own, keep, near_part, far_a, far_b, grad_a, grad_b, vecs)


def block_masks(size):
    return [m for m in range(size) if not m & 1] + [m for m in range(size) if m & 1]


def far_bits(size):
    bits, bit = [], 2
    while bit < size:
        bits.append(bit)
        bit *= 2
    return bits


def tied(*values):
    return lax.optimization_barrier(values)


class Line:
    def __init__(self, token):
        self.token = token

    def slot(self, sends=(), work=lambda: (), inputs=(), begin=(), end=()):
        values, begun, inputs, token = tied(
            [s[0] for s in sends], [s[0] for s in begin], list(inputs), self.token
        )
        found = [lax.ppermute(value, s[1], s[2]) for value, s in zip(values, sends)]
        started = [lax.ppermute(value, s[1], s[2]) for value, s in zip(begun, begin)]
        found, done, ended, self.token = tied(found, work(*inputs), list(end), token)
        return found, done, started, ended


def swap(value, bit, size):
    return (value, "seq", [(i, i ^ bit) for i in range(size)])


def cycle(n_dp):
    wide = int(round(math.sqrt(n_dp / 2)))
    if wide < 2 or wide * (n_dp // wide) != n_dp or (n_dp // wide) % 2:
        return list(range(n_dp))
    high = n_dp // wide
    order = [z * wide for z in range(high)]
    for turn, z in enumerate(range(high - 1, -1, -1)):
        line = list(range(1, wide))
        order += [z * wide + y for y in (line[::-1] if turn % 2 else line)]
    return order


class Ring:
    def __init__(self, n_dp):
        self.n = n_dp
        order = cycle(n_dp)
        where = np.argsort(np.array(order))
        table = np.array([[order[(where[d] + k) % n_dp] for k in range(n_dp)] for d in range(n_dp)], np.int32)
        row = lax.dynamic_index_in_dim(jnp.asarray(table), lax.axis_index("dp"), 0, keepdims=False)
        self.order = row
        self.ahead = [(order[i], order[(i + 1) % n_dp]) for i in range(n_dp)]
        self.back = [(order[i], order[(i - 1) % n_dp]) for i in range(n_dp)]
        self.far = n_dp // 2
        self.near = (n_dp - 1) // 2


class Gather:
    def __init__(self, ring, own):
        self.ring = ring
        self.step = 0
        self.pending = None
        self.ahead = self.back = own
        self.pieces = [own] + [None] * (ring.n - 1)

    def sends(self):
        self.step += 1
        ahead, back = self.ahead, self.back
        if self.step == self.ring.far:
            half = ahead.shape[0] // 2
            ahead, back = ahead[:half], back[half:]
        return [(ahead, "dp", self.ring.ahead), (back, "dp", self.ring.back)]

    def take(self, found):
        self.ahead, self.back = found
        if self.step == self.ring.far:
            self.pieces[self.step] = tuple(found)
        else:
            self.pieces[-self.step], self.pieces[self.step] = found

    @property
    def left(self):
        return self.ring.far - self.step


def ring_kernel(adds, *refs):
    count = len(adds)
    values = list(refs[1 + count : -count])
    for i, (add, out) in enumerate(zip(adds, refs[-count:])):
        total = refs[1 + i][0].astype(F32)
        for _ in range(add):
            total = total + values.pop(0)[...].astype(F32)
        out[...] = total.astype(out.dtype)


def ring_blocks(order, items, dtype=BF16):
    n_dp = order.shape[0]
    args, in_specs, outs, out_specs = [], [], [], []
    for terms, k, _ in items:
        dims = terms.shape[1:]
        in_specs.append(pl.BlockSpec((1,) + dims, lambda i, at, k=k % n_dp: (at[k], 0, 0)))
        out_specs.append(pl.BlockSpec(dims, lambda i, at: (0, 0)))
        outs.append(shape(dims, dtype))
        args.append(terms)
    for _, _, values in items:
        for value in values:
            in_specs.append(pl.BlockSpec(value.shape, lambda i, at: (0, 0)))
            args.append(value)
    return pl.pallas_call(
        functools.partial(ring_kernel, [len(i[2]) for i in items]),
        grid_spec=pltpu.PrefetchScalarGridSpec(
            num_scalar_prefetch=1, grid=(1,), in_specs=in_specs, out_specs=out_specs
        ),
        out_shape=outs,
        compiler_params=vmem(16),
        name="ring_blocks",
    )(order, *args)


def table_kernel(me_ref, lead_ref, a_ref, b_ref, last_ref, ua_ref, ub_ref, column_ref, out_ref):
    me = me_ref[0]
    width = out_ref.shape[1]
    cols = column_ref.shape[1] // 3
    extra = ua_ref.shape[1] * (width // cols) // width
    part = 128 // extra
    sums = a_ref[...] + b_ref[...]
    last = last_ref[...]
    column = column_ref[...]
    out_ref[...] = jnp.zeros_like(out_ref)
    out_ref[0:2, :] = last[0:2]
    mine = pl.ds(pl.multiple_of(me * cols, 128), cols)
    out_ref[2:3, mine] = column[:, :cols]
    out_ref[3:4, mine] = column[:, 2 * cols :]
    out_ref[4:5, :] = sums[2:3]
    out_ref[5:7, :] = sums[0:2]
    out_ref[7:8, :] = sums[3:4]
    start = last[2:3] + sums[4:5]
    out_ref[8:9, :] = lead_ref[0] * start
    out_ref[9:10, :] = start
    up = jnp.broadcast_to(ua_ref[...] + ub_ref[...], (8, width))
    here = lax.broadcasted_iota(jnp.int32, (1, width), 1) % 128 // part == me
    for k in range(extra):
        moved = pltpu.roll(up, ((me - k) * part + width) % width, 1)
        out_ref[10 + k : 11 + k, :] = jnp.where(here, moved[0:1, :], 0.0)


def small_table(me, lead, *args):
    width = args[0].shape[1]
    numbers = pl.BlockSpec(memory_space=pltpu.SMEM)
    return pl.pallas_call(
        table_kernel,
        grid=(1,),
        in_specs=[numbers] * 2 + [pl.BlockSpec(a.shape, lambda i: (0, 0)) for a in args],
        out_specs=pl.BlockSpec((16, width), lambda i: (0, 0)),
        out_shape=shape((16, width), F32),
        compiler_params=vmem(4),
        name="small_table",
    )(me, lead, *args)


def halve_kernel(side_ref, *refs):
    mine_ref, other_ref = refs[-2:]
    wide = mine_ref.shape[1]
    side = side_ref[0]
    for at, target in ((side, mine_ref), (1 - side, other_ref)):
        total = 0.0
        for ref in refs[:-2]:
            total = total + ref[:, pl.ds(pl.multiple_of(at * wide, 128), wide)]
        target[...] = total


def halve(side, values):
    rows, wide = values[0].shape
    half = pl.BlockSpec((rows, wide // 2), lambda i: (0, 0))
    return pl.pallas_call(
        halve_kernel,
        grid=(1,),
        in_specs=[pl.BlockSpec(memory_space=pltpu.SMEM)] + [pl.BlockSpec(v.shape, lambda i: (0, 0)) for v in values],
        out_specs=[half] * 2,
        out_shape=[shape((rows, wide // 2), F32)] * 2,
        compiler_params=vmem(4),
        name="halve",
    )(side, *values)


def owner_kernel(count, order_ref, me_ref, term_ref, *refs):
    part = refs[-1].shape[0]
    outs = refs[-count:]
    for mask, out in enumerate(outs):
        rows = pl.ds(pl.multiple_of((me_ref[0] ^ mask) * part, part), part)
        total = term_ref[0, rows, :].astype(F32)
        for ref in refs[:-count]:
            total = total + ref[rows, :].astype(F32)
        out[...] = total.astype(BF16)


def owner_blocks(order, me, terms, values, n_seq):
    _, rows, wide = terms.shape
    part = rows // n_seq
    if part % 16:
        (total,) = ring_blocks(order, [(terms, 0, values)])
        blocks = total.reshape(n_seq, part, wide)
        return [lax.dynamic_index_in_dim(blocks, me[0] ^ m, 0, keepdims=False) for m in range(n_seq)]
    return pl.pallas_call(
        functools.partial(owner_kernel, n_seq),
        grid_spec=pltpu.PrefetchScalarGridSpec(
            num_scalar_prefetch=2,
            grid=(1,),
            in_specs=[pl.BlockSpec((1, rows, wide), lambda i, at, me: (at[0], 0, 0))]
            + [pl.BlockSpec((rows, wide), lambda i, at, me: (0, 0))] * len(values),
            out_specs=[pl.BlockSpec((part, wide), lambda i, at, me: (0, 0))] * n_seq,
        ),
        out_shape=[shape((part, wide))] * n_seq,
        compiler_params=vmem(8),
        name="owner_blocks",
    )(order, me, terms, *values)


def unpack_kernel(groups, me_ref, *refs):
    outs = refs[-len(groups) :]
    pieces = refs[: -len(groups)]
    n_seq = len(pieces)
    for mask, ref in enumerate(pieces):
        at = 0
        for count, out in zip(groups, outs):
            wide = out.shape[1] // (count * n_seq)
            for i in range(count):
                start = pl.multiple_of((i * n_seq + (me_ref[0] ^ mask)) * wide, 128)
                out[:, pl.ds(start, wide)] = ref[:, at : at + wide].astype(F32)
                at += wide


def unpack(groups, widths, me, pieces):
    part = pieces[0].shape[0]
    n_seq = len(pieces)
    if any((wide // n_seq // count) % 128 for count, wide in zip(groups, widths)):
        whole = flipped(dict(enumerate(pieces)), n_seq)
        outs, at = [], 0
        for count, wide in zip(groups, widths):
            mine = whole[:, :, at : at + wide // n_seq].reshape(n_seq, part, count, -1)
            outs.append(jnp.moveaxis(mine, 0, 2).reshape(part, wide).astype(F32))
            at += wide // n_seq
        return outs
    return pl.pallas_call(
        functools.partial(unpack_kernel, groups),
        grid=(1,),
        in_specs=[NUMBERS] + [pl.BlockSpec(pieces[0].shape, lambda i: (0, 0))] * n_seq,
        out_specs=[pl.BlockSpec((part, wide), lambda i: (0, 0)) for wide in widths],
        out_shape=[shape((part, wide), F32) for wide in widths],
        compiler_params=vmem(8),
        name="unpack",
    )(me, *pieces)


class Scatter:
    def __init__(self, ring, terms):
        self.ring = ring
        self.terms = terms
        self.step = 0
        self.pending = None
        count = len(terms)
        found = ring_blocks(
            ring.order, [(t, ring.far, ()) for t in terms] + [(t, -ring.near, ()) for t in terms]
        )
        self.ahead, self.back = found[:count], found[count:]

    def sends(self):
        self.step += 1
        found = [(v, "dp", self.ring.ahead) for v in self.ahead]
        if self.step > self.ring.far - self.ring.near:
            found += [(v, "dp", self.ring.back) for v in self.back]
        return found

    def take(self, found):
        count = len(self.terms)
        left = self.ring.far - self.step
        ahead, back = found[:count], found[count:]
        if left:
            items = [(t, left, (v,)) for t, v in zip(self.terms, ahead)]
            items += [(t, -left, (v,)) for t, v in zip(self.terms, back)]
            found = ring_blocks(self.ring.order, items)
            ahead, back = found[:count], found[count:]
        self.ahead = ahead
        if back:
            self.back = back

    @property
    def left(self):
        return self.ring.far - self.step

    def total(self, dtype=F32):
        items = [(t, 0, (a, b)) for t, a, b in zip(self.terms, self.ahead, self.back)]
        return ring_blocks(self.ring.order, items, dtype)


def joint_kernel(items, order_ref, q_ref, o_ref, *refs):
    values, outs = list(refs[: -len(items)]), refs[-len(items) :]
    _, rows, edge = q_ref.shape
    _, part, width = o_ref.shape
    for (k, low, high, added), target in zip(items, outs):
        cols = target.shape[1] - edge
        value = values.pop(0) if added else None
        at = order_ref[k]

        def put(source, from_rows, row, lanes):
            cuts = sorted({row, row + len(from_rows)} | ({max(row, min(c, row + len(from_rows))) for c in added} if added else set()))
            for a, b in zip(cuts, cuts[1:]):
                total = source[from_rows[a - row] : from_rows[b - row - 1] + 1]
                if added and added[0] <= a and b <= added[1]:
                    total = (total.astype(F32) + value[a - added[0] : b - added[0], lanes].astype(F32)).astype(BF16)
                target[a - low : b - low, lanes] = total

        put(q_ref.at[at, :, slice(0, edge)], range(low, high), low, slice(0, edge))
        for t in range(rows // part):
            a, b = max(low, t * part), min(high, (t + 1) * part)
            if a < b:
                lanes = slice(t * cols, (t + 1) * cols)
                put(o_ref.at[at, :, lanes], range(a - t * part, b - t * part), a, slice(edge, edge + cols))


class JointScatter:
    def __init__(self, ring, qkv, out):
        self.ring = ring
        self.qkv = qkv
        self.out = out
        self.step = 0
        self.pending = None
        rows = qkv.shape[1]
        if ring.far:
            far = ring.far
            self.ahead, self.back = self.blocks([(far, 0, rows // 2, None), (far, rows // 2, rows, None)], ())

    def blocks(self, items, values):
        n_dp, rows, edge = self.qkv.shape
        _, part, width = self.out.shape
        wide = edge + width * part // rows
        items = [(k % n_dp, low, high, added) for k, low, high, added in items]
        return call(
            functools.partial(joint_kernel, items),
            near_in=range(1, 3 + len(values)),
            near_out=range(len(items)),
            in_specs=[NUMBERS] + [NEAR] * (2 + len(values)),
            out_specs=[NEAR] * len(items),
            out_shape=[shape((high - low, wide)) for _, low, high, _ in items],
            compiler_params=vmem(4),
            name="joint_blocks",
        )(self.ring.order, self.qkv, self.out, *values)

    def sends(self):
        self.step += 1
        return [(self.ahead, "dp", self.ring.ahead), (self.back, "dp", self.ring.back)]

    def take(self, found):
        left = self.ring.far - self.step
        rows = self.qkv.shape[1]
        if left:
            spans = ((0, rows // 2), (rows // 2, rows)) if self.step == 1 else ((0, rows), (0, rows))
            found = self.blocks([(sign * left, 0, rows, span) for sign, span in zip((1, -1), spans)], found)
        self.ahead, self.back = found

    @property
    def left(self):
        return self.ring.far - self.step

    def total(self, me, n_seq, dtype=BF16, beside=()):
        n_dp, rows, edge = self.qkv.shape
        _, part, width = self.out.shape
        wide = edge + width * part // rows
        values = [self.ahead, self.back]
        if self.ring.far == 1:
            values = [jnp.concatenate(values, axis=0)] * 2
            values[1] = jnp.zeros_like(values[1])
        cuts = 1 if rows // n_seq % 16 else n_seq
        more = list(beside) if cuts > 1 else []
        full = edge + (more[0].shape[1] if more else 0)
        found = pl.pallas_call(
            functools.partial(joint_owner_kernel, cuts, edge),
            grid_spec=pltpu.PrefetchScalarGridSpec(
                num_scalar_prefetch=2,
                grid=(1,),
                in_specs=[
                    pl.BlockSpec((1, rows, edge), lambda i, at, me: (at[0], 0, 0)),
                    pl.BlockSpec((1, part, width), lambda i, at, me: (at[0], 0, 0)),
                ]
                + [pl.BlockSpec((rows, wide), lambda i, at, me: (0, 0))] * len(values)
                + [pl.BlockSpec(m.shape, lambda i, at, me: (0, 0)) for m in more],
                out_specs=[pl.BlockSpec((rows // cuts, full), lambda i, at, me: (0, 0))] * cuts
                + [pl.BlockSpec((part, width), lambda i, at, me: (0, 0))],
            ),
            out_shape=[shape((rows // cuts, full))] * cuts + [shape((part, width), dtype)],
            compiler_params=vmem(8),
            name="joint_owner",
        )(self.ring.order, me, away(self.qkv), away(self.out), *[away(v) for v in values], *more)
        if cuts == n_seq:
            return list(found[:n_seq]), found[n_seq]
        blocks = found[0].reshape(n_seq, rows // n_seq, edge)
        blocks = [lax.dynamic_index_in_dim(blocks, me[0] ^ m, 0, keepdims=False) for m in range(n_seq)]
        return beside_all(blocks, beside), found[1]


def beside_all(blocks, beside):
    return [jnp.concatenate(pair, axis=1) for pair in zip(blocks, beside)] if beside else blocks


def joint_owner_kernel(cuts, edge, order_ref, me_ref, q_ref, o_ref, *refs):
    values, outs = refs[: -cuts - 1], refs[-cuts - 1 :]
    values, more = values[:2], values[2:]
    part = outs[0].shape[0]
    for mask, target in enumerate(outs[:-1]):
        rows = pl.ds(pl.multiple_of((me_ref[0] ^ mask) * part, part), part) if cuts > 1 else slice(None)
        total = q_ref[0, rows, :].astype(F32)
        for ref in values:
            total = total + ref[rows, :edge].astype(F32)
        target[:, :edge] = total.astype(BF16)
        if more:
            target[:, edge:] = more[mask][...]
    part, width = outs[-1].shape
    cols = values[0].shape[1] - edge
    for t in range(width // cols):
        total = o_ref[0, :, t * cols : (t + 1) * cols].astype(F32)
        for ref in values:
            total = total + ref[t * part : (t + 1) * part, edge:].astype(F32)
        outs[-1][:, t * cols : (t + 1) * cols] = total.astype(outs[-1].dtype)


class ApartScatter(Scatter):
    def __init__(self, ring, qkv, out):
        super().__init__(ring, [qkv, out])

    def total(self, me, n_seq, dtype=BF16, beside=()):
        qkv, out = self.terms
        blocks = owner_blocks(self.ring.order, me, qkv, (self.ahead[0], self.back[0]), n_seq)
        (out_sum,) = ring_blocks(self.ring.order, [(out, 0, (self.ahead[1], self.back[1]))])
        return beside_all(blocks, beside), out_sum


def flipped(pieces, bits):
    me = lax.axis_index("seq")
    size = len(pieces)
    held = [pieces[m] for m in range(size)]
    bit = 1
    while bit < size:
        turned = (me & bit) != 0
        held = [jnp.where(turned, held[m ^ bit], held[m]) for m in range(size)]
        bit *= 2
    return jnp.stack(held)


def make_body(n_dp, n_seq):
    masks = block_masks(n_seq)
    far = far_bits(n_seq)
    far_masks = [m for m in range(n_seq) if not m & 1]

    def body(
        tokens,
        lead_hours,
        valid_counts,
        patch_mask,
        first_gain,
        first_shift,
        qkv_weight,
        query_bias,
        value_bias,
        out_weight,
        out_bias,
        second_gain,
        second_shift,
        up_weight,
        up_bias,
        down_weight,
        down_bias,
        lead_weight,
        lead_bias,
        cotangent,
    ):
        me = lax.axis_index("seq")
        rows, width = tokens.shape[1], tokens.shape[2]
        length = rows * n_seq
        half = rows // HALVES
        part = qkv_weight.shape[0]
        ff_part = down_weight.shape[0]
        ff = up_weight.shape[1]
        extra = ff_part // part
        cols = width // n_seq
        ff_cols = ff // n_seq
        lead = lead_hours[0].astype(F32) / 100.0
        count = valid_counts[0]
        positions = me * rows + jnp.arange(rows, dtype=jnp.int32)
        loss_weight = (patch_mask[0] * (positions < count).astype(jnp.int32)).astype(BF16)
        ring = Ring(n_dp)
        me_ref = me.reshape(1).astype(jnp.int32)
        lead_ref = lead.reshape(1)
        order = ring.order

        def far_gather(own, at_bit):
            return [swap(own[m], far[at_bit], n_seq) for m in sorted(own)]

        line = Line(me_ref)

        def run(sends=(), work=lambda: (), inputs=(), start=(), finish=(), begin=(), end=()):
            sends, begin, end = list(sends), list(begin), list(end)
            plan = []
            for ring_part in finish:
                if ring_part.pending is not None:
                    plan.append((ring_part, "end", len(end), len(ring_part.pending)))
                    end += ring_part.pending
                    ring_part.pending = None
            n_sends, n_begin = len(sends), len(begin)
            ahead = []
            for ring_part in start:
                mine = ring_part.sends()
                if ring_part in finish:
                    plan.append((ring_part, "now", len(ahead), len(mine)))
                    ahead += mine
                else:
                    plan.append((ring_part, "later", len(begin), len(mine)))
                    begin += mine
            found, done, begun, ended = line.slot(ahead + sends, work, inputs, begin, end)
            early, found = found[: len(ahead)], found[len(ahead) :]
            n_end = len(end) - sum(p[3] for p in plan if p[1] == "end")
            for ring_part, kind, at, size in plan:
                if kind == "end":
                    ring_part.take(list(ended[at : at + size]))
                elif kind == "now":
                    ring_part.take(list(early[at : at + size]))
                else:
                    ring_part.pending = list(begun[at : at + size])
            return list(found[:n_sends]), done, list(begun[:n_begin]), list(ended[:n_end])

        def near_all(held):
            return [swap(held[m], 1, n_seq) for m in sorted(held)]

        def with_near(held, found):
            held.update({m ^ 1: v for m, v in zip(sorted(held), found)})

        def with_far(held, found, at_bit):
            held.update({m ^ far[at_bit]: v for m, v in zip(sorted(held), found)})

        def rest_far(held):
            for i in range(1, len(far)):
                found, _, _, _ = line.slot(far_gather(held, i))
                with_far(held, found, i)

        vectors = [
            first_gain,
            first_shift,
            query_bias,
            value_bias,
            out_bias,
            second_gain,
            second_shift,
            down_bias,
            lead_weight,
            lead_bias,
            up_bias,
        ]
        kinds = 10 + extra
        packed = pack(n_dp, n_seq, me_ref, qkv_weight, up_weight, vectors)
        found, outs_own, _, _ = run(
            [swap(packed[m], m, n_seq) for m in range(1, n_seq)],
            lambda c, w: tuple(c[h * half : (h + 1) * half] * w[h * half : (h + 1) * half, None] for h in range(HALVES)),
            (cotangent[0], loss_weight),
        )
        one_own = join_one(n_seq, me_ref, [packed[0]] + list(found), out_weight)

        g_one = Gather(ring, one_own)

        def steps(*rings):
            mine = [g for g in rings if g.left]
            return dict(start=mine, finish=mine)

        tokens_held = {0: tokens[0]}
        grad_held = [{0: g} for g in outs_own]
        found, _, _, _ = run([swap(packed[n_seq + m], m, n_seq) for m in range(1, n_seq)], **steps(g_one))
        up_found = [packed[n_seq]] + list(found)
        _, (two_own,), tokens_far, _ = run(
            work=lambda *a: (join_two(n_seq, me_ref, a[:-1], a[-1]),),
            inputs=(*up_found, down_weight),
            begin=far_gather(tokens_held, 0),
            **steps(g_one),
        )
        g_two = Gather(ring, two_own)
        _, _, _, tokens_far = run(end=tokens_far, **steps(g_one))
        with_far(tokens_held, tokens_far, 0)
        rest_far(tokens_held)
        while g_one.left > 1:
            run(**steps(g_one))
        found, _, _, _ = run(near_all(tokens_held), **steps(g_one))
        with_near(tokens_held, found)

        valid = count.reshape(1)
        pairs = cols // PAIR

        def begun(part_of):
            return dict(start=[part_of] if part_of.left else [])

        tokens_by = [tokens_held[m] for m in masks]
        ones_blocks = ordered(order, g_one.pieces)

        def attend_first(*a):
            blocks = Blocks(a[n_seq:], ones_blocks.spots, ones_blocks.rows)
            out_pack = middle_columns(blocks, 3 * cols, cols, n_dp)
            found = project(me_ref, order, lead_ref, a[:n_seq], blocks, kinds)
            return out_pack, found

        _, (out_pack, (normed, q, k, v, qkv, table, vecs)), _, _ = run(
            work=attend_first, inputs=tokens_by + list(ones_blocks.arrays), **steps(g_two)
        )
        out_held = {0: out_pack}

        def up_bias_of(table):
            u_bias = table[10 : 10 + extra].reshape(extra, n_dp, n_seq, part)
            u_bias = lax.dynamic_index_in_dim(u_bias, me, 2, keepdims=False)
            return jnp.swapaxes(u_bias, 0, 1).reshape(1, ff_cols)

        def attend_rest(q, k, v, table):
            lses, attended = [], None
            for p in range(pairs):
                attended, lse = attend(n_seq, p, me_ref, valid, q, k, v, attended)
                lses.append(lse)
            return attended, jnp.concatenate(lses, axis=0), up_bias_of(table)

        found, (attended, lse, u_bias), _, _ = run(
            far_gather(out_held, 0), work=attend_rest, inputs=(q, k, v, table), **steps(g_two)
        )
        with_far(out_held, found, 0)
        rest_far(out_held)
        att_held = {0: attended}
        nearby = near_all(out_held)
        found, _, _, _ = run(far_gather(att_held, 0) + nearby, **steps(g_two))
        with_near(out_held, found[-len(nearby) :])
        with_far(att_held, found[: -len(nearby)], 0)
        rest_far(att_held)
        found, _, _, _ = run(near_all(att_held))
        with_near(att_held, found)

        def out_whole(pieces):
            if part % 16 == 0:
                return pieces
            blocks = flipped(dict(enumerate(pieces)), n_seq).reshape(n_seq, n_dp, n_seq, part, cols)
            return [jnp.transpose(blocks, (1, 0, 3, 2, 4)).reshape(width, width)]

        found, (normed_two, middle_own, out_mine), _, _ = run(
            far_gather(grad_held[0], 0),
            work=lambda tok, att, outs, vecs: middle_norm(me_ref, order, tok, att, out_whole(outs), vecs),
            inputs=(
                tokens_by,
                [att_held[m] for m in masks],
                [out_held[m] for m in range(n_seq)],
                vecs,
            ),
            **steps(g_two),
        )
        with_far(grad_held[0], found, 0)
        rest_far(grad_held[0])
        while g_two.left:
            run(**steps(g_two))
        twos = ordered(order, g_two.pieces)
        downs = twos
        if twos.spots[0] is None:
            whole = twos.arrays[0]
            twos = Blocks([whole[:, :ff_cols]], [None], whole.shape[0])
            downs = Blocks([whole[:, ff_cols:].reshape(ff_cols, width)], [None], ff_cols)
        nearby = near_all(grad_held[0])
        found, (up, down, hidden, slope), _, _ = run(
            far_gather(grad_held[1], 0) + nearby,
            work=lambda n, b, a, d: up_part(
                order,
                n,
                b,
                Blocks(a, twos.spots, twos.rows),
                Blocks(d, downs.spots, downs.rows) if downs is not twos else None,
            ),
            inputs=(normed_two, u_bias, list(twos.arrays), list(downs.arrays) if downs is not twos else ()),
        )
        with_near(grad_held[0], found[-len(nearby) :])
        with_far(grad_held[1], found[: -len(nearby)], 0)
        rest_far(grad_held[1])

        def half_sum(keep, other):
            found = {}
            for at, m in enumerate(far_masks):
                if m:
                    rows_at = slice(at * half, (at + 1) * half)
                    found[m] = (keep[rows_at].astype(F32) + other[rows_at].astype(F32)).astype(BF16)
            return found

        def far_first(held):
            bit = far[-1]
            return [swap(held[m], bit, n_seq) for m in sorted(held) if m & bit]

        def far_rest(held, found):
            for at, bit in enumerate(reversed(far)):
                upper = sorted(m for m in held if m & bit)
                if at:
                    found, _, _, _ = line.slot([swap(held[m], bit, n_seq) for m in upper])
                kept = {m: held[m] for m in held if not m & bit}
                for m, value in zip(upper, found):
                    low = m ^ bit
                    if low in kept:
                        value = (kept[low].astype(F32) + value.astype(F32)).astype(BF16)
                    kept[low] = value
                held = kept
            return held[0]

        found, (pre, keep_a, send_a, branch_keep_a, branch_send_a, sum_a), _, _ = run(
            near_all(grad_held[1]),
            work=lambda *a: mlp_back(0, *a, None),
            inputs=(hidden, slope, up, down, [grad_held[0][m] for m in masks]),
        )
        with_near(grad_held[1], found)
        grads = [held[m] for held in grad_held for m in masks]
        (near_a,), (pre, keep_b, send_b, branch_keep_b, branch_send_b, sum_b), _, _ = run(
            [swap(send_a, 1, n_seq)],
            work=lambda *a: mlp_back(1, *a),
            inputs=(hidden, slope, up, down, [grad_held[1][m] for m in masks], pre),
        )
        def moved(value, axis, bit):
            count = n_dp if axis == "dp" else n_seq
            return lax.ppermute(value, axis, [(i, i ^ bit) for i in range(count)])

        held_a = half_sum(keep_a, near_a)
        sends = far_first(held_a)

        def weight_terms(hidden, grads, normed_two, pre):
            up_terms = dot(normed_two, pre, TN).astype(BF16).reshape(n_dp, n_seq * part, ff_cols)
            return dot(hidden, lay_rows(grads), TN).astype(BF16).reshape(n_dp, ff_part, width), up_terms

        found, (down_terms, up_terms), _, _ = run(
            sends + [swap(send_b, 1, n_seq)], work=weight_terms, inputs=(hidden, grads, normed_two, pre)
        )
        far_a, near_b = far_rest(held_a, found[: len(sends)]), found[-1]
        held_b = half_sum(keep_b, near_b)

        def back_half(at):
            return lambda *a: tuple(second_back(at, *a))

        scatter_two = JointScatter(ring, up_terms, down_terms)
        def both_halves(held, mids, outs_own, vecs, keep_a, near_a, far_a, keep_b, near_b):
            far_b = {}
            if far:
                bit = far[-1]
                far_b = [lax.ppermute(held[m], "seq", [(i, i ^ bit) for i in range(n_seq)]) for m in sorted(held) if m & bit]
            first = second_back(0, mids, keep_a, near_a, far_a, outs_own[0], vecs)
            sent = [lax.ppermute(first[1], "seq", [(i, i ^ far[0]) for i in range(n_seq)])] if far else []
            far_b = far_rest(held, far_b)
            return first, second_back(1, mids, keep_b, near_b, far_b, outs_own[1], vecs), sent

        if len(far) == 1:
            branch_other, (first, second, one_far_a), _, _ = run(
                [swap(branch_send_a, 1, n_seq), swap(branch_send_b, 1, n_seq)],
                work=both_halves,
                inputs=(held_b, middle_own, outs_own, vecs, keep_a, near_a, far_a, keep_b, near_b),
                **steps(scatter_two),
            )
            grad_mid_a, one_a, sums_a = first
            grad_mid_b, one_b, sums_b = second
        else:
            _, (grad_mid_a, one_a, sums_a), far_b, _ = run(
                work=back_half(0),
                inputs=(middle_own, keep_a, near_a, far_a, outs_own[0], vecs),
                begin=far_first(held_b),
                **begun(scatter_two),
            )
            _, _, one_far_a, far_b = run(begin=far_gather({0: one_a}, 0), end=far_b)
            far_b = far_rest(held_b, far_b)
            branch_other, (grad_mid_b, one_b, sums_b), _, one_far_a = run(
                [swap(branch_send_a, 1, n_seq), swap(branch_send_b, 1, n_seq)],
                work=back_half(1),
                inputs=(middle_own, keep_b, near_b, far_b, outs_own[1], vecs),
                end=one_far_a,
                finish=[scatter_two],
            )
        one_held_a = {0: one_a}
        with_far(one_held_a, one_far_a, 0)
        rest_far(one_held_a)
        one_held_b = {0: one_b}
        found, _, one_far_b, _ = run(
            near_all(one_held_a), begin=far_gather(one_held_b, 0), **begun(scatter_two)
        )
        with_near(one_held_a, found)
        _, (dq_a, dk_a, dv_a), _, one_far_b = run(
            work=lambda *a: attend_back(0, me_ref, valid, *a, None),
            inputs=(q, k, v, lse, out_mine, [one_held_a[m] for m in masks]),
            end=one_far_b,
            finish=[scatter_two],
        )
        with_far(one_held_b, one_far_b, 0)
        rest_far(one_held_b)
        found, _, _, _ = run(near_all(one_held_b), **begun(scatter_two))
        with_near(one_held_b, found)
        ones = [one_held_a[m] for m in masks] + [one_held_b[m] for m in masks]

        branch_held = {
            m: jnp.concatenate([value, half_sum(branch_keep_b, branch_other[1])[m]], axis=0)
            for m, value in half_sum(branch_keep_a, branch_other[0]).items()
        }

        def second_attend(q, k, v, lse, out_mine, grads, earlier, att, ones):
            sums = out_terms(att, ones, n_dp, part if part % 16 else n_seq * part)
            return attend_back(1, me_ref, valid, q, k, v, lse, out_mine, grads, earlier), sums

        branch_far, (grad_qkv, out_sums), _, _ = run(
            far_first(branch_held),
            work=second_attend,
            inputs=(
                q,
                k,
                v,
                lse,
                out_mine,
                [one_held_b[m] for m in masks],
                (dq_a, dk_a, dv_a),
                [attended],
                ones,
            ),
            finish=[scatter_two],
        )
        branch_far = far_rest(branch_held, branch_far)

        qkv_terms = dot(normed, grad_qkv, TN).astype(BF16).reshape(n_dp, n_seq * part, 3 * cols)
        scatter_one = (ApartScatter if part % 16 else JointScatter)(ring, qkv_terms, out_sums)
        late = [scatter_two] if scatter_two.left else []

        def far_moved(held):
            if not far:
                return []
            return [moved(held[m], "seq", far[-1]) for m in sorted(held) if m & far[-1]]

        def now(*beside):
            mine = [scatter_one] if scatter_one.left else []
            return dict(start=mine, finish=mine + list(beside))

        def final_rows(keep_a, keep_b, near_a, near_b, far_part, mid, bias):
            total = jnp.concatenate([keep_a[:half], keep_b[:half]], axis=0).astype(F32)
            total = total + jnp.concatenate([near_a[:half], near_b[:half]], axis=0).astype(F32)
            return (mid + (total + far_part.astype(F32) + bias[6:7])).astype(BF16)

        late = [scatter_two] if scatter_two.left else []
        options = now()
        _, (gn_keep, gn_send, column_sums, last_sums), _, _ = run(
            work=first_grad,
            inputs=(grad_qkv, qkv, vecs, tokens_by),
            start=options["start"] + late,
            finish=options["finish"] + late,
        )
        while scatter_two.left:
            run(**steps(scatter_two))
        plain = (width // n_dp) % 128 == 0 and extra == n_seq and n_seq * part == 128

        bits = []
        while 2 ** len(bits) < n_dp:
            bits.append(2 ** len(bits))
        bits = bits[::-1] if plain else []
        at_dp = lax.axis_index("dp")

        def loose_table():
            sums = sums_a + sums_b
            table = last_sums
            start_sums = table[2:3] + sums[4:5]
            q_sum = lax.dynamic_update_slice(jnp.zeros((1, width), F32), column_sums[:, :cols], (0, me * cols))
            v_sum = lax.dynamic_update_slice(jnp.zeros((1, width), F32), column_sums[:, 2 * cols :], (0, me * cols))
            u_sum = jnp.swapaxes((sum_a + sum_b).reshape(n_dp, extra, part), 0, 1)
            u_sum = lax.dynamic_update_index_in_dim(jnp.zeros((extra, n_dp, n_seq, part), F32), u_sum, me, 2)
            rows_out = [table[0:2], q_sum, v_sum, sums[2:3], sums[0:2], sums[3:4], lead * start_sums, start_sums]
            table = jnp.concatenate(rows_out + [u_sum.reshape(extra, width)], axis=0)
            return lax.psum_scatter(table, ("dp", "seq"), scatter_dimension=1, tiled=True)

        seq_bits = far + ([1] if n_seq > 1 else []) if plain else []

        def make_table():
            if not plain:
                return loose_table()
            return small_table(
                me_ref, lead_ref, sums_a, sums_b, last_sums, sum_a, sum_b, column_sums
            )

        def hop(held):
            if bits:
                bit = bits.pop(0)
                mine, other = halve(((at_dp // bit) % 2).reshape(1).astype(jnp.int32), held)
                return mine, [(other, "dp", [(i, i ^ bit) for i in range(n_dp)])]
            total = sum(held[1:], held[0])
            if seq_bits:
                return total, [swap(total, seq_bits.pop(0), n_seq)]
            return total, []

        def totals():
            blocks, total = scatter_two.total(me_ref, n_seq, F32)
            return *blocks, total

        mine, small = hop([make_table()])
        found, (*up_blocks, down_grad), _, _ = run([swap(gn_send, 1, n_seq)] + small, work=totals, **now())
        gn_near = found[0]
        held = [mine] + found[1:]
        size = half * len(far_masks)
        gn_held_a = half_sum(gn_keep[:size], gn_near[:size])
        mine, small = hop(held)
        sends = far_first(gn_held_a)
        found, (gn_held_b,), _, _ = run(
            sends + small, work=lambda k, n: (half_sum(k[size:], n[size:]),), inputs=(gn_keep, gn_near), **now()
        )
        gn_far_a = far_rest(gn_held_a, found[: len(sends)])
        held = [mine] + found[len(sends) :]
        mine, small = hop(held)
        sends = far_first(gn_held_b)
        found, (block_out,), _, _ = run(
            sends + small,
            work=lambda *a: (final_rows(*a),),
            inputs=(branch_keep_a, branch_keep_b, branch_other[0], branch_other[1], branch_far, middle_own, vecs),
            **now(),
        )
        gn_far_b = far_rest(gn_held_b, found[: len(sends)])
        held = [mine] + found[len(sends) :]
        while scatter_one.left:
            run(**steps(scatter_one))
        qkv_blocks, out_sum = scatter_one.total(me_ref, n_seq, beside=up_blocks)
        moves = []
        for dp_at in range(n_dp):
            for seq_at in range(n_seq):
                moves.append((dp_at * n_seq + seq_at, seq_at * n_dp + dp_at))
        final = [(out_sum, ("dp", "seq"), moves)] + [swap(qkv_blocks[m], m, n_seq) for m in range(1, n_seq)]

        mine, small = hop(held)
        found, (tokens_grad,), _, _ = run(
            final + small,
            work=lambda *a: (first_back(*a),),
            inputs=(tokens[0], gn_keep, gn_near, gn_far_a, gn_far_b, grad_mid_a, grad_mid_b, vecs),
        )
        last, held = found[: len(final)], [mine] + found[len(final) :]
        while bits or seq_bits:
            mine, small = hop(held)
            found, _, _, _ = run(small)
            held = [mine] + found
        small_sums = sum(held[1:], held[0])
        if plain:
            small_sums = lax.dynamic_slice_in_dim(small_sums, me * part, part, 1)
        owned = small_sums[:kinds]
        qkv_weight_grad, up_weight_grad = unpack(
            (3, n_dp), (3 * width, ff), me_ref, [qkv_blocks[0]] + list(last[1:])
        )
        out_weight_grad = last[0].reshape(-1, part, width * part // last[0].shape[0])
        out_weight_grad = jnp.moveaxis(out_weight_grad, 0, 1).reshape(part, width).astype(F32)
        return (
            block_out[None],
            tokens_grad[None],
            owned[0],
            owned[1],
            qkv_weight_grad,
            owned[2],
            owned[3],
            out_weight_grad,
            owned[4],
            owned[5],
            owned[6],
            up_weight_grad,
            owned[10 : 10 + extra].reshape(ff_part),
            down_grad[0] if down_grad.ndim == 3 else down_grad,
            owned[7],
            owned[8],
            owned[9],
        )

    return body


def solution(mesh):
    both = P(("dp", "seq"))
    matrix = P(("dp", "seq"), None)
    tokens = P("dp", "seq", None)
    in_specs = (tokens, P("dp"), P("dp"), P("dp", "seq"), both, both, matrix, both, both, matrix, both, both, both)
    in_specs += (matrix, both, matrix, both, both, both, tokens)
    out_specs = (tokens, tokens, both, both, matrix, both, both, matrix, both, both, both, matrix, both, matrix)
    out_specs += (both, both, both)
    return jax.shard_map(
        make_body(mesh.shape["dp"], mesh.shape["seq"]),
        mesh=mesh,
        in_specs=in_specs,
        out_specs=out_specs,
        check_vma=False,
    )
```

```python
import functools
import math

import jax
import jax.numpy as jnp
import numpy as np
from jax import lax
from jax.experimental import pallas as pl
from jax.experimental.pallas import tpu as pltpu
from jax.sharding import PartitionSpec as P

HEADS = 16
HEAD_DIM = 64
PAIR = 2 * HEAD_DIM
SCALE = 1.0 / math.sqrt(HEAD_DIM)
EPSILON = 1e-06
MASKED = -1e30
F32 = jnp.float32
BF16 = jnp.bfloat16
NN, NT, TN = ((1,), (0,)), ((1,), (1,)), ((0,), (0,))
HALVES = 2
MIB = 1024 * 1024
NEAR = pl.BlockSpec(memory_space=pltpu.VMEM)
AWAY = pl.BlockSpec(memory_space=pl.ANY)
NUMBERS = pl.BlockSpec(memory_space=pltpu.SMEM)


def dot(left, right, contract):
    return lax.dot_general(left, right, (contract, ((), ())), preferred_element_type=F32)


def shape(dims, dtype=BF16):
    return jax.ShapeDtypeStruct(dims, dtype)


def call(kernel, *, in_specs, out_shape, near_in=(), near_out=(), **options):
    def large(value):
        return math.prod(value.shape) * value.dtype.itemsize >= 65536

    def run(*args):
        kept = []
        for i, a in enumerate(args):
            if large(a):
                a = pltpu.with_memory_space_constraint(a, pltpu.VMEM if i in near_in else pltpu.HBM)
            kept.append(a)
        single = not isinstance(out_shape, (list, tuple))
        outs = [out_shape] if single else list(out_shape)
        outs = [
            ((pltpu.VMEM if i in near_out else pltpu.HBM)(o.shape, o.dtype) if large(o) else o)
            for i, o in enumerate(outs)
        ]
        return pl.pallas_call(kernel, in_specs=in_specs, out_shape=outs[0] if single else outs, **options)(*kept)

    return run


def away(value):
    return pltpu.with_memory_space_constraint(value, pltpu.HBM)


class Here:
    def __getitem__(self, at):
        return lax.axis_index("seq")


class Order:
    def __init__(self, cycle):
        self.cycle = cycle

    def __getitem__(self, k):
        n = len(self.cycle)
        mine = lax.axis_index("dp")
        spot = sum(jnp.where(mine == place, at, 0) for at, place in enumerate(self.cycle))
        spot = lax.rem(spot + k % n, n)
        return sum(jnp.where(spot == at, place, 0) for at, place in enumerate(self.cycle))


ME = Here()


def near(value):
    return pltpu.with_memory_space_constraint(value, pltpu.VMEM)


def vmem(mib):
    return pltpu.CompilerParams(vmem_limit_bytes=mib * MIB)


def cost(flops, moved, exps=0):
    return pl.CostEstimate(flops=int(flops), bytes_accessed=int(moved), transcendentals=int(exps))


def standardise(values):
    centered = values - jnp.mean(values, axis=-1, keepdims=True)
    rate = lax.rsqrt(jnp.mean(centered * centered, axis=-1, keepdims=True) + EPSILON)
    return centered * rate, rate


def norm_back(upstream, xhat, rate, gain):
    scaled = upstream * gain
    inner = jnp.mean(scaled * xhat, axis=-1, keepdims=True)
    return rate * (scaled - jnp.mean(scaled, axis=-1, keepdims=True) - xhat * inner)


def pack_kernel(n_dp, n_seq, me_ref, qkv_ref, up_ref, *refs):
    vectors, out_refs = refs[: -2 * n_seq], refs[-2 * n_seq :]
    out_refs, up_refs = out_refs[:n_seq], out_refs[n_seq:]
    me = me_ref[0]
    part = qkv_ref.shape[0]
    cols = qkv_ref.shape[1] // (3 * n_seq)
    piece = up_ref.shape[1] // (n_dp * n_seq)
    rows = [ref[...].astype(F32)[:, i : i + part] for ref in vectors for i in range(0, ref.shape[1], part)]
    kinds = len(rows)
    rows = jnp.concatenate(rows + [jnp.zeros((128 - kinds, part), F32)], axis=0)
    rows = jnp.concatenate([rows, jnp.zeros((128, 128 - part), F32)], axis=1)
    small = rows.T[:part, :].astype(BF16)
    for mask, ref in enumerate(out_refs):
        place = me ^ mask
        for i in range(3):
            start = pl.multiple_of((i * n_seq + place) * cols, 128)
            ref[:, i * cols : (i + 1) * cols] = qkv_ref[:, pl.ds(start, cols)]
        at = 3 * cols
        ref[:, at : at + 128] = small
        for i in range(n_dp):
            start = pl.multiple_of((i * n_seq + place) * piece, 128)
            up_refs[mask][:, i * piece : (i + 1) * piece] = up_ref[:, pl.ds(start, piece)]


def pack(n_dp, n_seq, me, qkv, up, vectors):
    part = qkv.shape[0]
    wide = qkv.shape[1] // n_seq + 128
    ff = up.shape[1] // n_seq
    if up.shape[1] // (n_dp * n_seq) % 128 or part % 16:
        small = jnp.concatenate(vectors).reshape(-1, part).T
        small = jnp.pad(small, ((0, 0), (0, 128 - small.shape[1])))
        qkv_split = qkv.reshape(part, 3, n_seq, -1)
        up_split = up.reshape(part, n_dp, n_seq, -1)

        def block(place):
            q = lax.dynamic_index_in_dim(qkv_split, place, 2, keepdims=False).reshape(part, -1)
            u = lax.dynamic_index_in_dim(up_split, place, 2, keepdims=False).reshape(part, -1)
            return jnp.concatenate([q, small], axis=1), u

        blocks = [block(me[0] ^ m) for m in range(n_seq)]
        return [b[0] for b in blocks] + [b[1] for b in blocks]
    args = [qkv, up] + [v.reshape(1, -1) for v in vectors]
    args = [pltpu.with_memory_space_constraint(a, pltpu.HBM) for a in args]
    return pl.pallas_call(
        functools.partial(pack_kernel, n_dp, n_seq, ME),
        grid=(1,),
        in_specs=[pl.BlockSpec(a.shape, lambda i: (0, 0)) for a in args],
        out_specs=[pl.BlockSpec((part, wide), lambda i: (0, 0))] * n_seq
        + [pl.BlockSpec((part, ff), lambda i: (0, 0))] * n_seq,
        out_shape=[shape((part, wide))] * n_seq + [shape((part, ff))] * n_seq,
        compiler_params=vmem(8),
        name="pack",
    )(*args)


def join_one_kernel(n_seq, me_ref, *refs):
    out_ref, left_ref = refs[-2:]
    part, wide = out_ref.shape
    cols = wide // n_seq
    edge = refs[0].shape[1] - 128
    for t, ref in enumerate(refs[:-2]):
        rows = pl.ds(pl.multiple_of((me_ref[0] ^ t) * part, part), part)
        left_ref[rows, :edge] = ref[:, :edge]
        left_ref[rows, edge + cols :] = ref[:, edge:]
        left_ref[t * part : (t + 1) * part, edge : edge + cols] = out_ref[:, t * cols : (t + 1) * cols]


def join_two_kernel(n_seq, me_ref, *refs):
    down_ref, right_ref = refs[-2:]
    half = down_ref.shape[1]
    part = refs[0].shape[0]
    right_ref[:, -half:] = down_ref[...]
    for t, ref in enumerate(refs[:-2]):
        right_ref[pl.ds(pl.multiple_of((me_ref[0] ^ t) * part, part), part), :-half] = ref[...]


def join(kernel, n_seq, me, pieces, weight, wide):
    rows = pieces[0].shape[0] * n_seq
    args = list(pieces) + [away(weight)]
    return pl.pallas_call(
        functools.partial(kernel, n_seq, ME),
        grid=(1,),
        in_specs=[pl.BlockSpec(a.shape, lambda i: (0, 0)) for a in args],
        out_specs=pl.BlockSpec((rows, wide), lambda i: (0, 0)),
        out_shape=shape((rows, wide)),
        compiler_params=vmem(8),
        name="join",
    )(*args)


def join_one(n_seq, me, pieces, out_weight):
    part, edge = pieces[0].shape
    edge -= 128
    cols = out_weight.shape[1] // n_seq
    if part % 16:
        whole = flipped(dict(enumerate(pieces)), n_seq).reshape(part * n_seq, edge + 128)
        beside = jnp.moveaxis(out_weight.reshape(part, n_seq, cols), 1, 0).reshape(part * n_seq, cols)
        return jnp.concatenate([whole[:, :edge], beside, whole[:, edge:]], axis=1)
    return join(join_one_kernel, n_seq, me, pieces, out_weight, edge + cols + 128)


def join_two(n_seq, me, pieces, down_weight):
    part, wide = pieces[0].shape
    rows = part * n_seq
    if part % 16:
        whole = flipped(dict(enumerate(pieces)), n_seq).reshape(rows, wide)
        return jnp.concatenate([whole, down_weight.reshape(rows, -1)], axis=1)
    return join(join_two_kernel, n_seq, me, pieces, down_weight, wide + down_weight.shape[1])


class Blocks:
    def __init__(self, arrays, spots, rows):
        self.arrays = arrays
        self.spots = spots
        self.rows = rows

    def place(self, order_ref, i, source=None):
        k, start = self.spots[i]
        count = self.arrays[i].shape[0]
        if order_ref is None:
            return slice(k * self.rows + start, k * self.rows + start + count)
        return pl.ds(pl.multiple_of(order_ref[k] * self.rows + start, math.gcd(self.rows, start or self.rows)), count)


def ordered(order, pieces):
    rows = pieces[0].shape[0]
    if rows % 128 == 0:
        arrays, spots = [], []
        for k, piece in enumerate(pieces):
            halves = piece if isinstance(piece, tuple) else (piece,)
            for i, half in enumerate(halves):
                arrays.append(half)
                spots.append((k, i * rows // 2))
        return Blocks(arrays, spots, rows)
    whole = jnp.stack([jnp.concatenate(p, axis=0) if isinstance(p, tuple) else p for p in pieces])
    out = whole
    for k in range(len(pieces)):
        out = lax.dynamic_update_index_in_dim(out, whole[k], order[k], 0)
    return Blocks([out.reshape(-1, out.shape[-1])], [None], len(pieces) * rows)


def lay(order_ref, blocks, refs, target, cols=slice(None)):
    for i, ref in enumerate(refs):
        if blocks.spots[i] is None:
            target[...] = ref[:, cols]
        else:
            target[blocks.place(order_ref, i), :] = ref[:, cols]


def middle_columns_kernel(blocks, *refs):
    for i, ref in enumerate(refs[:-1]):
        refs[-1][blocks.place(None, i), :] = ref[...]


def middle_columns(blocks, start, cols, n_dp):
    if blocks.spots[0] is None or start % cols:
        return blocks.arrays[0][:, start : start + cols]
    total = blocks.rows * n_dp
    return call(
        functools.partial(middle_columns_kernel, blocks),
        grid=(1,),
        in_specs=[pl.BlockSpec((a.shape[0], cols), lambda i: (0, start // cols)) for a in blocks.arrays],
        out_specs=pl.BlockSpec((total, cols), lambda i: (0, 0)),
        out_shape=shape((total, cols)),
        compiler_params=vmem(4),
        name="middle_columns",
    )(*blocks.arrays)


def project_kernel(n_seq, blocks, me_ref, order_ref, lead_ref, *refs):
    n_pieces = len(blocks.arrays)
    tokens = refs[:n_seq]
    pieces = refs[n_seq : n_seq + n_pieces]
    normed_ref, q_ref, k_ref, v_ref, qkv_ref, table_ref, vec_ref, small_ref = refs[n_seq + n_pieces :]
    cols = q_ref.shape[1]

    @pl.when(pl.program_id(0) == 0)
    def _():
        lay(order_ref, blocks, pieces, qkv_ref, slice(0, 3 * cols))
        lay(order_ref, blocks, pieces, small_ref, slice(4 * cols, 4 * cols + 128))
        table_ref[...] = small_ref[...].astype(F32).T[: table_ref.shape[0], :]
        for i, kind in enumerate((0, 0, 1, 4, 5, 6, 7, 7)):
            vec_ref[i : i + 1, :] = table_ref[kind : kind + 1, :]
        vec_ref[0:1, :] = lead_ref[0:1, 0:1] * table_ref[8:9, :] + table_ref[9:10, :]

    start = jnp.concatenate([ref[...] for ref in tokens], axis=0).astype(F32) + vec_ref[0:1, :]
    xhat, _ = standardise(start)
    normed = (xhat * vec_ref[1:2, :] + vec_ref[2:3, :]).astype(BF16)
    normed_ref[...] = normed
    mine = pl.ds(pl.multiple_of(me_ref[0] * cols, 128), cols)
    found = dot(normed, qkv_ref[...], NN)
    q_ref[...] = (found[:, :cols] + table_ref[2:3, mine]).astype(BF16)
    k_ref[...] = found[:, cols : 2 * cols].astype(BF16)
    v_ref[...] = (found[:, 2 * cols :] + table_ref[3:4, mine]).astype(BF16)


def project(me, order, lead, tokens, blocks, kinds):
    rows, width = tokens[0].shape
    n_seq = len(tokens)
    cols = width // n_seq
    length = rows * n_seq
    half = rows // HALVES
    count = length // HALVES
    numbers = pl.BlockSpec(memory_space=pltpu.SMEM)

    def whole(dims):
        return pl.BlockSpec(dims, lambda i: (0, 0))

    def step(wide):
        return pl.BlockSpec((count, wide), lambda i: (i, 0))

    return call(
        functools.partial(project_kernel, n_seq, blocks, ME, order),
        near_out=(1, 2, 3),
        grid=(HALVES,),
        in_specs=[whole(lead.shape)]
        + [pl.BlockSpec((half, width), lambda i: (i, 0))] * n_seq
        + [whole(a.shape) for a in blocks.arrays],
        out_specs=[step(width), step(cols), step(cols), step(cols)]
        + [whole((width, 3 * cols)), whole((kinds, width)), whole((8, width))],
        out_shape=[shape((length, width))]
        + [shape((length, cols))] * 3
        + [shape((width, 3 * cols)), shape((kinds, width), F32), shape((8, width), F32)],
        scratch_shapes=[pltpu.VMEM((width, 128), BF16)],
        compiler_params=vmem(28),
        cost_estimate=cost(6 * length * width * cols, 10 * length * width),
        name="project",
    )(lead, *tokens, *blocks.arrays)


def key_bias(n_seq, length, me, count):
    half = length // (n_seq * HALVES)
    parts = []
    for h in range(HALVES):
        for m in block_masks(n_seq):
            at = lax.broadcasted_iota(jnp.int32, (half, 1), 0) + ((me ^ m) * HALVES + h) * half
            parts.append(jnp.where(at < count, 0.0, MASKED).astype(F32))
    return jnp.concatenate(parts, axis=0)


def attend_kernel(n_seq, me_ref, pair_at, count_ref, q_ref, k_ref, v_ref, *refs):
    out_ref, lse_ref = refs[-2:]
    bias = key_bias(n_seq, k_ref.shape[0], me_ref[0], count_ref[0:1, 0:1])
    count = q_ref.shape[0] // 2

    def step(i, carry):
        rows = pl.ds(pl.multiple_of(i * count, count), count)
        for half in range(2):
            cols = slice(half * HEAD_DIM, (half + 1) * HEAD_DIM)
            mine = slice(pair_at * PAIR + cols.start, pair_at * PAIR + cols.stop)
            scores = dot(k_ref[:, mine], q_ref[rows, mine] * SCALE, NT) + bias
            top = jnp.max(scores, axis=0, keepdims=True)
            weights = jnp.exp(scores - top)
            total = jnp.sum(weights, axis=0, keepdims=True)
            mixed = dot(v_ref[:, mine], weights.astype(BF16), TN) / total
            out_ref[rows, cols] = mixed.T.astype(BF16)
            lse_ref[half, :, rows] = top + jnp.log(total)
        return carry

    lax.fori_loop(0, 2, step, 0)


def attend(n_seq, pair_at, me, valid, q, k, v, earlier):
    length, cols = q.shape
    pair = pl.BlockSpec((length, PAIR), lambda g: (0, pair_at))
    given = [] if earlier is None else [earlier]
    return call(
        functools.partial(attend_kernel, n_seq, ME, pair_at),
        near_in=(1, 2, 3),
        grid=(1,),
        in_specs=[pl.BlockSpec(valid.shape, lambda g: (0, 0)), NEAR, NEAR, NEAR] + [AWAY] * len(given),
        out_specs=[pair, pl.BlockSpec((2, 1, length), lambda g: (0, 0, 0))],
        out_shape=[shape((length, cols)), shape((2, 1, length), F32)],
        input_output_aliases={4: 0} if given else {},
        compiler_params=vmem(32),
        cost_estimate=cost(4 * length * length * PAIR, 8 * length * PAIR, 2 * length * length),
        name="attend",
    )(valid, q, k, v, *given)


def attend_back_kernel(first, n_seq, *refs):
    count_ref, q_ref, k_ref, v_ref, lse_ref, out_w_ref = refs[:6]
    grads = refs[6 : 6 + n_seq]
    rest = refs[6 + n_seq :]
    if first:
        dq_ref, dk_ref, dv_ref = rest
    else:
        dq_in, dk_in, dv_in, whole_ref, q_out, k_out, v_out, sems = rest
    length = k_ref.shape[0]
    count = q_ref.shape[0]
    pair = pl.program_id(0)
    spot = pair % 2
    bias = key_bias(n_seq, length, ME[0], count_ref[0:1, 0:1])
    upstream = jnp.concatenate([dot(ref[...], out_w_ref[...], NT).astype(BF16) for ref in grads], axis=0)
    for half in range(2):
        cols = slice(half * HEAD_DIM, (half + 1) * HEAD_DIM)
        k = k_ref[:, cols]
        q = q_ref[:, cols] * SCALE
        g = upstream[:, cols]
        probs = jnp.exp(dot(k, q, NT) + bias - lse_ref[half])
        dv = dot(probs.astype(BF16), g, NN)
        term = probs * dot(v_ref[:, cols], g, NT)
        grad = (term - probs * jnp.sum(term, axis=0, keepdims=True)).astype(BF16)
        dk = dot(grad, q, NN)
        dq = (dot(k, grad, TN) * SCALE).T.astype(BF16)
        if first:
            dq_ref[:, cols] = dq
            dk_ref[:, cols] = dk
            dv_ref[:, cols] = dv
        else:
            q_out[spot, :count, cols] = dq_in[:, cols]
            q_out[spot, count:, cols] = dq
            k_out[spot, :, cols] = (dk + dk_in[:, cols]).astype(BF16)
            v_out[spot, :, cols] = (dv + dv_in[:, cols]).astype(BF16)
    if first:
        return
    pairs = pl.num_programs(0)

    def copies(at):
        found = []
        for i, source in enumerate((q_out, k_out, v_out)):
            start = pl.multiple_of((i * pairs + at) * PAIR, PAIR)
            target = whole_ref.at[:, pl.ds(start, PAIR)]
            found.append(pltpu.make_async_copy(source.at[at % 2], target, sems.at[at % 2, i]))
        return found

    for copy in copies(pair):
        copy.start()

    @pl.when(pair > 0)
    def _():
        for copy in copies(pair - 1):
            copy.wait()

    @pl.when(pair == pairs - 1)
    def _():
        for copy in copies(pair):
            copy.wait()


def attend_back(at, me, valid, q, k, v, lse, out_mine, grads, earlier):
    length, cols = k.shape
    width = out_mine.shape[1]
    count = length // HALVES
    pair = pl.BlockSpec((length, PAIR), lambda g: (0, g))
    mine = pl.BlockSpec((count, PAIR), lambda g: (at, g))
    here = pl.BlockSpec((count, PAIR), lambda g: (0, g))
    first = earlier is None
    near_out = () if first else (0,)
    in_specs = [pl.BlockSpec(valid.shape, lambda g: (0, 0))] + [
        mine,
        pair,
        pair,
        pl.BlockSpec((2, 1, count), lambda g: (g, 0, at)),
        pl.BlockSpec((PAIR, width), lambda g: (g, 0)),
    ]
    in_specs += [pl.BlockSpec(piece.shape, lambda g: (0, 0)) for piece in grads]
    args = [valid, q, k, v, lse, out_mine] + list(grads)
    if first:
        out_specs = [here, pair, pair]
        out_shape = [shape((count, cols))] + [shape((length, cols), F32)] * 2
        scratch = []
    else:
        in_specs += [here, pair, pair]
        args += list(earlier)
        out_specs = AWAY
        out_shape = shape((length, 3 * cols))
        scratch = [pltpu.VMEM((2, length, PAIR), BF16)] * 3 + [pltpu.SemaphoreType.DMA((2, 3))]
    return call(
        functools.partial(attend_back_kernel, first, len(grads)),
        near_out=near_out,
        grid=(cols // PAIR,),
        in_specs=in_specs,
        out_specs=out_specs,
        out_shape=out_shape,
        scratch_shapes=scratch,
        compiler_params=vmem(36),
        cost_estimate=cost(10 * count * length * cols, 8 * length * cols, count * length * cols // HEAD_DIM),
        name="attend_back",
    )(*args)


def middle_kernel(n_seq, n_out, me_ref, order_ref, *refs):
    tokens, refs = refs[:n_seq], refs[n_seq:]
    outs, refs = refs[:n_out], refs[n_out:]
    att, refs = refs[:-5], refs[-5:]
    vec_ref, normed_ref, middle_ref, mine_ref, out_ref = refs
    masks = block_masks(n_seq)
    me = me_ref[0]
    pairs = len(att) // n_seq
    cols = pairs * att[0].shape[1]
    half = middle_ref.shape[0]
    width = normed_ref.shape[1]
    step = pl.program_id(0)

    @pl.when(step == 0)
    def _():
        if n_out == 1:
            out_ref[...] = outs[0][...]
        else:
            n_dp = len(order_ref.cycle)
            part = width // (n_dp * n_seq)
            for mask, ref in enumerate(outs):
                for k in range(n_dp):
                    start = pl.multiple_of((order_ref[k] * n_seq + (me ^ mask)) * part, part)
                    for t in range(n_seq):
                        at = (k * n_seq + t) * part
                        out_ref[pl.ds(start, part), t * cols : (t + 1) * cols] = ref[at : at + part, :]
        mine_ref[...] = out_ref[pl.ds(pl.multiple_of(me * cols, cols), cols), :]

    near = [tokens[i][...] for i in range(n_seq // 2)]
    other = [tokens[i][...] for i in range(n_seq // 2, n_seq)]
    start = [jnp.where(step % 2 == 0, a, b) for a, b in zip(near, other)]
    middle = jnp.concatenate(start, axis=0).astype(F32) + vec_ref[0:1, :] + vec_ref[3:4, :]
    for i, mask in enumerate(masks):
        at = pl.multiple_of((me ^ mask) * cols, cols)
        spots = [t ^ (mask >> 1) for t in range(n_seq // 2)]
        group = att[i * pairs : (i + 1) * pairs]
        found = [jnp.concatenate([ref[t * half : (t + 1) * half, :] for t in spots], axis=0) for ref in group]
        found = jnp.concatenate(found, axis=1)
        middle = middle + dot(found, out_ref[pl.ds(at, cols), :], NN)
    xhat, _ = standardise(middle)
    normed_ref[...] = (xhat * vec_ref[4:5, :] + vec_ref[5:6, :]).astype(BF16)

    @pl.when(step % 2 == 0)
    def _():
        middle_ref[...] = middle[:half, :]


def middle_norm(me, order, tokens, att, outs, vecs):
    rows, width = tokens[0].shape
    n_seq = len(tokens)
    length = rows * n_seq
    cols = width // n_seq
    block = length // (2 * HALVES)
    half = rows // HALVES
    numbers = pl.BlockSpec(memory_space=pltpu.SMEM)
    return call(
        functools.partial(middle_kernel, n_seq, len(outs), ME, order),
        near_out=(0,),
        grid=(2 * HALVES,),
        in_specs=[pl.BlockSpec((half, width), lambda i: (i // 2, 0))] * n_seq
        + [pl.BlockSpec(out.shape, lambda i: (0, 0)) for out in outs]
        + [
            pl.BlockSpec((block, att[0].shape[1]), lambda i, side=mask & 1: (i ^ side, 0))
            for mask in block_masks(n_seq)
            for _ in range(len(att) // n_seq)
        ]
        + [pl.BlockSpec(vecs.shape, lambda i: (0, 0))],
        out_specs=[
            pl.BlockSpec((block, width), lambda i: (i, 0)),
            pl.BlockSpec((half, width), lambda i: (i // 2, 0)),
            pl.BlockSpec((cols, width), lambda i: (0, 0)),
        ],
        out_shape=[shape((length, width)), shape((rows, width), F32), shape((cols, width))],
        scratch_shapes=[pltpu.VMEM((width, width), BF16)],
        compiler_params=vmem(24),
        cost_estimate=cost(2 * length * width * width, 10 * length * width),
        name="middle_norm",
    )(*tokens, *outs, *att, vecs)


def fetch(pairs, sems):
    copies = [pltpu.make_async_copy(a, b, sems.at[i]) for i, (a, b) in enumerate(pairs)]
    for copy in copies:
        copy.start()

    def wait():
        for copy in copies:
            copy.wait()

    return wait


def placed(order_ref, blocks, refs, target, start):
    if blocks.spots[0] is None:
        return [(refs[0], target)]
    cols = pl.ds(start, target.shape[1])
    return [(ref.at[:, cols], target.at[blocks.place(order_ref, i), :]) for i, ref in enumerate(refs)]


def up_kernel(ups, downs, block, order_ref, normed_ref, bias_ref, *refs):
    up_pieces, refs = refs[: len(ups.arrays)], refs[len(ups.arrays) :]
    if downs is None:
        downs, down_pieces = ups, up_pieces
    else:
        down_pieces, refs = refs[: len(downs.arrays)], refs[len(downs.arrays) :]
    up_ref, down_ref, hidden_ref, slope_ref, up_sems, down_sems = refs
    here = fetch(placed(order_ref, ups, up_pieces, up_ref, 0), up_sems)
    later = fetch(placed(order_ref, downs, down_pieces, down_ref, up_ref.shape[1]), down_sems)
    here()

    def step(i, carry):
        cols = pl.ds(pl.multiple_of(i * block, block), block)
        pre = dot(normed_ref[...], up_ref[:, cols], NN) + bias_ref[:, cols]
        phi = 0.5 + 0.5 * lax.erf(pre * math.sqrt(0.5))
        hidden_ref[:, cols] = (pre * phi).astype(BF16)
        slope_ref[:, cols] = phi + pre * (jnp.exp(-0.5 * pre * pre) * (1.0 / math.sqrt(2.0 * math.pi)))
        return carry

    lax.fori_loop(0, up_ref.shape[1] // block, step, 0)
    later()


def up_part(order, normed, bias, ups, downs, block=256):
    length, width = normed.shape
    ff = bias.shape[1]
    pieces = list(ups.arrays) + (list(downs.arrays) if downs is not None else [])
    return call(
        functools.partial(up_kernel, ups, downs, block, order),
        near_in=(0,),
        near_out=(0, 1, 2, 3),
        in_specs=[NEAR, NEAR] + [AWAY] * len(pieces),
        out_specs=[NEAR] * 4,
        out_shape=[shape((width, ff)), shape((ff, width)), shape((length, ff)), shape((length, ff), F32)],
        scratch_shapes=[pltpu.SemaphoreType.DMA((len(ups.arrays),)), pltpu.SemaphoreType.DMA((len((downs or ups).arrays),))],
        compiler_params=vmem(12),
        cost_estimate=cost(2 * length * width * ff, 8 * width * ff, 2 * length * ff),
        name="up_part",
    )(normed, bias, *pieces)


def mlp_back_kernel(first, at, block, n_grads, hidden_ref, slope_ref, up_ref, down_ref, *refs):
    grads, refs = refs[:n_grads], refs[n_grads:]
    if not first:
        refs = refs[2:]
    pre_ref, grad_ref, keep_ref, send_ref, branch_keep, branch_send, sum_ref, sems = refs
    count = 2 * keep_ref.shape[0]
    half = count // n_grads
    spots = [pl.ds(at * count + i * half, half) for i in range(n_grads)]
    ready = fetch([(ref, grad_ref.at[spot, :]) for ref, spot in zip(grads, spots)], sems)
    rows = pl.ds(at * count, count)
    side = keep_ref.shape[0]
    sides = ((0, keep_ref, branch_keep), (side, send_ref, branch_send))
    for start, _, branch_out in sides:
        branch_out[...] = dot(hidden_ref[pl.ds(at * count + start, side), :], down_ref[...], NN).astype(BF16)
    ready()

    def step(i, carry):
        cols = pl.ds(pl.multiple_of(i * block, block), block)
        grad = (slope_ref[rows, cols] * dot(grad_ref[rows, :], down_ref[cols, :], NT)).astype(BF16)
        pre_ref[rows, cols] = grad
        sum_ref[:, cols] = jnp.sum(grad.astype(F32), axis=0, keepdims=True)
        return carry

    lax.fori_loop(0, up_ref.shape[1] // block, step, 0)
    for start, back_out, _ in sides:
        back_out[...] = dot(pre_ref[pl.ds(at * count + start, side), :], up_ref[...], NT).astype(BF16)


def mlp_back(at, hidden, slope, up, down, grads, earlier, block=512):
    width = up.shape[0]
    length, ff = hidden.shape
    count = length // HALVES
    first = earlier is None
    given = 4 + len(grads)
    return call(
        functools.partial(mlp_back_kernel, first, at, min(block, ff // 2), len(grads)),
        near_in=(0, 1, 2, 3, given, given + 1),
        near_out=(0, 1, 2, 3, 4, 5),
        in_specs=[NEAR] * 4 + [AWAY] * len(grads) + ([] if first else [NEAR] * 2),
        out_specs=[NEAR] * 7,
        out_shape=[shape((length, ff)), shape((length, width))]
        + [shape((count // 2, width))] * 4
        + [shape((1, ff), F32)],
        scratch_shapes=[pltpu.SemaphoreType.DMA((len(grads),))],
        input_output_aliases={} if first else {given: 0, given + 1: 1},
        compiler_params=vmem(16),
        cost_estimate=cost(6 * count * width * ff, 8 * width * ff),
        name="mlp_back",
    )(hidden, slope, up, down, *grads, *([] if first else earlier))


def second_back_kernel(at, middle_ref, keep_ref, near_ref, far_ref, vec_ref, out_ref, grad_ref, one_ref, sum_ref, held, sems):
    half = far_ref.shape[0]
    ready = fetch([(out_ref, held)], sems)
    upstream = keep_ref[:half, :].astype(F32) + near_ref[:half, :].astype(F32) + far_ref[...].astype(F32)
    xhat, rate = standardise(middle_ref[at * half : (at + 1) * half, :])
    back = norm_back(upstream, xhat, rate, vec_ref[4:5, :])
    ready()
    grad_out = held[...].astype(F32)
    grad = grad_out + back
    one = grad.astype(BF16)
    grad_ref[...] = grad
    one_ref[...] = one
    sums = [upstream * xhat, upstream, one.astype(F32), grad_out, grad]
    sum_ref[...] = jnp.concatenate([jnp.sum(s, axis=0, keepdims=True) for s in sums], axis=0)


def second_back(at, middle_own, keep, near_part, far_part, grad_out, vecs):
    half, width = far_part.shape
    return call(
        functools.partial(second_back_kernel, at),
        near_in=(0, 1, 2, 3, 4),
        near_out=(0, 1),
        in_specs=[NEAR] * 5 + [AWAY],
        out_specs=[NEAR] * 3,
        out_shape=[shape((half, width), F32), shape((half, width)), shape((5, width), F32)],
        scratch_shapes=[pltpu.VMEM((half, width), BF16), pltpu.SemaphoreType.DMA((1,))],
        compiler_params=vmem(10),
        cost_estimate=cost(30 * half * width, 16 * half * width),
        name="second_back",
    )(middle_own, keep, near_part, far_part, vecs, grad_out)


def first_grad_kernel(n_seq, grad_ref, qkv_ref, vec_ref, *refs):
    tokens, (keep_ref, send_ref, sum_ref, last_ref) = refs[:n_seq], refs[n_seq:]
    step = pl.program_id(0)
    grad = grad_ref[...]
    total = dot(grad, qkv_ref[...], NT)
    column = jnp.sum(grad.astype(F32), axis=0, keepdims=True)
    sides = zip(tokens[: n_seq // 2], tokens[n_seq // 2 :])
    start = jnp.concatenate([jnp.where(step % 2 == 0, a[...], b[...]) for a, b in sides], axis=0).astype(F32)
    xhat, rate = standardise(start + vec_ref[0:1, :])
    back = norm_back(total, xhat, rate, vec_ref[1:2, :])
    last = jnp.concatenate([jnp.sum(t, axis=0, keepdims=True) for t in (total * xhat, total, back)], axis=0)
    total = total.astype(BF16)

    @pl.when(step == 0)
    def _():
        sum_ref[...] = column
        last_ref[...] = last

    @pl.when(step > 0)
    def _():
        sum_ref[...] += column
        last_ref[...] += last

    @pl.when(step % 2 == 0)
    def _():
        keep_ref[...] = total

    @pl.when(step % 2 == 1)
    def _():
        send_ref[...] = total


def first_grad(grad_qkv, qkv, vecs, tokens):
    length, wide = grad_qkv.shape
    n_seq = len(tokens)
    half = tokens[0].shape[0] // HALVES
    width = qkv.shape[0]
    block = length // (2 * HALVES)
    kept = pl.BlockSpec((block, width), lambda i: (i // 2, 0))
    return call(
        functools.partial(first_grad_kernel, n_seq),
        near_out=(0, 1),
        grid=(2 * HALVES,),
        in_specs=[
            pl.BlockSpec((block, wide), lambda i: (i, 0)),
            pl.BlockSpec(qkv.shape, lambda i: (0, 0)),
            pl.BlockSpec(vecs.shape, lambda i: (0, 0)),
        ]
        + [pl.BlockSpec((half, width), lambda i: (i // 2, 0))] * n_seq,
        out_specs=[kept, kept, pl.BlockSpec((1, wide), lambda i: (0, 0)), pl.BlockSpec((3, width), lambda i: (0, 0))],
        out_shape=[shape((length // 2, width))] * 2 + [shape((1, wide), F32), shape((3, width), F32)],
        compiler_params=vmem(20),
        cost_estimate=cost(length * wide * width, 4 * length * width),
        name="first_grad",
    )(grad_qkv, qkv, vecs, *tokens)


def out_terms_kernel(pairs, *refs):
    att, out_ref = refs[:pairs], refs[-1]
    total = None
    at = 0
    for ref in refs[pairs:-1]:
        rows = ref.shape[0]
        term = dot(jnp.concatenate([a[at : at + rows, :] for a in att], axis=1), ref[...], TN)
        total = term if total is None else total + term
        at += rows
    n_dp, rows, wide = out_ref.shape
    if wide == total.shape[1]:
        out_ref[...] = total.astype(BF16).reshape(out_ref.shape)
        return
    part = total.shape[0] // n_dp
    for i in range(n_dp):
        for t in range(rows // part):
            piece = total[i * part : (i + 1) * part, t * wide : (t + 1) * wide]
            out_ref[i, t * part : (t + 1) * part, :] = piece.astype(BF16)


def out_terms(att, grads, n_dp, rows):
    length = att[0].shape[0]
    cols = len(att) * att[0].shape[1]
    width = grads[0].shape[1]
    dims = (n_dp, rows, cols * width // (n_dp * rows))
    args = list(att) + list(grads)
    return call(
        functools.partial(out_terms_kernel, len(att)),
        near_out=(0,),
        grid=(1,),
        in_specs=[pl.BlockSpec(a.shape, lambda i: (0, 0)) for a in args],
        out_specs=pl.BlockSpec(dims, lambda i: (0, 0, 0)),
        out_shape=shape(dims),
        compiler_params=vmem(16),
        cost_estimate=cost(2 * length * cols * width, 2 * length * width),
        name="out_terms",
    )(*args)


def first_back_kernel(keep_ref, near_ref, far_a, far_b, a_ref, b_ref, vec_ref, tokens_ref, out_ref, held, made, sems):
    ready = fetch([(tokens_ref, held)], sems)
    half = far_a.shape[0]
    size = keep_ref.shape[0] // HALVES
    copies = []
    for h, (far_ref, grad_ref) in enumerate(((far_a, a_ref), (far_b, b_ref))):
        mine = slice(h * size, h * size + half)
        upstream = keep_ref[mine, :].astype(F32) + near_ref[mine, :].astype(F32) + far_ref[...].astype(F32)
        if h == 0:
            ready()
        rows = slice(h * half, (h + 1) * half)
        xhat, rate = standardise(held[rows, :].astype(F32) + vec_ref[0:1, :])
        grad = grad_ref[...] + norm_back(upstream, xhat, rate, vec_ref[1:2, :])
        made[rows, :] = grad.astype(BF16)
        copy = pltpu.make_async_copy(made.at[pl.ds(h * half, half), :], out_ref.at[pl.ds(h * half, half), :], sems.at[1 + h])
        copy.start()
        copies.append(copy)
    for copy in copies:
        copy.wait()


def first_back(tokens_own, keep, near_part, far_a, far_b, grad_a, grad_b, vecs):
    rows, width = tokens_own.shape
    return call(
        first_back_kernel,
        near_in=range(7),
        in_specs=[NEAR] * 7 + [AWAY],
        out_specs=AWAY,
        out_shape=shape((rows, width)),
        scratch_shapes=[pltpu.VMEM((rows, width), BF16)] * 2 + [pltpu.SemaphoreType.DMA((1 + HALVES,))],
        compiler_params=vmem(10),
        cost_estimate=cost(30 * rows * width, 16 * rows * width),
        name="first_back",
    )(keep, near_part, far_a, far_b, grad_a, grad_b, vecs, tokens_own)


def block_masks(size):
    return [m for m in range(size) if not m & 1] + [m for m in range(size) if m & 1]


def far_bits(size):
    bits, bit = [], 2
    while bit < size:
        bits.append(bit)
        bit *= 2
    return bits


def tied(*values):
    return lax.optimization_barrier(values)


class Line:
    def __init__(self, token):
        self.token = token

    def slot(self, sends=(), work=lambda: (), inputs=(), begin=(), end=()):
        values, begun, inputs, token = tied(
            [s[0] for s in sends], [s[0] for s in begin], list(inputs), self.token
        )
        found = [lax.ppermute(value, s[1], s[2]) for value, s in zip(values, sends)]
        started = [lax.ppermute(value, s[1], s[2]) for value, s in zip(begun, begin)]
        found, done, ended, self.token = tied(found, work(*inputs), list(end), token)
        return found, done, started, ended


def swap(value, bit, size):
    return (value, "seq", [(i, i ^ bit) for i in range(size)])


def cycle(n_dp):
    wide = int(round(math.sqrt(n_dp / 2)))
    if wide < 2 or wide * (n_dp // wide) != n_dp or (n_dp // wide) % 2:
        return list(range(n_dp))
    high = n_dp // wide
    order = [z * wide for z in range(high)]
    for turn, z in enumerate(range(high - 1, -1, -1)):
        line = list(range(1, wide))
        order += [z * wide + y for y in (line[::-1] if turn % 2 else line)]
    return order


class Ring:
    def __init__(self, n_dp):
        self.n = n_dp
        order = cycle(n_dp)
        where = np.argsort(np.array(order))
        table = np.array([[order[(where[d] + k) % n_dp] for k in range(n_dp)] for d in range(n_dp)], np.int32)
        row = lax.dynamic_index_in_dim(jnp.asarray(table), lax.axis_index("dp"), 0, keepdims=False)
        self.order = row
        self.steps = Order(order)
        self.ahead = [(order[i], order[(i + 1) % n_dp]) for i in range(n_dp)]
        self.back = [(order[i], order[(i - 1) % n_dp]) for i in range(n_dp)]
        self.far = n_dp // 2
        self.near = (n_dp - 1) // 2


class Gather:
    def __init__(self, ring, own):
        self.ring = ring
        self.step = 0
        self.pending = None
        self.ahead = self.back = own
        self.pieces = [own] + [None] * (ring.n - 1)

    def sends(self):
        self.step += 1
        ahead, back = self.ahead, self.back
        if self.step == self.ring.far:
            half = ahead.shape[0] // 2
            ahead, back = ahead[:half], back[half:]
        return [(ahead, "dp", self.ring.ahead), (back, "dp", self.ring.back)]

    def take(self, found):
        self.ahead, self.back = found
        if self.step == self.ring.far:
            self.pieces[self.step] = tuple(found)
        else:
            self.pieces[-self.step], self.pieces[self.step] = found

    @property
    def left(self):
        return self.ring.far - self.step


def ring_kernel(adds, *refs):
    count = len(adds)
    values = list(refs[1 + count : -count])
    for i, (add, out) in enumerate(zip(adds, refs[-count:])):
        total = refs[1 + i][0].astype(F32)
        for _ in range(add):
            total = total + values.pop(0)[...].astype(F32)
        out[...] = total.astype(out.dtype)


def ring_blocks(order, items, dtype=BF16):
    n_dp = order.shape[0]
    args, in_specs, outs, out_specs = [], [], [], []
    for terms, k, _ in items:
        dims = terms.shape[1:]
        in_specs.append(pl.BlockSpec((1,) + dims, lambda i, at, k=k % n_dp: (at[k], 0, 0)))
        out_specs.append(pl.BlockSpec(dims, lambda i, at: (0, 0)))
        outs.append(shape(dims, dtype))
        args.append(terms)
    for _, _, values in items:
        for value in values:
            in_specs.append(pl.BlockSpec(value.shape, lambda i, at: (0, 0)))
            args.append(value)
    return pl.pallas_call(
        functools.partial(ring_kernel, [len(i[2]) for i in items]),
        grid_spec=pltpu.PrefetchScalarGridSpec(
            num_scalar_prefetch=1, grid=(1,), in_specs=in_specs, out_specs=out_specs
        ),
        out_shape=outs,
        compiler_params=vmem(16),
        name="ring_blocks",
    )(order, *args)


def table_kernel(me_ref, lead_ref, a_ref, b_ref, last_ref, ua_ref, ub_ref, column_ref, out_ref):
    me = me_ref[0]
    width = out_ref.shape[1]
    cols = column_ref.shape[1] // 3
    extra = ua_ref.shape[1] * (width // cols) // width
    part = 128 // extra
    sums = a_ref[...] + b_ref[...]
    last = last_ref[...]
    column = column_ref[...]
    out_ref[...] = jnp.zeros_like(out_ref)
    out_ref[0:2, :] = last[0:2]
    mine = pl.ds(pl.multiple_of(me * cols, 128), cols)
    out_ref[2:3, mine] = column[:, :cols]
    out_ref[3:4, mine] = column[:, 2 * cols :]
    out_ref[4:5, :] = sums[2:3]
    out_ref[5:7, :] = sums[0:2]
    out_ref[7:8, :] = sums[3:4]
    start = last[2:3] + sums[4:5]
    out_ref[8:9, :] = lead_ref[0:1, 0:1] * start
    out_ref[9:10, :] = start
    up = jnp.broadcast_to(ua_ref[...] + ub_ref[...], (8, width))
    here = lax.broadcasted_iota(jnp.int32, (1, width), 1) % 128 // part == me
    for k in range(extra):
        moved = pltpu.roll(up, ((me - k) * part + width) % width, 1)
        out_ref[10 + k : 11 + k, :] = jnp.where(here, moved[0:1, :], 0.0)


def small_table(me, lead, *args):
    width = args[0].shape[1]
    return pl.pallas_call(
        functools.partial(table_kernel, ME),
        grid=(1,),
        in_specs=[pl.BlockSpec(a.shape, lambda i: (0, 0)) for a in (lead, *args)],
        out_specs=pl.BlockSpec((16, width), lambda i: (0, 0)),
        out_shape=shape((16, width), F32),
        compiler_params=vmem(4),
        name="small_table",
    )(lead, *args)


def halve_kernel(bit, *refs):
    mine_ref, other_ref = refs[-2:]
    wide = mine_ref.shape[1]
    side = lax.rem(lax.div(lax.axis_index("dp"), bit), 2)
    for at, target in ((side, mine_ref), (1 - side, other_ref)):
        total = 0.0
        for ref in refs[:-2]:
            total = total + ref[:, pl.ds(pl.multiple_of(at * wide, 128), wide)]
        target[...] = total


def halve(bit, values):
    rows, wide = values[0].shape
    return pl.pallas_call(
        functools.partial(halve_kernel, bit),
        in_specs=[NEAR] * len(values),
        out_specs=[NEAR] * 2,
        out_shape=[shape((rows, wide // 2), F32)] * 2,
        compiler_params=vmem(2),
        name="halve",
    )(*values)


def owner_kernel(count, order_ref, me_ref, term_ref, *refs):
    part = refs[-1].shape[0]
    outs = refs[-count:]
    for mask, out in enumerate(outs):
        rows = pl.ds(pl.multiple_of((me_ref[0] ^ mask) * part, part), part)
        total = term_ref[0, rows, :].astype(F32)
        for ref in refs[:-count]:
            total = total + ref[rows, :].astype(F32)
        out[...] = total.astype(BF16)


def owner_blocks(order, me, terms, values, n_seq):
    _, rows, wide = terms.shape
    part = rows // n_seq
    if part % 16:
        (total,) = ring_blocks(order, [(terms, 0, values)])
        blocks = total.reshape(n_seq, part, wide)
        return [lax.dynamic_index_in_dim(blocks, me[0] ^ m, 0, keepdims=False) for m in range(n_seq)]
    return pl.pallas_call(
        functools.partial(owner_kernel, n_seq),
        grid_spec=pltpu.PrefetchScalarGridSpec(
            num_scalar_prefetch=2,
            grid=(1,),
            in_specs=[pl.BlockSpec((1, rows, wide), lambda i, at, me: (at[0], 0, 0))]
            + [pl.BlockSpec((rows, wide), lambda i, at, me: (0, 0))] * len(values),
            out_specs=[pl.BlockSpec((part, wide), lambda i, at, me: (0, 0))] * n_seq,
        ),
        out_shape=[shape((part, wide))] * n_seq,
        compiler_params=vmem(8),
        name="owner_blocks",
    )(order, me, terms, *values)


def unpack_kernel(groups, me_ref, out_ref, *refs):
    outs, last_ref = refs[-len(groups) - 1 : -1], refs[-1]
    pieces = refs[: -len(groups) - 1]
    part = last_ref.shape[0]
    cols = out_ref.shape[1]
    for t in range(out_ref.shape[0] // part):
        last_ref[:, t * cols : (t + 1) * cols] = out_ref[t * part : (t + 1) * part, :].astype(F32)
    n_seq = len(pieces)
    for mask, ref in enumerate(pieces):
        at = 0
        for count, out in zip(groups, outs):
            wide = out.shape[1] // (count * n_seq)
            for i in range(count):
                start = pl.multiple_of((i * n_seq + (me_ref[0] ^ mask)) * wide, 128)
                out[:, pl.ds(start, wide)] = ref[:, at : at + wide].astype(F32)
                at += wide


def unpack(groups, widths, pieces, out_block):
    part = pieces[0].shape[0]
    n_seq = len(pieces)
    if any((wide // n_seq // count) % 128 for count, wide in zip(groups, widths)):
        whole = flipped(dict(enumerate(pieces)), n_seq)
        outs, at = [], 0
        for count, wide in zip(groups, widths):
            mine = whole[:, :, at : at + wide // n_seq].reshape(n_seq, part, count, -1)
            outs.append(jnp.moveaxis(mine, 0, 2).reshape(part, wide).astype(F32))
            at += wide // n_seq
        last = out_block.reshape(-1, part, out_block.shape[1])
        return *outs, jnp.moveaxis(last, 0, 1).reshape(part, -1).astype(F32)
    full = list(widths) + [out_block.size // part]
    return pl.pallas_call(
        functools.partial(unpack_kernel, groups, ME),
        grid=(1,),
        in_specs=[pl.BlockSpec(out_block.shape, lambda i: (0, 0))]
        + [pl.BlockSpec(pieces[0].shape, lambda i: (0, 0))] * n_seq,
        out_specs=[pl.BlockSpec((part, wide), lambda i: (0, 0)) for wide in full],
        out_shape=[shape((part, wide), F32) for wide in full],
        compiler_params=vmem(8),
        name="unpack",
    )(out_block, *pieces)


class Scatter:
    def __init__(self, ring, terms):
        self.ring = ring
        self.terms = terms
        self.step = 0
        self.pending = None
        count = len(terms)
        found = ring_blocks(
            ring.order, [(t, ring.far, ()) for t in terms] + [(t, -ring.near, ()) for t in terms]
        )
        self.ahead, self.back = found[:count], found[count:]

    def sends(self):
        self.step += 1
        found = [(v, "dp", self.ring.ahead) for v in self.ahead]
        if self.step > self.ring.far - self.ring.near:
            found += [(v, "dp", self.ring.back) for v in self.back]
        return found

    def take(self, found):
        count = len(self.terms)
        left = self.ring.far - self.step
        ahead, back = found[:count], found[count:]
        if left:
            items = [(t, left, (v,)) for t, v in zip(self.terms, ahead)]
            items += [(t, -left, (v,)) for t, v in zip(self.terms, back)]
            found = ring_blocks(self.ring.order, items)
            ahead, back = found[:count], found[count:]
        self.ahead = ahead
        if back:
            self.back = back

    @property
    def left(self):
        return self.ring.far - self.step

    def total(self, dtype=F32):
        items = [(t, 0, (a, b)) for t, a, b in zip(self.terms, self.ahead, self.back)]
        return ring_blocks(self.ring.order, items, dtype)


def joint_kernel(items, order_ref, q_ref, o_ref, *refs):
    values, outs = list(refs[: -len(items)]), refs[-len(items) :]
    _, rows, edge = q_ref.shape
    _, part, width = o_ref.shape
    for (k, low, high, added), target in zip(items, outs):
        cols = target.shape[1] - edge
        value = values.pop(0) if added else None
        at = order_ref[k]

        def put(source, from_rows, row, lanes):
            cuts = sorted({row, row + len(from_rows)} | ({max(row, min(c, row + len(from_rows))) for c in added} if added else set()))
            for a, b in zip(cuts, cuts[1:]):
                total = source[from_rows[a - row] : from_rows[b - row - 1] + 1]
                if added and added[0] <= a and b <= added[1]:
                    total = (total.astype(F32) + value[a - added[0] : b - added[0], lanes].astype(F32)).astype(BF16)
                target[a - low : b - low, lanes] = total

        put(q_ref.at[at, :, slice(0, edge)], range(low, high), low, slice(0, edge))
        for t in range(rows // part):
            a, b = max(low, t * part), min(high, (t + 1) * part)
            if a < b:
                lanes = slice(t * cols, (t + 1) * cols)
                put(o_ref.at[at, :, lanes], range(a - t * part, b - t * part), a, slice(edge, edge + cols))


class JointScatter:
    def __init__(self, ring, qkv, out):
        self.ring = ring
        self.qkv = qkv
        self.out = out
        self.step = 0
        self.pending = None
        rows = qkv.shape[1]
        if ring.far:
            far = ring.far
            self.ahead, self.back = self.blocks([(far, 0, rows // 2, None), (far, rows // 2, rows, None)], ())

    def blocks(self, items, values):
        n_dp, rows, edge = self.qkv.shape
        _, part, width = self.out.shape
        wide = edge + width * part // rows
        items = [(k % n_dp, low, high, added) for k, low, high, added in items]
        return call(
            functools.partial(joint_kernel, items, self.ring.steps),
            near_in=range(2 + len(values)),
            near_out=range(len(items)),
            in_specs=[NEAR] * (2 + len(values)),
            out_specs=[NEAR] * len(items),
            out_shape=[shape((high - low, wide)) for _, low, high, _ in items],
            compiler_params=vmem(4),
            name="joint_blocks",
        )(self.qkv, self.out, *values)

    def sends(self):
        self.step += 1
        return [(self.ahead, "dp", self.ring.ahead), (self.back, "dp", self.ring.back)]

    def take(self, found):
        left = self.ring.far - self.step
        rows = self.qkv.shape[1]
        if left:
            spans = ((0, rows // 2), (rows // 2, rows)) if self.step == 1 else ((0, rows), (0, rows))
            found = self.blocks([(sign * left, 0, rows, span) for sign, span in zip((1, -1), spans)], found)
        self.ahead, self.back = found

    @property
    def left(self):
        return self.ring.far - self.step

    def total(self, me, n_seq, dtype=BF16, beside=()):
        n_dp, rows, edge = self.qkv.shape
        _, part, width = self.out.shape
        wide = edge + width * part // rows
        values = [self.ahead, self.back]
        if self.ring.far == 1:
            values = [jnp.concatenate(values, axis=0)] * 2
            values[1] = jnp.zeros_like(values[1])
        cuts = 1 if rows // n_seq % 16 else n_seq
        more = list(beside) if cuts > 1 else []
        full = edge + (more[0].shape[1] if more else 0)
        args = [self.qkv, self.out] + values + more
        found = call(
            functools.partial(joint_owner_kernel, cuts, edge, ME),
            near_in=range(len(args)),
            near_out=range(cuts + 1),
            in_specs=[NEAR] * len(args),
            out_specs=[NEAR] * (cuts + 1),
            out_shape=[shape((rows // cuts, full))] * cuts + [shape((part, width), dtype)],
            compiler_params=vmem(8),
            name="joint_owner",
        )(*args)
        if cuts == n_seq:
            return list(found[:n_seq]), found[n_seq]
        blocks = found[0].reshape(n_seq, rows // n_seq, edge)
        blocks = [lax.dynamic_index_in_dim(blocks, me[0] ^ m, 0, keepdims=False) for m in range(n_seq)]
        return beside_all(blocks, beside), found[1]


def beside_all(blocks, beside):
    return [jnp.concatenate(pair, axis=1) for pair in zip(blocks, beside)] if beside else blocks


def joint_owner_kernel(cuts, edge, me_ref, q_ref, o_ref, *refs):
    values, outs = refs[: -cuts - 1], refs[-cuts - 1 :]
    values, more = values[:2], values[2:]
    part = outs[0].shape[0]
    for mask, target in enumerate(outs[:-1]):
        rows = pl.ds(pl.multiple_of((me_ref[0] ^ mask) * part, part), part) if cuts > 1 else slice(None)
        total = q_ref[lax.axis_index("dp"), rows, :].astype(F32)
        for ref in values:
            total = total + ref[rows, :edge].astype(F32)
        target[:, :edge] = total.astype(BF16)
        if more:
            target[:, edge:] = more[mask][...]
    part, width = outs[-1].shape
    cols = values[0].shape[1] - edge
    for t in range(width // cols):
        total = o_ref[lax.axis_index("dp"), :, t * cols : (t + 1) * cols].astype(F32)
        for ref in values:
            total = total + ref[t * part : (t + 1) * part, edge:].astype(F32)
        outs[-1][:, t * cols : (t + 1) * cols] = total.astype(outs[-1].dtype)


class ApartScatter(Scatter):
    def __init__(self, ring, qkv, out):
        super().__init__(ring, [qkv, out])

    def total(self, me, n_seq, dtype=BF16, beside=()):
        qkv, out = self.terms
        blocks = owner_blocks(self.ring.order, me, qkv, (self.ahead[0], self.back[0]), n_seq)
        (out_sum,) = ring_blocks(self.ring.order, [(out, 0, (self.ahead[1], self.back[1]))])
        return beside_all(blocks, beside), out_sum


def flipped(pieces, bits):
    me = lax.axis_index("seq")
    size = len(pieces)
    held = [pieces[m] for m in range(size)]
    bit = 1
    while bit < size:
        turned = (me & bit) != 0
        held = [jnp.where(turned, held[m ^ bit], held[m]) for m in range(size)]
        bit *= 2
    return jnp.stack(held)


def make_body(n_dp, n_seq):
    masks = block_masks(n_seq)
    far = far_bits(n_seq)
    far_masks = [m for m in range(n_seq) if not m & 1]

    def body(
        tokens,
        lead_hours,
        valid_counts,
        patch_mask,
        first_gain,
        first_shift,
        qkv_weight,
        query_bias,
        value_bias,
        out_weight,
        out_bias,
        second_gain,
        second_shift,
        up_weight,
        up_bias,
        down_weight,
        down_bias,
        lead_weight,
        lead_bias,
        cotangent,
    ):
        me = lax.axis_index("seq")
        rows, width = tokens.shape[1], tokens.shape[2]
        length = rows * n_seq
        half = rows // HALVES
        part = qkv_weight.shape[0]
        ff_part = down_weight.shape[0]
        ff = up_weight.shape[1]
        extra = ff_part // part
        cols = width // n_seq
        ff_cols = ff // n_seq
        lead = lead_hours[0].astype(F32) / 100.0
        count = valid_counts[0]
        positions = me * rows + jnp.arange(rows, dtype=jnp.int32)
        loss_weight = (patch_mask[0] * (positions < count).astype(jnp.int32)).astype(BF16)
        ring = Ring(n_dp)
        me_ref = me.reshape(1).astype(jnp.int32)
        lead_ref = jnp.broadcast_to(lead, (8, 128))
        order = ring.steps

        def far_gather(own, at_bit):
            return [swap(own[m], far[at_bit], n_seq) for m in sorted(own)]

        line = Line(me_ref)

        def run(sends=(), work=lambda: (), inputs=(), start=(), finish=(), begin=(), end=()):
            sends, begin, end = list(sends), list(begin), list(end)
            plan = []
            for ring_part in finish:
                if ring_part.pending is not None:
                    plan.append((ring_part, "end", len(end), len(ring_part.pending)))
                    end += ring_part.pending
                    ring_part.pending = None
            n_sends, n_begin = len(sends), len(begin)
            ahead = []
            for ring_part in start:
                mine = ring_part.sends()
                if ring_part in finish:
                    plan.append((ring_part, "now", len(ahead), len(mine)))
                    ahead += mine
                else:
                    plan.append((ring_part, "later", len(begin), len(mine)))
                    begin += mine
            found, done, begun, ended = line.slot(ahead + sends, work, inputs, begin, end)
            early, found = found[: len(ahead)], found[len(ahead) :]
            n_end = len(end) - sum(p[3] for p in plan if p[1] == "end")
            for ring_part, kind, at, size in plan:
                if kind == "end":
                    ring_part.take(list(ended[at : at + size]))
                elif kind == "now":
                    ring_part.take(list(early[at : at + size]))
                else:
                    ring_part.pending = list(begun[at : at + size])
            return list(found[:n_sends]), done, list(begun[:n_begin]), list(ended[:n_end])

        def near_all(held):
            return [swap(held[m], 1, n_seq) for m in sorted(held)]

        def with_near(held, found):
            held.update({m ^ 1: v for m, v in zip(sorted(held), found)})

        def with_far(held, found, at_bit):
            held.update({m ^ far[at_bit]: v for m, v in zip(sorted(held), found)})

        def rest_far(held):
            for i in range(1, len(far)):
                found, _, _, _ = line.slot(far_gather(held, i))
                with_far(held, found, i)

        vectors = [
            first_gain,
            first_shift,
            query_bias,
            value_bias,
            out_bias,
            second_gain,
            second_shift,
            down_bias,
            lead_weight,
            lead_bias,
            up_bias,
        ]
        kinds = 10 + extra
        packed = pack(n_dp, n_seq, me_ref, qkv_weight, up_weight, vectors)
        found, outs_own, _, _ = run(
            [swap(packed[m], m, n_seq) for m in range(1, n_seq)],
            lambda c, w: tuple(c[h * half : (h + 1) * half] * w[h * half : (h + 1) * half, None] for h in range(HALVES)),
            (cotangent[0], loss_weight),
        )
        one_own = join_one(n_seq, me_ref, [packed[0]] + list(found), out_weight)

        g_one = Gather(ring, one_own)

        def steps(*rings):
            mine = [g for g in rings if g.left]
            return dict(start=mine, finish=mine)

        tokens_held = {0: tokens[0]}
        grad_held = [{0: g} for g in outs_own]
        found, _, _, _ = run([swap(packed[n_seq + m], m, n_seq) for m in range(1, n_seq)], **steps(g_one))
        up_found = [packed[n_seq]] + list(found)
        _, (two_own,), tokens_far, _ = run(
            work=lambda *a: (join_two(n_seq, me_ref, a[:-1], a[-1]),),
            inputs=(*up_found, down_weight),
            begin=far_gather(tokens_held, 0),
            **steps(g_one),
        )
        g_two = Gather(ring, two_own)
        _, _, _, tokens_far = run(end=tokens_far, **steps(g_one))
        with_far(tokens_held, tokens_far, 0)
        rest_far(tokens_held)
        while g_one.left > 1:
            run(**steps(g_one))
        found, _, _, _ = run(near_all(tokens_held), **steps(g_one))
        with_near(tokens_held, found)

        valid = jnp.broadcast_to(count, (8, 128))
        pairs = cols // PAIR

        def begun(part_of):
            return dict(start=[part_of] if part_of.left else [])

        tokens_by = [tokens_held[m] for m in masks]
        ones_blocks = ordered(ring.order, g_one.pieces)

        def attend_first(*a):
            blocks = Blocks(a[n_seq:], ones_blocks.spots, ones_blocks.rows)
            out_pack = middle_columns(blocks, 3 * cols, cols, n_dp)
            found = project(me_ref, order, lead_ref, a[:n_seq], blocks, kinds)
            return out_pack, found

        _, (out_pack, (normed, q, k, v, qkv, table, vecs)), _, _ = run(
            work=attend_first, inputs=tokens_by + list(ones_blocks.arrays), **steps(g_two)
        )
        out_held = {0: out_pack}

        def up_bias_of(table):
            u_bias = table[10 : 10 + extra].reshape(extra, n_dp, n_seq, part)
            u_bias = lax.dynamic_index_in_dim(u_bias, me, 2, keepdims=False)
            return jnp.swapaxes(u_bias, 0, 1).reshape(1, ff_cols)

        def attend_rest(q, k, v, table):
            lses, attended = [], None
            for p in range(pairs):
                attended, lse = attend(n_seq, p, me_ref, valid, q, k, v, attended)
                lses.append(lse)
            return attended, jnp.concatenate(lses, axis=0), up_bias_of(table)

        found, (attended, lse, u_bias), _, _ = run(
            far_gather(out_held, 0), work=attend_rest, inputs=(q, k, v, table), **steps(g_two)
        )
        with_far(out_held, found, 0)
        rest_far(out_held)
        att_held = {0: attended}
        nearby = near_all(out_held)
        found, _, _, _ = run(far_gather(att_held, 0) + nearby, **steps(g_two))
        with_near(out_held, found[-len(nearby) :])
        with_far(att_held, found[: -len(nearby)], 0)
        rest_far(att_held)
        found, _, _, _ = run(near_all(att_held))
        with_near(att_held, found)

        def out_whole(pieces):
            if part % 16 == 0:
                return pieces
            blocks = flipped(dict(enumerate(pieces)), n_seq).reshape(n_seq, n_dp, n_seq, part, cols)
            return [jnp.transpose(blocks, (1, 0, 3, 2, 4)).reshape(width, width)]

        found, (normed_two, middle_own, out_mine), _, _ = run(
            far_gather(grad_held[0], 0),
            work=lambda tok, att, outs, vecs: middle_norm(me_ref, order, tok, att, out_whole(outs), vecs),
            inputs=(
                tokens_by,
                [att_held[m] for m in masks],
                [out_held[m] for m in range(n_seq)],
                vecs,
            ),
            **steps(g_two),
        )
        with_far(grad_held[0], found, 0)
        rest_far(grad_held[0])
        while g_two.left:
            run(**steps(g_two))
        twos = ordered(ring.order, g_two.pieces)
        downs = twos
        if twos.spots[0] is None:
            whole = twos.arrays[0]
            twos = Blocks([whole[:, :ff_cols]], [None], whole.shape[0])
            downs = Blocks([whole[:, ff_cols:].reshape(ff_cols, width)], [None], ff_cols)
        nearby = near_all(grad_held[0])
        found, (up, down, hidden, slope), _, _ = run(
            far_gather(grad_held[1], 0) + nearby,
            work=lambda n, b, a, d: up_part(
                order,
                n,
                b,
                Blocks(a, twos.spots, twos.rows),
                Blocks(d, downs.spots, downs.rows) if downs is not twos else None,
            ),
            inputs=(normed_two, u_bias, list(twos.arrays), list(downs.arrays) if downs is not twos else ()),
        )
        with_near(grad_held[0], found[-len(nearby) :])
        with_far(grad_held[1], found[: -len(nearby)], 0)
        rest_far(grad_held[1])

        def half_sum(keep, other):
            found = {}
            for at, m in enumerate(far_masks):
                if m:
                    rows_at = slice(at * half, (at + 1) * half)
                    found[m] = (keep[rows_at].astype(F32) + other[rows_at].astype(F32)).astype(BF16)
            return found

        def far_first(held):
            bit = far[-1]
            return [swap(held[m], bit, n_seq) for m in sorted(held) if m & bit]

        def far_rest(held, found):
            for at, bit in enumerate(reversed(far)):
                upper = sorted(m for m in held if m & bit)
                if at:
                    found, _, _, _ = line.slot([swap(held[m], bit, n_seq) for m in upper])
                kept = {m: held[m] for m in held if not m & bit}
                for m, value in zip(upper, found):
                    low = m ^ bit
                    if low in kept:
                        value = (kept[low].astype(F32) + value.astype(F32)).astype(BF16)
                    kept[low] = value
                held = kept
            return held[0]

        found, (pre, grad_out, keep_a, send_a, branch_keep_a, branch_send_a, sum_a), _, _ = run(
            near_all(grad_held[1]),
            work=lambda *a: mlp_back(0, *a, None),
            inputs=(hidden, slope, up, down, [grad_held[0][m] for m in masks]),
        )
        with_near(grad_held[1], found)
        (near_a,), (pre, grad_out, keep_b, send_b, branch_keep_b, branch_send_b, sum_b), _, _ = run(
            [swap(send_a, 1, n_seq)],
            work=lambda *a: mlp_back(1, *a),
            inputs=(hidden, slope, up, down, [grad_held[1][m] for m in masks], (pre, grad_out)),
        )
        def moved(value, axis, bit):
            count = n_dp if axis == "dp" else n_seq
            return lax.ppermute(value, axis, [(i, i ^ bit) for i in range(count)])

        held_a = half_sum(keep_a, near_a)
        sends = far_first(held_a)

        def weight_terms(hidden, grad_out, normed_two, pre):
            up_terms = dot(normed_two, pre, TN).astype(BF16).reshape(n_dp, n_seq * part, ff_cols)
            return dot(hidden, grad_out, TN).astype(BF16).reshape(n_dp, ff_part, width), up_terms

        found, (down_terms, up_terms), _, _ = run(
            sends + [swap(send_b, 1, n_seq)], work=weight_terms, inputs=(hidden, grad_out, normed_two, pre)
        )
        far_a, near_b = far_rest(held_a, found[: len(sends)]), found[-1]
        held_b = half_sum(keep_b, near_b)

        def back_half(at):
            return lambda *a: tuple(second_back(at, *a))

        scatter_two = JointScatter(ring, up_terms, down_terms)
        sends = far_first(held_b)
        found, (grad_mid_a, one_a, sums_a), _, _ = run(
            sends + [swap(branch_send_a, 1, n_seq), swap(branch_send_b, 1, n_seq)],
            work=back_half(0),
            inputs=(middle_own, keep_a, near_a, far_a, outs_own[0], vecs),
            **steps(scatter_two),
        )
        far_b, branch_other = far_rest(held_b, found[: len(sends)]), found[-2:]
        one_far_a, (grad_mid_b, one_b, sums_b), _, _ = run(
            far_gather({0: one_a}, 0),
            work=back_half(1),
            inputs=(middle_own, keep_b, near_b, far_b, outs_own[1], vecs),
            **begun(scatter_two),
        )
        one_held_a = {0: one_a}
        with_far(one_held_a, one_far_a, 0)
        rest_far(one_held_a)
        one_held_b = {0: one_b}
        found, _, one_far_b, _ = run(
            near_all(one_held_a), begin=far_gather(one_held_b, 0), finish=[scatter_two]
        )
        with_near(one_held_a, found)
        _, (dq_a, dk_a, dv_a), _, one_far_b = run(
            work=lambda *a: attend_back(0, me_ref, valid, *a, None),
            inputs=(q, k, v, lse, out_mine, [one_held_a[m] for m in masks]),
            end=one_far_b,
            **begun(scatter_two),
        )
        with_far(one_held_b, one_far_b, 0)
        rest_far(one_held_b)
        found, _, _, _ = run(near_all(one_held_b), finish=[scatter_two])
        with_near(one_held_b, found)
        ones = [one_held_a[m] for m in masks] + [one_held_b[m] for m in masks]

        branch_held = {
            m: jnp.concatenate([value, half_sum(branch_keep_b, branch_other[1])[m]], axis=0)
            for m, value in half_sum(branch_keep_a, branch_other[0]).items()
        }

        def second_attend(q, k, v, lse, out_mine, grads, earlier, att, ones):
            sums = out_terms(att, ones, n_dp, part if part % 16 else n_seq * part)
            return attend_back(1, me_ref, valid, q, k, v, lse, out_mine, grads, earlier), sums

        branch_far, (grad_qkv, out_sums), _, _ = run(
            far_first(branch_held),
            work=second_attend,
            inputs=(
                q,
                k,
                v,
                lse,
                out_mine,
                [one_held_b[m] for m in masks],
                (dq_a, dk_a, dv_a),
                [attended],
                ones,
            ),
            **steps(scatter_two),
        )
        branch_far = far_rest(branch_held, branch_far)

        qkv_terms = dot(normed, grad_qkv, TN).astype(BF16).reshape(n_dp, n_seq * part, 3 * cols)
        scatter_one = (ApartScatter if part % 16 else JointScatter)(ring, qkv_terms, out_sums)
        late = [scatter_two] if scatter_two.left else []

        def far_moved(held):
            if not far:
                return []
            return [moved(held[m], "seq", far[-1]) for m in sorted(held) if m & far[-1]]

        def now(*beside):
            mine = [scatter_one] if scatter_one.left else []
            return dict(start=mine, finish=mine + list(beside))

        def final_rows(keep_a, keep_b, near_a, near_b, far_part, mid, bias):
            total = jnp.concatenate([keep_a[:half], keep_b[:half]], axis=0).astype(F32)
            total = total + jnp.concatenate([near_a[:half], near_b[:half]], axis=0).astype(F32)
            return (mid + (total + far_part.astype(F32) + bias[6:7])).astype(BF16)

        late = [scatter_two] if scatter_two.left else []
        options = now()
        _, (gn_keep, gn_send, column_sums, last_sums), _, _ = run(
            work=first_grad,
            inputs=(grad_qkv, qkv, vecs, tokens_by),
            start=options["start"] + late,
            finish=options["finish"] + late,
        )
        while scatter_two.left:
            run(**steps(scatter_two))
        plain = (width // n_dp) % 128 == 0 and extra == n_seq and n_seq * part == 128

        bits = []
        while 2 ** len(bits) < n_dp:
            bits.append(2 ** len(bits))
        bits = bits[::-1] if plain else []
        at_dp = lax.axis_index("dp")

        def loose_table():
            sums = sums_a + sums_b
            table = last_sums
            start_sums = table[2:3] + sums[4:5]
            q_sum = lax.dynamic_update_slice(jnp.zeros((1, width), F32), column_sums[:, :cols], (0, me * cols))
            v_sum = lax.dynamic_update_slice(jnp.zeros((1, width), F32), column_sums[:, 2 * cols :], (0, me * cols))
            u_sum = jnp.swapaxes((sum_a + sum_b).reshape(n_dp, extra, part), 0, 1)
            u_sum = lax.dynamic_update_index_in_dim(jnp.zeros((extra, n_dp, n_seq, part), F32), u_sum, me, 2)
            rows_out = [table[0:2], q_sum, v_sum, sums[2:3], sums[0:2], sums[3:4], lead * start_sums, start_sums]
            table = jnp.concatenate(rows_out + [u_sum.reshape(extra, width)], axis=0)
            return lax.psum_scatter(table, ("dp", "seq"), scatter_dimension=1, tiled=True)

        seq_bits = far + ([1] if n_seq > 1 else []) if plain else []

        def make_table():
            if not plain:
                return loose_table()
            return small_table(
                me_ref, lead_ref, sums_a, sums_b, last_sums, sum_a, sum_b, column_sums
            )

        def hop(held):
            if bits:
                bit = bits.pop(0)
                mine, other = halve(bit, held)
                return mine, [(other, "dp", [(i, i ^ bit) for i in range(n_dp)])]
            total = sum(held[1:], held[0])
            if seq_bits:
                return total, [swap(total, seq_bits.pop(0), n_seq)]
            return total, []

        def totals():
            blocks, total = scatter_two.total(me_ref, n_seq, F32)
            return *blocks, total

        mine, small = hop([make_table()])
        found, (*up_blocks, down_grad), _, _ = run([swap(gn_send, 1, n_seq)] + small, work=totals, **now())
        gn_near = found[0]
        held = [mine] + found[1:]
        size = half * len(far_masks)
        gn_held_a = half_sum(gn_keep[:size], gn_near[:size])
        mine, small = hop(held)
        sends = far_first(gn_held_a)
        found, (gn_held_b,), _, _ = run(
            sends + small, work=lambda k, n: (half_sum(k[size:], n[size:]),), inputs=(gn_keep, gn_near), **now()
        )
        gn_far_a = far_rest(gn_held_a, found[: len(sends)])
        held = [mine] + found[len(sends) :]
        mine, small = hop(held)
        sends = far_first(gn_held_b)
        found, (block_out,), _, _ = run(
            sends + small,
            work=lambda *a: (final_rows(*a),),
            inputs=(branch_keep_a, branch_keep_b, branch_other[0], branch_other[1], branch_far, middle_own, vecs),
            **now(),
        )
        gn_far_b = far_rest(gn_held_b, found[: len(sends)])
        held = [mine] + found[len(sends) :]
        while scatter_one.left:
            run(**steps(scatter_one))
        qkv_blocks, out_sum = scatter_one.total(me_ref, n_seq, beside=up_blocks)
        moves = []
        for dp_at in range(n_dp):
            for seq_at in range(n_seq):
                moves.append((dp_at * n_seq + seq_at, seq_at * n_dp + dp_at))
        final = [(out_sum, ("dp", "seq"), moves)] + [swap(qkv_blocks[m], m, n_seq) for m in range(1, n_seq)]

        mine, small = hop(held)
        found, (tokens_grad,), _, _ = run(
            final + small,
            work=lambda *a: (first_back(*a),),
            inputs=(tokens[0], gn_keep, gn_near, gn_far_a, gn_far_b, grad_mid_a, grad_mid_b, vecs),
        )
        last, held = found[: len(final)], [mine] + found[len(final) :]
        while bits or seq_bits:
            mine, small = hop(held)
            found, _, _, _ = run(small)
            held = [mine] + found
        small_sums = sum(held[1:], held[0])
        if plain:
            small_sums = lax.dynamic_slice_in_dim(small_sums, me * part, part, 1)
        owned = small_sums[:kinds]
        qkv_weight_grad, up_weight_grad, out_weight_grad = unpack(
            (3, n_dp), (3 * width, ff), [qkv_blocks[0]] + list(last[1:]), last[0]
        )
        return (
            block_out[None],
            tokens_grad[None],
            owned[0],
            owned[1],
            qkv_weight_grad,
            owned[2],
            owned[3],
            out_weight_grad,
            owned[4],
            owned[5],
            owned[6],
            up_weight_grad,
            owned[10 : 10 + extra].reshape(ff_part),
            down_grad[0] if down_grad.ndim == 3 else down_grad,
            owned[7],
            owned[8],
            owned[9],
        )

    return body


def solution(mesh):
    both = P(("dp", "seq"))
    matrix = P(("dp", "seq"), None)
    tokens = P("dp", "seq", None)
    in_specs = (tokens, P("dp"), P("dp"), P("dp", "seq"), both, both, matrix, both, both, matrix, both, both, both)
    in_specs += (matrix, both, matrix, both, both, both, tokens)
    out_specs = (tokens, tokens, both, both, matrix, both, both, matrix, both, both, both, matrix, both, matrix)
    out_specs += (both, both, both)
    return jax.shard_map(
        make_body(mesh.shape["dp"], mesh.shape["seq"]),
        mesh=mesh,
        in_specs=in_specs,
        out_specs=out_specs,
        check_vma=False,
    )
```

```python
import functools
import math

import jax
import jax.numpy as jnp
import numpy as np
from jax import lax
from jax.experimental import pallas as pl
from jax.experimental.pallas import tpu as pltpu
from jax.sharding import PartitionSpec as P

HEADS = 16
HEAD_DIM = 64
PAIR = 2 * HEAD_DIM
SCALE = 1.0 / math.sqrt(HEAD_DIM)
EPSILON = 1e-06
MASKED = -1e30
F32 = jnp.float32
BF16 = jnp.bfloat16
NN, NT, TN = ((1,), (0,)), ((1,), (1,)), ((0,), (0,))
HALVES = 2
MIB = 1024 * 1024
NEAR = pl.BlockSpec(memory_space=pltpu.VMEM)
AWAY = pl.BlockSpec(memory_space=pl.ANY)
NUMBERS = pl.BlockSpec(memory_space=pltpu.SMEM)


def dot(left, right, contract):
    return lax.dot_general(left, right, (contract, ((), ())), preferred_element_type=F32)


def shape(dims, dtype=BF16):
    return jax.ShapeDtypeStruct(dims, dtype)


def call(kernel, *, in_specs, out_shape, near_in=(), near_out=(), **options):
    def large(value):
        return math.prod(value.shape) * value.dtype.itemsize >= 65536

    def run(*args):
        kept = []
        for i, a in enumerate(args):
            if large(a):
                a = pltpu.with_memory_space_constraint(a, pltpu.VMEM if i in near_in else pltpu.HBM)
            kept.append(a)
        single = not isinstance(out_shape, (list, tuple))
        outs = [out_shape] if single else list(out_shape)
        outs = [
            ((pltpu.VMEM if i in near_out else pltpu.HBM)(o.shape, o.dtype) if large(o) else o)
            for i, o in enumerate(outs)
        ]
        return pl.pallas_call(kernel, in_specs=in_specs, out_shape=outs[0] if single else outs, **options)(*kept)

    return run


def away(value):
    return pltpu.with_memory_space_constraint(value, pltpu.HBM)


class Here:
    def __getitem__(self, at):
        return lax.axis_index("seq")


class Order:
    def __init__(self, cycle):
        self.cycle = cycle

    def __getitem__(self, k):
        n = len(self.cycle)
        mine = lax.axis_index("dp")
        spot = sum(jnp.where(mine == place, at, 0) for at, place in enumerate(self.cycle))
        spot = lax.rem(spot + k % n, n)
        return sum(jnp.where(spot == at, place, 0) for at, place in enumerate(self.cycle))


ME = Here()


def near(value):
    return pltpu.with_memory_space_constraint(value, pltpu.VMEM)


def vmem(mib):
    return pltpu.CompilerParams(vmem_limit_bytes=mib * MIB)


def cost(flops, moved, exps=0):
    return pl.CostEstimate(flops=int(flops), bytes_accessed=int(moved), transcendentals=int(exps))


def standardise(values):
    centered = values - jnp.mean(values, axis=-1, keepdims=True)
    rate = lax.rsqrt(jnp.mean(centered * centered, axis=-1, keepdims=True) + EPSILON)
    return centered * rate, rate


def norm_back(upstream, xhat, rate, gain):
    scaled = upstream * gain
    inner = jnp.mean(scaled * xhat, axis=-1, keepdims=True)
    return rate * (scaled - jnp.mean(scaled, axis=-1, keepdims=True) - xhat * inner)


def pack_kernel(n_dp, n_seq, me_ref, qkv_ref, up_ref, *refs):
    vectors, out_refs = refs[: -2 * n_seq], refs[-2 * n_seq :]
    out_refs, up_refs = out_refs[:n_seq], out_refs[n_seq:]
    me = me_ref[0]
    part = qkv_ref.shape[0]
    cols = qkv_ref.shape[1] // (3 * n_seq)
    piece = up_ref.shape[1] // (n_dp * n_seq)
    rows = [ref[...].astype(F32)[:, i : i + part] for ref in vectors for i in range(0, ref.shape[1], part)]
    kinds = len(rows)
    rows = jnp.concatenate(rows + [jnp.zeros((128 - kinds, part), F32)], axis=0)
    rows = jnp.concatenate([rows, jnp.zeros((128, 128 - part), F32)], axis=1)
    small = rows.T[:part, :].astype(BF16)
    for mask, ref in enumerate(out_refs):
        place = me ^ mask
        for i in range(3):
            start = pl.multiple_of((i * n_seq + place) * cols, 128)
            ref[:, i * cols : (i + 1) * cols] = qkv_ref[:, pl.ds(start, cols)]
        at = 3 * cols
        ref[:, at : at + 128] = small
        for i in range(n_dp):
            start = pl.multiple_of((i * n_seq + place) * piece, 128)
            up_refs[mask][:, i * piece : (i + 1) * piece] = up_ref[:, pl.ds(start, piece)]


def pack(n_dp, n_seq, me, qkv, up, vectors):
    part = qkv.shape[0]
    wide = qkv.shape[1] // n_seq + 128
    ff = up.shape[1] // n_seq
    if up.shape[1] // (n_dp * n_seq) % 128 or part % 16:
        small = jnp.concatenate(vectors).reshape(-1, part).T
        small = jnp.pad(small, ((0, 0), (0, 128 - small.shape[1])))
        qkv_split = qkv.reshape(part, 3, n_seq, -1)
        up_split = up.reshape(part, n_dp, n_seq, -1)

        def block(place):
            q = lax.dynamic_index_in_dim(qkv_split, place, 2, keepdims=False).reshape(part, -1)
            u = lax.dynamic_index_in_dim(up_split, place, 2, keepdims=False).reshape(part, -1)
            return jnp.concatenate([q, small], axis=1), u

        blocks = [block(me[0] ^ m) for m in range(n_seq)]
        return [b[0] for b in blocks] + [b[1] for b in blocks]
    args = [qkv, up] + [v.reshape(1, -1) for v in vectors]
    args = [pltpu.with_memory_space_constraint(a, pltpu.HBM) for a in args]
    return pl.pallas_call(
        functools.partial(pack_kernel, n_dp, n_seq, ME),
        grid=(1,),
        in_specs=[pl.BlockSpec(a.shape, lambda i: (0, 0)) for a in args],
        out_specs=[pl.BlockSpec((part, wide), lambda i: (0, 0))] * n_seq
        + [pl.BlockSpec((part, ff), lambda i: (0, 0))] * n_seq,
        out_shape=[shape((part, wide))] * n_seq + [shape((part, ff))] * n_seq,
        compiler_params=vmem(8),
        name="pack",
    )(*args)


def join_one_kernel(n_seq, me_ref, *refs):
    out_ref, left_ref = refs[-2:]
    part, wide = out_ref.shape
    cols = wide // n_seq
    edge = refs[0].shape[1] - 128
    for t, ref in enumerate(refs[:-2]):
        rows = pl.ds(pl.multiple_of((me_ref[0] ^ t) * part, part), part)
        left_ref[rows, :edge] = ref[:, :edge]
        left_ref[rows, edge + cols :] = ref[:, edge:]
        left_ref[t * part : (t + 1) * part, edge : edge + cols] = out_ref[:, t * cols : (t + 1) * cols]


def join_two_kernel(n_seq, me_ref, *refs):
    down_ref, right_ref = refs[-2:]
    half = down_ref.shape[1]
    part = refs[0].shape[0]
    right_ref[:, -half:] = down_ref[...]
    for t, ref in enumerate(refs[:-2]):
        right_ref[pl.ds(pl.multiple_of((me_ref[0] ^ t) * part, part), part), :-half] = ref[...]


def join(kernel, n_seq, me, pieces, weight, wide):
    rows = pieces[0].shape[0] * n_seq
    args = list(pieces) + [away(weight)]
    return pl.pallas_call(
        functools.partial(kernel, n_seq, ME),
        grid=(1,),
        in_specs=[pl.BlockSpec(a.shape, lambda i: (0, 0)) for a in args],
        out_specs=pl.BlockSpec((rows, wide), lambda i: (0, 0)),
        out_shape=shape((rows, wide)),
        compiler_params=vmem(8),
        name="join",
    )(*args)


def join_one(n_seq, me, pieces, out_weight):
    part, edge = pieces[0].shape
    edge -= 128
    cols = out_weight.shape[1] // n_seq
    if part % 16:
        whole = flipped(dict(enumerate(pieces)), n_seq).reshape(part * n_seq, edge + 128)
        beside = jnp.moveaxis(out_weight.reshape(part, n_seq, cols), 1, 0).reshape(part * n_seq, cols)
        return jnp.concatenate([whole[:, :edge], beside, whole[:, edge:]], axis=1)
    return join(join_one_kernel, n_seq, me, pieces, out_weight, edge + cols + 128)


def join_two(n_seq, me, pieces, down_weight):
    part, wide = pieces[0].shape
    rows = part * n_seq
    if part % 16:
        whole = flipped(dict(enumerate(pieces)), n_seq).reshape(rows, wide)
        return jnp.concatenate([whole, down_weight.reshape(rows, -1)], axis=1)
    return join(join_two_kernel, n_seq, me, pieces, down_weight, wide + down_weight.shape[1])


class Blocks:
    def __init__(self, arrays, spots, rows):
        self.arrays = arrays
        self.spots = spots
        self.rows = rows

    def place(self, order_ref, i, source=None):
        k, start = self.spots[i]
        count = self.arrays[i].shape[0]
        if order_ref is None:
            return slice(k * self.rows + start, k * self.rows + start + count)
        return pl.ds(pl.multiple_of(order_ref[k] * self.rows + start, math.gcd(self.rows, start or self.rows)), count)


def ordered(order, pieces):
    rows = pieces[0].shape[0]
    if rows % 128 == 0:
        arrays, spots = [], []
        for k, piece in enumerate(pieces):
            halves = piece if isinstance(piece, tuple) else (piece,)
            for i, half in enumerate(halves):
                arrays.append(half)
                spots.append((k, i * rows // 2))
        return Blocks(arrays, spots, rows)
    whole = jnp.stack([jnp.concatenate(p, axis=0) if isinstance(p, tuple) else p for p in pieces])
    out = whole
    for k in range(len(pieces)):
        out = lax.dynamic_update_index_in_dim(out, whole[k], order[k], 0)
    return Blocks([out.reshape(-1, out.shape[-1])], [None], len(pieces) * rows)


def lay(order_ref, blocks, refs, target, cols=slice(None)):
    for i, ref in enumerate(refs):
        if blocks.spots[i] is None:
            target[...] = ref[:, cols]
        else:
            target[blocks.place(order_ref, i), :] = ref[:, cols]


def middle_columns_kernel(blocks, *refs):
    for i, ref in enumerate(refs[:-1]):
        refs[-1][blocks.place(None, i), :] = ref[...]


def middle_columns(blocks, start, cols, n_dp):
    if blocks.spots[0] is None or start % cols:
        return blocks.arrays[0][:, start : start + cols]
    total = blocks.rows * n_dp
    return call(
        functools.partial(middle_columns_kernel, blocks),
        grid=(1,),
        in_specs=[pl.BlockSpec((a.shape[0], cols), lambda i: (0, start // cols)) for a in blocks.arrays],
        out_specs=pl.BlockSpec((total, cols), lambda i: (0, 0)),
        out_shape=shape((total, cols)),
        compiler_params=vmem(4),
        name="middle_columns",
    )(*blocks.arrays)


def project_kernel(n_seq, blocks, me_ref, order_ref, lead_ref, *refs):
    n_pieces = len(blocks.arrays)
    tokens = refs[:n_seq]
    pieces = refs[n_seq : n_seq + n_pieces]
    normed_ref, q_ref, k_ref, v_ref, qkv_ref, table_ref, vec_ref, small_ref = refs[n_seq + n_pieces :]
    cols = q_ref.shape[1]

    @pl.when(pl.program_id(0) == 0)
    def _():
        lay(order_ref, blocks, pieces, qkv_ref, slice(0, 3 * cols))
        lay(order_ref, blocks, pieces, small_ref, slice(4 * cols, 4 * cols + 128))
        table_ref[...] = small_ref[...].astype(F32).T[: table_ref.shape[0], :]
        for i, kind in enumerate((0, 0, 1, 4, 5, 6, 7, 7)):
            vec_ref[i : i + 1, :] = table_ref[kind : kind + 1, :]
        vec_ref[0:1, :] = lead_ref[0:1, 0:1] * table_ref[8:9, :] + table_ref[9:10, :]

    start = jnp.concatenate([ref[...] for ref in tokens], axis=0).astype(F32) + vec_ref[0:1, :]
    xhat, _ = standardise(start)
    normed = (xhat * vec_ref[1:2, :] + vec_ref[2:3, :]).astype(BF16)
    normed_ref[...] = normed
    mine = pl.ds(pl.multiple_of(me_ref[0] * cols, 128), cols)
    found = dot(normed, qkv_ref[...], NN)
    q_ref[...] = (found[:, :cols] + table_ref[2:3, mine]).astype(BF16)
    k_ref[...] = found[:, cols : 2 * cols].astype(BF16)
    v_ref[...] = (found[:, 2 * cols :] + table_ref[3:4, mine]).astype(BF16)


def project(me, order, lead, tokens, blocks, kinds):
    rows, width = tokens[0].shape
    n_seq = len(tokens)
    cols = width // n_seq
    length = rows * n_seq
    half = rows // HALVES
    count = length // HALVES
    numbers = pl.BlockSpec(memory_space=pltpu.SMEM)

    def whole(dims):
        return pl.BlockSpec(dims, lambda i: (0, 0))

    def step(wide):
        return pl.BlockSpec((count, wide), lambda i: (i, 0))

    return call(
        functools.partial(project_kernel, n_seq, blocks, ME, order),
        near_out=(1, 2, 3),
        grid=(HALVES,),
        in_specs=[whole(lead.shape)]
        + [pl.BlockSpec((half, width), lambda i: (i, 0))] * n_seq
        + [whole(a.shape) for a in blocks.arrays],
        out_specs=[step(width), step(cols), step(cols), step(cols)]
        + [whole((width, 3 * cols)), whole((kinds, width)), whole((8, width))],
        out_shape=[shape((length, width))]
        + [shape((length, cols))] * 3
        + [shape((width, 3 * cols)), shape((kinds, width), F32), shape((8, width), F32)],
        scratch_shapes=[pltpu.VMEM((width, 128), BF16)],
        compiler_params=vmem(28),
        cost_estimate=cost(6 * length * width * cols, 10 * length * width),
        name="project",
    )(lead, *tokens, *blocks.arrays)


def key_bias(n_seq, length, me, count):
    half = length // (n_seq * HALVES)
    parts = []
    for h in range(HALVES):
        for m in block_masks(n_seq):
            at = lax.broadcasted_iota(jnp.int32, (half, 1), 0) + ((me ^ m) * HALVES + h) * half
            parts.append(jnp.where(at < count, 0.0, MASKED).astype(F32))
    return jnp.concatenate(parts, axis=0)


def attend_kernel(n_seq, me_ref, pair_at, count_ref, q_ref, k_ref, v_ref, *refs):
    out_ref, lse_ref = refs[-2:]
    bias = key_bias(n_seq, k_ref.shape[0], me_ref[0], count_ref[0:1, 0:1])
    count = q_ref.shape[0] // 2

    def step(i, carry):
        rows = pl.ds(pl.multiple_of(i * count, count), count)
        for half in range(2):
            cols = slice(half * HEAD_DIM, (half + 1) * HEAD_DIM)
            mine = slice(pair_at * PAIR + cols.start, pair_at * PAIR + cols.stop)
            scores = dot(k_ref[:, mine], q_ref[rows, mine] * SCALE, NT) + bias
            top = jnp.max(scores, axis=0, keepdims=True)
            weights = jnp.exp(scores - top)
            total = jnp.sum(weights, axis=0, keepdims=True)
            mixed = dot(v_ref[:, mine], weights.astype(BF16), TN) / total
            out_ref[rows, cols] = mixed.T.astype(BF16)
            lse_ref[half, :, rows] = top + jnp.log(total)
        return carry

    lax.fori_loop(0, 2, step, 0)


def attend(n_seq, pair_at, me, valid, q, k, v, earlier):
    length, cols = q.shape
    pair = pl.BlockSpec((length, PAIR), lambda g: (0, pair_at))
    given = [] if earlier is None else [earlier]
    return call(
        functools.partial(attend_kernel, n_seq, ME, pair_at),
        near_in=(1, 2, 3),
        grid=(1,),
        in_specs=[pl.BlockSpec(valid.shape, lambda g: (0, 0)), NEAR, NEAR, NEAR] + [AWAY] * len(given),
        out_specs=[pair, pl.BlockSpec((2, 1, length), lambda g: (0, 0, 0))],
        out_shape=[shape((length, cols)), shape((2, 1, length), F32)],
        input_output_aliases={4: 0} if given else {},
        compiler_params=vmem(32),
        cost_estimate=cost(4 * length * length * PAIR, 8 * length * PAIR, 2 * length * length),
        name="attend",
    )(valid, q, k, v, *given)


def attend_back_kernel(first, n_seq, *refs):
    count_ref, q_ref, k_ref, v_ref, lse_ref, out_w_ref = refs[:6]
    grads = refs[6 : 6 + n_seq]
    rest = refs[6 + n_seq :]
    if first:
        dq_ref, dk_ref, dv_ref = rest
    else:
        dq_in, dk_in, dv_in, whole_ref, q_out, k_out, v_out, sems = rest
    length = k_ref.shape[0]
    count = q_ref.shape[0]
    pair = pl.program_id(0)
    spot = pair % 2
    bias = key_bias(n_seq, length, ME[0], count_ref[0:1, 0:1])
    upstream = jnp.concatenate([dot(ref[...], out_w_ref[...], NT).astype(BF16) for ref in grads], axis=0)
    for half in range(2):
        cols = slice(half * HEAD_DIM, (half + 1) * HEAD_DIM)
        k = k_ref[:, cols]
        q = q_ref[:, cols] * SCALE
        g = upstream[:, cols]
        probs = jnp.exp(dot(k, q, NT) + bias - lse_ref[half])
        dv = dot(probs.astype(BF16), g, NN)
        term = probs * dot(v_ref[:, cols], g, NT)
        grad = (term - probs * jnp.sum(term, axis=0, keepdims=True)).astype(BF16)
        dk = dot(grad, q, NN)
        dq = (dot(k, grad, TN) * SCALE).T.astype(BF16)
        if first:
            dq_ref[:, cols] = dq
            dk_ref[:, cols] = dk
            dv_ref[:, cols] = dv
        else:
            q_out[spot, :count, cols] = dq_in[:, cols]
            q_out[spot, count:, cols] = dq
            k_out[spot, :, cols] = (dk + dk_in[:, cols]).astype(BF16)
            v_out[spot, :, cols] = (dv + dv_in[:, cols]).astype(BF16)
    if first:
        return
    pairs = pl.num_programs(0)

    def copies(at):
        found = []
        for i, source in enumerate((q_out, k_out, v_out)):
            start = pl.multiple_of((i * pairs + at) * PAIR, PAIR)
            target = whole_ref.at[:, pl.ds(start, PAIR)]
            found.append(pltpu.make_async_copy(source.at[at % 2], target, sems.at[at % 2, i]))
        return found

    for copy in copies(pair):
        copy.start()

    @pl.when(pair > 0)
    def _():
        for copy in copies(pair - 1):
            copy.wait()

    @pl.when(pair == pairs - 1)
    def _():
        for copy in copies(pair):
            copy.wait()


def attend_back(at, me, valid, q, k, v, lse, out_mine, grads, earlier):
    length, cols = k.shape
    width = out_mine.shape[1]
    count = length // HALVES
    pair = pl.BlockSpec((length, PAIR), lambda g: (0, g))
    mine = pl.BlockSpec((count, PAIR), lambda g: (at, g))
    here = pl.BlockSpec((count, PAIR), lambda g: (0, g))
    first = earlier is None
    near_out = () if first else (0,)
    in_specs = [pl.BlockSpec(valid.shape, lambda g: (0, 0))] + [
        mine,
        pair,
        pair,
        pl.BlockSpec((2, 1, count), lambda g: (g, 0, at)),
        pl.BlockSpec((PAIR, width), lambda g: (g, 0)),
    ]
    in_specs += [pl.BlockSpec(piece.shape, lambda g: (0, 0)) for piece in grads]
    args = [valid, q, k, v, lse, out_mine] + list(grads)
    if first:
        out_specs = [here, pair, pair]
        out_shape = [shape((count, cols))] + [shape((length, cols), F32)] * 2
        scratch = []
    else:
        in_specs += [here, pair, pair]
        args += list(earlier)
        out_specs = AWAY
        out_shape = shape((length, 3 * cols))
        scratch = [pltpu.VMEM((2, length, PAIR), BF16)] * 3 + [pltpu.SemaphoreType.DMA((2, 3))]
    return call(
        functools.partial(attend_back_kernel, first, len(grads)),
        near_in=range(6, 6 + len(grads)),
        near_out=near_out,
        grid=(cols // PAIR,),
        in_specs=in_specs,
        out_specs=out_specs,
        out_shape=out_shape,
        scratch_shapes=scratch,
        compiler_params=vmem(36),
        cost_estimate=cost(10 * count * length * cols, 8 * length * cols, count * length * cols // HEAD_DIM),
        name="attend_back",
    )(*args)


def middle_kernel(n_seq, n_out, me_ref, order_ref, *refs):
    tokens, refs = refs[:n_seq], refs[n_seq:]
    outs, refs = refs[:n_out], refs[n_out:]
    att, refs = refs[:n_seq], refs[n_seq:]
    vec_ref, normed_ref, middle_ref, mine_ref, out_ref, outs_here, att_here, tokens_here, sems = refs
    masks = block_masks(n_seq)
    me = me_ref[0]
    cols, width = mine_ref.shape
    half = tokens[0].shape[0] // HALVES
    block = n_seq * half // 2
    got_out = fetch([(ref, outs_here.at[i]) for i, ref in enumerate(outs)], sems.at[0])
    got_att = fetch([(ref, att_here.at[i]) for i, ref in enumerate(att)], sems.at[1])
    got_tokens = fetch([(ref, tokens_here.at[i]) for i, ref in enumerate(tokens)], sems.at[2])
    got_out()
    if n_out == 1:
        out_ref[...] = outs_here[0]
    else:
        n_dp = len(order_ref.cycle)
        part = width // (n_dp * n_seq)
        for i, mask in enumerate(range(n_seq)):
            for k in range(n_dp):
                start = pl.multiple_of((order_ref[k] * n_seq + (me ^ mask)) * part, part)
                for t in range(n_seq):
                    at = (k * n_seq + t) * part
                    out_ref[pl.ds(start, part), t * cols : (t + 1) * cols] = outs_here[i, at : at + part, :]
    sent = fetch([(out_ref.at[pl.ds(pl.multiple_of(me * cols, cols), cols), :], mine_ref)], sems.at[3])
    got_att()
    got_tokens()

    def step(h, carry):
        for side in range(2):
            places = range(side * n_seq // 2, (side + 1) * n_seq // 2)
            rows = pl.ds(pl.multiple_of(h * half, half), half)
            middle = jnp.concatenate([tokens_here[i, rows, :] for i in places], axis=0).astype(F32)
            middle = middle + vec_ref[0:1, :] + vec_ref[3:4, :]
            for i, mask in enumerate(masks):
                at = pl.multiple_of((me ^ mask) * cols, cols)
                first = (h * 2 + (side ^ (mask & 1))) * block
                spots = [pl.ds(pl.multiple_of(first + (t ^ (mask >> 1)) * half, half), half) for t in range(n_seq // 2)]
                found = jnp.concatenate([att_here[i, spot, :] for spot in spots], axis=0)
                middle = middle + dot(found, out_ref[pl.ds(at, cols), :], NN)
            xhat, _ = standardise(middle)
            mine = pl.ds(pl.multiple_of((h * 2 + side) * block, block), block)
            normed_ref[mine, :] = (xhat * vec_ref[4:5, :] + vec_ref[5:6, :]).astype(BF16)
            if side == 0:
                middle_ref[rows, :] = middle[:half, :]
        return carry

    lax.fori_loop(0, HALVES, step, 0)
    sent()


def middle_norm(me, order, tokens, att, outs, vecs):
    rows, width = tokens[0].shape
    n_seq = len(tokens)
    length = rows * n_seq
    cols = width // n_seq
    count = max(n_seq, len(outs))
    return call(
        functools.partial(middle_kernel, n_seq, len(outs), ME, order),
        near_in=(2 * n_seq + len(outs),),
        near_out=(0, 1),
        in_specs=[AWAY] * (2 * n_seq + len(outs)) + [NEAR],
        out_specs=[NEAR, NEAR, AWAY],
        out_shape=[shape((length, width)), shape((rows, width), F32), shape((cols, width))],
        scratch_shapes=[
            pltpu.VMEM((width, width), BF16),
            pltpu.VMEM((len(outs),) + outs[0].shape, BF16),
            pltpu.VMEM((n_seq, length, cols), BF16),
            pltpu.VMEM((n_seq, rows, width), BF16),
            pltpu.SemaphoreType.DMA((4, count)),
        ],
        compiler_params=vmem(24),
        cost_estimate=cost(2 * length * width * width, 10 * length * width),
        name="middle_norm",
    )(*tokens, *outs, *att, vecs)


def fetch(pairs, sems):
    copies = [pltpu.make_async_copy(a, b, sems.at[i]) for i, (a, b) in enumerate(pairs)]
    for copy in copies:
        copy.start()

    def wait():
        for copy in copies:
            copy.wait()

    return wait


def placed(order_ref, blocks, refs, target, start):
    if blocks.spots[0] is None:
        return [(refs[0], target)]
    cols = pl.ds(start, target.shape[1])
    return [(ref.at[:, cols], target.at[blocks.place(order_ref, i), :]) for i, ref in enumerate(refs)]


def up_kernel(ups, downs, block, order_ref, normed_ref, bias_ref, *refs):
    up_pieces, refs = refs[: len(ups.arrays)], refs[len(ups.arrays) :]
    if downs is None:
        downs, down_pieces = ups, up_pieces
    else:
        down_pieces, refs = refs[: len(downs.arrays)], refs[len(downs.arrays) :]
    up_ref, down_ref, hidden_ref, slope_ref, up_sems, down_sems = refs
    here = fetch(placed(order_ref, ups, up_pieces, up_ref, 0), up_sems)
    later = fetch(placed(order_ref, downs, down_pieces, down_ref, up_ref.shape[1]), down_sems)
    here()

    def step(i, carry):
        cols = pl.ds(pl.multiple_of(i * block, block), block)
        pre = dot(normed_ref[...], up_ref[:, cols], NN) + bias_ref[:, cols]
        phi = 0.5 + 0.5 * lax.erf(pre * math.sqrt(0.5))
        hidden_ref[:, cols] = (pre * phi).astype(BF16)
        slope_ref[:, cols] = phi + pre * (jnp.exp(-0.5 * pre * pre) * (1.0 / math.sqrt(2.0 * math.pi)))
        return carry

    lax.fori_loop(0, up_ref.shape[1] // block, step, 0)
    later()


def up_part(order, normed, bias, ups, downs, block=256):
    length, width = normed.shape
    ff = bias.shape[1]
    pieces = list(ups.arrays) + (list(downs.arrays) if downs is not None else [])
    return call(
        functools.partial(up_kernel, ups, downs, block, order),
        near_in=(0,),
        near_out=(0, 1, 2, 3),
        in_specs=[NEAR, NEAR] + [AWAY] * len(pieces),
        out_specs=[NEAR] * 4,
        out_shape=[shape((width, ff)), shape((ff, width)), shape((length, ff)), shape((length, ff), F32)],
        scratch_shapes=[pltpu.SemaphoreType.DMA((len(ups.arrays),)), pltpu.SemaphoreType.DMA((len((downs or ups).arrays),))],
        compiler_params=vmem(12),
        cost_estimate=cost(2 * length * width * ff, 8 * width * ff, 2 * length * ff),
        name="up_part",
    )(normed, bias, *pieces)


def mlp_back_kernel(first, at, block, n_grads, hidden_ref, slope_ref, up_ref, down_ref, *refs):
    grads, refs = refs[:n_grads], refs[n_grads:]
    if not first:
        refs = refs[2:]
    pre_ref, grad_ref, keep_ref, send_ref, branch_keep, branch_send, sum_ref, sems = refs
    count = 2 * keep_ref.shape[0]
    half = count // n_grads
    spots = [pl.ds(at * count + i * half, half) for i in range(n_grads)]
    ready = fetch([(ref, grad_ref.at[spot, :]) for ref, spot in zip(grads, spots)], sems)
    rows = pl.ds(at * count, count)
    side = keep_ref.shape[0]
    sides = ((0, keep_ref, branch_keep), (side, send_ref, branch_send))
    for start, _, branch_out in sides:
        branch_out[...] = dot(hidden_ref[pl.ds(at * count + start, side), :], down_ref[...], NN).astype(BF16)
    ready()

    def step(i, carry):
        cols = pl.ds(pl.multiple_of(i * block, block), block)
        grad = (slope_ref[rows, cols] * dot(grad_ref[rows, :], down_ref[cols, :], NT)).astype(BF16)
        pre_ref[rows, cols] = grad
        sum_ref[:, cols] = jnp.sum(grad.astype(F32), axis=0, keepdims=True)
        return carry

    lax.fori_loop(0, up_ref.shape[1] // block, step, 0)
    for start, back_out, _ in sides:
        back_out[...] = dot(pre_ref[pl.ds(at * count + start, side), :], up_ref[...], NT).astype(BF16)


def mlp_back(at, hidden, slope, up, down, grads, earlier, block=512):
    width = up.shape[0]
    length, ff = hidden.shape
    count = length // HALVES
    first = earlier is None
    given = 4 + len(grads)
    return call(
        functools.partial(mlp_back_kernel, first, at, min(block, ff // 2), len(grads)),
        near_in=range(given + 2),
        near_out=(0, 1, 2, 3, 4, 5),
        in_specs=[NEAR] * 4 + [AWAY] * len(grads) + ([] if first else [NEAR] * 2),
        out_specs=[NEAR] * 7,
        out_shape=[shape((length, ff)), shape((length, width))]
        + [shape((count // 2, width))] * 4
        + [shape((1, ff), F32)],
        scratch_shapes=[pltpu.SemaphoreType.DMA((len(grads),))],
        input_output_aliases={} if first else {given: 0, given + 1: 1},
        compiler_params=vmem(16),
        cost_estimate=cost(6 * count * width * ff, 8 * width * ff),
        name="mlp_back",
    )(hidden, slope, up, down, *grads, *([] if first else earlier))


def second_back_kernel(at, middle_ref, keep_ref, near_ref, far_ref, vec_ref, out_ref, grad_ref, one_ref, sum_ref, held, sems):
    half = far_ref.shape[0]
    ready = fetch([(out_ref, held)], sems)
    upstream = keep_ref[:half, :].astype(F32) + near_ref[:half, :].astype(F32) + far_ref[...].astype(F32)
    xhat, rate = standardise(middle_ref[at * half : (at + 1) * half, :])
    back = norm_back(upstream, xhat, rate, vec_ref[4:5, :])
    ready()
    grad_out = held[...].astype(F32)
    grad = grad_out + back
    one = grad.astype(BF16)
    grad_ref[...] = grad
    one_ref[...] = one
    sums = [upstream * xhat, upstream, one.astype(F32), grad_out, grad]
    sum_ref[...] = jnp.concatenate([jnp.sum(s, axis=0, keepdims=True) for s in sums], axis=0)


def second_back(at, middle_own, keep, near_part, far_part, grad_out, vecs):
    half, width = far_part.shape
    return call(
        functools.partial(second_back_kernel, at),
        near_in=(0, 1, 2, 3, 4),
        near_out=(0, 1),
        in_specs=[NEAR] * 5 + [AWAY],
        out_specs=[NEAR] * 3,
        out_shape=[shape((half, width), F32), shape((half, width)), shape((5, width), F32)],
        scratch_shapes=[pltpu.VMEM((half, width), BF16), pltpu.SemaphoreType.DMA((1,))],
        compiler_params=vmem(10),
        cost_estimate=cost(30 * half * width, 16 * half * width),
        name="second_back",
    )(middle_own, keep, near_part, far_part, vecs, grad_out)


def first_grad_kernel(n_seq, grad_ref, qkv_ref, vec_ref, *refs):
    tokens, (keep_ref, send_ref, sum_ref, last_ref) = refs[:n_seq], refs[n_seq:]
    step = pl.program_id(0)
    grad = grad_ref[...]
    total = dot(grad, qkv_ref[...], NT)
    column = jnp.sum(grad.astype(F32), axis=0, keepdims=True)
    sides = zip(tokens[: n_seq // 2], tokens[n_seq // 2 :])
    start = jnp.concatenate([jnp.where(step % 2 == 0, a[...], b[...]) for a, b in sides], axis=0).astype(F32)
    xhat, rate = standardise(start + vec_ref[0:1, :])
    back = norm_back(total, xhat, rate, vec_ref[1:2, :])
    last = jnp.concatenate([jnp.sum(t, axis=0, keepdims=True) for t in (total * xhat, total, back)], axis=0)
    total = total.astype(BF16)

    @pl.when(step == 0)
    def _():
        sum_ref[...] = column
        last_ref[...] = last

    @pl.when(step > 0)
    def _():
        sum_ref[...] += column
        last_ref[...] += last

    @pl.when(step % 2 == 0)
    def _():
        keep_ref[...] = total

    @pl.when(step % 2 == 1)
    def _():
        send_ref[...] = total


def first_grad(grad_qkv, qkv, vecs, tokens):
    length, wide = grad_qkv.shape
    n_seq = len(tokens)
    half = tokens[0].shape[0] // HALVES
    width = qkv.shape[0]
    block = length // (2 * HALVES)
    kept = pl.BlockSpec((block, width), lambda i: (i // 2, 0))
    return call(
        functools.partial(first_grad_kernel, n_seq),
        near_in=(1,),
        near_out=(0, 1),
        grid=(2 * HALVES,),
        in_specs=[
            pl.BlockSpec((block, wide), lambda i: (i, 0)),
            pl.BlockSpec(qkv.shape, lambda i: (0, 0)),
            pl.BlockSpec(vecs.shape, lambda i: (0, 0)),
        ]
        + [pl.BlockSpec((half, width), lambda i: (i // 2, 0))] * n_seq,
        out_specs=[kept, kept, pl.BlockSpec((1, wide), lambda i: (0, 0)), pl.BlockSpec((3, width), lambda i: (0, 0))],
        out_shape=[shape((length // 2, width))] * 2 + [shape((1, wide), F32), shape((3, width), F32)],
        compiler_params=vmem(20),
        cost_estimate=cost(length * wide * width, 4 * length * width),
        name="first_grad",
    )(grad_qkv, qkv, vecs, *tokens)


def out_terms_kernel(pairs, *refs):
    att, out_ref = refs[:pairs], refs[-1]
    total = None
    at = 0
    for ref in refs[pairs:-1]:
        rows = ref.shape[0]
        term = dot(jnp.concatenate([a[at : at + rows, :] for a in att], axis=1), ref[...], TN)
        total = term if total is None else total + term
        at += rows
    n_dp, rows, wide = out_ref.shape
    if wide == total.shape[1]:
        out_ref[...] = total.astype(BF16).reshape(out_ref.shape)
        return
    part = total.shape[0] // n_dp
    for i in range(n_dp):
        for t in range(rows // part):
            piece = total[i * part : (i + 1) * part, t * wide : (t + 1) * wide]
            out_ref[i, t * part : (t + 1) * part, :] = piece.astype(BF16)


def out_terms(att, grads, n_dp, rows):
    length = att[0].shape[0]
    cols = len(att) * att[0].shape[1]
    width = grads[0].shape[1]
    dims = (n_dp, rows, cols * width // (n_dp * rows))
    args = list(att) + list(grads)
    return call(
        functools.partial(out_terms_kernel, len(att)),
        near_in=range(len(att), len(att) + len(grads)),
        near_out=(0,),
        grid=(1,),
        in_specs=[pl.BlockSpec(a.shape, lambda i: (0, 0)) for a in args],
        out_specs=pl.BlockSpec(dims, lambda i: (0, 0, 0)),
        out_shape=shape(dims),
        compiler_params=vmem(16),
        cost_estimate=cost(2 * length * cols * width, 2 * length * width),
        name="out_terms",
    )(*args)


def first_back_kernel(keep_ref, near_ref, far_a, far_b, a_ref, b_ref, vec_ref, tokens_ref, out_ref, held, made, sems):
    ready = fetch([(tokens_ref, held)], sems)
    half = far_a.shape[0]
    size = keep_ref.shape[0] // HALVES
    copies = []
    for h, (far_ref, grad_ref) in enumerate(((far_a, a_ref), (far_b, b_ref))):
        mine = slice(h * size, h * size + half)
        upstream = keep_ref[mine, :].astype(F32) + near_ref[mine, :].astype(F32) + far_ref[...].astype(F32)
        if h == 0:
            ready()
        rows = slice(h * half, (h + 1) * half)
        xhat, rate = standardise(held[rows, :].astype(F32) + vec_ref[0:1, :])
        grad = grad_ref[...] + norm_back(upstream, xhat, rate, vec_ref[1:2, :])
        made[rows, :] = grad.astype(BF16)
        copy = pltpu.make_async_copy(made.at[pl.ds(h * half, half), :], out_ref.at[pl.ds(h * half, half), :], sems.at[1 + h])
        copy.start()
        copies.append(copy)
    for copy in copies:
        copy.wait()


def first_back(tokens_own, keep, near_part, far_a, far_b, grad_a, grad_b, vecs):
    rows, width = tokens_own.shape
    return call(
        first_back_kernel,
        near_in=range(7),
        in_specs=[NEAR] * 7 + [AWAY],
        out_specs=AWAY,
        out_shape=shape((rows, width)),
        scratch_shapes=[pltpu.VMEM((rows, width), BF16)] * 2 + [pltpu.SemaphoreType.DMA((1 + HALVES,))],
        compiler_params=vmem(10),
        cost_estimate=cost(30 * rows * width, 16 * rows * width),
        name="first_back",
    )(keep, near_part, far_a, far_b, grad_a, grad_b, vecs, tokens_own)


def block_masks(size):
    return [m for m in range(size) if not m & 1] + [m for m in range(size) if m & 1]


def far_bits(size):
    bits, bit = [], 2
    while bit < size:
        bits.append(bit)
        bit *= 2
    return bits


def tied(*values):
    return lax.optimization_barrier(values)


class Line:
    def __init__(self, token):
        self.token = token

    def slot(self, sends=(), work=lambda: (), inputs=(), begin=(), end=()):
        values, begun, inputs, token = tied(
            [s[0] for s in sends], [s[0] for s in begin], list(inputs), self.token
        )
        found = [lax.ppermute(value, s[1], s[2]) for value, s in zip(values, sends)]
        started = [lax.ppermute(value, s[1], s[2]) for value, s in zip(begun, begin)]
        found, done, ended, self.token = tied(found, work(*inputs), list(end), token)
        return found, done, started, ended


def swap(value, bit, size):
    return (value, "seq", [(i, i ^ bit) for i in range(size)])


def cycle(n_dp):
    wide = int(round(math.sqrt(n_dp / 2)))
    if wide < 2 or wide * (n_dp // wide) != n_dp or (n_dp // wide) % 2:
        return list(range(n_dp))
    high = n_dp // wide
    order = [z * wide for z in range(high)]
    for turn, z in enumerate(range(high - 1, -1, -1)):
        line = list(range(1, wide))
        order += [z * wide + y for y in (line[::-1] if turn % 2 else line)]
    return order


class Ring:
    def __init__(self, n_dp):
        self.n = n_dp
        order = cycle(n_dp)
        where = np.argsort(np.array(order))
        table = np.array([[order[(where[d] + k) % n_dp] for k in range(n_dp)] for d in range(n_dp)], np.int32)
        row = lax.dynamic_index_in_dim(jnp.asarray(table), lax.axis_index("dp"), 0, keepdims=False)
        self.order = row
        self.steps = Order(order)
        self.ahead = [(order[i], order[(i + 1) % n_dp]) for i in range(n_dp)]
        self.back = [(order[i], order[(i - 1) % n_dp]) for i in range(n_dp)]
        self.far = n_dp // 2
        self.near = (n_dp - 1) // 2


class Gather:
    def __init__(self, ring, own):
        self.ring = ring
        self.step = 0
        self.pending = None
        self.ahead = self.back = own
        self.pieces = [own] + [None] * (ring.n - 1)

    def sends(self):
        self.step += 1
        ahead, back = self.ahead, self.back
        if self.step == self.ring.far:
            half = ahead.shape[0] // 2
            ahead, back = ahead[:half], back[half:]
        return [(ahead, "dp", self.ring.ahead), (back, "dp", self.ring.back)]

    def take(self, found):
        self.ahead, self.back = found
        if self.step == self.ring.far:
            self.pieces[self.step] = tuple(found)
        else:
            self.pieces[-self.step], self.pieces[self.step] = found

    @property
    def left(self):
        return self.ring.far - self.step


def ring_kernel(adds, *refs):
    count = len(adds)
    values = list(refs[1 + count : -count])
    for i, (add, out) in enumerate(zip(adds, refs[-count:])):
        total = refs[1 + i][0].astype(F32)
        for _ in range(add):
            total = total + values.pop(0)[...].astype(F32)
        out[...] = total.astype(out.dtype)


def ring_blocks(order, items, dtype=BF16):
    n_dp = order.shape[0]
    args, in_specs, outs, out_specs = [], [], [], []
    for terms, k, _ in items:
        dims = terms.shape[1:]
        in_specs.append(pl.BlockSpec((1,) + dims, lambda i, at, k=k % n_dp: (at[k], 0, 0)))
        out_specs.append(pl.BlockSpec(dims, lambda i, at: (0, 0)))
        outs.append(shape(dims, dtype))
        args.append(terms)
    for _, _, values in items:
        for value in values:
            in_specs.append(pl.BlockSpec(value.shape, lambda i, at: (0, 0)))
            args.append(value)
    return pl.pallas_call(
        functools.partial(ring_kernel, [len(i[2]) for i in items]),
        grid_spec=pltpu.PrefetchScalarGridSpec(
            num_scalar_prefetch=1, grid=(1,), in_specs=in_specs, out_specs=out_specs
        ),
        out_shape=outs,
        compiler_params=vmem(16),
        name="ring_blocks",
    )(order, *args)


def table_kernel(me_ref, lead_ref, a_ref, b_ref, last_ref, ua_ref, ub_ref, column_ref, out_ref):
    me = me_ref[0]
    width = out_ref.shape[1]
    cols = column_ref.shape[1] // 3
    extra = ua_ref.shape[1] * (width // cols) // width
    part = 128 // extra
    sums = a_ref[...] + b_ref[...]
    last = last_ref[...]
    column = column_ref[...]
    out_ref[...] = jnp.zeros_like(out_ref)
    out_ref[0:2, :] = last[0:2]
    mine = pl.ds(pl.multiple_of(me * cols, 128), cols)
    out_ref[2:3, mine] = column[:, :cols]
    out_ref[3:4, mine] = column[:, 2 * cols :]
    out_ref[4:5, :] = sums[2:3]
    out_ref[5:7, :] = sums[0:2]
    out_ref[7:8, :] = sums[3:4]
    start = last[2:3] + sums[4:5]
    out_ref[8:9, :] = lead_ref[0:1, 0:1] * start
    out_ref[9:10, :] = start
    up = jnp.broadcast_to(ua_ref[...] + ub_ref[...], (8, width))
    here = lax.broadcasted_iota(jnp.int32, (1, width), 1) % 128 // part == me
    for k in range(extra):
        moved = pltpu.roll(up, ((me - k) * part + width) % width, 1)
        out_ref[10 + k : 11 + k, :] = jnp.where(here, moved[0:1, :], 0.0)


def small_table(me, lead, *args):
    width = args[0].shape[1]
    return pl.pallas_call(
        functools.partial(table_kernel, ME),
        grid=(1,),
        in_specs=[pl.BlockSpec(a.shape, lambda i: (0, 0)) for a in (lead, *args)],
        out_specs=pl.BlockSpec((16, width), lambda i: (0, 0)),
        out_shape=shape((16, width), F32),
        compiler_params=vmem(4),
        name="small_table",
    )(lead, *args)


def halve_kernel(bit, *refs):
    mine_ref, other_ref = refs[-2:]
    wide = mine_ref.shape[1]
    side = lax.rem(lax.div(lax.axis_index("dp"), bit), 2)
    for at, target in ((side, mine_ref), (1 - side, other_ref)):
        total = 0.0
        for ref in refs[:-2]:
            total = total + ref[:, pl.ds(pl.multiple_of(at * wide, 128), wide)]
        target[...] = total


def halve(bit, values):
    rows, wide = values[0].shape
    return pl.pallas_call(
        functools.partial(halve_kernel, bit),
        in_specs=[NEAR] * len(values),
        out_specs=[NEAR] * 2,
        out_shape=[shape((rows, wide // 2), F32)] * 2,
        compiler_params=vmem(2),
        name="halve",
    )(*values)


def owner_kernel(count, order_ref, me_ref, term_ref, *refs):
    part = refs[-1].shape[0]
    outs = refs[-count:]
    for mask, out in enumerate(outs):
        rows = pl.ds(pl.multiple_of((me_ref[0] ^ mask) * part, part), part)
        total = term_ref[0, rows, :].astype(F32)
        for ref in refs[:-count]:
            total = total + ref[rows, :].astype(F32)
        out[...] = total.astype(BF16)


def owner_blocks(order, me, terms, values, n_seq):
    _, rows, wide = terms.shape
    part = rows // n_seq
    if part % 16:
        (total,) = ring_blocks(order, [(terms, 0, values)])
        blocks = total.reshape(n_seq, part, wide)
        return [lax.dynamic_index_in_dim(blocks, me[0] ^ m, 0, keepdims=False) for m in range(n_seq)]
    return pl.pallas_call(
        functools.partial(owner_kernel, n_seq),
        grid_spec=pltpu.PrefetchScalarGridSpec(
            num_scalar_prefetch=2,
            grid=(1,),
            in_specs=[pl.BlockSpec((1, rows, wide), lambda i, at, me: (at[0], 0, 0))]
            + [pl.BlockSpec((rows, wide), lambda i, at, me: (0, 0))] * len(values),
            out_specs=[pl.BlockSpec((part, wide), lambda i, at, me: (0, 0))] * n_seq,
        ),
        out_shape=[shape((part, wide))] * n_seq,
        compiler_params=vmem(8),
        name="owner_blocks",
    )(order, me, terms, *values)


def unpack_kernel(groups, me_ref, out_ref, *refs):
    outs, last_ref = refs[-len(groups) - 1 : -1], refs[-1]
    pieces = refs[: -len(groups) - 1]
    part = last_ref.shape[0]
    cols = out_ref.shape[1]
    for t in range(out_ref.shape[0] // part):
        last_ref[:, t * cols : (t + 1) * cols] = out_ref[t * part : (t + 1) * part, :].astype(F32)
    n_seq = len(pieces)
    for mask, ref in enumerate(pieces):
        at = 0
        for count, out in zip(groups, outs):
            wide = out.shape[1] // (count * n_seq)
            for i in range(count):
                start = pl.multiple_of((i * n_seq + (me_ref[0] ^ mask)) * wide, 128)
                out[:, pl.ds(start, wide)] = ref[:, at : at + wide].astype(F32)
                at += wide


def unpack(groups, widths, pieces, out_block):
    part = pieces[0].shape[0]
    n_seq = len(pieces)
    if any((wide // n_seq // count) % 128 for count, wide in zip(groups, widths)):
        whole = flipped(dict(enumerate(pieces)), n_seq)
        outs, at = [], 0
        for count, wide in zip(groups, widths):
            mine = whole[:, :, at : at + wide // n_seq].reshape(n_seq, part, count, -1)
            outs.append(jnp.moveaxis(mine, 0, 2).reshape(part, wide).astype(F32))
            at += wide // n_seq
        last = out_block.reshape(-1, part, out_block.shape[1])
        return *outs, jnp.moveaxis(last, 0, 1).reshape(part, -1).astype(F32)
    full = list(widths) + [out_block.size // part]
    return pl.pallas_call(
        functools.partial(unpack_kernel, groups, ME),
        grid=(1,),
        in_specs=[pl.BlockSpec(out_block.shape, lambda i: (0, 0))]
        + [pl.BlockSpec(pieces[0].shape, lambda i: (0, 0))] * n_seq,
        out_specs=[pl.BlockSpec((part, wide), lambda i: (0, 0)) for wide in full],
        out_shape=[shape((part, wide), F32) for wide in full],
        compiler_params=vmem(8),
        name="unpack",
    )(out_block, *pieces)


class Scatter:
    def __init__(self, ring, terms):
        self.ring = ring
        self.terms = terms
        self.step = 0
        self.pending = None
        count = len(terms)
        found = ring_blocks(
            ring.order, [(t, ring.far, ()) for t in terms] + [(t, -ring.near, ()) for t in terms]
        )
        self.ahead, self.back = found[:count], found[count:]

    def sends(self):
        self.step += 1
        found = [(v, "dp", self.ring.ahead) for v in self.ahead]
        if self.step > self.ring.far - self.ring.near:
            found += [(v, "dp", self.ring.back) for v in self.back]
        return found

    def take(self, found):
        count = len(self.terms)
        left = self.ring.far - self.step
        ahead, back = found[:count], found[count:]
        if left:
            items = [(t, left, (v,)) for t, v in zip(self.terms, ahead)]
            items += [(t, -left, (v,)) for t, v in zip(self.terms, back)]
            found = ring_blocks(self.ring.order, items)
            ahead, back = found[:count], found[count:]
        self.ahead = ahead
        if back:
            self.back = back

    @property
    def left(self):
        return self.ring.far - self.step

    def total(self, dtype=F32):
        items = [(t, 0, (a, b)) for t, a, b in zip(self.terms, self.ahead, self.back)]
        return ring_blocks(self.ring.order, items, dtype)


def joint_kernel(items, order_ref, q_ref, o_ref, *refs):
    values, outs = list(refs[: -len(items)]), refs[-len(items) :]
    _, rows, edge = q_ref.shape
    _, part, width = o_ref.shape
    for (k, low, high, added), target in zip(items, outs):
        cols = target.shape[1] - edge
        value = values.pop(0) if added else None
        at = order_ref[k]

        def put(source, from_rows, row, lanes):
            cuts = sorted({row, row + len(from_rows)} | ({max(row, min(c, row + len(from_rows))) for c in added} if added else set()))
            for a, b in zip(cuts, cuts[1:]):
                total = source[from_rows[a - row] : from_rows[b - row - 1] + 1]
                if added and added[0] <= a and b <= added[1]:
                    total = (total.astype(F32) + value[a - added[0] : b - added[0], lanes].astype(F32)).astype(BF16)
                target[a - low : b - low, lanes] = total

        put(q_ref.at[at, :, slice(0, edge)], range(low, high), low, slice(0, edge))
        for t in range(rows // part):
            a, b = max(low, t * part), min(high, (t + 1) * part)
            if a < b:
                lanes = slice(t * cols, (t + 1) * cols)
                put(o_ref.at[at, :, lanes], range(a - t * part, b - t * part), a, slice(edge, edge + cols))


class JointScatter:
    def __init__(self, ring, qkv, out):
        self.ring = ring
        self.qkv = qkv
        self.out = out
        self.step = 0
        self.pending = None
        rows = qkv.shape[1]
        if ring.far:
            far = ring.far
            self.ahead, self.back = self.blocks([(far, 0, rows // 2, None), (far, rows // 2, rows, None)], ())

    def blocks(self, items, values):
        n_dp, rows, edge = self.qkv.shape
        _, part, width = self.out.shape
        wide = edge + width * part // rows
        items = [(k % n_dp, low, high, added) for k, low, high, added in items]
        return call(
            functools.partial(joint_kernel, items, self.ring.steps),
            near_in=range(2 + len(values)),
            near_out=range(len(items)),
            in_specs=[NEAR] * (2 + len(values)),
            out_specs=[NEAR] * len(items),
            out_shape=[shape((high - low, wide)) for _, low, high, _ in items],
            compiler_params=vmem(4),
            name="joint_blocks",
        )(self.qkv, self.out, *values)

    def sends(self):
        self.step += 1
        return [(self.ahead, "dp", self.ring.ahead), (self.back, "dp", self.ring.back)]

    def take(self, found):
        left = self.ring.far - self.step
        rows = self.qkv.shape[1]
        if left:
            spans = ((0, rows // 2), (rows // 2, rows)) if self.step == 1 else ((0, rows), (0, rows))
            found = self.blocks([(sign * left, 0, rows, span) for sign, span in zip((1, -1), spans)], found)
        self.ahead, self.back = found

    @property
    def left(self):
        return self.ring.far - self.step

    def total(self, me, n_seq, dtype=BF16, beside=()):
        n_dp, rows, edge = self.qkv.shape
        _, part, width = self.out.shape
        wide = edge + width * part // rows
        values = [self.ahead, self.back]
        if self.ring.far == 1:
            values = [jnp.concatenate(values, axis=0)] * 2
            values[1] = jnp.zeros_like(values[1])
        cuts = 1 if rows // n_seq % 16 else n_seq
        more = list(beside) if cuts > 1 else []
        full = edge + (more[0].shape[1] if more else 0)
        args = [self.qkv, self.out] + values + more
        found = call(
            functools.partial(joint_owner_kernel, cuts, edge, dtype == F32, ME),
            near_in=range(len(args)),
            near_out=range(cuts + (dtype != F32)),
            in_specs=[NEAR] * len(args),
            out_specs=[NEAR] * cuts + [AWAY if dtype == F32 else NEAR],
            scratch_shapes=[pltpu.VMEM((part, width), F32), pltpu.SemaphoreType.DMA((1,))] if dtype == F32 else [],
            out_shape=[shape((rows // cuts, full))] * cuts + [shape((part, width), dtype)],
            compiler_params=vmem(8),
            name="joint_owner",
        )(*args)
        if cuts == n_seq:
            return list(found[:n_seq]), found[n_seq]
        blocks = found[0].reshape(n_seq, rows // n_seq, edge)
        blocks = [lax.dynamic_index_in_dim(blocks, me[0] ^ m, 0, keepdims=False) for m in range(n_seq)]
        return beside_all(blocks, beside), found[1]


def beside_all(blocks, beside):
    return [jnp.concatenate(pair, axis=1) for pair in zip(blocks, beside)] if beside else blocks


def joint_owner_kernel(cuts, edge, last_away, me_ref, q_ref, o_ref, *refs):
    if last_away:
        refs, (last, target, sems) = refs[:-3], refs[-3:]
        refs = (*refs, target)
    values, outs = refs[: -cuts - 1], refs[-cuts - 1 :]
    values, more = values[:2], values[2:]
    part = outs[0].shape[0]
    for mask, target in enumerate(outs[:-1]):
        rows = pl.ds(pl.multiple_of((me_ref[0] ^ mask) * part, part), part) if cuts > 1 else slice(None)
        total = q_ref[lax.axis_index("dp"), rows, :].astype(F32)
        for ref in values:
            total = total + ref[rows, :edge].astype(F32)
        target[:, :edge] = total.astype(BF16)
        if more:
            target[:, edge:] = more[mask][...]
    part, width = outs[-1].shape
    cols = values[0].shape[1] - edge
    for t in range(width // cols):
        total = o_ref[lax.axis_index("dp"), :, t * cols : (t + 1) * cols].astype(F32)
        for ref in values:
            total = total + ref[t * part : (t + 1) * part, edge:].astype(F32)
        outs[-1][:, t * cols : (t + 1) * cols] = total.astype(outs[-1].dtype)
    if last_away:
        fetch([(outs[-1], last)], sems)()


class ApartScatter(Scatter):
    def __init__(self, ring, qkv, out):
        super().__init__(ring, [qkv, out])

    def total(self, me, n_seq, dtype=BF16, beside=()):
        qkv, out = self.terms
        blocks = owner_blocks(self.ring.order, me, qkv, (self.ahead[0], self.back[0]), n_seq)
        (out_sum,) = ring_blocks(self.ring.order, [(out, 0, (self.ahead[1], self.back[1]))])
        return beside_all(blocks, beside), out_sum


def flipped(pieces, bits):
    me = lax.axis_index("seq")
    size = len(pieces)
    held = [pieces[m] for m in range(size)]
    bit = 1
    while bit < size:
        turned = (me & bit) != 0
        held = [jnp.where(turned, held[m ^ bit], held[m]) for m in range(size)]
        bit *= 2
    return jnp.stack(held)


def make_body(n_dp, n_seq):
    masks = block_masks(n_seq)
    far = far_bits(n_seq)
    far_masks = [m for m in range(n_seq) if not m & 1]

    def body(
        tokens,
        lead_hours,
        valid_counts,
        patch_mask,
        first_gain,
        first_shift,
        qkv_weight,
        query_bias,
        value_bias,
        out_weight,
        out_bias,
        second_gain,
        second_shift,
        up_weight,
        up_bias,
        down_weight,
        down_bias,
        lead_weight,
        lead_bias,
        cotangent,
    ):
        me = lax.axis_index("seq")
        rows, width = tokens.shape[1], tokens.shape[2]
        length = rows * n_seq
        half = rows // HALVES
        part = qkv_weight.shape[0]
        ff_part = down_weight.shape[0]
        ff = up_weight.shape[1]
        extra = ff_part // part
        cols = width // n_seq
        ff_cols = ff // n_seq
        lead = lead_hours[0].astype(F32) / 100.0
        count = valid_counts[0]
        ring = Ring(n_dp)
        me_ref = me.reshape(1).astype(jnp.int32)
        lead_ref = jnp.broadcast_to(lead, (8, 128))
        order = ring.steps

        def far_gather(own, at_bit):
            return [swap(own[m], far[at_bit], n_seq) for m in sorted(own)]

        line = Line(me_ref)

        def run(sends=(), work=lambda: (), inputs=(), start=(), finish=(), begin=(), end=()):
            sends, begin, end = list(sends), list(begin), list(end)
            plan = []
            for ring_part in finish:
                if ring_part.pending is not None:
                    plan.append((ring_part, "end", len(end), len(ring_part.pending)))
                    end += ring_part.pending
                    ring_part.pending = None
            n_sends, n_begin = len(sends), len(begin)
            ahead = []
            for ring_part in start:
                mine = ring_part.sends()
                if ring_part in finish:
                    plan.append((ring_part, "now", len(ahead), len(mine)))
                    ahead += mine
                else:
                    plan.append((ring_part, "later", len(begin), len(mine)))
                    begin += mine
            found, done, begun, ended = line.slot(ahead + sends, work, inputs, begin, end)
            early, found = found[: len(ahead)], found[len(ahead) :]
            n_end = len(end) - sum(p[3] for p in plan if p[1] == "end")
            for ring_part, kind, at, size in plan:
                if kind == "end":
                    ring_part.take(list(ended[at : at + size]))
                elif kind == "now":
                    ring_part.take(list(early[at : at + size]))
                else:
                    ring_part.pending = list(begun[at : at + size])
            return list(found[:n_sends]), done, list(begun[:n_begin]), list(ended[:n_end])

        def near_all(held):
            return [swap(held[m], 1, n_seq) for m in sorted(held)]

        def with_near(held, found):
            held.update({m ^ 1: v for m, v in zip(sorted(held), found)})

        def with_far(held, found, at_bit):
            held.update({m ^ far[at_bit]: v for m, v in zip(sorted(held), found)})

        def rest_far(held):
            for i in range(1, len(far)):
                found, _, _, _ = line.slot(far_gather(held, i))
                with_far(held, found, i)

        vectors = [
            first_gain,
            first_shift,
            query_bias,
            value_bias,
            out_bias,
            second_gain,
            second_shift,
            down_bias,
            lead_weight,
            lead_bias,
            up_bias,
        ]
        kinds = 10 + extra
        packed = pack(n_dp, n_seq, me_ref, qkv_weight, up_weight, vectors)

        def masked_rows(cot, mask, count):
            positions = me * rows + jnp.arange(rows, dtype=jnp.int32)
            weight = (mask * (positions < count).astype(jnp.int32)).astype(BF16)[:, None]
            return tuple(cot[h * half : (h + 1) * half] * weight[h * half : (h + 1) * half] for h in range(HALVES))

        found, outs_own, _, _ = run(
            [swap(packed[m], m, n_seq) for m in range(1, n_seq)],
            masked_rows,
            (cotangent[0], patch_mask[0], count),
        )
        one_own = join_one(n_seq, me_ref, [packed[0]] + list(found), out_weight)

        g_one = Gather(ring, one_own)

        def steps(*rings):
            mine = [g for g in rings if g.left]
            return dict(start=mine, finish=mine)

        tokens_held = {0: tokens[0]}
        grad_held = [{0: g} for g in outs_own]
        found, _, _, _ = run([swap(packed[n_seq + m], m, n_seq) for m in range(1, n_seq)], **steps(g_one))
        up_found = [packed[n_seq]] + list(found)
        _, (two_own,), tokens_far, _ = run(
            work=lambda *a: (join_two(n_seq, me_ref, a[:-1], a[-1]),),
            inputs=(*up_found, down_weight),
            begin=far_gather(tokens_held, 0),
            **steps(g_one),
        )
        g_two = Gather(ring, two_own)
        _, _, _, tokens_far = run(end=tokens_far, **steps(g_one))
        with_far(tokens_held, tokens_far, 0)
        rest_far(tokens_held)
        while g_one.left > 1:
            run(**steps(g_one))
        found, _, _, _ = run(near_all(tokens_held), **steps(g_one))
        with_near(tokens_held, found)

        valid = jnp.broadcast_to(count, (8, 128))
        pairs = cols // PAIR

        def begun(part_of):
            return dict(start=[part_of] if part_of.left else [])

        tokens_by = [tokens_held[m] for m in masks]
        ones_blocks = ordered(ring.order, g_one.pieces)

        def attend_first(*a):
            blocks = Blocks(a[n_seq:], ones_blocks.spots, ones_blocks.rows)
            out_pack = middle_columns(blocks, 3 * cols, cols, n_dp)
            found = project(me_ref, order, lead_ref, a[:n_seq], blocks, kinds)
            return out_pack, found

        _, (out_pack, (normed, q, k, v, qkv, table, vecs)), _, _ = run(
            work=attend_first, inputs=tokens_by + list(ones_blocks.arrays), **steps(g_two)
        )
        out_held = {0: out_pack}

        def up_bias_of(table):
            u_bias = table[10 : 10 + extra].reshape(extra, n_dp, n_seq, part)
            u_bias = lax.dynamic_index_in_dim(u_bias, me, 2, keepdims=False)
            return jnp.swapaxes(u_bias, 0, 1).reshape(1, ff_cols)

        def attend_rest(q, k, v, table):
            lses, attended = [], None
            for p in range(pairs):
                attended, lse = attend(n_seq, p, me_ref, valid, q, k, v, attended)
                lses.append(lse)
            return attended, jnp.concatenate(lses, axis=0), up_bias_of(table)

        found, (attended, lse, u_bias), _, _ = run(
            far_gather(out_held, 0), work=attend_rest, inputs=(q, k, v, table), **steps(g_two)
        )
        with_far(out_held, found, 0)
        rest_far(out_held)
        att_held = {0: attended}
        nearby = near_all(out_held)
        found, _, _, _ = run(far_gather(att_held, 0) + nearby, **steps(g_two))
        with_near(out_held, found[-len(nearby) :])
        with_far(att_held, found[: -len(nearby)], 0)
        rest_far(att_held)
        found, _, _, _ = run(near_all(att_held))
        with_near(att_held, found)

        def out_whole(pieces):
            if part % 16 == 0:
                return pieces
            blocks = flipped(dict(enumerate(pieces)), n_seq).reshape(n_seq, n_dp, n_seq, part, cols)
            return [jnp.transpose(blocks, (1, 0, 3, 2, 4)).reshape(width, width)]

        found, (normed_two, middle_own, out_mine), _, _ = run(
            far_gather(grad_held[0], 0),
            work=lambda tok, att, outs, vecs: middle_norm(me_ref, order, tok, att, out_whole(outs), vecs),
            inputs=(
                tokens_by,
                [att_held[m] for m in masks],
                [out_held[m] for m in range(n_seq)],
                vecs,
            ),
            **steps(g_two),
        )
        with_far(grad_held[0], found, 0)
        rest_far(grad_held[0])
        while g_two.left:
            run(**steps(g_two))
        twos = ordered(ring.order, g_two.pieces)
        downs = twos
        if twos.spots[0] is None:
            whole = twos.arrays[0]
            twos = Blocks([whole[:, :ff_cols]], [None], whole.shape[0])
            downs = Blocks([whole[:, ff_cols:].reshape(ff_cols, width)], [None], ff_cols)
        nearby = near_all(grad_held[0])
        found, (up, down, hidden, slope), _, _ = run(
            far_gather(grad_held[1], 0) + nearby,
            work=lambda n, b, a, d: up_part(
                order,
                n,
                b,
                Blocks(a, twos.spots, twos.rows),
                Blocks(d, downs.spots, downs.rows) if downs is not twos else None,
            ),
            inputs=(normed_two, u_bias, list(twos.arrays), list(downs.arrays) if downs is not twos else ()),
        )
        with_near(grad_held[0], found[-len(nearby) :])
        with_far(grad_held[1], found[: -len(nearby)], 0)
        rest_far(grad_held[1])

        def half_sum(keep, other):
            found = {}
            for at, m in enumerate(far_masks):
                if m:
                    rows_at = slice(at * half, (at + 1) * half)
                    found[m] = (keep[rows_at].astype(F32) + other[rows_at].astype(F32)).astype(BF16)
            return found

        def far_first(held):
            bit = far[-1]
            return [swap(held[m], bit, n_seq) for m in sorted(held) if m & bit]

        def far_rest(held, found):
            for at, bit in enumerate(reversed(far)):
                upper = sorted(m for m in held if m & bit)
                if at:
                    found, _, _, _ = line.slot([swap(held[m], bit, n_seq) for m in upper])
                kept = {m: held[m] for m in held if not m & bit}
                for m, value in zip(upper, found):
                    low = m ^ bit
                    if low in kept:
                        value = (kept[low].astype(F32) + value.astype(F32)).astype(BF16)
                    kept[low] = value
                held = kept
            return held[0]

        found, (pre, grad_out, keep_a, send_a, branch_keep_a, branch_send_a, sum_a), _, _ = run(
            near_all(grad_held[1]),
            work=lambda *a: mlp_back(0, *a, None),
            inputs=(hidden, slope, up, down, [grad_held[0][m] for m in masks]),
        )
        with_near(grad_held[1], found)
        (near_a,), (pre, grad_out, keep_b, send_b, branch_keep_b, branch_send_b, sum_b), _, _ = run(
            [swap(send_a, 1, n_seq)],
            work=lambda *a: mlp_back(1, *a),
            inputs=(hidden, slope, up, down, [grad_held[1][m] for m in masks], (pre, grad_out)),
        )
        def moved(value, axis, bit):
            count = n_dp if axis == "dp" else n_seq
            return lax.ppermute(value, axis, [(i, i ^ bit) for i in range(count)])

        held_a = half_sum(keep_a, near_a)
        sends = far_first(held_a)

        def weight_terms(hidden, grad_out, normed_two, pre):
            up_terms = dot(normed_two, pre, TN).astype(BF16).reshape(n_dp, n_seq * part, ff_cols)
            return dot(hidden, grad_out, TN).astype(BF16).reshape(n_dp, ff_part, width), up_terms

        found, (down_terms, up_terms), _, _ = run(
            sends + [swap(send_b, 1, n_seq)], work=weight_terms, inputs=(hidden, grad_out, normed_two, pre)
        )
        far_a, near_b = far_rest(held_a, found[: len(sends)]), found[-1]
        held_b = half_sum(keep_b, near_b)

        def back_half(at):
            return lambda *a: tuple(second_back(at, *a))

        scatter_two = JointScatter(ring, up_terms, down_terms)
        sends = far_first(held_b)
        found, (grad_mid_a, one_a, sums_a), _, _ = run(
            sends + [swap(branch_send_a, 1, n_seq), swap(branch_send_b, 1, n_seq)],
            work=back_half(0),
            inputs=(middle_own, keep_a, near_a, far_a, outs_own[0], vecs),
            **steps(scatter_two),
        )
        far_b, branch_other = far_rest(held_b, found[: len(sends)]), found[-2:]
        one_far_a, (grad_mid_b, one_b, sums_b), _, _ = run(
            far_gather({0: one_a}, 0),
            work=back_half(1),
            inputs=(middle_own, keep_b, near_b, far_b, outs_own[1], vecs),
            **begun(scatter_two),
        )
        one_held_a = {0: one_a}
        with_far(one_held_a, one_far_a, 0)
        rest_far(one_held_a)
        one_held_b = {0: one_b}
        found, _, one_far_b, _ = run(
            near_all(one_held_a), begin=far_gather(one_held_b, 0), finish=[scatter_two]
        )
        with_near(one_held_a, found)
        _, (dq_a, dk_a, dv_a), _, one_far_b = run(
            work=lambda *a: attend_back(0, me_ref, valid, *a, None),
            inputs=(q, k, v, lse, out_mine, [one_held_a[m] for m in masks]),
            end=one_far_b,
            **begun(scatter_two),
        )
        with_far(one_held_b, one_far_b, 0)
        rest_far(one_held_b)
        found, _, _, _ = run(near_all(one_held_b), finish=[scatter_two])
        with_near(one_held_b, found)
        ones = [one_held_a[m] for m in masks] + [one_held_b[m] for m in masks]

        branch_held = {
            m: jnp.concatenate([value, half_sum(branch_keep_b, branch_other[1])[m]], axis=0)
            for m, value in half_sum(branch_keep_a, branch_other[0]).items()
        }

        def second_attend(q, k, v, lse, out_mine, grads, earlier, att, ones):
            sums = out_terms(att, ones, n_dp, part if part % 16 else n_seq * part)
            return attend_back(1, me_ref, valid, q, k, v, lse, out_mine, grads, earlier), sums

        branch_far, (grad_qkv, out_sums), _, _ = run(
            far_first(branch_held),
            work=second_attend,
            inputs=(
                q,
                k,
                v,
                lse,
                out_mine,
                [one_held_b[m] for m in masks],
                (dq_a, dk_a, dv_a),
                [attended],
                ones,
            ),
            **steps(scatter_two),
        )
        branch_far = far_rest(branch_held, branch_far)

        qkv_terms = dot(normed, grad_qkv, TN).astype(BF16).reshape(n_dp, n_seq * part, 3 * cols)
        scatter_one = (ApartScatter if part % 16 else JointScatter)(ring, qkv_terms, out_sums)
        late = [scatter_two] if scatter_two.left else []

        def far_moved(held):
            if not far:
                return []
            return [moved(held[m], "seq", far[-1]) for m in sorted(held) if m & far[-1]]

        def now(*beside):
            mine = [scatter_one] if scatter_one.left else []
            return dict(start=mine, finish=mine + list(beside))

        def final_rows(keep_a, keep_b, near_a, near_b, far_part, mid, bias):
            total = jnp.concatenate([keep_a[:half], keep_b[:half]], axis=0).astype(F32)
            total = total + jnp.concatenate([near_a[:half], near_b[:half]], axis=0).astype(F32)
            return (mid + (total + far_part.astype(F32) + bias[6:7])).astype(BF16)

        late = [scatter_two] if scatter_two.left else []
        options = now()
        _, (gn_keep, gn_send, column_sums, last_sums), _, _ = run(
            work=lambda g: first_grad(g, qkv, vecs, tokens_by),
            inputs=(grad_qkv,),
            start=options["start"] + late,
            finish=options["finish"] + late,
        )
        while scatter_two.left:
            run(**steps(scatter_two))
        plain = (width // n_dp) % 128 == 0 and extra == n_seq and n_seq * part == 128

        bits = []
        while 2 ** len(bits) < n_dp:
            bits.append(2 ** len(bits))
        bits = bits[::-1] if plain else []
        at_dp = lax.axis_index("dp")

        def loose_table():
            sums = sums_a + sums_b
            table = last_sums
            start_sums = table[2:3] + sums[4:5]
            q_sum = lax.dynamic_update_slice(jnp.zeros((1, width), F32), column_sums[:, :cols], (0, me * cols))
            v_sum = lax.dynamic_update_slice(jnp.zeros((1, width), F32), column_sums[:, 2 * cols :], (0, me * cols))
            u_sum = jnp.swapaxes((sum_a + sum_b).reshape(n_dp, extra, part), 0, 1)
            u_sum = lax.dynamic_update_index_in_dim(jnp.zeros((extra, n_dp, n_seq, part), F32), u_sum, me, 2)
            rows_out = [table[0:2], q_sum, v_sum, sums[2:3], sums[0:2], sums[3:4], lead * start_sums, start_sums]
            table = jnp.concatenate(rows_out + [u_sum.reshape(extra, width)], axis=0)
            return lax.psum_scatter(table, ("dp", "seq"), scatter_dimension=1, tiled=True)

        seq_bits = far + ([1] if n_seq > 1 else []) if plain else []

        def make_table():
            if not plain:
                return loose_table()
            return small_table(
                me_ref, lead_ref, sums_a, sums_b, last_sums, sum_a, sum_b, column_sums
            )

        def hop(held):
            if bits:
                bit = bits.pop(0)
                mine, other = halve(bit, held)
                return mine, [(other, "dp", [(i, i ^ bit) for i in range(n_dp)])]
            total = sum(held[1:], held[0])
            if seq_bits:
                return total, [swap(total, seq_bits.pop(0), n_seq)]
            return total, []

        def totals():
            blocks, total = scatter_two.total(me_ref, n_seq, F32)
            return *blocks, total

        mine, small = hop([make_table()])
        found, (*up_blocks, down_grad), _, _ = run([swap(gn_send, 1, n_seq)] + small, work=totals, **now())
        gn_near = found[0]
        held = [mine] + found[1:]
        size = half * len(far_masks)
        gn_held_a = half_sum(gn_keep[:size], gn_near[:size])
        mine, small = hop(held)
        sends = far_first(gn_held_a)
        found, (gn_held_b,), _, _ = run(
            sends + small, work=lambda k, n: (half_sum(k[size:], n[size:]),), inputs=(gn_keep, gn_near), **now()
        )
        gn_far_a = far_rest(gn_held_a, found[: len(sends)])
        held = [mine] + found[len(sends) :]
        mine, small = hop(held)
        sends = far_first(gn_held_b)
        found, (block_out,), _, _ = run(
            sends + small,
            work=lambda *a: (final_rows(*a),),
            inputs=(branch_keep_a, branch_keep_b, branch_other[0], branch_other[1], branch_far, middle_own, vecs),
            **now(),
        )
        gn_far_b = far_rest(gn_held_b, found[: len(sends)])
        held = [mine] + found[len(sends) :]
        while scatter_one.left:
            run(**steps(scatter_one))
        qkv_blocks, out_sum = scatter_one.total(me_ref, n_seq, beside=up_blocks)
        moves = []
        for dp_at in range(n_dp):
            for seq_at in range(n_seq):
                moves.append((dp_at * n_seq + seq_at, seq_at * n_dp + dp_at))
        final = [(out_sum, ("dp", "seq"), moves)] + [swap(qkv_blocks[m], m, n_seq) for m in range(1, n_seq)]

        mine, small = hop(held)
        found, (tokens_grad,), _, _ = run(
            final + small,
            work=lambda *a: (first_back(*a),),
            inputs=(tokens[0], gn_keep, gn_near, gn_far_a, gn_far_b, grad_mid_a, grad_mid_b, vecs),
        )
        last, held = found[: len(final)], [mine] + found[len(final) :]
        while bits or seq_bits:
            mine, small = hop(held)
            found, _, _, _ = run(small)
            held = [mine] + found
        small_sums = sum(held[1:], held[0])
        if plain:
            small_sums = lax.dynamic_slice_in_dim(small_sums, me * part, part, 1)
        owned = small_sums[:kinds]
        qkv_weight_grad, up_weight_grad, out_weight_grad = unpack(
            (3, n_dp), (3 * width, ff), [qkv_blocks[0]] + list(last[1:]), last[0]
        )
        return (
            block_out[None],
            tokens_grad[None],
            owned[0],
            owned[1],
            qkv_weight_grad,
            owned[2],
            owned[3],
            out_weight_grad,
            owned[4],
            owned[5],
            owned[6],
            up_weight_grad,
            owned[10 : 10 + extra].reshape(ff_part),
            down_grad[0] if down_grad.ndim == 3 else down_grad,
            owned[7],
            owned[8],
            owned[9],
        )

    return body


def solution(mesh):
    both = P(("dp", "seq"))
    matrix = P(("dp", "seq"), None)
    tokens = P("dp", "seq", None)
    in_specs = (tokens, P("dp"), P("dp"), P("dp", "seq"), both, both, matrix, both, both, matrix, both, both, both)
    in_specs += (matrix, both, matrix, both, both, both, tokens)
    out_specs = (tokens, tokens, both, both, matrix, both, both, matrix, both, both, both, matrix, both, matrix)
    out_specs += (both, both, both)
    return jax.shard_map(
        make_body(mesh.shape["dp"], mesh.shape["seq"]),
        mesh=mesh,
        in_specs=in_specs,
        out_specs=out_specs,
        check_vma=False,
    )
```

```python
import functools
import math

import jax
import jax.numpy as jnp
import numpy as np
from jax import lax
from jax.experimental import pallas as pl
from jax.experimental.pallas import tpu as pltpu
from jax.sharding import PartitionSpec as P

HEADS = 16
HEAD_DIM = 64
PAIR = 2 * HEAD_DIM
SCALE = 1.0 / math.sqrt(HEAD_DIM)
EPSILON = 1e-06
MASKED = -1e30
F32 = jnp.float32
BF16 = jnp.bfloat16
NN, NT, TN = ((1,), (0,)), ((1,), (1,)), ((0,), (0,))
HALVES = 2
MIB = 1024 * 1024
NEAR = pl.BlockSpec(memory_space=pltpu.VMEM)
AWAY = pl.BlockSpec(memory_space=pl.ANY)
NUMBERS = pl.BlockSpec(memory_space=pltpu.SMEM)


def dot(left, right, contract):
    return lax.dot_general(left, right, (contract, ((), ())), preferred_element_type=F32)


def shape(dims, dtype=BF16):
    return jax.ShapeDtypeStruct(dims, dtype)


def call(kernel, *, in_specs, out_shape, near_in=(), near_out=(), **options):
    def large(value):
        return math.prod(value.shape) * value.dtype.itemsize >= 65536

    def run(*args):
        kept = []
        for i, a in enumerate(args):
            if large(a):
                a = pltpu.with_memory_space_constraint(a, pltpu.VMEM if i in near_in else pltpu.HBM)
            kept.append(a)
        single = not isinstance(out_shape, (list, tuple))
        outs = [out_shape] if single else list(out_shape)
        outs = [
            ((pltpu.VMEM if i in near_out else pltpu.HBM)(o.shape, o.dtype) if large(o) else o)
            for i, o in enumerate(outs)
        ]
        return pl.pallas_call(kernel, in_specs=in_specs, out_shape=outs[0] if single else outs, **options)(*kept)

    return run


def away(value):
    return pltpu.with_memory_space_constraint(value, pltpu.HBM)


class Here:
    def __getitem__(self, at):
        return lax.axis_index("seq")


class Order:
    def __init__(self, cycle):
        self.cycle = cycle

    def __getitem__(self, k):
        n = len(self.cycle)
        mine = lax.axis_index("dp")
        spot = sum(jnp.where(mine == place, at, 0) for at, place in enumerate(self.cycle))
        spot = lax.rem(spot + k % n, n)
        return sum(jnp.where(spot == at, place, 0) for at, place in enumerate(self.cycle))


ME = Here()


def near(value):
    return pltpu.with_memory_space_constraint(value, pltpu.VMEM)


def vmem(mib):
    return pltpu.CompilerParams(vmem_limit_bytes=mib * MIB)


def cost(flops, moved, exps=0):
    return pl.CostEstimate(flops=int(flops), bytes_accessed=int(moved), transcendentals=int(exps))


def standardise(values):
    centered = values - jnp.mean(values, axis=-1, keepdims=True)
    rate = lax.rsqrt(jnp.mean(centered * centered, axis=-1, keepdims=True) + EPSILON)
    return centered * rate, rate


def norm_back(upstream, xhat, rate, gain):
    scaled = upstream * gain
    inner = jnp.mean(scaled * xhat, axis=-1, keepdims=True)
    return rate * (scaled - jnp.mean(scaled, axis=-1, keepdims=True) - xhat * inner)


def pack_kernel(n_dp, n_seq, me_ref, qkv_ref, up_ref, *refs):
    vectors, out_refs = refs[: -2 * n_seq], refs[-2 * n_seq :]
    out_refs, up_refs = out_refs[:n_seq], out_refs[n_seq:]
    me = me_ref[0]
    part = qkv_ref.shape[0]
    cols = qkv_ref.shape[1] // (3 * n_seq)
    piece = up_ref.shape[1] // (n_dp * n_seq)
    rows = [ref[...].astype(F32)[:, i : i + part] for ref in vectors for i in range(0, ref.shape[1], part)]
    kinds = len(rows)
    rows = jnp.concatenate(rows + [jnp.zeros((128 - kinds, part), F32)], axis=0)
    rows = jnp.concatenate([rows, jnp.zeros((128, 128 - part), F32)], axis=1)
    small = rows.T[:part, :].astype(BF16)
    for mask, ref in enumerate(out_refs):
        place = me ^ mask
        for i in range(3):
            start = pl.multiple_of((i * n_seq + place) * cols, 128)
            ref[:, i * cols : (i + 1) * cols] = qkv_ref[:, pl.ds(start, cols)]
        at = 3 * cols
        ref[:, at : at + 128] = small
        for i in range(n_dp):
            start = pl.multiple_of((i * n_seq + place) * piece, 128)
            up_refs[mask][:, i * piece : (i + 1) * piece] = up_ref[:, pl.ds(start, piece)]


def pack(n_dp, n_seq, me, qkv, up, vectors):
    part = qkv.shape[0]
    wide = qkv.shape[1] // n_seq + 128
    ff = up.shape[1] // n_seq
    if up.shape[1] // (n_dp * n_seq) % 128 or part % 16:
        small = jnp.concatenate(vectors).reshape(-1, part).T
        small = jnp.pad(small, ((0, 0), (0, 128 - small.shape[1])))
        qkv_split = qkv.reshape(part, 3, n_seq, -1)
        up_split = up.reshape(part, n_dp, n_seq, -1)

        def block(place):
            q = lax.dynamic_index_in_dim(qkv_split, place, 2, keepdims=False).reshape(part, -1)
            u = lax.dynamic_index_in_dim(up_split, place, 2, keepdims=False).reshape(part, -1)
            return jnp.concatenate([q, small], axis=1), u

        blocks = [block(me[0] ^ m) for m in range(n_seq)]
        return [b[0] for b in blocks] + [b[1] for b in blocks]
    args = [qkv, up] + [v.reshape(1, -1) for v in vectors]
    args = [pltpu.with_memory_space_constraint(a, pltpu.HBM) for a in args]
    return pl.pallas_call(
        functools.partial(pack_kernel, n_dp, n_seq, ME),
        grid=(1,),
        in_specs=[pl.BlockSpec(a.shape, lambda i: (0, 0)) for a in args],
        out_specs=[pl.BlockSpec((part, wide), lambda i: (0, 0))] * n_seq
        + [pl.BlockSpec((part, ff), lambda i: (0, 0))] * n_seq,
        out_shape=[shape((part, wide))] * n_seq + [shape((part, ff))] * n_seq,
        compiler_params=vmem(8),
        name="pack",
    )(*args)


def join_one_kernel(n_seq, me_ref, *refs):
    out_ref, left_ref = refs[-2:]
    part, wide = out_ref.shape
    cols = wide // n_seq
    edge = refs[0].shape[1] - 128
    for t, ref in enumerate(refs[:-2]):
        rows = pl.ds(pl.multiple_of((me_ref[0] ^ t) * part, part), part)
        left_ref[rows, :edge] = ref[:, :edge]
        left_ref[rows, edge + cols :] = ref[:, edge:]
        left_ref[t * part : (t + 1) * part, edge : edge + cols] = out_ref[:, t * cols : (t + 1) * cols]


def join_two_kernel(n_seq, me_ref, *refs):
    down_ref, right_ref = refs[-2:]
    half = down_ref.shape[1]
    part = refs[0].shape[0]
    right_ref[:, -half:] = down_ref[...]
    for t, ref in enumerate(refs[:-2]):
        right_ref[pl.ds(pl.multiple_of((me_ref[0] ^ t) * part, part), part), :-half] = ref[...]


def join(kernel, n_seq, me, pieces, weight, wide):
    rows = pieces[0].shape[0] * n_seq
    args = list(pieces) + [away(weight)]
    return pl.pallas_call(
        functools.partial(kernel, n_seq, ME),
        grid=(1,),
        in_specs=[pl.BlockSpec(a.shape, lambda i: (0, 0)) for a in args],
        out_specs=pl.BlockSpec((rows, wide), lambda i: (0, 0)),
        out_shape=shape((rows, wide)),
        compiler_params=vmem(8),
        name="join",
    )(*args)


def join_one(n_seq, me, pieces, out_weight):
    part, edge = pieces[0].shape
    edge -= 128
    cols = out_weight.shape[1] // n_seq
    if part % 16:
        whole = flipped(dict(enumerate(pieces)), n_seq).reshape(part * n_seq, edge + 128)
        beside = jnp.moveaxis(out_weight.reshape(part, n_seq, cols), 1, 0).reshape(part * n_seq, cols)
        return jnp.concatenate([whole[:, :edge], beside, whole[:, edge:]], axis=1)
    return join(join_one_kernel, n_seq, me, pieces, out_weight, edge + cols + 128)


def join_two(n_seq, me, pieces, down_weight):
    part, wide = pieces[0].shape
    rows = part * n_seq
    if part % 16:
        whole = flipped(dict(enumerate(pieces)), n_seq).reshape(rows, wide)
        return jnp.concatenate([whole, down_weight.reshape(rows, -1)], axis=1)
    return join(join_two_kernel, n_seq, me, pieces, down_weight, wide + down_weight.shape[1])


class Blocks:
    def __init__(self, arrays, spots, rows):
        self.arrays = arrays
        self.spots = spots
        self.rows = rows

    def place(self, order_ref, i, source=None):
        k, start = self.spots[i]
        count = self.arrays[i].shape[0]
        if order_ref is None:
            return slice(k * self.rows + start, k * self.rows + start + count)
        return pl.ds(pl.multiple_of(order_ref[k] * self.rows + start, math.gcd(self.rows, start or self.rows)), count)


def ordered(order, pieces):
    rows = pieces[0].shape[0]
    if rows % 128 == 0:
        arrays, spots = [], []
        for k, piece in enumerate(pieces):
            halves = piece if isinstance(piece, tuple) else (piece,)
            for i, half in enumerate(halves):
                arrays.append(half)
                spots.append((k, i * rows // 2))
        return Blocks(arrays, spots, rows)
    whole = jnp.stack([jnp.concatenate(p, axis=0) if isinstance(p, tuple) else p for p in pieces])
    out = whole
    for k in range(len(pieces)):
        out = lax.dynamic_update_index_in_dim(out, whole[k], order[k], 0)
    return Blocks([out.reshape(-1, out.shape[-1])], [None], len(pieces) * rows)


def lay(order_ref, blocks, refs, target, cols=slice(None)):
    for i, ref in enumerate(refs):
        if blocks.spots[i] is None:
            target[...] = ref[:, cols]
        else:
            target[blocks.place(order_ref, i), :] = ref[:, cols]


def middle_columns_kernel(blocks, *refs):
    for i, ref in enumerate(refs[:-1]):
        refs[-1][blocks.place(None, i), :] = ref[...]


def middle_columns(blocks, start, cols, n_dp):
    if blocks.spots[0] is None or start % cols:
        return blocks.arrays[0][:, start : start + cols]
    total = blocks.rows * n_dp
    return call(
        functools.partial(middle_columns_kernel, blocks),
        grid=(1,),
        in_specs=[pl.BlockSpec((a.shape[0], cols), lambda i: (0, start // cols)) for a in blocks.arrays],
        out_specs=pl.BlockSpec((total, cols), lambda i: (0, 0)),
        out_shape=shape((total, cols)),
        compiler_params=vmem(4),
        name="middle_columns",
    )(*blocks.arrays)


def project_kernel(n_seq, blocks, me_ref, order_ref, lead_ref, *refs):
    n_pieces = len(blocks.arrays)
    tokens = refs[:n_seq]
    pieces = refs[n_seq : n_seq + n_pieces]
    normed_ref, q_ref, k_ref, v_ref, qkv_ref, table_ref, vec_ref, small_ref = refs[n_seq + n_pieces :]
    cols = q_ref.shape[1]

    @pl.when(pl.program_id(0) == 0)
    def _():
        lay(order_ref, blocks, pieces, qkv_ref, slice(0, 3 * cols))
        lay(order_ref, blocks, pieces, small_ref, slice(4 * cols, 4 * cols + 128))
        table_ref[...] = small_ref[...].astype(F32).T[: table_ref.shape[0], :]
        for i, kind in enumerate((0, 0, 1, 4, 5, 6, 7, 7)):
            vec_ref[i : i + 1, :] = table_ref[kind : kind + 1, :]
        vec_ref[0:1, :] = lead_ref[0:1, 0:1] * table_ref[8:9, :] + table_ref[9:10, :]

    start = jnp.concatenate([ref[...] for ref in tokens], axis=0).astype(F32) + vec_ref[0:1, :]
    xhat, _ = standardise(start)
    normed = (xhat * vec_ref[1:2, :] + vec_ref[2:3, :]).astype(BF16)
    normed_ref[...] = normed
    mine = pl.ds(pl.multiple_of(me_ref[0] * cols, 128), cols)
    found = dot(normed, qkv_ref[...], NN)
    q_ref[...] = (found[:, :cols] + table_ref[2:3, mine]).astype(BF16)
    k_ref[...] = found[:, cols : 2 * cols].astype(BF16)
    v_ref[...] = (found[:, 2 * cols :] + table_ref[3:4, mine]).astype(BF16)


def project(me, order, lead, tokens, blocks, kinds):
    rows, width = tokens[0].shape
    n_seq = len(tokens)
    cols = width // n_seq
    length = rows * n_seq
    half = rows // HALVES
    count = length // HALVES
    numbers = pl.BlockSpec(memory_space=pltpu.SMEM)

    def whole(dims):
        return pl.BlockSpec(dims, lambda i: (0, 0))

    def step(wide):
        return pl.BlockSpec((count, wide), lambda i: (i, 0))

    return call(
        functools.partial(project_kernel, n_seq, blocks, ME, order),
        near_out=(1, 2, 3),
        grid=(HALVES,),
        in_specs=[whole(lead.shape)]
        + [pl.BlockSpec((half, width), lambda i: (i, 0))] * n_seq
        + [whole(a.shape) for a in blocks.arrays],
        out_specs=[step(width), step(cols), step(cols), step(cols)]
        + [whole((width, 3 * cols)), whole((kinds, width)), whole((8, width))],
        out_shape=[shape((length, width))]
        + [shape((length, cols))] * 3
        + [shape((width, 3 * cols)), shape((kinds, width), F32), shape((8, width), F32)],
        scratch_shapes=[pltpu.VMEM((width, 128), BF16)],
        compiler_params=vmem(28),
        cost_estimate=cost(6 * length * width * cols, 10 * length * width),
        name="project",
    )(lead, *tokens, *blocks.arrays)


def key_bias(n_seq, length, me, count):
    half = length // (n_seq * HALVES)
    parts = []
    for h in range(HALVES):
        for m in block_masks(n_seq):
            at = lax.broadcasted_iota(jnp.int32, (half, 1), 0) + ((me ^ m) * HALVES + h) * half
            parts.append(jnp.where(at < count, 0.0, MASKED).astype(F32))
    return jnp.concatenate(parts, axis=0)


def attend_kernel(n_seq, me_ref, pair_at, count_ref, q_ref, k_ref, v_ref, *refs):
    out_ref, lse_ref = refs[-2:]
    bias = key_bias(n_seq, k_ref.shape[0], me_ref[0], count_ref[0:1, 0:1])
    count = q_ref.shape[0]

    def step(i, carry):
        rows = pl.ds(i * count, count)
        for half in range(2):
            cols = slice(half * HEAD_DIM, (half + 1) * HEAD_DIM)
            mine = slice(pair_at * PAIR + cols.start, pair_at * PAIR + cols.stop)
            scores = dot(k_ref[:, mine], q_ref[rows, mine] * SCALE, NT) + bias
            top = jnp.max(scores, axis=0, keepdims=True)
            weights = jnp.exp(scores - top)
            total = jnp.sum(weights, axis=0, keepdims=True)
            mixed = dot(v_ref[:, mine], weights.astype(BF16), TN) / total
            out_ref[rows, cols] = mixed.T.astype(BF16)
            lse_ref[half, :, rows] = top + jnp.log(total)
        return carry

    step(0, 0)


def attend(n_seq, pair_at, me, valid, q, k, v, earlier):
    length, cols = q.shape
    pair = pl.BlockSpec((length, PAIR), lambda g: (0, pair_at))
    given = [] if earlier is None else [earlier]
    return call(
        functools.partial(attend_kernel, n_seq, ME, pair_at),
        near_in=(1, 2, 3),
        grid=(1,),
        in_specs=[pl.BlockSpec(valid.shape, lambda g: (0, 0)), NEAR, NEAR, NEAR] + [AWAY] * len(given),
        out_specs=[pair, pl.BlockSpec((2, 1, length), lambda g: (0, 0, 0))],
        out_shape=[shape((length, cols)), shape((2, 1, length), F32)],
        input_output_aliases={4: 0} if given else {},
        compiler_params=vmem(32),
        cost_estimate=cost(4 * length * length * PAIR, 8 * length * PAIR, 2 * length * length),
        name="attend",
    )(valid, q, k, v, *given)


def attend_back_kernel(first, n_seq, *refs):
    count_ref, q_ref, k_ref, v_ref, lse_ref, out_w_ref = refs[:6]
    grads = refs[6 : 6 + n_seq]
    rest = refs[6 + n_seq :]
    if first:
        dq_ref, dk_ref, dv_ref = rest
    else:
        dq_in, dk_in, dv_in, whole_ref, q_out, k_out, v_out, sems = rest
    length = k_ref.shape[0]
    count = q_ref.shape[0]
    pair = pl.program_id(0)
    spot = pair % 2
    bias = key_bias(n_seq, length, ME[0], count_ref[0:1, 0:1])
    upstream = jnp.concatenate([dot(ref[...], out_w_ref[...], NT).astype(BF16) for ref in grads], axis=0)
    for half in range(2):
        cols = slice(half * HEAD_DIM, (half + 1) * HEAD_DIM)
        k = k_ref[:, cols]
        q = q_ref[:, cols] * SCALE
        g = upstream[:, cols]
        probs = jnp.exp(dot(k, q, NT) + bias - lse_ref[half])
        dv = dot(probs.astype(BF16), g, NN)
        term = probs * dot(v_ref[:, cols], g, NT)
        grad = (term - probs * jnp.sum(term, axis=0, keepdims=True)).astype(BF16)
        dk = dot(grad, q, NN)
        dq = (dot(k, grad, TN) * SCALE).T.astype(BF16)
        if first:
            dq_ref[:, cols] = dq
            dk_ref[:, cols] = dk
            dv_ref[:, cols] = dv
        else:
            q_out[spot, :count, cols] = dq_in[:, cols]
            q_out[spot, count:, cols] = dq
            k_out[spot, :, cols] = (dk + dk_in[:, cols]).astype(BF16)
            v_out[spot, :, cols] = (dv + dv_in[:, cols]).astype(BF16)
    if first:
        return
    pairs = pl.num_programs(0)

    def copies(at):
        found = []
        for i, source in enumerate((q_out, k_out, v_out)):
            start = pl.multiple_of((i * pairs + at) * PAIR, PAIR)
            target = whole_ref.at[:, pl.ds(start, PAIR)]
            found.append(pltpu.make_async_copy(source.at[at % 2], target, sems.at[at % 2, i]))
        return found

    for copy in copies(pair):
        copy.start()

    @pl.when(pair > 0)
    def _():
        for copy in copies(pair - 1):
            copy.wait()

    @pl.when(pair == pairs - 1)
    def _():
        for copy in copies(pair):
            copy.wait()


def attend_back(at, me, valid, q, k, v, lse, out_mine, grads, earlier):
    length, cols = k.shape
    width = out_mine.shape[1]
    count = length // HALVES
    pair = pl.BlockSpec((length, PAIR), lambda g: (0, g))
    mine = pl.BlockSpec((count, PAIR), lambda g: (at, g))
    here = pl.BlockSpec((count, PAIR), lambda g: (0, g))
    first = earlier is None
    near_out = () if first else (0,)
    in_specs = [pl.BlockSpec(valid.shape, lambda g: (0, 0))] + [
        mine,
        pair,
        pair,
        pl.BlockSpec((2, 1, count), lambda g: (g, 0, at)),
        pl.BlockSpec((PAIR, width), lambda g: (g, 0)),
    ]
    in_specs += [pl.BlockSpec(piece.shape, lambda g: (0, 0)) for piece in grads]
    args = [valid, q, k, v, lse, out_mine] + list(grads)
    if first:
        out_specs = [here, pair, pair]
        out_shape = [shape((count, cols))] + [shape((length, cols), F32)] * 2
        scratch = []
    else:
        in_specs += [here, pair, pair]
        args += list(earlier)
        out_specs = AWAY
        out_shape = shape((length, 3 * cols))
        scratch = [pltpu.VMEM((2, length, PAIR), BF16)] * 3 + [pltpu.SemaphoreType.DMA((2, 3))]
    return call(
        functools.partial(attend_back_kernel, first, len(grads)),
        near_in=range(6, 6 + len(grads)),
        near_out=near_out,
        grid=(cols // PAIR,),
        in_specs=in_specs,
        out_specs=out_specs,
        out_shape=out_shape,
        scratch_shapes=scratch,
        compiler_params=vmem(36),
        cost_estimate=cost(10 * count * length * cols, 8 * length * cols, count * length * cols // HEAD_DIM),
        name="attend_back",
    )(*args)


def middle_kernel(n_seq, n_out, me_ref, order_ref, *refs):
    tokens, refs = refs[:n_seq], refs[n_seq:]
    outs, refs = refs[:n_out], refs[n_out:]
    att, refs = refs[:n_seq], refs[n_seq:]
    vec_ref, normed_ref, middle_ref, mine_ref, out_ref, outs_here, att_here, tokens_here, sems = refs
    masks = block_masks(n_seq)
    me = me_ref[0]
    cols, width = mine_ref.shape
    half = tokens[0].shape[0] // HALVES
    block = n_seq * half // 2
    got_out = fetch([(ref, outs_here.at[i]) for i, ref in enumerate(outs)], sems.at[0])
    got_att = fetch([(ref, att_here.at[i]) for i, ref in enumerate(att)], sems.at[1])
    got_tokens = fetch([(ref, tokens_here.at[i]) for i, ref in enumerate(tokens)], sems.at[2])
    got_out()
    if n_out == 1:
        out_ref[...] = outs_here[0]
    else:
        n_dp = len(order_ref.cycle)
        part = width // (n_dp * n_seq)
        for i, mask in enumerate(range(n_seq)):
            for k in range(n_dp):
                start = pl.multiple_of((order_ref[k] * n_seq + (me ^ mask)) * part, part)
                for t in range(n_seq):
                    at = (k * n_seq + t) * part
                    out_ref[pl.ds(start, part), t * cols : (t + 1) * cols] = outs_here[i, at : at + part, :]
    sent = fetch([(out_ref.at[pl.ds(pl.multiple_of(me * cols, cols), cols), :], mine_ref)], sems.at[3])
    got_att()
    got_tokens()

    def step(h, carry):
        for side in range(2):
            places = range(side * n_seq // 2, (side + 1) * n_seq // 2)
            rows = pl.ds(pl.multiple_of(h * half, half), half)
            middle = jnp.concatenate([tokens_here[i, rows, :] for i in places], axis=0).astype(F32)
            middle = middle + vec_ref[0:1, :] + vec_ref[3:4, :]
            for i, mask in enumerate(masks):
                at = pl.multiple_of((me ^ mask) * cols, cols)
                first = (h * 2 + (side ^ (mask & 1))) * block
                spots = [pl.ds(pl.multiple_of(first + (t ^ (mask >> 1)) * half, half), half) for t in range(n_seq // 2)]
                found = jnp.concatenate([att_here[i, spot, :] for spot in spots], axis=0)
                middle = middle + dot(found, out_ref[pl.ds(at, cols), :], NN)
            xhat, _ = standardise(middle)
            mine = pl.ds(pl.multiple_of((h * 2 + side) * block, block), block)
            normed_ref[mine, :] = (xhat * vec_ref[4:5, :] + vec_ref[5:6, :]).astype(BF16)
            if side == 0:
                middle_ref[rows, :] = middle[:half, :]
        return carry

    lax.fori_loop(0, HALVES, step, 0)
    sent()


def middle_norm(me, order, tokens, att, outs, vecs):
    rows, width = tokens[0].shape
    n_seq = len(tokens)
    length = rows * n_seq
    cols = width // n_seq
    count = max(n_seq, len(outs))
    return call(
        functools.partial(middle_kernel, n_seq, len(outs), ME, order),
        near_in=(2 * n_seq + len(outs),),
        near_out=(0, 1),
        in_specs=[AWAY] * (2 * n_seq + len(outs)) + [NEAR],
        out_specs=[NEAR, NEAR, AWAY],
        out_shape=[shape((length, width)), shape((rows, width), F32), shape((cols, width))],
        scratch_shapes=[
            pltpu.VMEM((width, width), BF16),
            pltpu.VMEM((len(outs),) + outs[0].shape, BF16),
            pltpu.VMEM((n_seq, length, cols), BF16),
            pltpu.VMEM((n_seq, rows, width), BF16),
            pltpu.SemaphoreType.DMA((4, count)),
        ],
        compiler_params=vmem(24),
        cost_estimate=cost(2 * length * width * width, 10 * length * width),
        name="middle_norm",
    )(*tokens, *outs, *att, vecs)


def fetch(pairs, sems):
    copies = [pltpu.make_async_copy(a, b, sems.at[i]) for i, (a, b) in enumerate(pairs)]
    for copy in copies:
        copy.start()

    def wait():
        for copy in copies:
            copy.wait()

    return wait


def placed(order_ref, blocks, refs, target, start):
    if blocks.spots[0] is None:
        return [(refs[0], target)]
    cols = pl.ds(start, target.shape[1])
    return [(ref.at[:, cols], target.at[blocks.place(order_ref, i), :]) for i, ref in enumerate(refs)]


def up_kernel(ups, downs, block, order_ref, normed_ref, bias_ref, *refs):
    up_pieces, refs = refs[: len(ups.arrays)], refs[len(ups.arrays) :]
    if downs is None:
        downs, down_pieces = ups, up_pieces
    else:
        down_pieces, refs = refs[: len(downs.arrays)], refs[len(downs.arrays) :]
    up_ref, down_ref, hidden_ref, slope_ref, up_sems, down_sems = refs
    here = fetch(placed(order_ref, ups, up_pieces, up_ref, 0), up_sems)
    later = fetch(placed(order_ref, downs, down_pieces, down_ref, up_ref.shape[1]), down_sems)
    here()

    def step(i, carry):
        cols = pl.ds(pl.multiple_of(i * block, block), block)
        pre = dot(normed_ref[...], up_ref[:, cols], NN) + bias_ref[:, cols]
        phi = 0.5 + 0.5 * lax.erf(pre * math.sqrt(0.5))
        hidden_ref[:, cols] = (pre * phi).astype(BF16)
        slope_ref[:, cols] = phi + pre * (jnp.exp(-0.5 * pre * pre) * (1.0 / math.sqrt(2.0 * math.pi)))
        return carry

    lax.fori_loop(0, up_ref.shape[1] // block, step, 0)
    later()


def up_part(order, normed, bias, ups, downs, block=256):
    length, width = normed.shape
    ff = bias.shape[1]
    pieces = list(ups.arrays) + (list(downs.arrays) if downs is not None else [])
    return call(
        functools.partial(up_kernel, ups, downs, block, order),
        near_in=(0,),
        near_out=(0, 1, 2, 3),
        in_specs=[NEAR, NEAR] + [AWAY] * len(pieces),
        out_specs=[NEAR] * 4,
        out_shape=[shape((width, ff)), shape((ff, width)), shape((length, ff)), shape((length, ff), F32)],
        scratch_shapes=[pltpu.SemaphoreType.DMA((len(ups.arrays),)), pltpu.SemaphoreType.DMA((len((downs or ups).arrays),))],
        compiler_params=vmem(12),
        cost_estimate=cost(2 * length * width * ff, 8 * width * ff, 2 * length * ff),
        name="up_part",
    )(normed, bias, *pieces)


def mlp_back_kernel(first, at, block, n_grads, hidden_ref, slope_ref, up_ref, down_ref, *refs):
    grads, refs = refs[:n_grads], refs[n_grads:]
    if not first:
        refs = refs[2:]
    pre_ref, grad_ref, keep_ref, send_ref, branch_keep, branch_send, sum_ref, sems = refs
    count = 2 * keep_ref.shape[0]
    half = count // n_grads
    spots = [pl.ds(at * count + i * half, half) for i in range(n_grads)]
    ready = fetch([(ref, grad_ref.at[spot, :]) for ref, spot in zip(grads, spots)], sems)
    rows = pl.ds(at * count, count)
    side = keep_ref.shape[0]
    sides = ((0, keep_ref, branch_keep), (side, send_ref, branch_send))
    for start, _, branch_out in sides:
        branch_out[...] = dot(hidden_ref[pl.ds(at * count + start, side), :], down_ref[...], NN).astype(BF16)
    ready()

    def step(i, carry):
        cols = pl.ds(pl.multiple_of(i * block, block), block)
        grad = (slope_ref[rows, cols] * dot(grad_ref[rows, :], down_ref[cols, :], NT)).astype(BF16)
        pre_ref[rows, cols] = grad
        sum_ref[:, cols] = jnp.sum(grad.astype(F32), axis=0, keepdims=True)
        return carry

    lax.fori_loop(0, up_ref.shape[1] // block, step, 0)
    for start, back_out, _ in sides:
        back_out[...] = dot(pre_ref[pl.ds(at * count + start, side), :], up_ref[...], NT).astype(BF16)


def mlp_back(at, hidden, slope, up, down, grads, earlier, block=512):
    width = up.shape[0]
    length, ff = hidden.shape
    count = length // HALVES
    first = earlier is None
    given = 4 + len(grads)
    return call(
        functools.partial(mlp_back_kernel, first, at, min(block, ff // 2), len(grads)),
        near_in=range(given + 2),
        near_out=(0, 1, 2, 3, 4, 5),
        in_specs=[NEAR] * 4 + [AWAY] * len(grads) + ([] if first else [NEAR] * 2),
        out_specs=[NEAR] * 7,
        out_shape=[shape((length, ff)), shape((length, width))]
        + [shape((count // 2, width))] * 4
        + [shape((1, ff), F32)],
        scratch_shapes=[pltpu.SemaphoreType.DMA((len(grads),))],
        input_output_aliases={} if first else {given: 0, given + 1: 1},
        compiler_params=vmem(16),
        cost_estimate=cost(6 * count * width * ff, 8 * width * ff),
        name="mlp_back",
    )(hidden, slope, up, down, *grads, *([] if first else earlier))


def second_back_kernel(at, middle_ref, keep_ref, near_ref, far_ref, vec_ref, out_ref, grad_ref, one_ref, sum_ref, held, sems):
    half = far_ref.shape[0]
    ready = fetch([(out_ref, held)], sems)
    upstream = keep_ref[:half, :].astype(F32) + near_ref[:half, :].astype(F32) + far_ref[...].astype(F32)
    xhat, rate = standardise(middle_ref[at * half : (at + 1) * half, :])
    back = norm_back(upstream, xhat, rate, vec_ref[4:5, :])
    ready()
    grad_out = held[...].astype(F32)
    grad = grad_out + back
    one = grad.astype(BF16)
    grad_ref[...] = grad
    one_ref[...] = one
    sums = [upstream * xhat, upstream, one.astype(F32), grad_out, grad]
    sum_ref[...] = jnp.concatenate([jnp.sum(s, axis=0, keepdims=True) for s in sums], axis=0)


def second_back(at, middle_own, keep, near_part, far_part, grad_out, vecs):
    half, width = far_part.shape
    return call(
        functools.partial(second_back_kernel, at),
        near_in=(0, 1, 2, 3, 4),
        near_out=(0, 1),
        in_specs=[NEAR] * 5 + [AWAY],
        out_specs=[NEAR] * 3,
        out_shape=[shape((half, width), F32), shape((half, width)), shape((5, width), F32)],
        scratch_shapes=[pltpu.VMEM((half, width), BF16), pltpu.SemaphoreType.DMA((1,))],
        compiler_params=vmem(10),
        cost_estimate=cost(30 * half * width, 16 * half * width),
        name="second_back",
    )(middle_own, keep, near_part, far_part, vecs, grad_out)


def first_grad_kernel(n_seq, grad_ref, qkv_ref, vec_ref, *refs):
    tokens, (keep_ref, send_ref, sum_ref, last_ref) = refs[:n_seq], refs[n_seq:]
    step = pl.program_id(0)
    grad = grad_ref[...]
    total = dot(grad, qkv_ref[...], NT)
    column = jnp.sum(grad.astype(F32), axis=0, keepdims=True)
    sides = zip(tokens[: n_seq // 2], tokens[n_seq // 2 :])
    start = jnp.concatenate([jnp.where(step % 2 == 0, a[...], b[...]) for a, b in sides], axis=0).astype(F32)
    xhat, rate = standardise(start + vec_ref[0:1, :])
    back = norm_back(total, xhat, rate, vec_ref[1:2, :])
    last = jnp.concatenate([jnp.sum(t, axis=0, keepdims=True) for t in (total * xhat, total, back)], axis=0)
    total = total.astype(BF16)

    @pl.when(step == 0)
    def _():
        sum_ref[...] = column
        last_ref[...] = last

    @pl.when(step > 0)
    def _():
        sum_ref[...] += column
        last_ref[...] += last

    @pl.when(step % 2 == 0)
    def _():
        keep_ref[...] = total

    @pl.when(step % 2 == 1)
    def _():
        send_ref[...] = total


def first_grad(grad_qkv, qkv, vecs, tokens):
    length, wide = grad_qkv.shape
    n_seq = len(tokens)
    half = tokens[0].shape[0] // HALVES
    width = qkv.shape[0]
    block = length // (2 * HALVES)
    kept = pl.BlockSpec((block, width), lambda i: (i // 2, 0))
    return call(
        functools.partial(first_grad_kernel, n_seq),
        near_in=(1,),
        near_out=(0, 1),
        grid=(2 * HALVES,),
        in_specs=[
            pl.BlockSpec((block, wide), lambda i: (i, 0)),
            pl.BlockSpec(qkv.shape, lambda i: (0, 0)),
            pl.BlockSpec(vecs.shape, lambda i: (0, 0)),
        ]
        + [pl.BlockSpec((half, width), lambda i: (i // 2, 0))] * n_seq,
        out_specs=[kept, kept, pl.BlockSpec((1, wide), lambda i: (0, 0)), pl.BlockSpec((3, width), lambda i: (0, 0))],
        out_shape=[shape((length // 2, width))] * 2 + [shape((1, wide), F32), shape((3, width), F32)],
        compiler_params=vmem(20),
        cost_estimate=cost(length * wide * width, 4 * length * width),
        name="first_grad",
    )(grad_qkv, qkv, vecs, *tokens)


def out_terms_kernel(pairs, *refs):
    att, out_ref = refs[:pairs], refs[-1]
    total = None
    at = 0
    for ref in refs[pairs:-1]:
        rows = ref.shape[0]
        term = dot(jnp.concatenate([a[at : at + rows, :] for a in att], axis=1), ref[...], TN)
        total = term if total is None else total + term
        at += rows
    n_dp, rows, wide = out_ref.shape
    if wide == total.shape[1]:
        out_ref[...] = total.astype(BF16).reshape(out_ref.shape)
        return
    part = total.shape[0] // n_dp
    for i in range(n_dp):
        for t in range(rows // part):
            piece = total[i * part : (i + 1) * part, t * wide : (t + 1) * wide]
            out_ref[i, t * part : (t + 1) * part, :] = piece.astype(BF16)


def out_terms(att, grads, n_dp, rows):
    length = att[0].shape[0]
    cols = len(att) * att[0].shape[1]
    width = grads[0].shape[1]
    dims = (n_dp, rows, cols * width // (n_dp * rows))
    args = list(att) + list(grads)
    return call(
        functools.partial(out_terms_kernel, len(att)),
        near_in=range(len(att), len(att) + len(grads)),
        near_out=(0,),
        grid=(1,),
        in_specs=[pl.BlockSpec(a.shape, lambda i: (0, 0)) for a in args],
        out_specs=pl.BlockSpec(dims, lambda i: (0, 0, 0)),
        out_shape=shape(dims),
        compiler_params=vmem(16),
        cost_estimate=cost(2 * length * cols * width, 2 * length * width),
        name="out_terms",
    )(*args)


def first_back_kernel(keep_ref, near_ref, far_a, far_b, a_ref, b_ref, vec_ref, tokens_ref, out_ref, held, made, sems):
    ready = fetch([(tokens_ref, held)], sems)
    half = far_a.shape[0]
    size = keep_ref.shape[0] // HALVES
    copies = []
    for h, (far_ref, grad_ref) in enumerate(((far_a, a_ref), (far_b, b_ref))):
        mine = slice(h * size, h * size + half)
        upstream = keep_ref[mine, :].astype(F32) + near_ref[mine, :].astype(F32) + far_ref[...].astype(F32)
        if h == 0:
            ready()
        rows = slice(h * half, (h + 1) * half)
        xhat, rate = standardise(held[rows, :].astype(F32) + vec_ref[0:1, :])
        grad = grad_ref[...] + norm_back(upstream, xhat, rate, vec_ref[1:2, :])
        made[rows, :] = grad.astype(BF16)
        copy = pltpu.make_async_copy(made.at[pl.ds(h * half, half), :], out_ref.at[pl.ds(h * half, half), :], sems.at[1 + h])
        copy.start()
        copies.append(copy)
    for copy in copies:
        copy.wait()


def first_back(tokens_own, keep, near_part, far_a, far_b, grad_a, grad_b, vecs):
    rows, width = tokens_own.shape
    return call(
        first_back_kernel,
        near_in=range(7),
        in_specs=[NEAR] * 7 + [AWAY],
        out_specs=AWAY,
        out_shape=shape((rows, width)),
        scratch_shapes=[pltpu.VMEM((rows, width), BF16)] * 2 + [pltpu.SemaphoreType.DMA((1 + HALVES,))],
        compiler_params=vmem(10),
        cost_estimate=cost(30 * rows * width, 16 * rows * width),
        name="first_back",
    )(keep, near_part, far_a, far_b, grad_a, grad_b, vecs, tokens_own)


def block_masks(size):
    return [m for m in range(size) if not m & 1] + [m for m in range(size) if m & 1]


def far_bits(size):
    bits, bit = [], 2
    while bit < size:
        bits.append(bit)
        bit *= 2
    return bits


def tied(*values):
    return lax.optimization_barrier(values)


class Line:
    def __init__(self, token):
        self.token = token

    def slot(self, sends=(), work=lambda: (), inputs=(), begin=(), end=()):
        values, begun, inputs, token = tied(
            [s[0] for s in sends], [s[0] for s in begin], list(inputs), self.token
        )
        found = [lax.ppermute(value, s[1], s[2]) for value, s in zip(values, sends)]
        started = [lax.ppermute(value, s[1], s[2]) for value, s in zip(begun, begin)]
        found, done, ended, self.token = tied(found, work(*inputs), list(end), token)
        return found, done, started, ended


def swap(value, bit, size):
    return (value, "seq", [(i, i ^ bit) for i in range(size)])


def cycle(n_dp):
    wide = int(round(math.sqrt(n_dp / 2)))
    if wide < 2 or wide * (n_dp // wide) != n_dp or (n_dp // wide) % 2:
        return list(range(n_dp))
    high = n_dp // wide
    order = [z * wide for z in range(high)]
    for turn, z in enumerate(range(high - 1, -1, -1)):
        line = list(range(1, wide))
        order += [z * wide + y for y in (line[::-1] if turn % 2 else line)]
    return order


class Ring:
    def __init__(self, n_dp):
        self.n = n_dp
        order = cycle(n_dp)
        where = np.argsort(np.array(order))
        table = np.array([[order[(where[d] + k) % n_dp] for k in range(n_dp)] for d in range(n_dp)], np.int32)
        row = lax.dynamic_index_in_dim(jnp.asarray(table), lax.axis_index("dp"), 0, keepdims=False)
        self.order = row
        self.steps = Order(order)
        self.ahead = [(order[i], order[(i + 1) % n_dp]) for i in range(n_dp)]
        self.back = [(order[i], order[(i - 1) % n_dp]) for i in range(n_dp)]
        self.far = n_dp // 2
        self.near = (n_dp - 1) // 2


class Gather:
    def __init__(self, ring, own):
        self.ring = ring
        self.step = 0
        self.pending = None
        self.ahead = self.back = own
        self.pieces = [own] + [None] * (ring.n - 1)

    def sends(self):
        self.step += 1
        ahead, back = self.ahead, self.back
        if self.step == self.ring.far:
            half = ahead.shape[0] // 2
            ahead, back = ahead[:half], back[half:]
        return [(ahead, "dp", self.ring.ahead), (back, "dp", self.ring.back)]

    def take(self, found):
        self.ahead, self.back = found
        if self.step == self.ring.far:
            self.pieces[self.step] = tuple(found)
        else:
            self.pieces[-self.step], self.pieces[self.step] = found

    @property
    def left(self):
        return self.ring.far - self.step


def ring_kernel(adds, *refs):
    count = len(adds)
    values = list(refs[1 + count : -count])
    for i, (add, out) in enumerate(zip(adds, refs[-count:])):
        total = refs[1 + i][0].astype(F32)
        for _ in range(add):
            total = total + values.pop(0)[...].astype(F32)
        out[...] = total.astype(out.dtype)


def ring_blocks(order, items, dtype=BF16):
    n_dp = order.shape[0]
    args, in_specs, outs, out_specs = [], [], [], []
    for terms, k, _ in items:
        dims = terms.shape[1:]
        in_specs.append(pl.BlockSpec((1,) + dims, lambda i, at, k=k % n_dp: (at[k], 0, 0)))
        out_specs.append(pl.BlockSpec(dims, lambda i, at: (0, 0)))
        outs.append(shape(dims, dtype))
        args.append(terms)
    for _, _, values in items:
        for value in values:
            in_specs.append(pl.BlockSpec(value.shape, lambda i, at: (0, 0)))
            args.append(value)
    return pl.pallas_call(
        functools.partial(ring_kernel, [len(i[2]) for i in items]),
        grid_spec=pltpu.PrefetchScalarGridSpec(
            num_scalar_prefetch=1, grid=(1,), in_specs=in_specs, out_specs=out_specs
        ),
        out_shape=outs,
        compiler_params=vmem(16),
        name="ring_blocks",
    )(order, *args)


def table_kernel(me_ref, lead_ref, a_ref, b_ref, last_ref, ua_ref, ub_ref, column_ref, out_ref):
    me = me_ref[0]
    width = out_ref.shape[1]
    cols = column_ref.shape[1] // 3
    extra = ua_ref.shape[1] * (width // cols) // width
    part = 128 // extra
    sums = a_ref[...] + b_ref[...]
    last = last_ref[...]
    column = column_ref[...]
    out_ref[...] = jnp.zeros_like(out_ref)
    out_ref[0:2, :] = last[0:2]
    mine = pl.ds(pl.multiple_of(me * cols, 128), cols)
    out_ref[2:3, mine] = column[:, :cols]
    out_ref[3:4, mine] = column[:, 2 * cols :]
    out_ref[4:5, :] = sums[2:3]
    out_ref[5:7, :] = sums[0:2]
    out_ref[7:8, :] = sums[3:4]
    start = last[2:3] + sums[4:5]
    out_ref[8:9, :] = lead_ref[0:1, 0:1] * start
    out_ref[9:10, :] = start
    up = jnp.broadcast_to(ua_ref[...] + ub_ref[...], (8, width))
    here = lax.broadcasted_iota(jnp.int32, (1, width), 1) % 128 // part == me
    for k in range(extra):
        moved = pltpu.roll(up, ((me - k) * part + width) % width, 1)
        out_ref[10 + k : 11 + k, :] = jnp.where(here, moved[0:1, :], 0.0)


def small_table(me, lead, *args):
    width = args[0].shape[1]
    return pl.pallas_call(
        functools.partial(table_kernel, ME),
        grid=(1,),
        in_specs=[pl.BlockSpec(a.shape, lambda i: (0, 0)) for a in (lead, *args)],
        out_specs=pl.BlockSpec((16, width), lambda i: (0, 0)),
        out_shape=shape((16, width), F32),
        compiler_params=vmem(4),
        name="small_table",
    )(lead, *args)


def halve_kernel(bit, *refs):
    mine_ref, other_ref = refs[-2:]
    wide = mine_ref.shape[1]
    side = lax.rem(lax.div(lax.axis_index("dp"), bit), 2)
    for at, target in ((side, mine_ref), (1 - side, other_ref)):
        for i in range(wide // 128):
            total = 0.0
            for ref in refs[:-2]:
                total = total + ref[:, pl.ds(pl.multiple_of((2 * i + at) * 128, 128), 128)]
            target[:, i * 128 : (i + 1) * 128] = total


def halve(bit, values):
    rows, wide = values[0].shape
    return pl.pallas_call(
        functools.partial(halve_kernel, bit),
        in_specs=[NEAR] * len(values),
        out_specs=[NEAR] * 2,
        out_shape=[shape((rows, wide // 2), F32)] * 2,
        compiler_params=vmem(2),
        name="halve",
    )(*values)


def owner_kernel(count, order_ref, me_ref, term_ref, *refs):
    part = refs[-1].shape[0]
    outs = refs[-count:]
    for mask, out in enumerate(outs):
        rows = pl.ds(pl.multiple_of((me_ref[0] ^ mask) * part, part), part)
        total = term_ref[0, rows, :].astype(F32)
        for ref in refs[:-count]:
            total = total + ref[rows, :].astype(F32)
        out[...] = total.astype(BF16)


def owner_blocks(order, me, terms, values, n_seq):
    _, rows, wide = terms.shape
    part = rows // n_seq
    if part % 16:
        (total,) = ring_blocks(order, [(terms, 0, values)])
        blocks = total.reshape(n_seq, part, wide)
        return [lax.dynamic_index_in_dim(blocks, me[0] ^ m, 0, keepdims=False) for m in range(n_seq)]
    return pl.pallas_call(
        functools.partial(owner_kernel, n_seq),
        grid_spec=pltpu.PrefetchScalarGridSpec(
            num_scalar_prefetch=2,
            grid=(1,),
            in_specs=[pl.BlockSpec((1, rows, wide), lambda i, at, me: (at[0], 0, 0))]
            + [pl.BlockSpec((rows, wide), lambda i, at, me: (0, 0))] * len(values),
            out_specs=[pl.BlockSpec((part, wide), lambda i, at, me: (0, 0))] * n_seq,
        ),
        out_shape=[shape((part, wide))] * n_seq,
        compiler_params=vmem(8),
        name="owner_blocks",
    )(order, me, terms, *values)


def unpack_kernel(groups, me_ref, out_ref, *refs):
    outs, last_ref = refs[-len(groups) - 1 : -1], refs[-1]
    pieces = refs[: -len(groups) - 1]
    part = last_ref.shape[0]
    cols = out_ref.shape[1]
    for t in range(out_ref.shape[0] // part):
        last_ref[:, t * cols : (t + 1) * cols] = out_ref[t * part : (t + 1) * part, :].astype(F32)
    n_seq = len(pieces)
    for mask, ref in enumerate(pieces):
        at = 0
        for count, out in zip(groups, outs):
            wide = out.shape[1] // (count * n_seq)
            for i in range(count):
                start = pl.multiple_of((i * n_seq + (me_ref[0] ^ mask)) * wide, 128)
                out[:, pl.ds(start, wide)] = ref[:, at : at + wide].astype(F32)
                at += wide


def unpack(groups, widths, pieces, out_block):
    part = pieces[0].shape[0]
    n_seq = len(pieces)
    if any((wide // n_seq // count) % 128 for count, wide in zip(groups, widths)):
        whole = flipped(dict(enumerate(pieces)), n_seq)
        outs, at = [], 0
        for count, wide in zip(groups, widths):
            mine = whole[:, :, at : at + wide // n_seq].reshape(n_seq, part, count, -1)
            outs.append(jnp.moveaxis(mine, 0, 2).reshape(part, wide).astype(F32))
            at += wide // n_seq
        last = out_block.reshape(-1, part, out_block.shape[1])
        return *outs, jnp.moveaxis(last, 0, 1).reshape(part, -1).astype(F32)
    full = list(widths) + [out_block.size // part]
    return pl.pallas_call(
        functools.partial(unpack_kernel, groups, ME),
        grid=(1,),
        in_specs=[pl.BlockSpec(out_block.shape, lambda i: (0, 0))]
        + [pl.BlockSpec(pieces[0].shape, lambda i: (0, 0))] * n_seq,
        out_specs=[pl.BlockSpec((part, wide), lambda i: (0, 0)) for wide in full],
        out_shape=[shape((part, wide), F32) for wide in full],
        compiler_params=vmem(8),
        name="unpack",
    )(out_block, *pieces)


class Scatter:
    def __init__(self, ring, terms):
        self.ring = ring
        self.terms = terms
        self.step = 0
        self.pending = None
        count = len(terms)
        found = ring_blocks(
            ring.order, [(t, ring.far, ()) for t in terms] + [(t, -ring.near, ()) for t in terms]
        )
        self.ahead, self.back = found[:count], found[count:]

    def sends(self):
        self.step += 1
        found = [(v, "dp", self.ring.ahead) for v in self.ahead]
        if self.step > self.ring.far - self.ring.near:
            found += [(v, "dp", self.ring.back) for v in self.back]
        return found

    def take(self, found):
        count = len(self.terms)
        left = self.ring.far - self.step
        ahead, back = found[:count], found[count:]
        if left:
            items = [(t, left, (v,)) for t, v in zip(self.terms, ahead)]
            items += [(t, -left, (v,)) for t, v in zip(self.terms, back)]
            found = ring_blocks(self.ring.order, items)
            ahead, back = found[:count], found[count:]
        self.ahead = ahead
        if back:
            self.back = back

    @property
    def left(self):
        return self.ring.far - self.step

    def total(self, dtype=F32):
        items = [(t, 0, (a, b)) for t, a, b in zip(self.terms, self.ahead, self.back)]
        return ring_blocks(self.ring.order, items, dtype)


def joint_kernel(items, order_ref, q_ref, o_ref, *refs):
    values, outs = list(refs[: -len(items)]), refs[-len(items) :]
    _, rows, edge = q_ref.shape
    _, part, width = o_ref.shape
    for (k, low, high, added), target in zip(items, outs):
        cols = target.shape[1] - edge
        value = values.pop(0) if added else None
        at = order_ref[k]

        def put(source, from_rows, row, lanes):
            cuts = sorted({row, row + len(from_rows)} | ({max(row, min(c, row + len(from_rows))) for c in added} if added else set()))
            for a, b in zip(cuts, cuts[1:]):
                total = source[from_rows[a - row] : from_rows[b - row - 1] + 1]
                if added and added[0] <= a and b <= added[1]:
                    total = (total.astype(F32) + value[a - added[0] : b - added[0], lanes].astype(F32)).astype(BF16)
                target[a - low : b - low, lanes] = total

        put(q_ref.at[at, :, slice(0, edge)], range(low, high), low, slice(0, edge))
        for t in range(rows // part):
            a, b = max(low, t * part), min(high, (t + 1) * part)
            if a < b:
                lanes = slice(t * cols, (t + 1) * cols)
                put(o_ref.at[at, :, lanes], range(a - t * part, b - t * part), a, slice(edge, edge + cols))


class JointScatter:
    def __init__(self, ring, qkv, out):
        self.ring = ring
        self.qkv = qkv
        self.out = out
        self.step = 0
        self.pending = None
        rows = qkv.shape[1]
        if ring.far:
            far = ring.far
            self.ahead, self.back = self.blocks([(far, 0, rows // 2, None), (far, rows // 2, rows, None)], ())

    def blocks(self, items, values):
        n_dp, rows, edge = self.qkv.shape
        _, part, width = self.out.shape
        wide = edge + width * part // rows
        items = [(k % n_dp, low, high, added) for k, low, high, added in items]
        return call(
            functools.partial(joint_kernel, items, self.ring.steps),
            near_in=range(2 + len(values)),
            near_out=range(len(items)),
            in_specs=[NEAR] * (2 + len(values)),
            out_specs=[NEAR] * len(items),
            out_shape=[shape((high - low, wide)) for _, low, high, _ in items],
            compiler_params=vmem(4),
            name="joint_blocks",
        )(self.qkv, self.out, *values)

    def sends(self):
        self.step += 1
        return [(self.ahead, "dp", self.ring.ahead), (self.back, "dp", self.ring.back)]

    def take(self, found):
        left = self.ring.far - self.step
        rows = self.qkv.shape[1]
        if left:
            spans = ((0, rows // 2), (rows // 2, rows)) if self.step == 1 else ((0, rows), (0, rows))
            found = self.blocks([(sign * left, 0, rows, span) for sign, span in zip((1, -1), spans)], found)
        self.ahead, self.back = found

    @property
    def left(self):
        return self.ring.far - self.step

    def total(self, me, n_seq, dtype=BF16, beside=()):
        n_dp, rows, edge = self.qkv.shape
        _, part, width = self.out.shape
        wide = edge + width * part // rows
        values = [self.ahead, self.back]
        if self.ring.far == 1:
            values = [jnp.concatenate(values, axis=0)] * 2
            values[1] = jnp.zeros_like(values[1])
        cuts = 1 if rows // n_seq % 16 else n_seq
        more = list(beside) if cuts > 1 else []
        full = edge + (more[0].shape[1] if more else 0)
        args = [self.qkv, self.out] + values + more
        found = call(
            functools.partial(joint_owner_kernel, cuts, edge, dtype == F32, ME),
            near_in=range(len(args)),
            near_out=range(cuts + (dtype != F32)),
            in_specs=[NEAR] * len(args),
            out_specs=[NEAR] * cuts + [AWAY if dtype == F32 else NEAR],
            scratch_shapes=[pltpu.VMEM((part, width), F32), pltpu.SemaphoreType.DMA((1,))] if dtype == F32 else [],
            out_shape=[shape((rows // cuts, full))] * cuts + [shape((part, width), dtype)],
            compiler_params=vmem(8),
            name="joint_owner",
        )(*args)
        if cuts == n_seq:
            return list(found[:n_seq]), found[n_seq]
        blocks = found[0].reshape(n_seq, rows // n_seq, edge)
        blocks = [lax.dynamic_index_in_dim(blocks, me[0] ^ m, 0, keepdims=False) for m in range(n_seq)]
        return beside_all(blocks, beside), found[1]


def beside_all(blocks, beside):
    return [jnp.concatenate(pair, axis=1) for pair in zip(blocks, beside)] if beside else blocks


def joint_owner_kernel(cuts, edge, last_away, me_ref, q_ref, o_ref, *refs):
    if last_away:
        refs, (last, target, sems) = refs[:-3], refs[-3:]
        refs = (*refs, target)
    values, outs = refs[: -cuts - 1], refs[-cuts - 1 :]
    values, more = values[:2], values[2:]
    part = outs[0].shape[0]
    for mask, target in enumerate(outs[:-1]):
        rows = pl.ds(pl.multiple_of((me_ref[0] ^ mask) * part, part), part) if cuts > 1 else slice(None)
        total = q_ref[lax.axis_index("dp"), rows, :].astype(F32)
        for ref in values:
            total = total + ref[rows, :edge].astype(F32)
        target[:, :edge] = total.astype(BF16)
        if more:
            target[:, edge:] = more[mask][...]
    part, width = outs[-1].shape
    cols = values[0].shape[1] - edge
    for t in range(width // cols):
        total = o_ref[lax.axis_index("dp"), :, t * cols : (t + 1) * cols].astype(F32)
        for ref in values:
            total = total + ref[t * part : (t + 1) * part, edge:].astype(F32)
        outs[-1][:, t * cols : (t + 1) * cols] = total.astype(outs[-1].dtype)
    if last_away:
        fetch([(outs[-1], last)], sems)()


class ApartScatter(Scatter):
    def __init__(self, ring, qkv, out):
        super().__init__(ring, [qkv, out])

    def total(self, me, n_seq, dtype=BF16, beside=()):
        qkv, out = self.terms
        blocks = owner_blocks(self.ring.order, me, qkv, (self.ahead[0], self.back[0]), n_seq)
        (out_sum,) = ring_blocks(self.ring.order, [(out, 0, (self.ahead[1], self.back[1]))])
        return beside_all(blocks, beside), out_sum


def flipped(pieces, bits):
    me = lax.axis_index("seq")
    size = len(pieces)
    held = [pieces[m] for m in range(size)]
    bit = 1
    while bit < size:
        turned = (me & bit) != 0
        held = [jnp.where(turned, held[m ^ bit], held[m]) for m in range(size)]
        bit *= 2
    return jnp.stack(held)


def make_body(n_dp, n_seq):
    masks = block_masks(n_seq)
    far = far_bits(n_seq)
    far_masks = [m for m in range(n_seq) if not m & 1]

    def body(
        tokens,
        lead_hours,
        valid_counts,
        patch_mask,
        first_gain,
        first_shift,
        qkv_weight,
        query_bias,
        value_bias,
        out_weight,
        out_bias,
        second_gain,
        second_shift,
        up_weight,
        up_bias,
        down_weight,
        down_bias,
        lead_weight,
        lead_bias,
        cotangent,
    ):
        me = lax.axis_index("seq")
        rows, width = tokens.shape[1], tokens.shape[2]
        length = rows * n_seq
        half = rows // HALVES
        part = qkv_weight.shape[0]
        ff_part = down_weight.shape[0]
        ff = up_weight.shape[1]
        extra = ff_part // part
        cols = width // n_seq
        ff_cols = ff // n_seq
        lead = lead_hours[0].astype(F32) / 100.0
        count = valid_counts[0]
        ring = Ring(n_dp)
        me_ref = me.reshape(1).astype(jnp.int32)
        lead_ref = jnp.broadcast_to(lead, (8, 128))
        order = ring.steps

        def far_gather(own, at_bit):
            return [swap(own[m], far[at_bit], n_seq) for m in sorted(own)]

        line = Line(me_ref)

        def run(sends=(), work=lambda: (), inputs=(), start=(), finish=(), begin=(), end=()):
            sends, begin, end = list(sends), list(begin), list(end)
            plan = []
            for ring_part in finish:
                if ring_part.pending is not None:
                    plan.append((ring_part, "end", len(end), len(ring_part.pending)))
                    end += ring_part.pending
                    ring_part.pending = None
            n_sends, n_begin = len(sends), len(begin)
            ahead = []
            for ring_part in start:
                mine = ring_part.sends()
                if ring_part in finish:
                    plan.append((ring_part, "now", len(ahead), len(mine)))
                    ahead += mine
                else:
                    plan.append((ring_part, "later", len(begin), len(mine)))
                    begin += mine
            found, done, begun, ended = line.slot(ahead + sends, work, inputs, begin, end)
            early, found = found[: len(ahead)], found[len(ahead) :]
            n_end = len(end) - sum(p[3] for p in plan if p[1] == "end")
            for ring_part, kind, at, size in plan:
                if kind == "end":
                    ring_part.take(list(ended[at : at + size]))
                elif kind == "now":
                    ring_part.take(list(early[at : at + size]))
                else:
                    ring_part.pending = list(begun[at : at + size])
            return list(found[:n_sends]), done, list(begun[:n_begin]), list(ended[:n_end])

        def near_all(held):
            return [swap(held[m], 1, n_seq) for m in sorted(held)]

        def with_near(held, found):
            held.update({m ^ 1: v for m, v in zip(sorted(held), found)})

        def with_far(held, found, at_bit):
            held.update({m ^ far[at_bit]: v for m, v in zip(sorted(held), found)})

        def rest_far(held):
            for i in range(1, len(far)):
                found, _, _, _ = line.slot(far_gather(held, i))
                with_far(held, found, i)

        vectors = [
            first_gain,
            first_shift,
            query_bias,
            value_bias,
            out_bias,
            second_gain,
            second_shift,
            down_bias,
            lead_weight,
            lead_bias,
            up_bias,
        ]
        kinds = 10 + extra
        packed = pack(n_dp, n_seq, me_ref, qkv_weight, up_weight, vectors)

        def masked_rows(cot, mask, count):
            positions = me * rows + jnp.arange(rows, dtype=jnp.int32)
            weight = (mask * (positions < count).astype(jnp.int32)).astype(BF16)[:, None]
            return tuple(cot[h * half : (h + 1) * half] * weight[h * half : (h + 1) * half] for h in range(HALVES))

        found, outs_own, _, _ = run(
            [swap(packed[m], m, n_seq) for m in range(1, n_seq)],
            masked_rows,
            (cotangent[0], patch_mask[0], count),
        )
        one_own = join_one(n_seq, me_ref, [packed[0]] + list(found), out_weight)

        g_one = Gather(ring, one_own)

        def steps(*rings):
            mine = [g for g in rings if g.left]
            return dict(start=mine, finish=mine)

        tokens_held = {0: tokens[0]}
        grad_held = [{0: g} for g in outs_own]
        found, _, _, _ = run([swap(packed[n_seq + m], m, n_seq) for m in range(1, n_seq)], **steps(g_one))
        up_found = [packed[n_seq]] + list(found)
        _, (two_own,), tokens_far, _ = run(
            work=lambda *a: (join_two(n_seq, me_ref, a[:-1], a[-1]),),
            inputs=(*up_found, down_weight),
            begin=far_gather(tokens_held, 0),
            **steps(g_one),
        )
        g_two = Gather(ring, two_own)
        _, _, _, tokens_far = run(end=tokens_far, **steps(g_one))
        with_far(tokens_held, tokens_far, 0)
        rest_far(tokens_held)
        while g_one.left > 1:
            run(**steps(g_one))
        found, _, _, _ = run(near_all(tokens_held), **steps(g_one))
        with_near(tokens_held, found)

        valid = jnp.broadcast_to(count, (8, 128))
        pairs = cols // PAIR

        def begun(part_of):
            return dict(start=[part_of] if part_of.left else [])

        tokens_by = [tokens_held[m] for m in masks]
        ones_blocks = ordered(ring.order, g_one.pieces)

        def attend_first(*a):
            blocks = Blocks(a[n_seq:], ones_blocks.spots, ones_blocks.rows)
            out_pack = middle_columns(blocks, 3 * cols, cols, n_dp)
            found = project(me_ref, order, lead_ref, a[:n_seq], blocks, kinds)
            return out_pack, found

        _, (out_pack, (normed, q, k, v, qkv, table, vecs)), _, _ = run(
            work=attend_first, inputs=tokens_by + list(ones_blocks.arrays), **steps(g_two)
        )
        out_held = {0: out_pack}

        def up_bias_of(table):
            u_bias = table[10 : 10 + extra].reshape(extra, n_dp, n_seq, part)
            u_bias = lax.dynamic_index_in_dim(u_bias, me, 2, keepdims=False)
            return jnp.swapaxes(u_bias, 0, 1).reshape(1, ff_cols)

        def attend_rest(q, k, v, table):
            lses, attended = [], None
            for p in range(pairs):
                attended, lse = attend(n_seq, p, me_ref, valid, q, k, v, attended)
                lses.append(lse)
            return attended, jnp.concatenate(lses, axis=0), up_bias_of(table)

        found, (attended, lse, u_bias), _, _ = run(
            far_gather(out_held, 0), work=attend_rest, inputs=(q, k, v, table), **steps(g_two)
        )
        with_far(out_held, found, 0)
        rest_far(out_held)
        att_held = {0: attended}
        nearby = near_all(out_held)
        found, _, _, _ = run(far_gather(att_held, 0) + nearby, **steps(g_two))
        with_near(out_held, found[-len(nearby) :])
        with_far(att_held, found[: -len(nearby)], 0)
        rest_far(att_held)
        found, _, _, _ = run(near_all(att_held))
        with_near(att_held, found)

        def out_whole(pieces):
            if part % 16 == 0:
                return pieces
            blocks = flipped(dict(enumerate(pieces)), n_seq).reshape(n_seq, n_dp, n_seq, part, cols)
            return [jnp.transpose(blocks, (1, 0, 3, 2, 4)).reshape(width, width)]

        found, (normed_two, middle_own, out_mine), _, _ = run(
            far_gather(grad_held[0], 0),
            work=lambda tok, att, outs, vecs: middle_norm(me_ref, order, tok, att, out_whole(outs), vecs),
            inputs=(
                tokens_by,
                [att_held[m] for m in masks],
                [out_held[m] for m in range(n_seq)],
                vecs,
            ),
            **steps(g_two),
        )
        with_far(grad_held[0], found, 0)
        rest_far(grad_held[0])
        while g_two.left:
            run(**steps(g_two))
        twos = ordered(ring.order, g_two.pieces)
        downs = twos
        if twos.spots[0] is None:
            whole = twos.arrays[0]
            twos = Blocks([whole[:, :ff_cols]], [None], whole.shape[0])
            downs = Blocks([whole[:, ff_cols:].reshape(ff_cols, width)], [None], ff_cols)
        nearby = near_all(grad_held[0])
        found, (up, down, hidden, slope), _, _ = run(
            far_gather(grad_held[1], 0) + nearby,
            work=lambda n, b, a, d: up_part(
                order,
                n,
                b,
                Blocks(a, twos.spots, twos.rows),
                Blocks(d, downs.spots, downs.rows) if downs is not twos else None,
            ),
            inputs=(normed_two, u_bias, list(twos.arrays), list(downs.arrays) if downs is not twos else ()),
        )
        with_near(grad_held[0], found[-len(nearby) :])
        with_far(grad_held[1], found[: -len(nearby)], 0)
        rest_far(grad_held[1])

        def half_sum(keep, other):
            found = {}
            for at, m in enumerate(far_masks):
                if m:
                    rows_at = slice(at * half, (at + 1) * half)
                    found[m] = (keep[rows_at].astype(F32) + other[rows_at].astype(F32)).astype(BF16)
            return found

        def far_first(held):
            bit = far[-1]
            return [swap(held[m], bit, n_seq) for m in sorted(held) if m & bit]

        def far_rest(held, found):
            for at, bit in enumerate(reversed(far)):
                upper = sorted(m for m in held if m & bit)
                if at:
                    found, _, _, _ = line.slot([swap(held[m], bit, n_seq) for m in upper])
                kept = {m: held[m] for m in held if not m & bit}
                for m, value in zip(upper, found):
                    low = m ^ bit
                    if low in kept:
                        value = (kept[low].astype(F32) + value.astype(F32)).astype(BF16)
                    kept[low] = value
                held = kept
            return held[0]

        found, (pre, grad_out, keep_a, send_a, branch_keep_a, branch_send_a, sum_a), _, _ = run(
            near_all(grad_held[1]),
            work=lambda *a: mlp_back(0, *a, None),
            inputs=(hidden, slope, up, down, [grad_held[0][m] for m in masks]),
        )
        with_near(grad_held[1], found)
        (near_a,), (pre, grad_out, keep_b, send_b, branch_keep_b, branch_send_b, sum_b), _, _ = run(
            [swap(send_a, 1, n_seq)],
            work=lambda *a: mlp_back(1, *a),
            inputs=(hidden, slope, up, down, [grad_held[1][m] for m in masks], (pre, grad_out)),
        )
        def moved(value, axis, bit):
            count = n_dp if axis == "dp" else n_seq
            return lax.ppermute(value, axis, [(i, i ^ bit) for i in range(count)])

        held_a = half_sum(keep_a, near_a)
        sends = far_first(held_a)

        def weight_terms(hidden, grad_out, normed_two, pre):
            up_terms = dot(normed_two, pre, TN).astype(BF16).reshape(n_dp, n_seq * part, ff_cols)
            return dot(hidden, grad_out, TN).astype(BF16).reshape(n_dp, ff_part, width), up_terms

        found, (down_terms, up_terms), _, _ = run(
            sends + [swap(send_b, 1, n_seq)], work=weight_terms, inputs=(hidden, grad_out, normed_two, pre)
        )
        far_a, near_b = far_rest(held_a, found[: len(sends)]), found[-1]
        held_b = half_sum(keep_b, near_b)

        def back_half(at):
            return lambda *a: tuple(second_back(at, *a))

        scatter_two = JointScatter(ring, up_terms, down_terms)
        sends = far_first(held_b)
        found, (grad_mid_a, one_a, sums_a), _, _ = run(
            sends + [swap(branch_send_a, 1, n_seq), swap(branch_send_b, 1, n_seq)],
            work=back_half(0),
            inputs=(middle_own, keep_a, near_a, far_a, outs_own[0], vecs),
            **steps(scatter_two),
        )
        far_b, branch_other = far_rest(held_b, found[: len(sends)]), found[-2:]
        one_far_a, (grad_mid_b, one_b, sums_b), _, _ = run(
            far_gather({0: one_a}, 0),
            work=back_half(1),
            inputs=(middle_own, keep_b, near_b, far_b, outs_own[1], vecs),
            **begun(scatter_two),
        )
        one_held_a = {0: one_a}
        with_far(one_held_a, one_far_a, 0)
        rest_far(one_held_a)
        one_held_b = {0: one_b}
        found, _, one_far_b, _ = run(
            near_all(one_held_a), begin=far_gather(one_held_b, 0), finish=[scatter_two]
        )
        with_near(one_held_a, found)
        _, (dq_a, dk_a, dv_a), _, one_far_b = run(
            work=lambda *a: attend_back(0, me_ref, valid, *a, None),
            inputs=(q, k, v, lse, out_mine, [one_held_a[m] for m in masks]),
            end=one_far_b,
            **begun(scatter_two),
        )
        with_far(one_held_b, one_far_b, 0)
        rest_far(one_held_b)
        found, _, _, _ = run(near_all(one_held_b), finish=[scatter_two])
        with_near(one_held_b, found)
        ones = [one_held_a[m] for m in masks] + [one_held_b[m] for m in masks]

        branch_held = {
            m: jnp.concatenate([value, half_sum(branch_keep_b, branch_other[1])[m]], axis=0)
            for m, value in half_sum(branch_keep_a, branch_other[0]).items()
        }

        def second_attend(q, k, v, lse, out_mine, grads, earlier, att, ones):
            sums = out_terms(att, ones, n_dp, part if part % 16 else n_seq * part)
            return attend_back(1, me_ref, valid, q, k, v, lse, out_mine, grads, earlier), sums

        branch_far, (grad_qkv, out_sums), _, _ = run(
            far_first(branch_held),
            work=second_attend,
            inputs=(
                q,
                k,
                v,
                lse,
                out_mine,
                [one_held_b[m] for m in masks],
                (dq_a, dk_a, dv_a),
                [attended],
                ones,
            ),
            **steps(scatter_two),
        )
        branch_far = far_rest(branch_held, branch_far)

        qkv_terms = dot(normed, grad_qkv, TN).astype(BF16).reshape(n_dp, n_seq * part, 3 * cols)
        scatter_one = (ApartScatter if part % 16 else JointScatter)(ring, qkv_terms, out_sums)
        late = [scatter_two] if scatter_two.left else []

        def far_moved(held):
            if not far:
                return []
            return [moved(held[m], "seq", far[-1]) for m in sorted(held) if m & far[-1]]

        def now(*beside):
            mine = [scatter_one] if scatter_one.left else []
            return dict(start=mine, finish=mine + list(beside))

        def final_rows(keep_a, keep_b, near_a, near_b, far_part, mid, bias):
            total = jnp.concatenate([keep_a[:half], keep_b[:half]], axis=0).astype(F32)
            total = total + jnp.concatenate([near_a[:half], near_b[:half]], axis=0).astype(F32)
            return (mid + (total + far_part.astype(F32) + bias[6:7])).astype(BF16)

        late = [scatter_two] if scatter_two.left else []
        options = now()
        _, (gn_keep, gn_send, column_sums, last_sums), _, _ = run(
            work=lambda g: first_grad(g, qkv, vecs, tokens_by),
            inputs=(grad_qkv,),
            start=options["start"] + late,
            finish=options["finish"] + late,
        )
        while scatter_two.left:
            run(**steps(scatter_two))
        plain = (width // n_dp) % 128 == 0 and extra == n_seq and n_seq * part == 128

        bits = []
        while 2 ** len(bits) < n_dp:
            bits.append(2 ** len(bits))
        bits = bits if plain else []
        at_dp = lax.axis_index("dp")

        def loose_table():
            sums = sums_a + sums_b
            table = last_sums
            start_sums = table[2:3] + sums[4:5]
            q_sum = lax.dynamic_update_slice(jnp.zeros((1, width), F32), column_sums[:, :cols], (0, me * cols))
            v_sum = lax.dynamic_update_slice(jnp.zeros((1, width), F32), column_sums[:, 2 * cols :], (0, me * cols))
            u_sum = jnp.swapaxes((sum_a + sum_b).reshape(n_dp, extra, part), 0, 1)
            u_sum = lax.dynamic_update_index_in_dim(jnp.zeros((extra, n_dp, n_seq, part), F32), u_sum, me, 2)
            rows_out = [table[0:2], q_sum, v_sum, sums[2:3], sums[0:2], sums[3:4], lead * start_sums, start_sums]
            table = jnp.concatenate(rows_out + [u_sum.reshape(extra, width)], axis=0)
            return lax.psum_scatter(table, ("dp", "seq"), scatter_dimension=1, tiled=True)

        seq_bits = far + ([1] if n_seq > 1 else []) if plain else []

        def make_table():
            if not plain:
                return loose_table()
            return small_table(
                me_ref, lead_ref, sums_a, sums_b, last_sums, sum_a, sum_b, column_sums
            )

        def hop(held):
            if bits:
                bit = bits.pop(0)
                mine, other = halve(bit, held)
                return mine, [(other, "dp", [(i, i ^ bit) for i in range(n_dp)])]
            total = sum(held[1:], held[0])
            if seq_bits:
                return total, [swap(total, seq_bits.pop(0), n_seq)]
            return total, []

        def totals():
            blocks, total = scatter_two.total(me_ref, n_seq, F32)
            return *blocks, total

        mine, small = hop([make_table()])
        found, (*up_blocks, down_grad), _, _ = run([swap(gn_send, 1, n_seq)] + small, work=totals, **now())
        gn_near = found[0]
        held = [mine] + found[1:]
        size = half * len(far_masks)
        gn_held_a = half_sum(gn_keep[:size], gn_near[:size])
        mine, small = hop(held)
        sends = far_first(gn_held_a)
        found, (gn_held_b,), _, _ = run(
            sends + small, work=lambda k, n: (half_sum(k[size:], n[size:]),), inputs=(gn_keep, gn_near), **now()
        )
        gn_far_a = far_rest(gn_held_a, found[: len(sends)])
        held = [mine] + found[len(sends) :]
        mine, small = hop(held)
        sends = far_first(gn_held_b)
        found, (block_out,), _, _ = run(
            sends + small,
            work=lambda *a: (final_rows(*a),),
            inputs=(branch_keep_a, branch_keep_b, branch_other[0], branch_other[1], branch_far, middle_own, vecs),
            **now(),
        )
        gn_far_b = far_rest(gn_held_b, found[: len(sends)])
        held = [mine] + found[len(sends) :]
        while scatter_one.left:
            run(**steps(scatter_one))
        qkv_blocks, out_sum = scatter_one.total(me_ref, n_seq, beside=up_blocks)
        moves = []
        for dp_at in range(n_dp):
            for seq_at in range(n_seq):
                moves.append((dp_at * n_seq + seq_at, seq_at * n_dp + dp_at))
        final = [(out_sum, ("dp", "seq"), moves)] + [swap(qkv_blocks[m], m, n_seq) for m in range(1, n_seq)]

        mine, small = hop(held)
        found, (tokens_grad,), _, _ = run(
            final + small,
            work=lambda *a: (first_back(*a),),
            inputs=(tokens[0], gn_keep, gn_near, gn_far_a, gn_far_b, grad_mid_a, grad_mid_b, vecs),
        )
        last, held = found[: len(final)], [mine] + found[len(final) :]
        while bits or seq_bits:
            mine, small = hop(held)
            found, _, _, _ = run(small)
            held = [mine] + found
        small_sums = sum(held[1:], held[0])
        if plain:
            small_sums = lax.dynamic_slice_in_dim(small_sums, me * part, part, 1)
        owned = small_sums[:kinds]
        qkv_weight_grad, up_weight_grad, out_weight_grad = unpack(
            (3, n_dp), (3 * width, ff), [qkv_blocks[0]] + list(last[1:]), last[0]
        )
        return (
            block_out[None],
            tokens_grad[None],
            owned[0],
            owned[1],
            qkv_weight_grad,
            owned[2],
            owned[3],
            out_weight_grad,
            owned[4],
            owned[5],
            owned[6],
            up_weight_grad,
            owned[10 : 10 + extra].reshape(ff_part),
            down_grad[0] if down_grad.ndim == 3 else down_grad,
            owned[7],
            owned[8],
            owned[9],
        )

    return body


def solution(mesh):
    both = P(("dp", "seq"))
    matrix = P(("dp", "seq"), None)
    tokens = P("dp", "seq", None)
    in_specs = (tokens, P("dp"), P("dp"), P("dp", "seq"), both, both, matrix, both, both, matrix, both, both, both)
    in_specs += (matrix, both, matrix, both, both, both, tokens)
    out_specs = (tokens, tokens, both, both, matrix, both, both, matrix, both, both, both, matrix, both, matrix)
    out_specs += (both, both, both)
    return jax.shard_map(
        make_body(mesh.shape["dp"], mesh.shape["seq"]),
        mesh=mesh,
        in_specs=in_specs,
        out_specs=out_specs,
        check_vma=False,
    )
```

```python
import functools
import math

import jax
import jax.numpy as jnp
import numpy as np
from jax import lax
from jax.experimental import pallas as pl
from jax.experimental.pallas import tpu as pltpu
from jax.sharding import PartitionSpec as P

HEADS = 16
HEAD_DIM = 64
PAIR = 2 * HEAD_DIM
SCALE = 1.0 / math.sqrt(HEAD_DIM)
EPSILON = 1e-06
MASKED = -1e30
F32 = jnp.float32
BF16 = jnp.bfloat16
NN, NT, TN = ((1,), (0,)), ((1,), (1,)), ((0,), (0,))
HALVES = 2
MIB = 1024 * 1024
NEAR = pl.BlockSpec(memory_space=pltpu.VMEM)
AWAY = pl.BlockSpec(memory_space=pl.ANY)
NUMBERS = pl.BlockSpec(memory_space=pltpu.SMEM)


def dot(left, right, contract):
    return lax.dot_general(left, right, (contract, ((), ())), preferred_element_type=F32)


def shape(dims, dtype=BF16):
    return jax.ShapeDtypeStruct(dims, dtype)


def call(kernel, *, in_specs, out_shape, near_in=(), near_out=(), **options):
    def large(value):
        return math.prod(value.shape) * value.dtype.itemsize >= 65536

    def run(*args):
        kept = []
        for i, a in enumerate(args):
            if large(a):
                a = pltpu.with_memory_space_constraint(a, pltpu.VMEM if i in near_in else pltpu.HBM)
            kept.append(a)
        single = not isinstance(out_shape, (list, tuple))
        outs = [out_shape] if single else list(out_shape)
        outs = [
            ((pltpu.VMEM if i in near_out else pltpu.HBM)(o.shape, o.dtype) if large(o) else o)
            for i, o in enumerate(outs)
        ]
        return pl.pallas_call(kernel, in_specs=in_specs, out_shape=outs[0] if single else outs, **options)(*kept)

    return run


def away(value):
    return pltpu.with_memory_space_constraint(value, pltpu.HBM)


class Here:
    def __getitem__(self, at):
        return lax.axis_index("seq")


class Order:
    def __init__(self, cycle):
        self.cycle = cycle

    def __getitem__(self, k):
        n = len(self.cycle)
        mine = lax.axis_index("dp")
        spot = sum(jnp.where(mine == place, at, 0) for at, place in enumerate(self.cycle))
        spot = lax.rem(spot + k % n, n)
        return sum(jnp.where(spot == at, place, 0) for at, place in enumerate(self.cycle))


ME = Here()


def near(value):
    return pltpu.with_memory_space_constraint(value, pltpu.VMEM)


def vmem(mib):
    return pltpu.CompilerParams(vmem_limit_bytes=mib * MIB)


def cost(flops, moved, exps=0):
    return pl.CostEstimate(flops=int(flops), bytes_accessed=int(moved), transcendentals=int(exps))


def standardise(values):
    centered = values - jnp.mean(values, axis=-1, keepdims=True)
    rate = lax.rsqrt(jnp.mean(centered * centered, axis=-1, keepdims=True) + EPSILON)
    return centered * rate, rate


def norm_back(upstream, xhat, rate, gain):
    scaled = upstream * gain
    inner = jnp.mean(scaled * xhat, axis=-1, keepdims=True)
    return rate * (scaled - jnp.mean(scaled, axis=-1, keepdims=True) - xhat * inner)


def pack_kernel(n_dp, n_seq, me_ref, qkv_ref, up_ref, *refs):
    vectors, out_refs = refs[: -2 * n_seq], refs[-2 * n_seq :]
    out_refs, up_refs = out_refs[:n_seq], out_refs[n_seq:]
    me = me_ref[0]
    part = qkv_ref.shape[0]
    cols = qkv_ref.shape[1] // (3 * n_seq)
    piece = up_ref.shape[1] // (n_dp * n_seq)
    rows = [ref[...].astype(F32)[:, i : i + part] for ref in vectors for i in range(0, ref.shape[1], part)]
    kinds = len(rows)
    rows = jnp.concatenate(rows + [jnp.zeros((128 - kinds, part), F32)], axis=0)
    rows = jnp.concatenate([rows, jnp.zeros((128, 128 - part), F32)], axis=1)
    small = rows.T[:part, :].astype(BF16)
    for mask, ref in enumerate(out_refs):
        place = me ^ mask
        for i in range(3):
            start = pl.multiple_of((i * n_seq + place) * cols, 128)
            ref[:, i * cols : (i + 1) * cols] = qkv_ref[:, pl.ds(start, cols)]
        at = 3 * cols
        ref[:, at : at + 128] = small
        for i in range(n_dp):
            start = pl.multiple_of((i * n_seq + place) * piece, 128)
            up_refs[mask][:, i * piece : (i + 1) * piece] = up_ref[:, pl.ds(start, piece)]


def pack(n_dp, n_seq, me, qkv, up, vectors):
    part = qkv.shape[0]
    wide = qkv.shape[1] // n_seq + 128
    ff = up.shape[1] // n_seq
    if up.shape[1] // (n_dp * n_seq) % 128 or part % 16:
        small = jnp.concatenate(vectors).reshape(-1, part).T
        small = jnp.pad(small, ((0, 0), (0, 128 - small.shape[1])))
        qkv_split = qkv.reshape(part, 3, n_seq, -1)
        up_split = up.reshape(part, n_dp, n_seq, -1)

        def block(place):
            q = lax.dynamic_index_in_dim(qkv_split, place, 2, keepdims=False).reshape(part, -1)
            u = lax.dynamic_index_in_dim(up_split, place, 2, keepdims=False).reshape(part, -1)
            return jnp.concatenate([q, small], axis=1), u

        blocks = [block(me[0] ^ m) for m in range(n_seq)]
        return [b[0] for b in blocks] + [b[1] for b in blocks]
    args = [qkv, up] + [v.reshape(1, -1) for v in vectors]
    args = [pltpu.with_memory_space_constraint(a, pltpu.HBM) for a in args]
    return pl.pallas_call(
        functools.partial(pack_kernel, n_dp, n_seq, ME),
        grid=(1,),
        in_specs=[pl.BlockSpec(a.shape, lambda i: (0, 0)) for a in args],
        out_specs=[pl.BlockSpec((part, wide), lambda i: (0, 0))] * n_seq
        + [pl.BlockSpec((part, ff), lambda i: (0, 0))] * n_seq,
        out_shape=[shape((part, wide))] * n_seq + [shape((part, ff))] * n_seq,
        compiler_params=vmem(8),
        name="pack",
    )(*args)


def join_one_kernel(n_seq, me_ref, *refs):
    out_ref, left_ref = refs[-2:]
    part, wide = out_ref.shape
    cols = wide // n_seq
    edge = refs[0].shape[1] - 128
    for t, ref in enumerate(refs[:-2]):
        rows = pl.ds(pl.multiple_of((me_ref[0] ^ t) * part, part), part)
        left_ref[rows, :edge] = ref[:, :edge]
        left_ref[rows, edge + cols :] = ref[:, edge:]
        left_ref[t * part : (t + 1) * part, edge : edge + cols] = out_ref[:, t * cols : (t + 1) * cols]


def join_two_kernel(n_seq, me_ref, *refs):
    down_ref, right_ref = refs[-2:]
    half = down_ref.shape[1]
    part = refs[0].shape[0]
    right_ref[:, -half:] = down_ref[...]
    for t, ref in enumerate(refs[:-2]):
        right_ref[pl.ds(pl.multiple_of((me_ref[0] ^ t) * part, part), part), :-half] = ref[...]


def join(kernel, n_seq, me, pieces, weight, wide):
    rows = pieces[0].shape[0] * n_seq
    args = list(pieces) + [away(weight)]
    return pl.pallas_call(
        functools.partial(kernel, n_seq, ME),
        grid=(1,),
        in_specs=[pl.BlockSpec(a.shape, lambda i: (0, 0)) for a in args],
        out_specs=pl.BlockSpec((rows, wide), lambda i: (0, 0)),
        out_shape=shape((rows, wide)),
        compiler_params=vmem(8),
        name="join",
    )(*args)


def join_one(n_seq, me, pieces, out_weight):
    part, edge = pieces[0].shape
    edge -= 128
    cols = out_weight.shape[1] // n_seq
    if part % 16:
        whole = flipped(dict(enumerate(pieces)), n_seq).reshape(part * n_seq, edge + 128)
        beside = jnp.moveaxis(out_weight.reshape(part, n_seq, cols), 1, 0).reshape(part * n_seq, cols)
        return jnp.concatenate([whole[:, :edge], beside, whole[:, edge:]], axis=1)
    return join(join_one_kernel, n_seq, me, pieces, out_weight, edge + cols + 128)


def join_two(n_seq, me, pieces, down_weight):
    part, wide = pieces[0].shape
    rows = part * n_seq
    if part % 16:
        whole = flipped(dict(enumerate(pieces)), n_seq).reshape(rows, wide)
        return jnp.concatenate([whole, down_weight.reshape(rows, -1)], axis=1)
    return join(join_two_kernel, n_seq, me, pieces, down_weight, wide + down_weight.shape[1])


class Blocks:
    def __init__(self, arrays, spots, rows):
        self.arrays = arrays
        self.spots = spots
        self.rows = rows

    def place(self, order_ref, i, source=None):
        k, start = self.spots[i]
        count = self.arrays[i].shape[0]
        if order_ref is None:
            return slice(k * self.rows + start, k * self.rows + start + count)
        return pl.ds(pl.multiple_of(order_ref[k] * self.rows + start, math.gcd(self.rows, start or self.rows)), count)


def ordered(order, pieces):
    rows = pieces[0].shape[0]
    if rows % 128 == 0:
        arrays, spots = [], []
        for k, piece in enumerate(pieces):
            halves = piece if isinstance(piece, tuple) else (piece,)
            for i, half in enumerate(halves):
                arrays.append(half)
                spots.append((k, i * rows // 2))
        return Blocks(arrays, spots, rows)
    whole = jnp.stack([jnp.concatenate(p, axis=0) if isinstance(p, tuple) else p for p in pieces])
    out = whole
    for k in range(len(pieces)):
        out = lax.dynamic_update_index_in_dim(out, whole[k], order[k], 0)
    return Blocks([out.reshape(-1, out.shape[-1])], [None], len(pieces) * rows)


def lay(order_ref, blocks, refs, target, cols=slice(None)):
    for i, ref in enumerate(refs):
        if blocks.spots[i] is None:
            target[...] = ref[:, cols]
        else:
            target[blocks.place(order_ref, i), :] = ref[:, cols]


def middle_columns_kernel(blocks, *refs):
    for i, ref in enumerate(refs[:-1]):
        refs[-1][blocks.place(None, i), :] = ref[...]


def middle_columns(blocks, start, cols, n_dp):
    if blocks.spots[0] is None or start % cols:
        return blocks.arrays[0][:, start : start + cols]
    total = blocks.rows * n_dp
    return call(
        functools.partial(middle_columns_kernel, blocks),
        grid=(1,),
        in_specs=[pl.BlockSpec((a.shape[0], cols), lambda i: (0, start // cols)) for a in blocks.arrays],
        out_specs=pl.BlockSpec((total, cols), lambda i: (0, 0)),
        out_shape=shape((total, cols)),
        compiler_params=vmem(4),
        name="middle_columns",
    )(*blocks.arrays)


def project_kernel(n_seq, blocks, me_ref, order_ref, lead_ref, *refs):
    n_pieces = len(blocks.arrays)
    tokens = refs[:n_seq]
    pieces = refs[n_seq : n_seq + n_pieces]
    normed_ref, q_ref, k_ref, v_ref, qkv_ref, table_ref, vec_ref, small_ref = refs[n_seq + n_pieces :]
    cols = q_ref.shape[1]

    @pl.when(pl.program_id(0) == 0)
    def _():
        lay(order_ref, blocks, pieces, qkv_ref, slice(0, 3 * cols))
        lay(order_ref, blocks, pieces, small_ref, slice(4 * cols, 4 * cols + 128))
        table_ref[...] = small_ref[...].astype(F32).T[: table_ref.shape[0], :]
        for i, kind in enumerate((0, 0, 1, 4, 5, 6, 7, 7)):
            vec_ref[i : i + 1, :] = table_ref[kind : kind + 1, :]
        vec_ref[0:1, :] = lead_ref[0:1, 0:1] * table_ref[8:9, :] + table_ref[9:10, :]

    start = jnp.concatenate([ref[...] for ref in tokens], axis=0).astype(F32) + vec_ref[0:1, :]
    xhat, _ = standardise(start)
    normed = (xhat * vec_ref[1:2, :] + vec_ref[2:3, :]).astype(BF16)
    normed_ref[...] = normed
    mine = pl.ds(pl.multiple_of(me_ref[0] * cols, 128), cols)
    found = dot(normed, qkv_ref[...], NN)
    q_ref[...] = (found[:, :cols] + table_ref[2:3, mine]).astype(BF16)
    k_ref[...] = found[:, cols : 2 * cols].astype(BF16)
    v_ref[...] = (found[:, 2 * cols :] + table_ref[3:4, mine]).astype(BF16)


def project(me, order, lead, tokens, blocks, kinds):
    rows, width = tokens[0].shape
    n_seq = len(tokens)
    cols = width // n_seq
    length = rows * n_seq
    half = rows // HALVES
    count = length // HALVES
    numbers = pl.BlockSpec(memory_space=pltpu.SMEM)

    def whole(dims):
        return pl.BlockSpec(dims, lambda i: (0, 0))

    def step(wide):
        return pl.BlockSpec((count, wide), lambda i: (i, 0))

    return call(
        functools.partial(project_kernel, n_seq, blocks, ME, order),
        near_out=(1, 2, 3),
        grid=(HALVES,),
        in_specs=[whole(lead.shape)]
        + [pl.BlockSpec((half, width), lambda i: (i, 0))] * n_seq
        + [whole(a.shape) for a in blocks.arrays],
        out_specs=[step(width), step(cols), step(cols), step(cols)]
        + [whole((width, 3 * cols)), whole((kinds, width)), whole((8, width))],
        out_shape=[shape((length, width))]
        + [shape((length, cols))] * 3
        + [shape((width, 3 * cols)), shape((kinds, width), F32), shape((8, width), F32)],
        scratch_shapes=[pltpu.VMEM((width, 128), BF16)],
        compiler_params=vmem(28),
        cost_estimate=cost(6 * length * width * cols, 10 * length * width),
        name="project",
    )(lead, *tokens, *blocks.arrays)


def key_bias(n_seq, length, me, count):
    half = length // (n_seq * HALVES)
    parts = []
    for h in range(HALVES):
        for m in block_masks(n_seq):
            at = lax.broadcasted_iota(jnp.int32, (half, 1), 0) + ((me ^ m) * HALVES + h) * half
            parts.append(jnp.where(at < count, 0.0, MASKED).astype(F32))
    return jnp.concatenate(parts, axis=0)


def attend_kernel(n_seq, me_ref, pair_at, count_ref, q_ref, k_ref, v_ref, *refs):
    out_ref, lse_ref = refs[-2:]
    bias = key_bias(n_seq, k_ref.shape[0], me_ref[0], count_ref[0:1, 0:1])
    count = q_ref.shape[0] // 2

    def step(i, carry):
        rows = pl.ds(pl.multiple_of(i * count, count), count)
        for half in range(2):
            cols = slice(half * HEAD_DIM, (half + 1) * HEAD_DIM)
            mine = slice(pair_at * PAIR + cols.start, pair_at * PAIR + cols.stop)
            scores = dot(k_ref[:, mine], q_ref[rows, mine] * SCALE, NT) + bias
            top = jnp.max(scores, axis=0, keepdims=True)
            weights = jnp.exp(scores - top)
            total = jnp.sum(weights, axis=0, keepdims=True)
            mixed = dot(v_ref[:, mine], weights.astype(BF16), TN) / total
            out_ref[rows, cols] = mixed.T.astype(BF16)
            lse_ref[half, :, rows] = top + jnp.log(total)
        return carry

    lax.fori_loop(0, 2, step, 0)


def attend(n_seq, pair_at, me, valid, q, k, v, earlier):
    length, cols = q.shape
    pair = pl.BlockSpec((length, PAIR), lambda g: (0, pair_at))
    given = [] if earlier is None else [earlier]
    return call(
        functools.partial(attend_kernel, n_seq, ME, pair_at),
        near_in=(1, 2, 3),
        grid=(1,),
        in_specs=[pl.BlockSpec(valid.shape, lambda g: (0, 0)), NEAR, NEAR, NEAR] + [AWAY] * len(given),
        out_specs=[pair, pl.BlockSpec((2, 1, length), lambda g: (0, 0, 0))],
        out_shape=[shape((length, cols)), shape((2, 1, length), F32)],
        input_output_aliases={4: 0} if given else {},
        compiler_params=vmem(32),
        cost_estimate=cost(4 * length * length * PAIR, 8 * length * PAIR, 2 * length * length),
        name="attend",
    )(valid, q, k, v, *given)


def attend_back_kernel(first, n_seq, *refs):
    count_ref, q_ref, k_ref, v_ref, lse_ref, out_w_ref = refs[:6]
    grads = refs[6 : 6 + n_seq]
    rest = refs[6 + n_seq :]
    if first:
        dq_ref, dk_ref, dv_ref = rest
    else:
        dq_in, dk_in, dv_in, whole_ref, q_out, k_out, v_out, sems = rest
    length = k_ref.shape[0]
    count = q_ref.shape[0]
    pair = pl.program_id(0)
    spot = pair % 2
    bias = key_bias(n_seq, length, ME[0], count_ref[0:1, 0:1])
    upstream = jnp.concatenate([dot(ref[...], out_w_ref[...], NT).astype(BF16) for ref in grads], axis=0)
    for half in range(2):
        cols = slice(half * HEAD_DIM, (half + 1) * HEAD_DIM)
        k = k_ref[:, cols]
        q = q_ref[:, cols] * SCALE
        g = upstream[:, cols]
        probs = jnp.exp(dot(k, q, NT) + bias - lse_ref[half])
        dv = dot(probs.astype(BF16), g, NN)
        term = probs * dot(v_ref[:, cols], g, NT)
        grad = (term - probs * jnp.sum(term, axis=0, keepdims=True)).astype(BF16)
        dk = dot(grad, q, NN)
        dq = (dot(k, grad, TN) * SCALE).T.astype(BF16)
        if first:
            dq_ref[:, cols] = dq
            dk_ref[:, cols] = dk
            dv_ref[:, cols] = dv
        else:
            q_out[spot, :count, cols] = dq_in[:, cols]
            q_out[spot, count:, cols] = dq
            k_out[spot, :, cols] = (dk + dk_in[:, cols]).astype(BF16)
            v_out[spot, :, cols] = (dv + dv_in[:, cols]).astype(BF16)
    if first:
        return
    pairs = pl.num_programs(0)

    def copies(at):
        found = []
        for i, source in enumerate((q_out, k_out, v_out)):
            start = pl.multiple_of((i * pairs + at) * PAIR, PAIR)
            target = whole_ref.at[:, pl.ds(start, PAIR)]
            found.append(pltpu.make_async_copy(source.at[at % 2], target, sems.at[at % 2, i]))
        return found

    for copy in copies(pair):
        copy.start()

    @pl.when(pair > 0)
    def _():
        for copy in copies(pair - 1):
            copy.wait()

    @pl.when(pair == pairs - 1)
    def _():
        for copy in copies(pair):
            copy.wait()


def attend_back(at, me, valid, q, k, v, lse, out_mine, grads, earlier):
    length, cols = k.shape
    width = out_mine.shape[1]
    count = length // HALVES
    pair = pl.BlockSpec((length, PAIR), lambda g: (0, g))
    mine = pl.BlockSpec((count, PAIR), lambda g: (at, g))
    here = pl.BlockSpec((count, PAIR), lambda g: (0, g))
    first = earlier is None
    near_out = () if first else (0,)
    in_specs = [pl.BlockSpec(valid.shape, lambda g: (0, 0))] + [
        mine,
        pair,
        pair,
        pl.BlockSpec((2, 1, count), lambda g: (g, 0, at)),
        pl.BlockSpec((PAIR, width), lambda g: (g, 0)),
    ]
    in_specs += [pl.BlockSpec(piece.shape, lambda g: (0, 0)) for piece in grads]
    args = [valid, q, k, v, lse, out_mine] + list(grads)
    if first:
        out_specs = [here, pair, pair]
        out_shape = [shape((count, cols))] + [shape((length, cols), F32)] * 2
        scratch = []
    else:
        in_specs += [here, pair, pair]
        args += list(earlier)
        out_specs = AWAY
        out_shape = shape((length, 3 * cols))
        scratch = [pltpu.VMEM((2, length, PAIR), BF16)] * 3 + [pltpu.SemaphoreType.DMA((2, 3))]
    return call(
        functools.partial(attend_back_kernel, first, len(grads)),
        near_in=range(6, 6 + len(grads)),
        near_out=near_out,
        grid=(cols // PAIR,),
        in_specs=in_specs,
        out_specs=out_specs,
        out_shape=out_shape,
        scratch_shapes=scratch,
        compiler_params=vmem(36),
        cost_estimate=cost(10 * count * length * cols, 8 * length * cols, count * length * cols // HEAD_DIM),
        name="attend_back",
    )(*args)


def middle_kernel(n_seq, n_out, me_ref, order_ref, *refs):
    tokens, refs = refs[:n_seq], refs[n_seq:]
    outs, refs = refs[:n_out], refs[n_out:]
    att, refs = refs[:n_seq], refs[n_seq:]
    vec_ref, normed_ref, middle_ref, mine_ref, out_ref, outs_here, att_here, tokens_here, sems = refs
    masks = block_masks(n_seq)
    me = me_ref[0]
    cols, width = mine_ref.shape
    half = tokens[0].shape[0] // HALVES
    block = n_seq * half // 2
    got_out = fetch([(ref, outs_here.at[i]) for i, ref in enumerate(outs)], sems.at[0])
    got_att = fetch([(ref, att_here.at[i]) for i, ref in enumerate(att)], sems.at[1])
    got_tokens = fetch([(ref, tokens_here.at[i]) for i, ref in enumerate(tokens)], sems.at[2])
    got_out()
    if n_out == 1:
        out_ref[...] = outs_here[0]
    else:
        n_dp = len(order_ref.cycle)
        part = width // (n_dp * n_seq)
        for i, mask in enumerate(range(n_seq)):
            for k in range(n_dp):
                start = pl.multiple_of((order_ref[k] * n_seq + (me ^ mask)) * part, part)
                for t in range(n_seq):
                    at = (k * n_seq + t) * part
                    out_ref[pl.ds(start, part), t * cols : (t + 1) * cols] = outs_here[i, at : at + part, :]
    sent = fetch([(out_ref.at[pl.ds(pl.multiple_of(me * cols, cols), cols), :], mine_ref)], sems.at[3])
    got_att()
    got_tokens()

    def step(h, carry):
        for side in range(2):
            places = range(side * n_seq // 2, (side + 1) * n_seq // 2)
            rows = pl.ds(pl.multiple_of(h * half, half), half)
            middle = jnp.concatenate([tokens_here[i, rows, :] for i in places], axis=0).astype(F32)
            middle = middle + vec_ref[0:1, :] + vec_ref[3:4, :]
            for i, mask in enumerate(masks):
                at = pl.multiple_of((me ^ mask) * cols, cols)
                first = (h * 2 + (side ^ (mask & 1))) * block
                spots = [pl.ds(pl.multiple_of(first + (t ^ (mask >> 1)) * half, half), half) for t in range(n_seq // 2)]
                found = jnp.concatenate([att_here[i, spot, :] for spot in spots], axis=0)
                middle = middle + dot(found, out_ref[pl.ds(at, cols), :], NN)
            xhat, _ = standardise(middle)
            mine = pl.ds(pl.multiple_of((h * 2 + side) * block, block), block)
            normed_ref[mine, :] = (xhat * vec_ref[4:5, :] + vec_ref[5:6, :]).astype(BF16)
            if side == 0:
                middle_ref[rows, :] = middle[:half, :]
        return carry

    lax.fori_loop(0, HALVES, step, 0)
    sent()


def middle_norm(me, order, tokens, att, outs, vecs):
    rows, width = tokens[0].shape
    n_seq = len(tokens)
    length = rows * n_seq
    cols = width // n_seq
    count = max(n_seq, len(outs))
    return call(
        functools.partial(middle_kernel, n_seq, len(outs), ME, order),
        near_in=(2 * n_seq + len(outs),),
        near_out=(0, 1),
        in_specs=[AWAY] * (2 * n_seq + len(outs)) + [NEAR],
        out_specs=[NEAR, NEAR, AWAY],
        out_shape=[shape((length, width)), shape((rows, width), F32), shape((cols, width))],
        scratch_shapes=[
            pltpu.VMEM((width, width), BF16),
            pltpu.VMEM((len(outs),) + outs[0].shape, BF16),
            pltpu.VMEM((n_seq, length, cols), BF16),
            pltpu.VMEM((n_seq, rows, width), BF16),
            pltpu.SemaphoreType.DMA((4, count)),
        ],
        compiler_params=vmem(24),
        cost_estimate=cost(2 * length * width * width, 10 * length * width),
        name="middle_norm",
    )(*tokens, *outs, *att, vecs)


def fetch(pairs, sems):
    copies = [pltpu.make_async_copy(a, b, sems.at[i]) for i, (a, b) in enumerate(pairs)]
    for copy in copies:
        copy.start()

    def wait():
        for copy in copies:
            copy.wait()

    return wait


def placed(order_ref, blocks, refs, target, start):
    if blocks.spots[0] is None:
        return [(refs[0], target)]
    cols = pl.ds(start, target.shape[1])
    return [(ref.at[:, cols], target.at[blocks.place(order_ref, i), :]) for i, ref in enumerate(refs)]


def up_kernel(ups, downs, block, order_ref, normed_ref, bias_ref, *refs):
    up_pieces, refs = refs[: len(ups.arrays)], refs[len(ups.arrays) :]
    if downs is None:
        downs, down_pieces = ups, up_pieces
    else:
        down_pieces, refs = refs[: len(downs.arrays)], refs[len(downs.arrays) :]
    up_ref, down_ref, hidden_ref, slope_ref, up_sems, down_sems = refs
    here = fetch(placed(order_ref, ups, up_pieces, up_ref, 0), up_sems)
    later = fetch(placed(order_ref, downs, down_pieces, down_ref, up_ref.shape[1]), down_sems)
    here()

    def step(i, carry):
        cols = pl.ds(pl.multiple_of(i * block, block), block)
        pre = dot(normed_ref[...], up_ref[:, cols], NN) + bias_ref[:, cols]
        phi = 0.5 + 0.5 * lax.erf(pre * math.sqrt(0.5))
        hidden_ref[:, cols] = (pre * phi).astype(BF16)
        slope_ref[:, cols] = phi + pre * (jnp.exp(-0.5 * pre * pre) * (1.0 / math.sqrt(2.0 * math.pi)))
        return carry

    lax.fori_loop(0, up_ref.shape[1] // block, step, 0)
    later()


def up_part(order, normed, bias, ups, downs, block=512):
    length, width = normed.shape
    ff = bias.shape[1]
    pieces = list(ups.arrays) + (list(downs.arrays) if downs is not None else [])
    return call(
        functools.partial(up_kernel, ups, downs, block, order),
        near_in=(0,),
        near_out=(0, 1, 2, 3),
        in_specs=[NEAR, NEAR] + [AWAY] * len(pieces),
        out_specs=[NEAR] * 4,
        out_shape=[shape((width, ff)), shape((ff, width)), shape((length, ff)), shape((length, ff), F32)],
        scratch_shapes=[pltpu.SemaphoreType.DMA((len(ups.arrays),)), pltpu.SemaphoreType.DMA((len((downs or ups).arrays),))],
        compiler_params=vmem(12),
        cost_estimate=cost(2 * length * width * ff, 8 * width * ff, 2 * length * ff),
        name="up_part",
    )(normed, bias, *pieces)


def mlp_back_kernel(first, at, block, n_grads, hidden_ref, slope_ref, up_ref, down_ref, *refs):
    grads, refs = refs[:n_grads], refs[n_grads:]
    if not first:
        refs = refs[2:]
    pre_ref, grad_ref, keep_ref, send_ref, branch_keep, branch_send, sum_ref, sems = refs
    count = 2 * keep_ref.shape[0]
    half = count // n_grads
    spots = [pl.ds(at * count + i * half, half) for i in range(n_grads)]
    ready = fetch([(ref, grad_ref.at[spot, :]) for ref, spot in zip(grads, spots)], sems)
    rows = pl.ds(at * count, count)
    side = keep_ref.shape[0]
    sides = ((0, keep_ref, branch_keep), (side, send_ref, branch_send))
    for start, _, branch_out in sides:
        branch_out[...] = dot(hidden_ref[pl.ds(at * count + start, side), :], down_ref[...], NN).astype(BF16)
    ready()

    def step(i, carry):
        cols = pl.ds(pl.multiple_of(i * block, block), block)
        grad = (slope_ref[rows, cols] * dot(grad_ref[rows, :], down_ref[cols, :], NT)).astype(BF16)
        pre_ref[rows, cols] = grad
        sum_ref[:, cols] = jnp.sum(grad.astype(F32), axis=0, keepdims=True)
        return carry

    lax.fori_loop(0, up_ref.shape[1] // block, step, 0)
    for start, back_out, _ in sides:
        back_out[...] = dot(pre_ref[pl.ds(at * count + start, side), :], up_ref[...], NT).astype(BF16)


def mlp_back(at, hidden, slope, up, down, grads, earlier, block=512):
    width = up.shape[0]
    length, ff = hidden.shape
    count = length // HALVES
    first = earlier is None
    given = 4 + len(grads)
    return call(
        functools.partial(mlp_back_kernel, first, at, min(block, ff // 2), len(grads)),
        near_in=range(given + 2),
        near_out=(0, 1, 2, 3, 4, 5),
        in_specs=[NEAR] * 4 + [AWAY] * len(grads) + ([] if first else [NEAR] * 2),
        out_specs=[NEAR] * 7,
        out_shape=[shape((length, ff)), shape((length, width))]
        + [shape((count // 2, width))] * 4
        + [shape((1, ff), F32)],
        scratch_shapes=[pltpu.SemaphoreType.DMA((len(grads),))],
        input_output_aliases={} if first else {given: 0, given + 1: 1},
        compiler_params=vmem(16),
        cost_estimate=cost(6 * count * width * ff, 8 * width * ff),
        name="mlp_back",
    )(hidden, slope, up, down, *grads, *([] if first else earlier))


def second_back_kernel(at, middle_ref, keep_ref, near_ref, far_ref, vec_ref, out_ref, grad_ref, one_ref, sum_ref, held, sems):
    half = far_ref.shape[0]
    ready = fetch([(out_ref, held)], sems)
    upstream = keep_ref[:half, :].astype(F32) + near_ref[:half, :].astype(F32) + far_ref[...].astype(F32)
    xhat, rate = standardise(middle_ref[at * half : (at + 1) * half, :])
    back = norm_back(upstream, xhat, rate, vec_ref[4:5, :])
    ready()
    grad_out = held[...].astype(F32)
    grad = grad_out + back
    one = grad.astype(BF16)
    grad_ref[...] = grad
    one_ref[...] = one
    sums = [upstream * xhat, upstream, one.astype(F32), grad_out, grad]
    sum_ref[...] = jnp.concatenate([jnp.sum(s, axis=0, keepdims=True) for s in sums], axis=0)


def second_back(at, middle_own, keep, near_part, far_part, grad_out, vecs):
    half, width = far_part.shape
    return call(
        functools.partial(second_back_kernel, at),
        near_in=(0, 1, 2, 3, 4),
        near_out=(0, 1),
        in_specs=[NEAR] * 5 + [AWAY],
        out_specs=[NEAR] * 3,
        out_shape=[shape((half, width), F32), shape((half, width)), shape((5, width), F32)],
        scratch_shapes=[pltpu.VMEM((half, width), BF16), pltpu.SemaphoreType.DMA((1,))],
        compiler_params=vmem(10),
        cost_estimate=cost(30 * half * width, 16 * half * width),
        name="second_back",
    )(middle_own, keep, near_part, far_part, vecs, grad_out)


def first_grad_kernel(n_seq, grad_ref, qkv_ref, vec_ref, *refs):
    tokens, (keep_ref, send_ref, sum_ref, last_ref) = refs[:n_seq], refs[n_seq:]
    step = pl.program_id(0)
    grad = grad_ref[...]
    total = dot(grad, qkv_ref[...], NT)
    column = jnp.sum(grad.astype(F32), axis=0, keepdims=True)
    sides = zip(tokens[: n_seq // 2], tokens[n_seq // 2 :])
    start = jnp.concatenate([jnp.where(step % 2 == 0, a[...], b[...]) for a, b in sides], axis=0).astype(F32)
    xhat, rate = standardise(start + vec_ref[0:1, :])
    back = norm_back(total, xhat, rate, vec_ref[1:2, :])
    last = jnp.concatenate([jnp.sum(t, axis=0, keepdims=True) for t in (total * xhat, total, back)], axis=0)
    total = total.astype(BF16)

    @pl.when(step == 0)
    def _():
        sum_ref[...] = column
        last_ref[...] = last

    @pl.when(step > 0)
    def _():
        sum_ref[...] += column
        last_ref[...] += last

    @pl.when(step % 2 == 0)
    def _():
        keep_ref[...] = total

    @pl.when(step % 2 == 1)
    def _():
        send_ref[...] = total


def first_grad(grad_qkv, qkv, vecs, tokens):
    length, wide = grad_qkv.shape
    n_seq = len(tokens)
    half = tokens[0].shape[0] // HALVES
    width = qkv.shape[0]
    block = length // (2 * HALVES)
    kept = pl.BlockSpec((block, width), lambda i: (i // 2, 0))
    return call(
        functools.partial(first_grad_kernel, n_seq),
        near_in=(1,),
        near_out=(0, 1),
        grid=(2 * HALVES,),
        in_specs=[
            pl.BlockSpec((block, wide), lambda i: (i, 0)),
            pl.BlockSpec(qkv.shape, lambda i: (0, 0)),
            pl.BlockSpec(vecs.shape, lambda i: (0, 0)),
        ]
        + [pl.BlockSpec((half, width), lambda i: (i // 2, 0))] * n_seq,
        out_specs=[kept, kept, pl.BlockSpec((1, wide), lambda i: (0, 0)), pl.BlockSpec((3, width), lambda i: (0, 0))],
        out_shape=[shape((length // 2, width))] * 2 + [shape((1, wide), F32), shape((3, width), F32)],
        compiler_params=vmem(20),
        cost_estimate=cost(length * wide * width, 4 * length * width),
        name="first_grad",
    )(grad_qkv, qkv, vecs, *tokens)


def out_terms_kernel(pairs, *refs):
    att, out_ref = refs[:pairs], refs[-1]
    total = None
    at = 0
    for ref in refs[pairs:-1]:
        rows = ref.shape[0]
        term = dot(jnp.concatenate([a[at : at + rows, :] for a in att], axis=1), ref[...], TN)
        total = term if total is None else total + term
        at += rows
    n_dp, rows, wide = out_ref.shape
    if wide == total.shape[1]:
        out_ref[...] = total.astype(BF16).reshape(out_ref.shape)
        return
    part = total.shape[0] // n_dp
    for i in range(n_dp):
        for t in range(rows // part):
            piece = total[i * part : (i + 1) * part, t * wide : (t + 1) * wide]
            out_ref[i, t * part : (t + 1) * part, :] = piece.astype(BF16)


def out_terms(att, grads, n_dp, rows):
    length = att[0].shape[0]
    cols = len(att) * att[0].shape[1]
    width = grads[0].shape[1]
    dims = (n_dp, rows, cols * width // (n_dp * rows))
    args = list(att) + list(grads)
    return call(
        functools.partial(out_terms_kernel, len(att)),
        near_in=range(len(att), len(att) + len(grads)),
        near_out=(0,),
        grid=(1,),
        in_specs=[pl.BlockSpec(a.shape, lambda i: (0, 0)) for a in args],
        out_specs=pl.BlockSpec(dims, lambda i: (0, 0, 0)),
        out_shape=shape(dims),
        compiler_params=vmem(16),
        cost_estimate=cost(2 * length * cols * width, 2 * length * width),
        name="out_terms",
    )(*args)


def first_back_kernel(keep_ref, near_ref, far_a, far_b, a_ref, b_ref, vec_ref, tokens_ref, out_ref, held, made, sems):
    ready = fetch([(tokens_ref, held)], sems)
    half = far_a.shape[0]
    size = keep_ref.shape[0] // HALVES
    copies = []
    for h, (far_ref, grad_ref) in enumerate(((far_a, a_ref), (far_b, b_ref))):
        mine = slice(h * size, h * size + half)
        upstream = keep_ref[mine, :].astype(F32) + near_ref[mine, :].astype(F32) + far_ref[...].astype(F32)
        if h == 0:
            ready()
        rows = slice(h * half, (h + 1) * half)
        xhat, rate = standardise(held[rows, :].astype(F32) + vec_ref[0:1, :])
        grad = grad_ref[...] + norm_back(upstream, xhat, rate, vec_ref[1:2, :])
        made[rows, :] = grad.astype(BF16)
        copy = pltpu.make_async_copy(made.at[pl.ds(h * half, half), :], out_ref.at[pl.ds(h * half, half), :], sems.at[1 + h])
        copy.start()
        copies.append(copy)
    for copy in copies:
        copy.wait()


def first_back(tokens_own, keep, near_part, far_a, far_b, grad_a, grad_b, vecs):
    rows, width = tokens_own.shape
    return call(
        first_back_kernel,
        near_in=range(7),
        in_specs=[NEAR] * 7 + [AWAY],
        out_specs=AWAY,
        out_shape=shape((rows, width)),
        scratch_shapes=[pltpu.VMEM((rows, width), BF16)] * 2 + [pltpu.SemaphoreType.DMA((1 + HALVES,))],
        compiler_params=vmem(10),
        cost_estimate=cost(30 * rows * width, 16 * rows * width),
        name="first_back",
    )(keep, near_part, far_a, far_b, grad_a, grad_b, vecs, tokens_own)


def block_masks(size):
    return [m for m in range(size) if not m & 1] + [m for m in range(size) if m & 1]


def far_bits(size):
    bits, bit = [], 2
    while bit < size:
        bits.append(bit)
        bit *= 2
    return bits


def tied(*values):
    return lax.optimization_barrier(values)


class Line:
    def __init__(self, token):
        self.token = token

    def slot(self, sends=(), work=lambda: (), inputs=(), begin=(), end=()):
        values, begun, inputs, token = tied(
            [s[0] for s in sends], [s[0] for s in begin], list(inputs), self.token
        )
        found = [lax.ppermute(value, s[1], s[2]) for value, s in zip(values, sends)]
        started = [lax.ppermute(value, s[1], s[2]) for value, s in zip(begun, begin)]
        found, done, ended, self.token = tied(found, work(*inputs), list(end), token)
        return found, done, started, ended


def swap(value, bit, size):
    return (value, "seq", [(i, i ^ bit) for i in range(size)])


def cycle(n_dp):
    wide = int(round(math.sqrt(n_dp / 2)))
    if wide < 2 or wide * (n_dp // wide) != n_dp or (n_dp // wide) % 2:
        return list(range(n_dp))
    high = n_dp // wide
    order = [z * wide for z in range(high)]
    for turn, z in enumerate(range(high - 1, -1, -1)):
        line = list(range(1, wide))
        order += [z * wide + y for y in (line[::-1] if turn % 2 else line)]
    return order


class Ring:
    def __init__(self, n_dp):
        self.n = n_dp
        order = cycle(n_dp)
        where = np.argsort(np.array(order))
        table = np.array([[order[(where[d] + k) % n_dp] for k in range(n_dp)] for d in range(n_dp)], np.int32)
        row = lax.dynamic_index_in_dim(jnp.asarray(table), lax.axis_index("dp"), 0, keepdims=False)
        self.order = row
        self.steps = Order(order)
        self.ahead = [(order[i], order[(i + 1) % n_dp]) for i in range(n_dp)]
        self.back = [(order[i], order[(i - 1) % n_dp]) for i in range(n_dp)]
        self.far = n_dp // 2
        self.near = (n_dp - 1) // 2


class Gather:
    def __init__(self, ring, own):
        self.ring = ring
        self.step = 0
        self.pending = None
        self.ahead = self.back = own
        self.pieces = [own] + [None] * (ring.n - 1)

    def sends(self):
        self.step += 1
        ahead, back = self.ahead, self.back
        if self.step == self.ring.far:
            half = ahead.shape[0] // 2
            ahead, back = ahead[:half], back[half:]
        return [(ahead, "dp", self.ring.ahead), (back, "dp", self.ring.back)]

    def take(self, found):
        self.ahead, self.back = found
        if self.step == self.ring.far:
            self.pieces[self.step] = tuple(found)
        else:
            self.pieces[-self.step], self.pieces[self.step] = found

    @property
    def left(self):
        return self.ring.far - self.step


def ring_kernel(adds, *refs):
    count = len(adds)
    values = list(refs[1 + count : -count])
    for i, (add, out) in enumerate(zip(adds, refs[-count:])):
        total = refs[1 + i][0].astype(F32)
        for _ in range(add):
            total = total + values.pop(0)[...].astype(F32)
        out[...] = total.astype(out.dtype)


def ring_blocks(order, items, dtype=BF16):
    n_dp = order.shape[0]
    args, in_specs, outs, out_specs = [], [], [], []
    for terms, k, _ in items:
        dims = terms.shape[1:]
        in_specs.append(pl.BlockSpec((1,) + dims, lambda i, at, k=k % n_dp: (at[k], 0, 0)))
        out_specs.append(pl.BlockSpec(dims, lambda i, at: (0, 0)))
        outs.append(shape(dims, dtype))
        args.append(terms)
    for _, _, values in items:
        for value in values:
            in_specs.append(pl.BlockSpec(value.shape, lambda i, at: (0, 0)))
            args.append(value)
    return pl.pallas_call(
        functools.partial(ring_kernel, [len(i[2]) for i in items]),
        grid_spec=pltpu.PrefetchScalarGridSpec(
            num_scalar_prefetch=1, grid=(1,), in_specs=in_specs, out_specs=out_specs
        ),
        out_shape=outs,
        compiler_params=vmem(16),
        name="ring_blocks",
    )(order, *args)


def table_kernel(me_ref, lead_ref, a_ref, b_ref, last_ref, ua_ref, ub_ref, column_ref, out_ref):
    me = me_ref[0]
    width = out_ref.shape[1]
    cols = column_ref.shape[1] // 3
    extra = ua_ref.shape[1] * (width // cols) // width
    part = 128 // extra
    sums = a_ref[...] + b_ref[...]
    last = last_ref[...]
    column = column_ref[...]
    out_ref[...] = jnp.zeros_like(out_ref)
    out_ref[0:2, :] = last[0:2]
    mine = pl.ds(pl.multiple_of(me * cols, 128), cols)
    out_ref[2:3, mine] = column[:, :cols]
    out_ref[3:4, mine] = column[:, 2 * cols :]
    out_ref[4:5, :] = sums[2:3]
    out_ref[5:7, :] = sums[0:2]
    out_ref[7:8, :] = sums[3:4]
    start = last[2:3] + sums[4:5]
    out_ref[8:9, :] = lead_ref[0:1, 0:1] * start
    out_ref[9:10, :] = start
    up = jnp.broadcast_to(ua_ref[...] + ub_ref[...], (8, width))
    here = lax.broadcasted_iota(jnp.int32, (1, width), 1) % 128 // part == me
    for k in range(extra):
        moved = pltpu.roll(up, ((me - k) * part + width) % width, 1)
        out_ref[10 + k : 11 + k, :] = jnp.where(here, moved[0:1, :], 0.0)


def small_table(me, lead, *args):
    width = args[0].shape[1]
    return pl.pallas_call(
        functools.partial(table_kernel, ME),
        grid=(1,),
        in_specs=[pl.BlockSpec(a.shape, lambda i: (0, 0)) for a in (lead, *args)],
        out_specs=pl.BlockSpec((16, width), lambda i: (0, 0)),
        out_shape=shape((16, width), F32),
        compiler_params=vmem(4),
        name="small_table",
    )(lead, *args)


def halve_kernel(bit, *refs):
    mine_ref, other_ref = refs[-2:]
    wide = mine_ref.shape[1]
    side = lax.rem(lax.div(lax.axis_index("dp"), bit), 2)
    for at, target in ((side, mine_ref), (1 - side, other_ref)):
        for i in range(wide // 128):
            total = 0.0
            for ref in refs[:-2]:
                total = total + ref[:, pl.ds(pl.multiple_of((2 * i + at) * 128, 128), 128)]
            target[:, i * 128 : (i + 1) * 128] = total


def halve(bit, values):
    rows, wide = values[0].shape
    return pl.pallas_call(
        functools.partial(halve_kernel, bit),
        in_specs=[NEAR] * len(values),
        out_specs=[NEAR] * 2,
        out_shape=[shape((rows, wide // 2), F32)] * 2,
        compiler_params=vmem(2),
        name="halve",
    )(*values)


def owner_kernel(count, order_ref, me_ref, term_ref, *refs):
    part = refs[-1].shape[0]
    outs = refs[-count:]
    for mask, out in enumerate(outs):
        rows = pl.ds(pl.multiple_of((me_ref[0] ^ mask) * part, part), part)
        total = term_ref[0, rows, :].astype(F32)
        for ref in refs[:-count]:
            total = total + ref[rows, :].astype(F32)
        out[...] = total.astype(BF16)


def owner_blocks(order, me, terms, values, n_seq):
    _, rows, wide = terms.shape
    part = rows // n_seq
    if part % 16:
        (total,) = ring_blocks(order, [(terms, 0, values)])
        blocks = total.reshape(n_seq, part, wide)
        return [lax.dynamic_index_in_dim(blocks, me[0] ^ m, 0, keepdims=False) for m in range(n_seq)]
    return pl.pallas_call(
        functools.partial(owner_kernel, n_seq),
        grid_spec=pltpu.PrefetchScalarGridSpec(
            num_scalar_prefetch=2,
            grid=(1,),
            in_specs=[pl.BlockSpec((1, rows, wide), lambda i, at, me: (at[0], 0, 0))]
            + [pl.BlockSpec((rows, wide), lambda i, at, me: (0, 0))] * len(values),
            out_specs=[pl.BlockSpec((part, wide), lambda i, at, me: (0, 0))] * n_seq,
        ),
        out_shape=[shape((part, wide))] * n_seq,
        compiler_params=vmem(8),
        name="owner_blocks",
    )(order, me, terms, *values)


def unpack_kernel(groups, me_ref, out_ref, *refs):
    outs, last_ref = refs[-len(groups) - 1 : -1], refs[-1]
    pieces = refs[: -len(groups) - 1]
    part = last_ref.shape[0]
    cols = out_ref.shape[1]
    for t in range(out_ref.shape[0] // part):
        last_ref[:, t * cols : (t + 1) * cols] = out_ref[t * part : (t + 1) * part, :].astype(F32)
    n_seq = len(pieces)
    for mask, ref in enumerate(pieces):
        at = 0
        for count, out in zip(groups, outs):
            wide = out.shape[1] // (count * n_seq)
            for i in range(count):
                start = pl.multiple_of((i * n_seq + (me_ref[0] ^ mask)) * wide, 128)
                out[:, pl.ds(start, wide)] = ref[:, at : at + wide].astype(F32)
                at += wide


def unpack(groups, widths, pieces, out_block):
    part = pieces[0].shape[0]
    n_seq = len(pieces)
    if any((wide // n_seq // count) % 128 for count, wide in zip(groups, widths)):
        whole = flipped(dict(enumerate(pieces)), n_seq)
        outs, at = [], 0
        for count, wide in zip(groups, widths):
            mine = whole[:, :, at : at + wide // n_seq].reshape(n_seq, part, count, -1)
            outs.append(jnp.moveaxis(mine, 0, 2).reshape(part, wide).astype(F32))
            at += wide // n_seq
        last = out_block.reshape(-1, part, out_block.shape[1])
        return *outs, jnp.moveaxis(last, 0, 1).reshape(part, -1).astype(F32)
    full = list(widths) + [out_block.size // part]
    return pl.pallas_call(
        functools.partial(unpack_kernel, groups, ME),
        grid=(1,),
        in_specs=[pl.BlockSpec(out_block.shape, lambda i: (0, 0))]
        + [pl.BlockSpec(pieces[0].shape, lambda i: (0, 0))] * n_seq,
        out_specs=[pl.BlockSpec((part, wide), lambda i: (0, 0)) for wide in full],
        out_shape=[shape((part, wide), F32) for wide in full],
        compiler_params=vmem(8),
        name="unpack",
    )(out_block, *pieces)


class Scatter:
    def __init__(self, ring, terms):
        self.ring = ring
        self.terms = terms
        self.step = 0
        self.pending = None
        count = len(terms)
        found = ring_blocks(
            ring.order, [(t, ring.far, ()) for t in terms] + [(t, -ring.near, ()) for t in terms]
        )
        self.ahead, self.back = found[:count], found[count:]

    def sends(self):
        self.step += 1
        found = [(v, "dp", self.ring.ahead) for v in self.ahead]
        if self.step > self.ring.far - self.ring.near:
            found += [(v, "dp", self.ring.back) for v in self.back]
        return found

    def take(self, found):
        count = len(self.terms)
        left = self.ring.far - self.step
        ahead, back = found[:count], found[count:]
        if left:
            items = [(t, left, (v,)) for t, v in zip(self.terms, ahead)]
            items += [(t, -left, (v,)) for t, v in zip(self.terms, back)]
            found = ring_blocks(self.ring.order, items)
            ahead, back = found[:count], found[count:]
        self.ahead = ahead
        if back:
            self.back = back

    @property
    def left(self):
        return self.ring.far - self.step

    def total(self, dtype=F32):
        items = [(t, 0, (a, b)) for t, a, b in zip(self.terms, self.ahead, self.back)]
        return ring_blocks(self.ring.order, items, dtype)


def joint_kernel(items, order_ref, q_ref, o_ref, *refs):
    values, outs = list(refs[: -len(items)]), refs[-len(items) :]
    _, rows, edge = q_ref.shape
    _, part, width = o_ref.shape
    for (k, low, high, added), target in zip(items, outs):
        cols = target.shape[1] - edge
        value = values.pop(0) if added else None
        at = order_ref[k]

        def put(source, from_rows, row, lanes):
            cuts = sorted({row, row + len(from_rows)} | ({max(row, min(c, row + len(from_rows))) for c in added} if added else set()))
            for a, b in zip(cuts, cuts[1:]):
                total = source[from_rows[a - row] : from_rows[b - row - 1] + 1]
                if added and added[0] <= a and b <= added[1]:
                    total = (total.astype(F32) + value[a - added[0] : b - added[0], lanes].astype(F32)).astype(BF16)
                target[a - low : b - low, lanes] = total

        put(q_ref.at[at, :, slice(0, edge)], range(low, high), low, slice(0, edge))
        for t in range(rows // part):
            a, b = max(low, t * part), min(high, (t + 1) * part)
            if a < b:
                lanes = slice(t * cols, (t + 1) * cols)
                put(o_ref.at[at, :, lanes], range(a - t * part, b - t * part), a, slice(edge, edge + cols))


class JointScatter:
    def __init__(self, ring, qkv, out):
        self.ring = ring
        self.qkv = qkv
        self.out = out
        self.step = 0
        self.pending = None
        rows = qkv.shape[1]
        if ring.far:
            far = ring.far
            self.ahead, self.back = self.blocks([(far, 0, rows // 2, None), (far, rows // 2, rows, None)], ())

    def blocks(self, items, values):
        n_dp, rows, edge = self.qkv.shape
        _, part, width = self.out.shape
        wide = edge + width * part // rows
        items = [(k % n_dp, low, high, added) for k, low, high, added in items]
        return call(
            functools.partial(joint_kernel, items, self.ring.steps),
            near_in=range(2 + len(values)),
            near_out=range(len(items)),
            in_specs=[NEAR] * (2 + len(values)),
            out_specs=[NEAR] * len(items),
            out_shape=[shape((high - low, wide)) for _, low, high, _ in items],
            compiler_params=vmem(4),
            name="joint_blocks",
        )(self.qkv, self.out, *values)

    def sends(self):
        self.step += 1
        return [(self.ahead, "dp", self.ring.ahead), (self.back, "dp", self.ring.back)]

    def take(self, found):
        left = self.ring.far - self.step
        rows = self.qkv.shape[1]
        if left:
            spans = ((0, rows // 2), (rows // 2, rows)) if self.step == 1 else ((0, rows), (0, rows))
            found = self.blocks([(sign * left, 0, rows, span) for sign, span in zip((1, -1), spans)], found)
        self.ahead, self.back = found

    @property
    def left(self):
        return self.ring.far - self.step

    def total(self, me, n_seq, dtype=BF16, beside=()):
        n_dp, rows, edge = self.qkv.shape
        _, part, width = self.out.shape
        wide = edge + width * part // rows
        values = [self.ahead, self.back]
        if self.ring.far == 1:
            values = [jnp.concatenate(values, axis=0)] * 2
            values[1] = jnp.zeros_like(values[1])
        cuts = 1 if rows // n_seq % 16 else n_seq
        more = list(beside) if cuts > 1 else []
        full = edge + (more[0].shape[1] if more else 0)
        args = [self.qkv, self.out] + values + more
        found = call(
            functools.partial(joint_owner_kernel, cuts, edge, dtype == F32, ME),
            near_in=range(len(args)),
            near_out=range(cuts + (dtype != F32)),
            in_specs=[NEAR] * len(args),
            out_specs=[NEAR] * cuts + [AWAY if dtype == F32 else NEAR],
            scratch_shapes=[pltpu.VMEM((part, width), F32), pltpu.SemaphoreType.DMA((1,))] if dtype == F32 else [],
            out_shape=[shape((rows // cuts, full))] * cuts + [shape((part, width), dtype)],
            compiler_params=vmem(8),
            name="joint_owner",
        )(*args)
        if cuts == n_seq:
            return list(found[:n_seq]), found[n_seq]
        blocks = found[0].reshape(n_seq, rows // n_seq, edge)
        blocks = [lax.dynamic_index_in_dim(blocks, me[0] ^ m, 0, keepdims=False) for m in range(n_seq)]
        return beside_all(blocks, beside), found[1]


def beside_all(blocks, beside):
    return [jnp.concatenate(pair, axis=1) for pair in zip(blocks, beside)] if beside else blocks


def joint_owner_kernel(cuts, edge, last_away, me_ref, q_ref, o_ref, *refs):
    if last_away:
        refs, (last, target, sems) = refs[:-3], refs[-3:]
        refs = (*refs, target)
    values, outs = refs[: -cuts - 1], refs[-cuts - 1 :]
    values, more = values[:2], values[2:]
    part = outs[0].shape[0]
    for mask, target in enumerate(outs[:-1]):
        rows = pl.ds(pl.multiple_of((me_ref[0] ^ mask) * part, part), part) if cuts > 1 else slice(None)
        total = q_ref[lax.axis_index("dp"), rows, :].astype(F32)
        for ref in values:
            total = total + ref[rows, :edge].astype(F32)
        target[:, :edge] = total.astype(BF16)
        if more:
            target[:, edge:] = more[mask][...]
    part, width = outs[-1].shape
    cols = values[0].shape[1] - edge
    for t in range(width // cols):
        total = o_ref[lax.axis_index("dp"), :, t * cols : (t + 1) * cols].astype(F32)
        for ref in values:
            total = total + ref[t * part : (t + 1) * part, edge:].astype(F32)
        outs[-1][:, t * cols : (t + 1) * cols] = total.astype(outs[-1].dtype)
    if last_away:
        fetch([(outs[-1], last)], sems)()


class ApartScatter(Scatter):
    def __init__(self, ring, qkv, out):
        super().__init__(ring, [qkv, out])

    def total(self, me, n_seq, dtype=BF16, beside=()):
        qkv, out = self.terms
        blocks = owner_blocks(self.ring.order, me, qkv, (self.ahead[0], self.back[0]), n_seq)
        (out_sum,) = ring_blocks(self.ring.order, [(out, 0, (self.ahead[1], self.back[1]))])
        return beside_all(blocks, beside), out_sum


def flipped(pieces, bits):
    me = lax.axis_index("seq")
    size = len(pieces)
    held = [pieces[m] for m in range(size)]
    bit = 1
    while bit < size:
        turned = (me & bit) != 0
        held = [jnp.where(turned, held[m ^ bit], held[m]) for m in range(size)]
        bit *= 2
    return jnp.stack(held)


def make_body(n_dp, n_seq):
    masks = block_masks(n_seq)
    far = far_bits(n_seq)
    far_masks = [m for m in range(n_seq) if not m & 1]

    def body(
        tokens,
        lead_hours,
        valid_counts,
        patch_mask,
        first_gain,
        first_shift,
        qkv_weight,
        query_bias,
        value_bias,
        out_weight,
        out_bias,
        second_gain,
        second_shift,
        up_weight,
        up_bias,
        down_weight,
        down_bias,
        lead_weight,
        lead_bias,
        cotangent,
    ):
        me = lax.axis_index("seq")
        rows, width = tokens.shape[1], tokens.shape[2]
        length = rows * n_seq
        half = rows // HALVES
        part = qkv_weight.shape[0]
        ff_part = down_weight.shape[0]
        ff = up_weight.shape[1]
        extra = ff_part // part
        cols = width // n_seq
        ff_cols = ff // n_seq
        lead = lead_hours[0].astype(F32) / 100.0
        count = valid_counts[0]
        ring = Ring(n_dp)
        me_ref = me.reshape(1).astype(jnp.int32)
        lead_ref = jnp.broadcast_to(lead, (8, 128))
        order = ring.steps

        def far_gather(own, at_bit):
            return [swap(own[m], far[at_bit], n_seq) for m in sorted(own)]

        line = Line(me_ref)

        def run(sends=(), work=lambda: (), inputs=(), start=(), finish=(), begin=(), end=()):
            sends, begin, end = list(sends), list(begin), list(end)
            plan = []
            for ring_part in finish:
                if ring_part.pending is not None:
                    plan.append((ring_part, "end", len(end), len(ring_part.pending)))
                    end += ring_part.pending
                    ring_part.pending = None
            n_sends, n_begin = len(sends), len(begin)
            ahead = []
            for ring_part in start:
                mine = ring_part.sends()
                if ring_part in finish:
                    plan.append((ring_part, "now", len(ahead), len(mine)))
                    ahead += mine
                else:
                    plan.append((ring_part, "later", len(begin), len(mine)))
                    begin += mine
            found, done, begun, ended = line.slot(ahead + sends, work, inputs, begin, end)
            early, found = found[: len(ahead)], found[len(ahead) :]
            n_end = len(end) - sum(p[3] for p in plan if p[1] == "end")
            for ring_part, kind, at, size in plan:
                if kind == "end":
                    ring_part.take(list(ended[at : at + size]))
                elif kind == "now":
                    ring_part.take(list(early[at : at + size]))
                else:
                    ring_part.pending = list(begun[at : at + size])
            return list(found[:n_sends]), done, list(begun[:n_begin]), list(ended[:n_end])

        def near_all(held):
            return [swap(held[m], 1, n_seq) for m in sorted(held)]

        def with_near(held, found):
            held.update({m ^ 1: v for m, v in zip(sorted(held), found)})

        def with_far(held, found, at_bit):
            held.update({m ^ far[at_bit]: v for m, v in zip(sorted(held), found)})

        def rest_far(held):
            for i in range(1, len(far)):
                found, _, _, _ = line.slot(far_gather(held, i))
                with_far(held, found, i)

        vectors = [
            first_gain,
            first_shift,
            query_bias,
            value_bias,
            out_bias,
            second_gain,
            second_shift,
            down_bias,
            lead_weight,
            lead_bias,
            up_bias,
        ]
        kinds = 10 + extra
        packed = pack(n_dp, n_seq, me_ref, qkv_weight, up_weight, vectors)

        def masked_rows(cot, mask, count):
            positions = me * rows + jnp.arange(rows, dtype=jnp.int32)
            weight = (mask * (positions < count).astype(jnp.int32)).astype(BF16)[:, None]
            return tuple(cot[h * half : (h + 1) * half] * weight[h * half : (h + 1) * half] for h in range(HALVES))

        found, outs_own, _, _ = run(
            [swap(packed[m], m, n_seq) for m in range(1, n_seq)],
            masked_rows,
            (cotangent[0], patch_mask[0], count),
        )
        one_own = join_one(n_seq, me_ref, [packed[0]] + list(found), out_weight)

        g_one = Gather(ring, one_own)

        def steps(*rings):
            mine = [g for g in rings if g.left]
            return dict(start=mine, finish=mine)

        tokens_held = {0: tokens[0]}
        grad_held = [{0: g} for g in outs_own]
        found, _, _, _ = run([swap(packed[n_seq + m], m, n_seq) for m in range(1, n_seq)], **steps(g_one))
        up_found = [packed[n_seq]] + list(found)
        _, (two_own,), tokens_far, _ = run(
            work=lambda *a: (join_two(n_seq, me_ref, a[:-1], a[-1]),),
            inputs=(*up_found, down_weight),
            begin=far_gather(tokens_held, 0),
            **steps(g_one),
        )
        g_two = Gather(ring, two_own)
        _, _, _, tokens_far = run(end=tokens_far, **steps(g_one))
        with_far(tokens_held, tokens_far, 0)
        rest_far(tokens_held)
        while g_one.left > 1:
            run(**steps(g_one))
        found, _, _, _ = run(near_all(tokens_held), **steps(g_one))
        with_near(tokens_held, found)

        valid = jnp.broadcast_to(count, (8, 128))
        pairs = cols // PAIR

        def begun(part_of):
            return dict(start=[part_of] if part_of.left else [])

        tokens_by = [tokens_held[m] for m in masks]
        ones_blocks = ordered(ring.order, g_one.pieces)

        def attend_first(*a):
            blocks = Blocks(a[n_seq:], ones_blocks.spots, ones_blocks.rows)
            out_pack = middle_columns(blocks, 3 * cols, cols, n_dp)
            found = project(me_ref, order, lead_ref, a[:n_seq], blocks, kinds)
            return out_pack, found

        _, (out_pack, (normed, q, k, v, qkv, table, vecs)), _, _ = run(
            work=attend_first, inputs=tokens_by + list(ones_blocks.arrays), **steps(g_two)
        )
        out_held = {0: out_pack}

        def up_bias_of(table):
            u_bias = table[10 : 10 + extra].reshape(extra, n_dp, n_seq, part)
            u_bias = lax.dynamic_index_in_dim(u_bias, me, 2, keepdims=False)
            return jnp.swapaxes(u_bias, 0, 1).reshape(1, ff_cols)

        def attend_rest(q, k, v, table):
            lses, attended = [], None
            for p in range(pairs):
                attended, lse = attend(n_seq, p, me_ref, valid, q, k, v, attended)
                lses.append(lse)
            return attended, jnp.concatenate(lses, axis=0), up_bias_of(table)

        found, (attended, lse, u_bias), _, _ = run(
            far_gather(out_held, 0), work=attend_rest, inputs=(q, k, v, table), **steps(g_two)
        )
        with_far(out_held, found, 0)
        rest_far(out_held)
        att_held = {0: attended}
        nearby = near_all(out_held)
        found, _, _, _ = run(far_gather(att_held, 0) + nearby, **steps(g_two))
        with_near(out_held, found[-len(nearby) :])
        with_far(att_held, found[: -len(nearby)], 0)
        rest_far(att_held)
        found, _, _, _ = run(near_all(att_held))
        with_near(att_held, found)

        def out_whole(pieces):
            if part % 16 == 0:
                return pieces
            blocks = flipped(dict(enumerate(pieces)), n_seq).reshape(n_seq, n_dp, n_seq, part, cols)
            return [jnp.transpose(blocks, (1, 0, 3, 2, 4)).reshape(width, width)]

        found, (normed_two, middle_own, out_mine), _, _ = run(
            far_gather(grad_held[0], 0),
            work=lambda tok, att, outs, vecs: middle_norm(me_ref, order, tok, att, out_whole(outs), vecs),
            inputs=(
                tokens_by,
                [att_held[m] for m in masks],
                [out_held[m] for m in range(n_seq)],
                vecs,
            ),
            **steps(g_two),
        )
        with_far(grad_held[0], found, 0)
        rest_far(grad_held[0])
        while g_two.left:
            run(**steps(g_two))
        twos = ordered(ring.order, g_two.pieces)
        downs = twos
        if twos.spots[0] is None:
            whole = twos.arrays[0]
            twos = Blocks([whole[:, :ff_cols]], [None], whole.shape[0])
            downs = Blocks([whole[:, ff_cols:].reshape(ff_cols, width)], [None], ff_cols)
        nearby = near_all(grad_held[0])
        found, (up, down, hidden, slope), _, _ = run(
            far_gather(grad_held[1], 0) + nearby,
            work=lambda n, b, a, d: up_part(
                order,
                n,
                b,
                Blocks(a, twos.spots, twos.rows),
                Blocks(d, downs.spots, downs.rows) if downs is not twos else None,
            ),
            inputs=(normed_two, u_bias, list(twos.arrays), list(downs.arrays) if downs is not twos else ()),
        )
        with_near(grad_held[0], found[-len(nearby) :])
        with_far(grad_held[1], found[: -len(nearby)], 0)
        rest_far(grad_held[1])

        def half_sum(keep, other):
            found = {}
            for at, m in enumerate(far_masks):
                if m:
                    rows_at = slice(at * half, (at + 1) * half)
                    found[m] = (keep[rows_at].astype(F32) + other[rows_at].astype(F32)).astype(BF16)
            return found

        def far_first(held):
            bit = far[-1]
            return [swap(held[m], bit, n_seq) for m in sorted(held) if m & bit]

        def far_rest(held, found):
            for at, bit in enumerate(reversed(far)):
                upper = sorted(m for m in held if m & bit)
                if at:
                    found, _, _, _ = line.slot([swap(held[m], bit, n_seq) for m in upper])
                kept = {m: held[m] for m in held if not m & bit}
                for m, value in zip(upper, found):
                    low = m ^ bit
                    if low in kept:
                        value = (kept[low].astype(F32) + value.astype(F32)).astype(BF16)
                    kept[low] = value
                held = kept
            return held[0]

        found, (pre, grad_out, keep_a, send_a, branch_keep_a, branch_send_a, sum_a), _, _ = run(
            near_all(grad_held[1]),
            work=lambda *a: mlp_back(0, *a, None),
            inputs=(hidden, slope, up, down, [grad_held[0][m] for m in masks]),
        )
        with_near(grad_held[1], found)
        (near_a,), (pre, grad_out, keep_b, send_b, branch_keep_b, branch_send_b, sum_b), _, _ = run(
            [swap(send_a, 1, n_seq)],
            work=lambda *a: mlp_back(1, *a),
            inputs=(hidden, slope, up, down, [grad_held[1][m] for m in masks], (pre, grad_out)),
        )
        def moved(value, axis, bit):
            count = n_dp if axis == "dp" else n_seq
            return lax.ppermute(value, axis, [(i, i ^ bit) for i in range(count)])

        held_a = half_sum(keep_a, near_a)
        sends = far_first(held_a)

        def weight_terms(hidden, grad_out, normed_two, pre):
            up_terms = dot(normed_two, pre, TN).astype(BF16).reshape(n_dp, n_seq * part, ff_cols)
            return dot(hidden, grad_out, TN).astype(BF16).reshape(n_dp, ff_part, width), up_terms

        found, (down_terms, up_terms), _, _ = run(
            sends + [swap(send_b, 1, n_seq)], work=weight_terms, inputs=(hidden, grad_out, normed_two, pre)
        )
        far_a, near_b = far_rest(held_a, found[: len(sends)]), found[-1]
        held_b = half_sum(keep_b, near_b)

        def back_half(at):
            return lambda *a: tuple(second_back(at, *a))

        scatter_two = JointScatter(ring, up_terms, down_terms)
        sends = far_first(held_b)
        found, (grad_mid_a, one_a, sums_a), _, _ = run(
            sends + [swap(branch_send_a, 1, n_seq), swap(branch_send_b, 1, n_seq)],
            work=back_half(0),
            inputs=(middle_own, keep_a, near_a, far_a, outs_own[0], vecs),
            **steps(scatter_two),
        )
        far_b, branch_other = far_rest(held_b, found[: len(sends)]), found[-2:]
        one_far_a, (grad_mid_b, one_b, sums_b), _, _ = run(
            far_gather({0: one_a}, 0),
            work=back_half(1),
            inputs=(middle_own, keep_b, near_b, far_b, outs_own[1], vecs),
            **begun(scatter_two),
        )
        one_held_a = {0: one_a}
        with_far(one_held_a, one_far_a, 0)
        rest_far(one_held_a)
        one_held_b = {0: one_b}
        found, _, one_far_b, _ = run(
            near_all(one_held_a), begin=far_gather(one_held_b, 0), finish=[scatter_two]
        )
        with_near(one_held_a, found)
        _, (dq_a, dk_a, dv_a), _, one_far_b = run(
            work=lambda *a: attend_back(0, me_ref, valid, *a, None),
            inputs=(q, k, v, lse, out_mine, [one_held_a[m] for m in masks]),
            end=one_far_b,
            **begun(scatter_two),
        )
        with_far(one_held_b, one_far_b, 0)
        rest_far(one_held_b)
        found, _, _, _ = run(near_all(one_held_b), finish=[scatter_two])
        with_near(one_held_b, found)
        ones = [one_held_a[m] for m in masks] + [one_held_b[m] for m in masks]

        branch_held = {
            m: jnp.concatenate([value, half_sum(branch_keep_b, branch_other[1])[m]], axis=0)
            for m, value in half_sum(branch_keep_a, branch_other[0]).items()
        }

        def second_attend(q, k, v, lse, out_mine, grads, earlier, att, ones):
            sums = out_terms(att, ones, n_dp, part if part % 16 else n_seq * part)
            return attend_back(1, me_ref, valid, q, k, v, lse, out_mine, grads, earlier), sums

        branch_far, (grad_qkv, out_sums), _, _ = run(
            far_first(branch_held),
            work=second_attend,
            inputs=(
                q,
                k,
                v,
                lse,
                out_mine,
                [one_held_b[m] for m in masks],
                (dq_a, dk_a, dv_a),
                [attended],
                ones,
            ),
            **steps(scatter_two),
        )
        branch_far = far_rest(branch_held, branch_far)

        qkv_terms = dot(normed, grad_qkv, TN).astype(BF16).reshape(n_dp, n_seq * part, 3 * cols)
        scatter_one = (ApartScatter if part % 16 else JointScatter)(ring, qkv_terms, out_sums)
        late = [scatter_two] if scatter_two.left else []

        def far_moved(held):
            if not far:
                return []
            return [moved(held[m], "seq", far[-1]) for m in sorted(held) if m & far[-1]]

        def now(*beside):
            mine = [scatter_one] if scatter_one.left else []
            return dict(start=mine, finish=mine + list(beside))

        def final_rows(keep_a, keep_b, near_a, near_b, far_part, mid, bias):
            total = jnp.concatenate([keep_a[:half], keep_b[:half]], axis=0).astype(F32)
            total = total + jnp.concatenate([near_a[:half], near_b[:half]], axis=0).astype(F32)
            return (mid + (total + far_part.astype(F32) + bias[6:7])).astype(BF16)

        late = [scatter_two] if scatter_two.left else []
        options = now()
        _, (gn_keep, gn_send, column_sums, last_sums), _, _ = run(
            work=lambda g: first_grad(g, qkv, vecs, tokens_by),
            inputs=(grad_qkv,),
            start=options["start"] + late,
            finish=options["finish"] + late,
        )
        while scatter_two.left:
            run(**steps(scatter_two))
        plain = (width // n_dp) % 128 == 0 and extra == n_seq and n_seq * part == 128

        bits = []
        while 2 ** len(bits) < n_dp:
            bits.append(2 ** len(bits))
        bits = bits if plain else []
        at_dp = lax.axis_index("dp")

        def loose_table():
            sums = sums_a + sums_b
            table = last_sums
            start_sums = table[2:3] + sums[4:5]
            q_sum = lax.dynamic_update_slice(jnp.zeros((1, width), F32), column_sums[:, :cols], (0, me * cols))
            v_sum = lax.dynamic_update_slice(jnp.zeros((1, width), F32), column_sums[:, 2 * cols :], (0, me * cols))
            u_sum = jnp.swapaxes((sum_a + sum_b).reshape(n_dp, extra, part), 0, 1)
            u_sum = lax.dynamic_update_index_in_dim(jnp.zeros((extra, n_dp, n_seq, part), F32), u_sum, me, 2)
            rows_out = [table[0:2], q_sum, v_sum, sums[2:3], sums[0:2], sums[3:4], lead * start_sums, start_sums]
            table = jnp.concatenate(rows_out + [u_sum.reshape(extra, width)], axis=0)
            return lax.psum_scatter(table, ("dp", "seq"), scatter_dimension=1, tiled=True)

        seq_bits = far + ([1] if n_seq > 1 else []) if plain else []

        def make_table():
            if not plain:
                return loose_table()
            return small_table(
                me_ref, lead_ref, sums_a, sums_b, last_sums, sum_a, sum_b, column_sums
            )

        def hop(held):
            if bits:
                bit = bits.pop(0)
                mine, other = halve(bit, held)
                return mine, [(other, "dp", [(i, i ^ bit) for i in range(n_dp)])]
            total = sum(held[1:], held[0])
            if seq_bits:
                return total, [swap(total, seq_bits.pop(0), n_seq)]
            return total, []

        def totals():
            blocks, total = scatter_two.total(me_ref, n_seq, F32)
            return *blocks, total

        mine, small = hop([make_table()])
        found, (*up_blocks, down_grad), _, _ = run([swap(gn_send, 1, n_seq)] + small, work=totals, **now())
        gn_near = found[0]
        held = [mine] + found[1:]
        size = half * len(far_masks)
        gn_held_a = half_sum(gn_keep[:size], gn_near[:size])
        mine, small = hop(held)
        sends = far_first(gn_held_a)
        found, (gn_held_b,), _, _ = run(
            sends + small, work=lambda k, n: (half_sum(k[size:], n[size:]),), inputs=(gn_keep, gn_near), **now()
        )
        gn_far_a = far_rest(gn_held_a, found[: len(sends)])
        held = [mine] + found[len(sends) :]
        mine, small = hop(held)
        sends = far_first(gn_held_b)
        found, (block_out,), _, _ = run(
            sends + small,
            work=lambda *a: (final_rows(*a),),
            inputs=(branch_keep_a, branch_keep_b, branch_other[0], branch_other[1], branch_far, middle_own, vecs),
            **now(),
        )
        gn_far_b = far_rest(gn_held_b, found[: len(sends)])
        held = [mine] + found[len(sends) :]
        while scatter_one.left:
            run(**steps(scatter_one))
        qkv_blocks, out_sum = scatter_one.total(me_ref, n_seq, beside=up_blocks)
        moves = []
        for dp_at in range(n_dp):
            for seq_at in range(n_seq):
                moves.append((dp_at * n_seq + seq_at, seq_at * n_dp + dp_at))
        final = [(out_sum, ("dp", "seq"), moves)] + [swap(qkv_blocks[m], m, n_seq) for m in range(1, n_seq)]

        mine, small = hop(held)
        found, (tokens_grad,), _, _ = run(
            final + small,
            work=lambda *a: (first_back(*a),),
            inputs=(tokens[0], gn_keep, gn_near, gn_far_a, gn_far_b, grad_mid_a, grad_mid_b, vecs),
        )
        last, held = found[: len(final)], [mine] + found[len(final) :]
        while bits or seq_bits:
            mine, small = hop(held)
            found, _, _, _ = run(small)
            held = [mine] + found
        small_sums = sum(held[1:], held[0])
        if plain:
            small_sums = lax.dynamic_slice_in_dim(small_sums, me * part, part, 1)
        owned = small_sums[:kinds]
        qkv_weight_grad, up_weight_grad, out_weight_grad = unpack(
            (3, n_dp), (3 * width, ff), [qkv_blocks[0]] + list(last[1:]), last[0]
        )
        return (
            block_out[None],
            tokens_grad[None],
            owned[0],
            owned[1],
            qkv_weight_grad,
            owned[2],
            owned[3],
            out_weight_grad,
            owned[4],
            owned[5],
            owned[6],
            up_weight_grad,
            jnp.concatenate([owned[10 + i] for i in range(extra)]),
            down_grad[0] if down_grad.ndim == 3 else down_grad,
            owned[7],
            owned[8],
            owned[9],
        )

    return body


def solution(mesh):
    both = P(("dp", "seq"))
    matrix = P(("dp", "seq"), None)
    tokens = P("dp", "seq", None)
    in_specs = (tokens, P("dp"), P("dp"), P("dp", "seq"), both, both, matrix, both, both, matrix, both, both, both)
    in_specs += (matrix, both, matrix, both, both, both, tokens)
    out_specs = (tokens, tokens, both, both, matrix, both, both, matrix, both, both, both, matrix, both, matrix)
    out_specs += (both, both, both)
    return jax.shard_map(
        make_body(mesh.shape["dp"], mesh.shape["seq"]),
        mesh=mesh,
        in_specs=in_specs,
        out_specs=out_specs,
        check_vma=False,
    )
```
